32 devices in a mesh: dp: 4 (over y, x), tensor: 8 (over z, core).
Axes of the slice: x: 2, y: 2, z: 4, core: 2. Of those that a mesh axis runs over, the one named last changes fastest.
Arguments:
- tokens: bfloat16 [4096, 2048], P(('dp', 'tensor')), may hold values from -6 to 6
- segment_ids: int32 [4, 1024], P('dp'), may hold values from 0 to 3, never falling along the last dimension, each value on 1 to 512 neighbouring positions
- w_query: bfloat16 [2048, 2048], P(None, 'tensor'), may hold values from -0.125 to 0.125
- w_key: bfloat16 [2048, 2048], P(None, 'tensor'), may hold values from -0.125 to 0.125
- w_value: bfloat16 [2048, 2048], P(None, 'tensor'), may hold values from -0.125 to 0.125
- w_out: bfloat16 [2048, 2048], P('tensor'), may hold values from -0.125 to 0.125
- w_gate: bfloat16 [2048, 8192], P(None, 'tensor'), may hold values from -0.125 to 0.125
- w_up: bfloat16 [2048, 8192], P(None, 'tensor'), may hold values from -0.125 to 0.125
- w_down: bfloat16 [8192, 2048], P('tensor'), may hold values from -0.0625 to 0.0625
- q_gain: float32 [2048], P('tensor'), may hold values from 0.5 to 2, as said below
- k_gain: float32 [2048], P('tensor'), may hold values from 0.5 to 2, as said below
- attn_gain: float32 [2048], replicated, may hold values from 0.5 to 1.5
- ffn_gain: float32 [2048], replicated, may hold values from 0.5 to 1.5
- cotangent: bfloat16 [4096, 2048], P(('dp', 'tensor')), may hold values from -6 to 6
Outputs:
- block_out: bfloat16 [4096, 2048], P(('dp', 'tensor'))
- grad_tokens: float32 [4096, 2048], P(('dp', 'tensor'))
- grad_w_query: float32 [2048, 2048], P(None, 'tensor')
- grad_w_key: float32 [2048, 2048], P(None, 'tensor')
- grad_w_value: float32 [2048, 2048], P(None, 'tensor')
- grad_w_out: float32 [2048, 2048], P('tensor')
- grad_w_gate: float32 [2048, 8192], P(None, 'tensor')
- grad_w_up: float32 [2048, 8192], P(None, 'tensor')
- grad_w_down: float32 [8192, 2048], P('tensor')
- grad_q_gain: float32 [2048], P('tensor')
- grad_k_gain: float32 [2048], P('tensor')
- grad_attn_gain: float32 [2048], replicated
- grad_ffn_gain: float32 [2048], replicated
The draws below stay inside these ranges and needn't reach their ends.
Inputs may be any that keep to these rules, and one draw needn't show every extreme that they name: `segment_ids`: within each packed sequence the segment number never falls; a segment holds 1 to 512 tokens. `q_gain`: positive gains. `k_gain`: positive gains.
All inputs are finite; a program needn't handle non-finite values.
Results may differ from the reference program's by a relative error of at most 0.017.
Values may be sent and summed in bfloat16 or wider, within the bound.
A program may use at most 256 MiB of HBM per device.

```python
import math
import jax
import jax.numpy as jnp
import numpy as np
from jax import lax

D = 2048
HEADS = 16
HD = 128
FF = 8192
LENGTH = 1024
DOCS = 4
TOK_DEV = 1024
SEQS = 4
TOKENS = 4096


def gain_law(key):
    return jax.random.uniform(key, (D,), jnp.float32, 0.5, 2.0)


def draw_q_gain(key, part):
    return gain_law(jax.random.fold_in(key, 11))


def draw_k_gain(key, part):
    return gain_law(jax.random.fold_in(key, 23))


def block_levels(stream_key, shape, cuts, least, top_value):
    level = 1.0
    for position, shards_of in cuts:
        steps = jax.random.uniform(jax.random.fold_in(jax.random.fold_in(stream_key, 6), position), (shards_of,), jnp.float32, least / len(cuts), top_value / len(cuts))
        level = level * jnp.repeat(jnp.exp(steps), shape[position] // shards_of).reshape((-1,) + (1,) * (len(shape) - 1 - position))
    return level


def length_profile(amount, total, bound, lean):
    weights = [(1 << 20) // math.isqrt(standing ** lean) + 1 for standing in range(2, amount + 1)]
    rest, counts = total - bound - (amount - 1), [1] * (amount - 1)
    while rest > 0:
        candidates = [i for i in range(amount - 1) if counts[i] < bound]
        mass, left = sum([weights[i] for i in candidates]), rest
        for i in candidates:
            extra = min(bound - counts[i], max(1, left * weights[i] // mass), rest)
            counts[i] = counts[i] + extra
            rest = rest - extra
    return np.array([bound] + counts)


def uneven(stream_key, number_of, total, reach, slope):
    if number_of == 2:
        one = jax.random.randint(stream_key, (), max(1, total - reach), min(reach, total - 1) + 1)
        return jnp.stack([one, total - one])
    sizes = jnp.asarray(length_profile(number_of, total, reach, slope), jnp.int32)
    pairs = (number_of - 1) // 2
    source_of, sink = sizes[1:1 + 2 * pairs:2], sizes[2:2 + 2 * pairs:2]
    room = jnp.minimum(source_of - 1, reach - sink)
    passed = jax.random.randint(jax.random.fold_in(stream_key, 1), (pairs,), 0, 1 << 20) % (room + 1)
    sizes = sizes.at[1:1 + 2 * pairs:2].set(source_of - passed).at[2:2 + 2 * pairs:2].set(sink + passed)
    return sizes[jax.random.permutation(jax.random.fold_in(stream_key, 2), number_of)]


def scatter_about(key, extent, deviation, most, cuts=(), held_as=jnp.bfloat16):
    values = deviation * jax.random.normal(key, extent, jnp.float32)
    if cuts:
        values = values * block_levels(key, extent, cuts, -0.22, 0.18)
    return jnp.clip(values, -most, most).astype(held_as)


def setup_inputs(seed: int = 0) -> dict:
    key_list = jax.random.split(jax.random.key(seed), 15)
    return {
        "tokens": scatter_about(key_list[0], (TOKENS, D), 1.0, 6.0, ((0, 32),)),
        "segment_ids": jax.vmap(lambda own: jnp.searchsorted(jnp.cumsum(uneven(own, DOCS, LENGTH, LENGTH // 2, 2)), jnp.arange(LENGTH), side="right"))(jax.random.split(key_list[1], SEQS)).reshape((SEQS, LENGTH)).astype(jnp.int32),
        "w_query": scatter_about(key_list[2], (D, D), D ** -0.5, 0.125, ((1, 8),)),
        "w_key": scatter_about(key_list[3], (D, D), D ** -0.5, 0.125, ((1, 8),)),
        "w_value": scatter_about(key_list[4], (D, D), D ** -0.5, 0.125, ((1, 8),)),
        "w_out": scatter_about(key_list[5], (D, D), D ** -0.5, 0.125, ((0, 8),)),
        "w_gate": scatter_about(key_list[6], (D, FF), D ** -0.5, 0.125, ((1, 8),)),
        "w_up": scatter_about(key_list[7], (D, FF), D ** -0.5, 0.125, ((1, 8),)),
        "w_down": scatter_about(key_list[8], (FF, D), FF ** -0.5, 0.0625, ((0, 8),)),
        "q_gain": draw_q_gain(jax.random.fold_in(key_list[14], 71), 0),
        "k_gain": draw_k_gain(jax.random.fold_in(key_list[14], 71), 0),
        "attn_gain": jnp.clip(jax.random.uniform(key_list[11], (D,), jnp.float32, 0.5, 1.5), 0.5, 1.5),
        "ffn_gain": jnp.clip(jax.random.uniform(key_list[12], (D,), jnp.float32, 0.5, 1.5), 0.5, 1.5),
        "cotangent": scatter_about(key_list[13], (TOKENS, D), 1.0, 6.0, ((0, 32),)),
    }


@jax.custom_vjp
def low(v):
    return lax.optimization_barrier(v.astype(jnp.bfloat16)).astype(jnp.float32)

@jax.custom_vjp
def low_back(v):
    return v

def low_keep(v):
    return (low(v), None)

def low_pass(kept, grad):
    return (grad,)

def back_keep(v):
    return (v, None)

def back_low(kept, grad):
    return (low(grad),)
low.defvjp(low_keep, low_pass)
low_back.defvjp(back_keep, back_low)
EPS = 1e-06
THETA = 500000.0
HIGH = lax.Precision.HIGHEST

def both_round(value):
    return low(low_back(value))

def matmul(left, right):
    return jnp.dot(left, right, precision=HIGH, preferred_element_type=jnp.float32)

def rms_scale(value, gain):
    return value * lax.rsqrt(lax.optimization_barrier(jnp.mean(value * value, axis=-1, keepdims=True)) + EPS) * gain

def positions_of(segment_ids):
    length = segment_ids.shape[-1]
    places = jnp.arange(length, dtype=jnp.int32)
    earlier = jnp.concatenate([segment_ids[:, :1] - 1, segment_ids[:, :-1]], axis=1)
    starts = jnp.where(segment_ids != earlier, places[None, :], jnp.zeros_like(segment_ids))
    starts = lax.cummax(starts, axis=1)
    return (places[None, :] - starts).astype(jnp.int32)

def rotary_tables(positions):
    half = HD // 2
    freq = THETA ** (-(jnp.arange(half, dtype=jnp.float32) * 2.0 / HD))
    angle = positions.astype(jnp.float32)[:, None] * freq[None, :]
    cosine = jnp.concatenate([jnp.cos(angle), jnp.cos(angle)], axis=1)
    sine = jnp.concatenate([jnp.sin(angle), jnp.sin(angle)], axis=1)
    return (cosine, sine)

def rotate(value, cosine, sine):
    half = value.shape[-1] // 2
    turned = jnp.concatenate([-value[..., half:], value[..., :half]], axis=-1)
    return value * cosine[:, None, :] + turned * sine[:, None, :]

def block_forward(params, inputs, positions, segments):
    w_query, w_key, w_value, w_out, w_gate, w_up, w_down, q_gain, k_gain, attn_gain, ffn_gain = params
    count = inputs.shape[0]
    seq_count = count // LENGTH
    q_raw = low_back(matmul(inputs, w_query))
    k_raw = low_back(matmul(inputs, w_key))
    values = both_round(matmul(inputs, w_value)).reshape(seq_count, LENGTH, HEADS, HD)
    cosine, sine = rotary_tables(positions)
    queries = both_round(rotate(rms_scale(q_raw, q_gain).reshape(count, HEADS, HD), cosine, sine))
    keys = both_round(rotate(rms_scale(k_raw, k_gain).reshape(count, HEADS, HD), cosine, sine))
    places = jnp.arange(LENGTH, dtype=jnp.int32)
    causal = places[:, None] >= places[None, :]
    att_scale = HD ** (-0.5)

    def attend(pieces):
        query_block, key_block, value_block, seg_row = pieces
        scores = jnp.einsum('qhd,khd->hqk', query_block, key_block, precision=HIGH) * att_scale
        scores = low_back(scores)
        allowed = causal & (seg_row[:, None] == seg_row[None, :])
        scores = jnp.where(allowed[None], scores, -1e+30)
        top = lax.optimization_barrier(jnp.max(scores, axis=-1, keepdims=True))
        expo = jnp.exp(scores - top)
        probs = expo / lax.optimization_barrier(jnp.sum(expo, axis=-1, keepdims=True))
        return jnp.einsum('hqk,khd->qhd', low(probs), value_block, precision=HIGH)
    mixed = lax.map(jax.checkpoint(attend), (queries.reshape(seq_count, LENGTH, HEADS, HD), keys.reshape(seq_count, LENGTH, HEADS, HD), values, segments))
    mixed = both_round(mixed.reshape(count, D))
    branch = low_back(matmul(mixed, w_out))
    hidden = inputs + rms_scale(branch, attn_gain)
    h_low = low(hidden)
    gate = low_back(matmul(h_low, w_gate))
    up = low_back(matmul(h_low, w_up))
    act = low(jax.nn.silu(gate) * up)
    down = low_back(matmul(act, w_down))
    return hidden + rms_scale(down, ffn_gain)

def reference(tokens, segment_ids, w_query, w_key, w_value, w_out, w_gate, w_up, w_down, q_gain, k_gain, attn_gain, ffn_gain, cotangent):
    params = tuple((item.astype(jnp.float32) for item in (w_query, w_key, w_value, w_out, w_gate, w_up, w_down, q_gain, k_gain, attn_gain, ffn_gain)))
    positions = positions_of(segment_ids)
    group_count = TOKENS // TOK_DEV

    def group_step(totals, pieces):
        inputs, group_pos, group_seg, grad_output = pieces
        output, pullback = jax.vjp(lambda weights, values: block_forward(weights, values, group_pos, group_seg), params, inputs)
        grad_params, grad_inputs = pullback(grad_output)
        totals = jax.tree.map(lambda first, second: first + second, totals, grad_params)
        return (totals, (output.astype(jnp.bfloat16), grad_inputs))
    zeros = jax.tree.map(lambda item: jnp.zeros(item.shape, jnp.float32), params)
    scanned = (tokens.astype(jnp.float32).reshape(group_count, TOK_DEV, D), positions.reshape(group_count, TOK_DEV), segment_ids.reshape(group_count, TOK_DEV // LENGTH, LENGTH), cotangent.astype(jnp.float32).reshape(group_count, TOK_DEV, D))
    totals, (outputs, grad_inputs) = lax.scan(group_step, zeros, scanned)
    g_query, g_key, g_value, g_out, g_gate, g_up, g_down, g_qgain, g_kgain, g_again, g_fgain = totals
    return (outputs.reshape(TOKENS, D), grad_inputs.reshape(TOKENS, D), g_query, g_key, g_value, g_out, g_gate, g_up, g_down, g_qgain, g_kgain, g_again, g_fgain)
```

```python
import jax
import jax.numpy as jnp
from jax import lax
from jax.sharding import PartitionSpec as P

HD = 128


EPS = 1e-06
THETA = 500000.0


def rounded(value):
    return lax.optimization_barrier(value.astype(jnp.bfloat16)).astype(jnp.float32)


def dot_last(left, right):
    return lax.dot_general(
        left, right, (((1,), (1,)), ((), ())), preferred_element_type=jnp.float32
    )


def dot_first(left, right):
    return lax.dot_general(
        left, right, (((0,), (0,)), ((), ())), preferred_element_type=jnp.float32
    )


def positions_of(segment_ids):
    length = segment_ids.shape[-1]
    places = jnp.arange(length, dtype=jnp.int32)
    below = (segment_ids[:, None, :] < segment_ids[:, :, None]).astype(jnp.int32)
    return places[None, :] - jnp.sum(below, axis=2)


def rotary_tables(positions):
    half = HD // 2
    freq = THETA ** (-(jnp.arange(half, dtype=jnp.float32) * 2.0 / HD))
    angle = positions.astype(jnp.float32)[:, None] * freq[None, :]
    cosine = jnp.concatenate([jnp.cos(angle), jnp.cos(angle)], axis=1)
    sine = jnp.concatenate([jnp.sin(angle), jnp.sin(angle)], axis=1)
    return (cosine, sine)


def rotate(value, cosine, sine):
    half = value.shape[-1] // 2
    turned = jnp.concatenate([-value[..., half:], value[..., :half]], axis=-1)
    return value * cosine[:, None, :] + turned * sine[:, None, :]


def rotate_back(grad, cosine, sine):
    half = grad.shape[-1] // 2
    scaled = grad * sine[:, None, :]
    unturned = jnp.concatenate([scaled[..., half:], -scaled[..., :half]], axis=-1)
    return grad * cosine[:, None, :] + unturned


def norm_back(grad_out, unit, inverse, gain):
    inner = grad_out * gain
    return inverse * (inner - unit * jnp.mean(inner * unit, axis=1, keepdims=True))


def on_device(
    tokens,
    segment_ids,
    w_query,
    w_key,
    w_value,
    w_out,
    w_gate,
    w_up,
    w_down,
    q_gain,
    k_gain,
    attn_gain,
    ffn_gain,
    cotangent,
):
    row_count, full_width = tokens.shape
    head_cols = w_query.shape[1]
    heads_here = head_cols // HD
    ff_cols = w_gate.shape[1]
    seqs_here, seq_len = segment_ids.shape
    token_count = seqs_here * seq_len
    att_scale = HD ** (-0.5)
    whole_x = lax.all_gather(tokens, "tensor", axis=0, tiled=True)
    w_qkv = jnp.concatenate([w_query, w_key, w_value], axis=1)
    projected = jnp.dot(whole_x, w_qkv, preferred_element_type=jnp.float32)
    q_raw = projected[:, :head_cols]
    k_raw = projected[:, head_cols : 2 * head_cols]
    values = projected[:, 2 * head_cols :].astype(jnp.bfloat16)
    q_total, k_total = lax.psum(
        (jnp.sum(q_raw * q_raw, axis=1), jnp.sum(k_raw * k_raw, axis=1)), "tensor"
    )
    q_inverse = lax.rsqrt(q_total / full_width + EPS)[:, None]
    k_inverse = lax.rsqrt(k_total / full_width + EPS)[:, None]
    q_unit = q_raw * q_inverse
    k_unit = k_raw * k_inverse
    cosine, sine = rotary_tables(positions_of(segment_ids).reshape(token_count))
    queries = rotate((q_unit * q_gain).reshape(token_count, heads_here, HD), cosine, sine).astype(
        jnp.bfloat16
    )
    keys = rotate((k_unit * k_gain).reshape(token_count, heads_here, HD), cosine, sine).astype(
        jnp.bfloat16
    )
    shaped = (seqs_here, seq_len, heads_here, HD)
    query_seqs = queries.reshape(shaped)
    key_seqs = keys.reshape(shaped)
    value_seqs = values.reshape(shaped)
    places = jnp.arange(seq_len, dtype=jnp.int32)
    causal = places[:, None] >= places[None, :]

    def scores_of(query_block, key_block, seg_row):
        raw = (
            jnp.einsum("qhd,khd->hqk", query_block, key_block, preferred_element_type=jnp.float32)
            * att_scale
        )
        allowed = causal & (seg_row[:, None] == seg_row[None, :])
        return jnp.where(allowed[None], raw, -1e30)

    def attend(pieces):
        query_block, key_block, value_block, seg_row = pieces
        scores = scores_of(query_block, key_block, seg_row)
        top = jnp.max(scores, axis=-1, keepdims=True)
        expo = jnp.exp(scores - top)
        total = jnp.sum(expo, axis=-1, keepdims=True)
        probs = (expo / total).astype(jnp.bfloat16)
        mixed_block = jnp.einsum(
            "hqk,khd->qhd", probs, value_block, preferred_element_type=jnp.float32
        )
        return (mixed_block.astype(jnp.bfloat16), (top + jnp.log(total))[..., 0])

    mixed, log_total = lax.map(attend, (query_seqs, key_seqs, value_seqs, segment_ids))
    mixed = mixed.reshape(token_count, head_cols)
    x_rows = tokens.astype(jnp.float32)
    branch = lax.psum_scatter(
        jnp.dot(mixed, w_out, preferred_element_type=jnp.float32).astype(jnp.bfloat16),
        "tensor",
        scatter_dimension=0,
        tiled=True,
    ).astype(jnp.float32)
    a_inverse = lax.rsqrt(jnp.mean(branch * branch, axis=1, keepdims=True) + EPS)
    hidden = x_rows + branch * a_inverse * attn_gain
    h_low = lax.all_gather(hidden.astype(jnp.bfloat16), "tensor", axis=0, tiled=True)
    a_unit = branch * a_inverse
    w_gate_up = jnp.concatenate([w_gate, w_up], axis=1)
    gate_up = jnp.dot(h_low, w_gate_up, preferred_element_type=jnp.float32)
    gate = gate_up[:, :ff_cols]
    up = gate_up[:, ff_cols:]
    sigma_gate = jax.nn.sigmoid(gate)
    silu_gate = gate * sigma_gate
    act = (silu_gate * up).astype(jnp.bfloat16)
    down = lax.psum_scatter(
        jnp.dot(act, w_down, preferred_element_type=jnp.float32).astype(jnp.bfloat16),
        "tensor",
        scatter_dimension=0,
        tiled=True,
    ).astype(jnp.float32)
    f_inverse = lax.rsqrt(jnp.mean(down * down, axis=1, keepdims=True) + EPS)
    f_unit = down * f_inverse
    block_out = (hidden + f_unit * ffn_gain).astype(jnp.bfloat16)
    grad_out = cotangent.astype(jnp.float32)
    grad_ffn_part = jnp.sum(grad_out * f_unit, axis=0)
    grad_down = norm_back(grad_out, f_unit, f_inverse, ffn_gain).astype(jnp.bfloat16)
    grad_down_all = lax.all_gather(grad_down, "tensor", axis=0, tiled=True)
    grad_act = dot_last(grad_down_all, w_down)
    grad_w_down = dot_first(act, grad_down_all)
    grad_gate = grad_act * up * sigma_gate * (1.0 + gate * (1.0 - sigma_gate))
    grad_up = grad_act * silu_gate
    grad_gate_up = jnp.concatenate([grad_gate, grad_up], axis=1).astype(jnp.bfloat16)
    grad_w_gate_up = dot_first(h_low, grad_gate_up)
    grad_hidden = grad_out + lax.psum_scatter(
        dot_last(grad_gate_up, w_gate_up).astype(jnp.bfloat16), "tensor", scatter_dimension=0, tiled=True
    ).astype(jnp.float32)
    grad_attn_part = jnp.sum(grad_hidden * a_unit, axis=0)
    grad_branch = norm_back(grad_hidden, a_unit, a_inverse, attn_gain).astype(jnp.bfloat16)
    grad_branch_all = lax.all_gather(grad_branch, "tensor", axis=0, tiled=True)
    grad_w_out = dot_first(mixed, grad_branch_all)
    grad_mixed = dot_last(grad_branch_all, w_out).astype(jnp.bfloat16).reshape(shaped)

    def attend_back(pieces):
        query_block, key_block, value_block, seg_row, log_block, grad_block = pieces
        scores = scores_of(query_block, key_block, seg_row)
        probs = jnp.exp(scores - log_block[..., None])
        grad_probs = jnp.einsum(
            "qhd,khd->hqk", grad_block, value_block, preferred_element_type=jnp.float32
        )
        grad_scores = (
            probs * (grad_probs - jnp.sum(probs * grad_probs, axis=-1, keepdims=True))
        ).astype(jnp.bfloat16)
        grad_query = (
            jnp.einsum("hqk,khd->qhd", grad_scores, key_block, preferred_element_type=jnp.float32)
            * att_scale
        )
        grad_key = (
            jnp.einsum("hqk,qhd->khd", grad_scores, query_block, preferred_element_type=jnp.float32)
            * att_scale
        )
        grad_value = jnp.einsum(
            "hqk,qhd->khd",
            probs.astype(jnp.bfloat16),
            grad_block,
            preferred_element_type=jnp.float32,
        )
        return (grad_query, grad_key, grad_value.astype(jnp.bfloat16))

    grad_query, grad_key, grad_value = lax.map(
        attend_back, (query_seqs, key_seqs, value_seqs, segment_ids, log_total, grad_mixed)
    )
    grad_q_normed = rotate_back(
        rounded(grad_query.reshape(token_count, heads_here, HD)), cosine, sine
    ).reshape(token_count, head_cols)
    grad_k_normed = rotate_back(
        rounded(grad_key.reshape(token_count, heads_here, HD)), cosine, sine
    ).reshape(token_count, head_cols)
    grad_q_gain = jnp.sum(grad_q_normed * q_unit, axis=0)
    grad_k_gain = jnp.sum(grad_k_normed * k_unit, axis=0)
    inner_q = grad_q_normed * q_gain
    inner_k = grad_k_normed * k_gain
    q_inner_sum, k_inner_sum = lax.psum(
        (jnp.sum(inner_q * q_unit, axis=1), jnp.sum(inner_k * k_unit, axis=1)), "tensor"
    )
    grad_q_raw = q_inverse * (inner_q - q_unit * (q_inner_sum / full_width)[:, None])
    grad_k_raw = k_inverse * (inner_k - k_unit * (k_inner_sum / full_width)[:, None])
    grad_qkv = jnp.concatenate(
        [
            grad_q_raw.astype(jnp.bfloat16),
            grad_k_raw.astype(jnp.bfloat16),
            grad_value.reshape(token_count, head_cols),
        ],
        axis=1,
    )
    grad_w_qkv = dot_first(whole_x, grad_qkv)
    grad_tokens = grad_hidden + lax.psum_scatter(
        dot_last(grad_qkv, w_qkv).astype(jnp.bfloat16), "tensor", scatter_dimension=0, tiled=True
    ).astype(jnp.float32)
    grad_w_qkv, grad_w_out, grad_w_gate_up, grad_w_down = [
        lax.psum(part.astype(jnp.bfloat16), "dp").astype(jnp.float32)
        for part in (grad_w_qkv, grad_w_out, grad_w_gate_up, grad_w_down)
    ]
    grad_q_gain, grad_k_gain = lax.psum((grad_q_gain, grad_k_gain), "dp")
    grad_attn_gain, grad_ffn_gain = lax.psum((grad_attn_part, grad_ffn_part), ("dp", "tensor"))
    return (
        block_out,
        grad_tokens,
        grad_w_qkv[:, :head_cols],
        grad_w_qkv[:, head_cols : 2 * head_cols],
        grad_w_qkv[:, 2 * head_cols :],
        grad_w_out,
        grad_w_gate_up[:, :ff_cols],
        grad_w_gate_up[:, ff_cols:],
        grad_w_down,
        grad_q_gain,
        grad_k_gain,
        grad_attn_gain,
        grad_ffn_gain,
    )


def solution(mesh):
    placed = (
        P(("dp", "tensor"), None),
        P("dp", None),
        P(None, "tensor"),
        P(None, "tensor"),
        P(None, "tensor"),
        P("tensor", None),
        P(None, "tensor"),
        P(None, "tensor"),
        P("tensor", None),
        P("tensor"),
        P("tensor"),
        P(),
        P(),
        P(("dp", "tensor"), None),
    )
    return jax.shard_map(
        on_device,
        mesh=mesh,
        in_specs=placed,
        out_specs=(
            P(("dp", "tensor"), None),
            P(("dp", "tensor"), None),
            P(None, "tensor"),
            P(None, "tensor"),
            P(None, "tensor"),
            P("tensor", None),
            P(None, "tensor"),
            P(None, "tensor"),
            P("tensor", None),
            P("tensor"),
            P("tensor"),
            P(),
            P(),
        ),
        check_vma=False,
    )
```

```python
import jax
import jax.numpy as jnp
from jax import lax
from jax.experimental import pallas as pl
from jax.experimental.pallas import tpu as pltpu
from jax.sharding import PartitionSpec as P

HD = 128


EPS = 1e-06
THETA = 500000.0


def rounded(value):
    return lax.optimization_barrier(value.astype(jnp.bfloat16)).astype(jnp.float32)


def dot_last(left, right):
    return lax.dot_general(
        left, right, (((1,), (1,)), ((), ())), preferred_element_type=jnp.float32
    )


def dot_first(left, right):
    return lax.dot_general(
        left, right, (((0,), (0,)), ((), ())), preferred_element_type=jnp.float32
    )


def positions_of(segment_ids):
    length = segment_ids.shape[-1]
    places = jnp.arange(length, dtype=jnp.int32)
    below = (segment_ids[:, None, :] < segment_ids[:, :, None]).astype(jnp.int32)
    return places[None, :] - jnp.sum(below, axis=2)


def rotary_tables(positions):
    half = HD // 2
    freq = THETA ** (-(jnp.arange(half, dtype=jnp.float32) * 2.0 / HD))
    angle = positions.astype(jnp.float32)[:, None] * freq[None, :]
    cosine = jnp.concatenate([jnp.cos(angle), jnp.cos(angle)], axis=1)
    sine = jnp.concatenate([jnp.sin(angle), jnp.sin(angle)], axis=1)
    return (cosine, sine)


def rotate(value, cosine, sine):
    half = value.shape[-1] // 2
    turned = jnp.concatenate([-value[..., half:], value[..., :half]], axis=-1)
    return value * cosine[:, None, :] + turned * sine[:, None, :]


def rotate_back(grad, cosine, sine):
    half = grad.shape[-1] // 2
    scaled = grad * sine[:, None, :]
    unturned = jnp.concatenate([scaled[..., half:], -scaled[..., :half]], axis=-1)
    return grad * cosine[:, None, :] + unturned


def norm_back(grad_out, unit, inverse, gain):
    inner = grad_out * gain
    return inverse * (inner - unit * jnp.mean(inner * unit, axis=1, keepdims=True))


def on_device(
    tokens,
    segment_ids,
    w_query,
    w_key,
    w_value,
    w_out,
    w_gate,
    w_up,
    w_down,
    q_gain,
    k_gain,
    attn_gain,
    ffn_gain,
    cotangent,
):
    row_count, full_width = tokens.shape
    head_cols = w_query.shape[1]
    heads_here = head_cols // HD
    ff_cols = w_gate.shape[1]
    seqs_here, seq_len = segment_ids.shape
    token_count = seqs_here * seq_len
    att_scale = HD ** (-0.5)
    whole_x = lax.all_gather(tokens, "tensor", axis=0, tiled=True)
    w_qkv = jnp.concatenate([w_query, w_key, w_value], axis=1)
    projected = jnp.dot(whole_x, w_qkv, preferred_element_type=jnp.float32)
    q_raw = projected[:, :head_cols]
    k_raw = projected[:, head_cols : 2 * head_cols]
    values = projected[:, 2 * head_cols :].astype(jnp.bfloat16)
    q_total, k_total = lax.psum(
        (jnp.sum(q_raw * q_raw, axis=1), jnp.sum(k_raw * k_raw, axis=1)), "tensor"
    )
    q_inverse = lax.rsqrt(q_total / full_width + EPS)[:, None]
    k_inverse = lax.rsqrt(k_total / full_width + EPS)[:, None]
    q_unit = q_raw * q_inverse
    k_unit = k_raw * k_inverse
    cosine, sine = rotary_tables(positions_of(segment_ids).reshape(token_count))
    queries = rotate((q_unit * q_gain).reshape(token_count, heads_here, HD), cosine, sine).astype(
        jnp.bfloat16
    )
    keys = rotate((k_unit * k_gain).reshape(token_count, heads_here, HD), cosine, sine).astype(
        jnp.bfloat16
    )
    shaped = (seqs_here, seq_len, heads_here, HD)
    query_seqs = queries.reshape(shaped)
    key_seqs = keys.reshape(shaped)
    value_seqs = values.reshape(shaped)
    places = jnp.arange(seq_len, dtype=jnp.int32)
    causal = places[:, None] >= places[None, :]

    def scores_of(query_block, key_block, seg_row):
        raw = (
            jnp.einsum("qhd,khd->hqk", query_block, key_block, preferred_element_type=jnp.float32)
            * att_scale
        )
        allowed = causal & (seg_row[:, None] == seg_row[None, :])
        return jnp.where(allowed[None], raw, -1e30)

    def attend(pieces):
        query_block, key_block, value_block, seg_row = pieces
        scores = scores_of(query_block, key_block, seg_row)
        top = jnp.max(scores, axis=-1, keepdims=True)
        expo = jnp.exp(scores - top)
        total = jnp.sum(expo, axis=-1, keepdims=True)
        probs = (expo / total).astype(jnp.bfloat16)
        mixed_block = jnp.einsum(
            "hqk,khd->qhd", probs, value_block, preferred_element_type=jnp.float32
        )
        return (mixed_block.astype(jnp.bfloat16), (top + jnp.log(total))[..., 0])

    mixed, log_total = lax.map(attend, (query_seqs, key_seqs, value_seqs, segment_ids))
    mixed = mixed.reshape(token_count, head_cols)
    x_rows = tokens.astype(jnp.float32)
    branch = lax.psum_scatter(
        jnp.dot(mixed, w_out, preferred_element_type=jnp.float32).astype(jnp.bfloat16),
        "tensor",
        scatter_dimension=0,
        tiled=True,
    ).astype(jnp.float32)
    a_inverse = lax.rsqrt(jnp.mean(branch * branch, axis=1, keepdims=True) + EPS)
    hidden = x_rows + branch * a_inverse * attn_gain
    h_low = lax.all_gather(hidden.astype(jnp.bfloat16), "tensor", axis=0, tiled=True)
    a_unit = branch * a_inverse
    w_gate_up = jnp.concatenate([w_gate, w_up], axis=1)
    gate_up = jnp.dot(h_low, w_gate_up, preferred_element_type=jnp.float32)
    gate = gate_up[:, :ff_cols]
    up = gate_up[:, ff_cols:]
    sigma_gate = jax.nn.sigmoid(gate)
    silu_gate = gate * sigma_gate
    act = (silu_gate * up).astype(jnp.bfloat16)
    down = lax.psum_scatter(
        jnp.dot(act, w_down, preferred_element_type=jnp.float32).astype(jnp.bfloat16),
        "tensor",
        scatter_dimension=0,
        tiled=True,
    ).astype(jnp.float32)
    f_inverse = lax.rsqrt(jnp.mean(down * down, axis=1, keepdims=True) + EPS)
    f_unit = down * f_inverse
    block_out = (hidden + f_unit * ffn_gain).astype(jnp.bfloat16)
    grad_out = cotangent.astype(jnp.float32)
    grad_ffn_part = jnp.sum(grad_out * f_unit, axis=0)
    grad_down = norm_back(grad_out, f_unit, f_inverse, ffn_gain).astype(jnp.bfloat16)
    grad_down_all = lax.all_gather(grad_down, "tensor", axis=0, tiled=True)
    grad_act = dot_last(grad_down_all, w_down)
    grad_w_down = dot_first(act, grad_down_all)
    grad_gate = grad_act * up * sigma_gate * (1.0 + gate * (1.0 - sigma_gate))
    grad_up = grad_act * silu_gate
    grad_gate_up = jnp.concatenate([grad_gate, grad_up], axis=1).astype(jnp.bfloat16)
    grad_w_gate_up = dot_first(h_low, grad_gate_up)
    grad_hidden = grad_out + lax.psum_scatter(
        dot_last(grad_gate_up, w_gate_up).astype(jnp.bfloat16), "tensor", scatter_dimension=0, tiled=True
    ).astype(jnp.float32)
    grad_attn_part = jnp.sum(grad_hidden * a_unit, axis=0)
    grad_branch = norm_back(grad_hidden, a_unit, a_inverse, attn_gain).astype(jnp.bfloat16)
    grad_branch_all = lax.all_gather(grad_branch, "tensor", axis=0, tiled=True)
    grad_w_out = dot_first(mixed, grad_branch_all)
    grad_mixed = dot_last(grad_branch_all, w_out).astype(jnp.bfloat16).reshape(shaped)

    def attend_back(pieces):
        query_block, key_block, value_block, seg_row, log_block, grad_block = pieces
        scores = scores_of(query_block, key_block, seg_row)
        probs = jnp.exp(scores - log_block[..., None])
        grad_probs = jnp.einsum(
            "qhd,khd->hqk", grad_block, value_block, preferred_element_type=jnp.float32
        )
        grad_scores = (
            probs * (grad_probs - jnp.sum(probs * grad_probs, axis=-1, keepdims=True))
        ).astype(jnp.bfloat16)
        grad_query = (
            jnp.einsum("hqk,khd->qhd", grad_scores, key_block, preferred_element_type=jnp.float32)
            * att_scale
        )
        grad_key = (
            jnp.einsum("hqk,qhd->khd", grad_scores, query_block, preferred_element_type=jnp.float32)
            * att_scale
        )
        grad_value = jnp.einsum(
            "hqk,qhd->khd",
            probs.astype(jnp.bfloat16),
            grad_block,
            preferred_element_type=jnp.float32,
        )
        return (grad_query, grad_key, grad_value.astype(jnp.bfloat16))

    grad_query, grad_key, grad_value = lax.map(
        attend_back, (query_seqs, key_seqs, value_seqs, segment_ids, log_total, grad_mixed)
    )
    grad_q_normed = rotate_back(
        rounded(grad_query.reshape(token_count, heads_here, HD)), cosine, sine
    ).reshape(token_count, head_cols)
    grad_k_normed = rotate_back(
        rounded(grad_key.reshape(token_count, heads_here, HD)), cosine, sine
    ).reshape(token_count, head_cols)
    grad_q_gain = jnp.sum(grad_q_normed * q_unit, axis=0)
    grad_k_gain = jnp.sum(grad_k_normed * k_unit, axis=0)
    inner_q = grad_q_normed * q_gain
    inner_k = grad_k_normed * k_gain
    q_inner_sum, k_inner_sum = lax.psum(
        (jnp.sum(inner_q * q_unit, axis=1), jnp.sum(inner_k * k_unit, axis=1)), "tensor"
    )
    grad_q_raw = q_inverse * (inner_q - q_unit * (q_inner_sum / full_width)[:, None])
    grad_k_raw = k_inverse * (inner_k - k_unit * (k_inner_sum / full_width)[:, None])
    grad_qkv = jnp.concatenate(
        [
            grad_q_raw.astype(jnp.bfloat16),
            grad_k_raw.astype(jnp.bfloat16),
            grad_value.reshape(token_count, head_cols),
        ],
        axis=1,
    )
    grad_w_qkv = dot_first(whole_x, grad_qkv)
    grad_tokens = grad_hidden + lax.psum_scatter(
        dot_last(grad_qkv, w_qkv).astype(jnp.bfloat16), "tensor", scatter_dimension=0, tiled=True
    ).astype(jnp.float32)
    grad_w_qkv, grad_w_out, grad_w_gate_up, grad_w_down = [
        lax.psum(part.astype(jnp.bfloat16), "dp").astype(jnp.float32)
        for part in (grad_w_qkv, grad_w_out, grad_w_gate_up, grad_w_down)
    ]
    grad_q_gain, grad_k_gain = lax.psum((grad_q_gain, grad_k_gain), "dp")
    grad_attn_gain, grad_ffn_gain = lax.psum((grad_attn_part, grad_ffn_part), ("dp", "tensor"))
    return (
        block_out,
        grad_tokens,
        grad_w_qkv[:, :head_cols],
        grad_w_qkv[:, head_cols : 2 * head_cols],
        grad_w_qkv[:, 2 * head_cols :],
        grad_w_out,
        grad_w_gate_up[:, :ff_cols],
        grad_w_gate_up[:, ff_cols:],
        grad_w_down,
        grad_q_gain,
        grad_k_gain,
        grad_attn_gain,
        grad_ffn_gain,
    )


MESH = pl.DeviceIdType.MESH
LANES = 2


def places_of():
    d = lax.axis_index("dp")
    t = lax.axis_index("tensor")
    z, c = lax.div(t, 2), lax.rem(t, 2)
    dx = d + 1 - 2 * lax.rem(d, 2)
    dy = lax.rem(d + 2, 4)
    zs = (z, z + 1 - 2 * lax.rem(z, 2), lax.rem(z + 2, 4), 3 - z)
    inner = lax.rem(z + 1, 4) >= 2
    return d, dx, dy, zs, c, inner


def remote(src, dst, send, recv, dp, tensor):
    return pltpu.make_async_remote_copy(
        src_ref=src, dst_ref=dst, send_sem=send, recv_sem=recv, device_id=(dp, tensor), device_id_type=MESH
    )


def enter(d, zs, c, dx=None, dy=None):
    barrier = pltpu.get_barrier_semaphore()
    peers = [(d, 2 * zs[r] + c) for r in (1, 2, 3)] + [(d, 2 * zs[0] + 1 - c)]
    if dx is not None:
        peers += [(dx, 2 * zs[0] + c), (dy, 2 * zs[0] + c)]
    for peer in peers:
        pl.semaphore_signal(barrier, inc=1, device_id=peer, device_id_type=MESH)
    pl.semaphore_wait(barrier, len(peers))


class Gather:
    def __init__(self, full, send, recv, place):
        self.full, self.send, self.recv = full, send, recv
        self.d, _, _, self.zs, self.c, self.inner = place
        self.t = 2 * self.zs[0] + self.c

    def lane(self, r):
        return self.full.at[2 * self.zs[r] + self.c]

    def other(self, r):
        return self.full.at[2 * self.zs[r] + 1 - self.c]

    def to_z(self, r, k, via):
        return remote(self.lane(r), self.lane(r), self.send.at[via if r == 0 else 7], self.recv.at[k], self.d, 2 * self.zs[via] + self.c)

    def to_core(self, r):
        return remote(self.lane(r), self.lane(r), self.send.at[0 if r == 0 else 3 + r], self.recv.at[4 + r], self.d, 2 * self.zs[0] + 1 - self.c)

    def start(self):
        self.to_z(0, 2, 2).start()
        self.to_z(0, 1, 1).start()
        self.to_core(0).start()

    def start_inner(self):
        @pl.when(self.inner)
        def _():
            self.to_z(0, 2, 2).wait_send()
            self.to_z(0, 3, 3).start()

    def arrive(self, r):
        self.to_z(r, r, r).wait_recv()
        if r == 2:
            @pl.when(self.inner)
            def _():
                self.to_z(2, 3, 1).start()
        self.to_core(r).start()

    def ready(self, r):
        remote(self.other(r), self.other(r), self.send.at[0], self.recv.at[4 + r], self.d, self.t).wait_recv()

    def finish(self):
        @pl.when(jnp.logical_not(self.inner))
        def _():
            self.to_z(0, 2, 2).wait_send()

        @pl.when(self.inner)
        def _():
            self.to_z(0, 3, 3).wait_send()
            self.to_z(2, 3, 1).wait_send()

        self.to_z(0, 1, 1).wait_send()
        for r in range(4):
            self.to_core(r).wait_send()


class Scatter:
    def __init__(self, parts, pair, land, send, recv, place):
        self.parts, self.pair, self.land, self.send, self.recv = parts, pair, land, send, recv
        self.d, _, _, self.zs, self.c, self.inner = place
        self.t = 2 * self.zs[0] + self.c

    def mine(self, r):
        return self.parts.at[2 * self.zs[r] + self.c]

    def to_core(self, r):
        src = self.parts.at[2 * self.zs[r] + 1 - self.c]
        return remote(src, self.pair.at[r], self.send.at[r], self.recv.at[r], self.d, 2 * self.zs[0] + 1 - self.c)

    def to_z(self, r, k, via):
        return remote(self.mine(r), self.land.at[k], self.send.at[4 + r], self.recv.at[4 + k], self.d, 2 * self.zs[via] + self.c)

    def add_pair(self, r):
        self.to_core(r).wait_recv()
        add_into(self.mine(r), self.pair.at[r])

    def pass_on(self, r):
        if r == 1:
            self.to_z(1, 1, 1).start()
        if r == 2:
            @pl.when(jnp.logical_not(self.inner))
            def _():
                self.to_z(2, 2, 2).start()
        if r == 3:
            @pl.when(self.inner)
            def _():
                self.to_z(3, 3, 3).start()

            @pl.when(jnp.logical_not(self.inner))
            def _():
                self.to_z(3, 0, 1).start()

    def relay(self):
        @pl.when(self.inner)
        def _():
            self.to_z(3, 0, 1).wait_recv()
            add_into(self.mine(2), self.land.at[0])
            self.to_z(2, 2, 2).start()

    def arrived(self):
        self.to_z(1, 1, 1).wait_recv()
        self.to_z(2, 2, 2).wait_recv()

        @pl.when(self.inner)
        def _():
            self.to_z(3, 3, 3).wait_recv()

        @pl.when(jnp.logical_not(self.inner))
        def _():
            self.land[3] = jnp.zeros(self.land.shape[1:], self.land.dtype)

    def total(self, rows):
        own = self.parts[2 * self.zs[0] + self.c, rows, :].astype(jnp.float32)
        return own + self.land[1, rows, :].astype(jnp.float32) + self.land[2, rows, :].astype(jnp.float32) + self.land[3, rows, :].astype(jnp.float32)

    def finish(self):
        for r in range(4):
            self.to_core(r).wait_send()
        for r in (1, 2, 3):
            self.to_z(r, 1, 1).wait_send()


def add_into(into, other):
    rows = into.shape[0]

    def step(i, carry):
        at = pl.ds(pl.multiple_of(i * 32, 32), 32)
        into[at, :] = (into[at, :].astype(jnp.float32) + other[at, :].astype(jnp.float32)).astype(into.dtype)
        return carry

    lax.fori_loop(0, rows // 32, step, 0)


class Spread:
    def __init__(self, full, whole, send, recv, own_sem, place):
        self.full, self.whole, self.send, self.recv, self.own_sem = full, whole, send, recv, own_sem
        self.d, self.dx, self.dy, self.zs, self.c, _ = place
        self.t = 2 * self.zs[0] + self.c
        self.dd = 3 - self.d

    def slot(self, g, r):
        return self.whole.at[g, 2 * self.zs[r] + self.c]

    def own(self, r, k):
        src = self.full.at[2 * self.zs[r] + self.c]
        return remote(src, self.slot(self.d, r), self.send.at[k * 4 + r], self.recv.at[k * 4 + r], (self.dx, self.dy)[k], self.t)

    def start(self, r):
        self.own(r, 0).start()
        self.own(r, 1).start()

    def hop(self, r):
        group, target = (self.dx, self.dy) if r in (0, 3) else (self.dy, self.dx)
        return remote(self.slot(group, r), self.slot(group, r), self.send.at[8 + r], self.recv.at[8 + r], target, self.t)

    def to_core(self, r, k):
        group = (self.dx, self.dy, self.dd)[k]
        return remote(self.slot(group, r), self.slot(group, r), self.send.at[12 + k * 4 + r], self.recv.at[12 + k * 4 + r], self.d, 2 * self.zs[0] + 1 - self.c)

    def pass_on(self, r):
        remote(self.slot(self.dx, r), self.slot(self.dx, r), self.send.at[0], self.recv.at[r], self.dx, self.t).wait_recv()
        remote(self.slot(self.dy, r), self.slot(self.dy, r), self.send.at[0], self.recv.at[4 + r], self.dy, self.t).wait_recv()
        self.hop(r).start()
        self.to_core(r, 0).start()
        self.to_core(r, 1).start()

    def last(self, r):
        remote(self.slot(self.dd, r), self.slot(self.dd, r), self.send.at[0], self.recv.at[8 + r], self.dx, self.t).wait_recv()
        self.to_core(r, 2).start()

    def keep(self):
        return pltpu.make_async_copy(self.full, self.whole.at[self.d], self.own_sem)

    def finish(self):
        for r in range(4):
            self.own(r, 0).wait_send()
            self.own(r, 1).wait_send()
            self.hop(r).wait_send()
            for k in range(3):
                self.to_core(r, k).wait()
        self.keep().wait()


def dot_nt(left, right):
    return lax.dot_general(left, right, (((1,), (1,)), ((), ())), preferred_element_type=jnp.float32)


def ffn_kernel(
    h_ref, hid_ref, cot_ref, gain_ref, wg_ref, wu_ref, wd_ref,
    bo_ref, gh_ref, fg_ref, hall_ref, gdall_ref,
    hfull, gfull, gate, up, act, gg, gu, parts, pair, land,
    ag_send, ag_recv, rs_send, rs_recv, xy_send, xy_recv, own_sem,
):
    place = places_of()
    d, dx, dy, zs, c, inner = place
    t = 2 * zs[0] + c
    width = wg_ref.shape[1]
    wide = h_ref.shape[1]
    rows = h_ref.shape[0]
    ft, dt = 512, 1024
    hfull[t] = h_ref[...]
    enter(d, zs, c, dx, dy)

    def unit_forward(zz):
        both = pl.ds(2 * zz, 2)
        at = pl.ds(pl.multiple_of(zz * 2 * rows, 2 * rows), 2 * rows)

        def mid(j, carry):
            cols = pl.ds(pl.multiple_of(j * ft, ft), ft)
            block = hfull[both].reshape(2 * rows, wide)
            g = jnp.dot(block, wg_ref[:, cols], preferred_element_type=jnp.float32)
            u = jnp.dot(block, wu_ref[:, cols], preferred_element_type=jnp.float32)
            gate[at, cols] = g
            up[at, cols] = u
            act[:, cols] = (g * jax.nn.sigmoid(g) * u).astype(jnp.bfloat16)
            return carry

        lax.fori_loop(0, width // ft, mid, 0)

        def out(j, carry):
            cols = pl.ds(pl.multiple_of(j * dt, dt), dt)
            p = jnp.dot(act[...], wd_ref[:, cols], preferred_element_type=jnp.float32)
            parts[both, :, cols] = p.astype(jnp.bfloat16).reshape(2, rows, dt)
            return carry

        lax.fori_loop(0, wide // dt, out, 0)

    def unit_backward(zz):
        both = pl.ds(2 * zz, 2)
        at = pl.ds(pl.multiple_of(zz * 2 * rows, 2 * rows), 2 * rows)

        def mid(j, carry):
            cols = pl.ds(pl.multiple_of(j * ft, ft), ft)
            block = gfull[both].reshape(2 * rows, wide)
            ga = dot_nt(block, wd_ref[cols, :])
            g, u = gate[at, cols], up[at, cols]
            s = jax.nn.sigmoid(g)
            gg[:, cols] = (ga * u * s * (1.0 + g * (1.0 - s))).astype(jnp.bfloat16)
            gu[:, cols] = (ga * (g * s)).astype(jnp.bfloat16)
            return carry

        lax.fori_loop(0, width // ft, mid, 0)

        def out(j, carry):
            cols = pl.ds(pl.multiple_of(j * dt, dt), dt)
            p = dot_nt(gg[...], wg_ref[cols, :]) + dot_nt(gu[...], wu_ref[cols, :])
            parts[both, :, cols] = p.astype(jnp.bfloat16).reshape(2, rows, dt)
            return carry

        lax.fori_loop(0, wide // dt, out, 0)

    def phase(p, full, whole, unit):
        ag = Gather(full, ag_send.at[p], ag_recv.at[p], place)
        rs = Scatter(parts, pair.at[p], land.at[p], rs_send.at[p], rs_recv.at[p], place)
        xy = Spread(full, whole, xy_send.at[p], xy_recv.at[p], own_sem.at[p], place)
        ag.start()
        xy.start(0)
        ag.ready(0)
        unit(zs[0])
        rs.to_core(0).start()
        ag.start_inner()
        ag.arrive(2)
        xy.start(2)
        ag.arrive(1)
        xy.start(1)
        ag.ready(2)
        unit(zs[2])
        rs.to_core(2).start()
        ag.ready(1)
        unit(zs[1])
        rs.to_core(1).start()
        rs.add_pair(2)
        rs.pass_on(2)
        rs.add_pair(1)
        rs.pass_on(1)
        ag.arrive(3)
        xy.start(3)
        ag.ready(3)
        unit(zs[3])
        rs.to_core(3).start()
        xy.keep().start()
        rs.add_pair(3)
        rs.pass_on(3)
        rs.add_pair(0)
        xy.pass_on(0)
        xy.pass_on(2)
        xy.pass_on(1)
        rs.relay()
        rs.arrived()
        return ag, rs, xy

    ag, rs, xy_h = phase(0, hfull, hall_ref, unit_forward)
    gain = gain_ref[...]
    fg_ref[...] = jnp.zeros_like(fg_ref)
    step_rows = 32

    def middle(i, carry):
        at = pl.ds(pl.multiple_of(i * step_rows, step_rows), step_rows)
        down = rs.total(at)
        inverse = lax.rsqrt(jnp.mean(down * down, axis=1, keepdims=True) + EPS)
        unit = down * inverse
        bo_ref[at, :] = (hid_ref[at, :] + unit * gain).astype(jnp.bfloat16)
        grad = cot_ref[at, :].astype(jnp.float32)
        fg_ref[...] += jnp.sum(grad * unit, axis=0, keepdims=True)
        inner_grad = grad * gain
        gfull[t, at, :] = (inverse * (inner_grad - unit * jnp.mean(inner_grad * unit, axis=1, keepdims=True))).astype(jnp.bfloat16)
        return carry

    lax.fori_loop(0, rows // step_rows, middle, 0)
    ag.finish()
    rs.finish()
    xy_h.pass_on(3)
    for r in range(4):
        xy_h.last(r)
    ag, rs, xy = phase(1, gfull, gdall_ref, unit_backward)

    def ending(i, carry):
        at = pl.ds(pl.multiple_of(i * step_rows, step_rows), step_rows)
        gh_ref[at, :] = cot_ref[at, :].astype(jnp.float32) + rs.total(at)
        return carry

    lax.fori_loop(0, rows // step_rows, ending, 0)
    ag.finish()
    rs.finish()
    xy.pass_on(3)
    for r in range(4):
        xy.last(r)
    xy_h.finish()
    xy.finish()


def ffn(h_own, hidden, cot, gain, w_gate, w_up, w_down):
    rows, wide = h_own.shape
    width = w_gate.shape[1]
    groups, world = 4, 8
    vmem = pl.BlockSpec(memory_space=pltpu.VMEM)
    anywhere = pl.BlockSpec(memory_space=pl.ANY)
    bf, f32 = jnp.bfloat16, jnp.float32
    whole = jax.ShapeDtypeStruct((groups, world, rows, wide), bf)
    dma = pltpu.SemaphoreType.DMA
    return pl.pallas_call(
        ffn_kernel,
        out_shape=(
            jax.ShapeDtypeStruct((rows, wide), bf),
            jax.ShapeDtypeStruct((rows, wide), f32),
            jax.ShapeDtypeStruct((1, wide), f32),
            whole,
            whole,
        ),
        in_specs=[vmem] * 7,
        out_specs=(vmem, vmem, vmem, anywhere, anywhere),
        scratch_shapes=[
            pltpu.VMEM((world, rows, wide), bf),
            pltpu.VMEM((world, rows, wide), bf),
            pltpu.VMEM((world * rows, width), f32),
            pltpu.VMEM((world * rows, width), f32),
            pltpu.VMEM((2 * rows, width), bf),
            pltpu.VMEM((2 * rows, width), bf),
            pltpu.VMEM((2 * rows, width), bf),
            pltpu.VMEM((world, rows, wide), bf),
            pltpu.VMEM((2, 4, rows, wide), bf),
            pltpu.VMEM((2, 4, rows, wide), bf),
            dma((2, 8)),
            dma((2, 8)),
            dma((2, 8)),
            dma((2, 8)),
            dma((2, 24)),
            dma((2, 24)),
            dma((2,)),
        ],
        compiler_params=pltpu.CompilerParams(
            collective_id=2, has_side_effects=True, vmem_limit_bytes=60 * 2**20
        ),
        name="ffn",
    )(h_own, hidden, cot, gain.reshape(1, wide), w_gate, w_up, w_down)


def on_device_fused(
    tokens,
    segment_ids,
    w_query,
    w_key,
    w_value,
    w_out,
    w_gate,
    w_up,
    w_down,
    q_gain,
    k_gain,
    attn_gain,
    ffn_gain,
    cotangent,
):
    row_count, full_width = tokens.shape
    head_cols = w_query.shape[1]
    heads_here = head_cols // HD
    ff_cols = w_gate.shape[1]
    seqs_here, seq_len = segment_ids.shape
    token_count = seqs_here * seq_len
    att_scale = HD ** (-0.5)
    whole_x = lax.all_gather(tokens, "tensor", axis=0, tiled=True)
    w_qkv = jnp.concatenate([w_query, w_key, w_value], axis=1)
    projected = jnp.dot(whole_x, w_qkv, preferred_element_type=jnp.float32)
    q_raw = projected[:, :head_cols]
    k_raw = projected[:, head_cols : 2 * head_cols]
    values = projected[:, 2 * head_cols :].astype(jnp.bfloat16)
    q_total, k_total = lax.psum(
        (jnp.sum(q_raw * q_raw, axis=1), jnp.sum(k_raw * k_raw, axis=1)), "tensor"
    )
    q_inverse = lax.rsqrt(q_total / full_width + EPS)[:, None]
    k_inverse = lax.rsqrt(k_total / full_width + EPS)[:, None]
    q_unit = q_raw * q_inverse
    k_unit = k_raw * k_inverse
    cosine, sine = rotary_tables(positions_of(segment_ids).reshape(token_count))
    queries = rotate((q_unit * q_gain).reshape(token_count, heads_here, HD), cosine, sine).astype(
        jnp.bfloat16
    )
    keys = rotate((k_unit * k_gain).reshape(token_count, heads_here, HD), cosine, sine).astype(
        jnp.bfloat16
    )
    shaped = (seqs_here, seq_len, heads_here, HD)
    query_seqs = queries.reshape(shaped)
    key_seqs = keys.reshape(shaped)
    value_seqs = values.reshape(shaped)
    places = jnp.arange(seq_len, dtype=jnp.int32)
    causal = places[:, None] >= places[None, :]

    def scores_of(query_block, key_block, seg_row):
        raw = (
            jnp.einsum("qhd,khd->hqk", query_block, key_block, preferred_element_type=jnp.float32)
            * att_scale
        )
        allowed = causal & (seg_row[:, None] == seg_row[None, :])
        return jnp.where(allowed[None], raw, -1e30)

    def attend(pieces):
        query_block, key_block, value_block, seg_row = pieces
        scores = scores_of(query_block, key_block, seg_row)
        top = jnp.max(scores, axis=-1, keepdims=True)
        expo = jnp.exp(scores - top)
        total = jnp.sum(expo, axis=-1, keepdims=True)
        probs = (expo / total).astype(jnp.bfloat16)
        mixed_block = jnp.einsum(
            "hqk,khd->qhd", probs, value_block, preferred_element_type=jnp.float32
        )
        return (mixed_block.astype(jnp.bfloat16), (top + jnp.log(total))[..., 0])

    mixed, log_total = lax.map(attend, (query_seqs, key_seqs, value_seqs, segment_ids))
    mixed = mixed.reshape(token_count, head_cols)
    x_rows = tokens.astype(jnp.float32)
    branch = lax.psum_scatter(
        jnp.dot(mixed, w_out, preferred_element_type=jnp.float32).astype(jnp.bfloat16),
        "tensor",
        scatter_dimension=0,
        tiled=True,
    ).astype(jnp.float32)
    a_inverse = lax.rsqrt(jnp.mean(branch * branch, axis=1, keepdims=True) + EPS)
    hidden = x_rows + branch * a_inverse * attn_gain
    a_unit = branch * a_inverse
    block_out, grad_hidden, grad_ffn_part, h_all, grad_down_all = ffn(
        hidden.astype(jnp.bfloat16), hidden, cotangent, ffn_gain, w_gate, w_up, w_down
    )
    grad_ffn_part = grad_ffn_part[0]
    h_all = h_all.reshape(-1, full_width)
    grad_down_all = grad_down_all.reshape(-1, full_width)
    gate = jnp.dot(h_all, w_gate, preferred_element_type=jnp.float32)
    up = jnp.dot(h_all, w_up, preferred_element_type=jnp.float32)
    sigma_gate = jax.nn.sigmoid(gate)
    silu_gate = gate * sigma_gate
    act = (silu_gate * up).astype(jnp.bfloat16)
    grad_act = dot_last(grad_down_all, w_down)
    grad_w_down = dot_first(act, grad_down_all)
    grad_gate = grad_act * up * sigma_gate * (1.0 + gate * (1.0 - sigma_gate))
    grad_up = grad_act * silu_gate
    grad_w_gate = dot_first(h_all, grad_gate.astype(jnp.bfloat16))
    grad_w_up = dot_first(h_all, grad_up.astype(jnp.bfloat16))
    grad_attn_part = jnp.sum(grad_hidden * a_unit, axis=0)
    grad_branch = norm_back(grad_hidden, a_unit, a_inverse, attn_gain).astype(jnp.bfloat16)
    grad_branch_all = lax.all_gather(grad_branch, "tensor", axis=0, tiled=True)
    grad_w_out = dot_first(mixed, grad_branch_all)
    grad_mixed = dot_last(grad_branch_all, w_out).astype(jnp.bfloat16).reshape(shaped)

    def attend_back(pieces):
        query_block, key_block, value_block, seg_row, log_block, grad_block = pieces
        scores = scores_of(query_block, key_block, seg_row)
        probs = jnp.exp(scores - log_block[..., None])
        grad_probs = jnp.einsum(
            "qhd,khd->hqk", grad_block, value_block, preferred_element_type=jnp.float32
        )
        grad_scores = (
            probs * (grad_probs - jnp.sum(probs * grad_probs, axis=-1, keepdims=True))
        ).astype(jnp.bfloat16)
        grad_query = (
            jnp.einsum("hqk,khd->qhd", grad_scores, key_block, preferred_element_type=jnp.float32)
            * att_scale
        )
        grad_key = (
            jnp.einsum("hqk,qhd->khd", grad_scores, query_block, preferred_element_type=jnp.float32)
            * att_scale
        )
        grad_value = jnp.einsum(
            "hqk,qhd->khd",
            probs.astype(jnp.bfloat16),
            grad_block,
            preferred_element_type=jnp.float32,
        )
        return (grad_query, grad_key, grad_value.astype(jnp.bfloat16))

    grad_query, grad_key, grad_value = lax.map(
        attend_back, (query_seqs, key_seqs, value_seqs, segment_ids, log_total, grad_mixed)
    )
    grad_q_normed = rotate_back(
        rounded(grad_query.reshape(token_count, heads_here, HD)), cosine, sine
    ).reshape(token_count, head_cols)
    grad_k_normed = rotate_back(
        rounded(grad_key.reshape(token_count, heads_here, HD)), cosine, sine
    ).reshape(token_count, head_cols)
    grad_q_gain = jnp.sum(grad_q_normed * q_unit, axis=0)
    grad_k_gain = jnp.sum(grad_k_normed * k_unit, axis=0)
    inner_q = grad_q_normed * q_gain
    inner_k = grad_k_normed * k_gain
    q_inner_sum, k_inner_sum = lax.psum(
        (jnp.sum(inner_q * q_unit, axis=1), jnp.sum(inner_k * k_unit, axis=1)), "tensor"
    )
    grad_q_raw = q_inverse * (inner_q - q_unit * (q_inner_sum / full_width)[:, None])
    grad_k_raw = k_inverse * (inner_k - k_unit * (k_inner_sum / full_width)[:, None])
    grad_qkv = jnp.concatenate(
        [
            grad_q_raw.astype(jnp.bfloat16),
            grad_k_raw.astype(jnp.bfloat16),
            grad_value.reshape(token_count, head_cols),
        ],
        axis=1,
    )
    grad_w_qkv = dot_first(whole_x, grad_qkv)
    grad_tokens = grad_hidden + lax.psum_scatter(
        dot_last(grad_qkv, w_qkv).astype(jnp.bfloat16), "tensor", scatter_dimension=0, tiled=True
    ).astype(jnp.float32)
    grad_w_qkv, grad_w_out = [
        lax.psum(part.astype(jnp.bfloat16), "dp").astype(jnp.float32)
        for part in (grad_w_qkv, grad_w_out)
    ]
    grad_q_gain, grad_k_gain = lax.psum((grad_q_gain, grad_k_gain), "dp")
    grad_attn_gain, grad_ffn_gain = lax.psum((grad_attn_part, grad_ffn_part), ("dp", "tensor"))
    return (
        block_out,
        grad_tokens,
        grad_w_qkv[:, :head_cols],
        grad_w_qkv[:, head_cols : 2 * head_cols],
        grad_w_qkv[:, 2 * head_cols :],
        grad_w_out,
        grad_w_gate,
        grad_w_up,
        grad_w_down,
        grad_q_gain,
        grad_k_gain,
        grad_attn_gain,
        grad_ffn_gain,
    )


def solution(mesh):
    placed = (
        P(("dp", "tensor"), None),
        P("dp", None),
        P(None, "tensor"),
        P(None, "tensor"),
        P(None, "tensor"),
        P("tensor", None),
        P(None, "tensor"),
        P(None, "tensor"),
        P("tensor", None),
        P("tensor"),
        P("tensor"),
        P(),
        P(),
        P(("dp", "tensor"), None),
    )
    return jax.shard_map(
        on_device_fused if dict(mesh.shape) == {"dp": 4, "tensor": 8} else on_device,
        mesh=mesh,
        in_specs=placed,
        out_specs=(
            P(("dp", "tensor"), None),
            P(("dp", "tensor"), None),
            P(None, "tensor"),
            P(None, "tensor"),
            P(None, "tensor"),
            P("tensor", None),
            P(None, "tensor"),
            P(None, "tensor"),
            P("tensor", None),
            P("tensor"),
            P("tensor"),
            P(),
            P(),
        ),
        check_vma=False,
    )
```

```python
import jax
import jax.numpy as jnp
from jax import lax
from jax.experimental import pallas as pl
from jax.experimental.pallas import tpu as pltpu
from jax.sharding import PartitionSpec as P

HD = 128


EPS = 1e-06
THETA = 500000.0


def rounded(value):
    return lax.optimization_barrier(value.astype(jnp.bfloat16)).astype(jnp.float32)


def dot_last(left, right):
    return lax.dot_general(
        left, right, (((1,), (1,)), ((), ())), preferred_element_type=jnp.float32
    )


def dot_first(left, right):
    return lax.dot_general(
        left, right, (((0,), (0,)), ((), ())), preferred_element_type=jnp.float32
    )


def positions_of(segment_ids):
    length = segment_ids.shape[-1]
    places = jnp.arange(length, dtype=jnp.int32)
    below = (segment_ids[:, None, :] < segment_ids[:, :, None]).astype(jnp.int32)
    return places[None, :] - jnp.sum(below, axis=2)


def rotary_tables(positions):
    half = HD // 2
    freq = THETA ** (-(jnp.arange(half, dtype=jnp.float32) * 2.0 / HD))
    angle = positions.astype(jnp.float32)[:, None] * freq[None, :]
    cosine = jnp.concatenate([jnp.cos(angle), jnp.cos(angle)], axis=1)
    sine = jnp.concatenate([jnp.sin(angle), jnp.sin(angle)], axis=1)
    return (cosine, sine)


def rotate(value, cosine, sine):
    half = value.shape[-1] // 2
    turned = jnp.concatenate([-value[..., half:], value[..., :half]], axis=-1)
    return value * cosine[:, None, :] + turned * sine[:, None, :]


def rotate_back(grad, cosine, sine):
    half = grad.shape[-1] // 2
    scaled = grad * sine[:, None, :]
    unturned = jnp.concatenate([scaled[..., half:], -scaled[..., :half]], axis=-1)
    return grad * cosine[:, None, :] + unturned


def norm_back(grad_out, unit, inverse, gain):
    inner = grad_out * gain
    return inverse * (inner - unit * jnp.mean(inner * unit, axis=1, keepdims=True))


def on_device(
    tokens,
    segment_ids,
    w_query,
    w_key,
    w_value,
    w_out,
    w_gate,
    w_up,
    w_down,
    q_gain,
    k_gain,
    attn_gain,
    ffn_gain,
    cotangent,
):
    row_count, full_width = tokens.shape
    head_cols = w_query.shape[1]
    heads_here = head_cols // HD
    ff_cols = w_gate.shape[1]
    seqs_here, seq_len = segment_ids.shape
    token_count = seqs_here * seq_len
    att_scale = HD ** (-0.5)
    whole_x = lax.all_gather(tokens, "tensor", axis=0, tiled=True)
    w_qkv = jnp.concatenate([w_query, w_key, w_value], axis=1)
    projected = jnp.dot(whole_x, w_qkv, preferred_element_type=jnp.float32)
    q_raw = projected[:, :head_cols]
    k_raw = projected[:, head_cols : 2 * head_cols]
    values = projected[:, 2 * head_cols :].astype(jnp.bfloat16)
    q_total, k_total = lax.psum(
        (jnp.sum(q_raw * q_raw, axis=1), jnp.sum(k_raw * k_raw, axis=1)), "tensor"
    )
    q_inverse = lax.rsqrt(q_total / full_width + EPS)[:, None]
    k_inverse = lax.rsqrt(k_total / full_width + EPS)[:, None]
    q_unit = q_raw * q_inverse
    k_unit = k_raw * k_inverse
    cosine, sine = rotary_tables(positions_of(segment_ids).reshape(token_count))
    queries = rotate((q_unit * q_gain).reshape(token_count, heads_here, HD), cosine, sine).astype(
        jnp.bfloat16
    )
    keys = rotate((k_unit * k_gain).reshape(token_count, heads_here, HD), cosine, sine).astype(
        jnp.bfloat16
    )
    shaped = (seqs_here, seq_len, heads_here, HD)
    query_seqs = queries.reshape(shaped)
    key_seqs = keys.reshape(shaped)
    value_seqs = values.reshape(shaped)
    places = jnp.arange(seq_len, dtype=jnp.int32)
    causal = places[:, None] >= places[None, :]

    def scores_of(query_block, key_block, seg_row):
        raw = (
            jnp.einsum("qhd,khd->hqk", query_block, key_block, preferred_element_type=jnp.float32)
            * att_scale
        )
        allowed = causal & (seg_row[:, None] == seg_row[None, :])
        return jnp.where(allowed[None], raw, -1e30)

    def attend(pieces):
        query_block, key_block, value_block, seg_row = pieces
        scores = scores_of(query_block, key_block, seg_row)
        top = jnp.max(scores, axis=-1, keepdims=True)
        expo = jnp.exp(scores - top)
        total = jnp.sum(expo, axis=-1, keepdims=True)
        probs = (expo / total).astype(jnp.bfloat16)
        mixed_block = jnp.einsum(
            "hqk,khd->qhd", probs, value_block, preferred_element_type=jnp.float32
        )
        return (mixed_block.astype(jnp.bfloat16), (top + jnp.log(total))[..., 0])

    mixed, log_total = lax.map(attend, (query_seqs, key_seqs, value_seqs, segment_ids))
    mixed = mixed.reshape(token_count, head_cols)
    x_rows = tokens.astype(jnp.float32)
    branch = lax.psum_scatter(
        jnp.dot(mixed, w_out, preferred_element_type=jnp.float32).astype(jnp.bfloat16),
        "tensor",
        scatter_dimension=0,
        tiled=True,
    ).astype(jnp.float32)
    a_inverse = lax.rsqrt(jnp.mean(branch * branch, axis=1, keepdims=True) + EPS)
    hidden = x_rows + branch * a_inverse * attn_gain
    h_low = lax.all_gather(hidden.astype(jnp.bfloat16), "tensor", axis=0, tiled=True)
    a_unit = branch * a_inverse
    w_gate_up = jnp.concatenate([w_gate, w_up], axis=1)
    gate_up = jnp.dot(h_low, w_gate_up, preferred_element_type=jnp.float32)
    gate = gate_up[:, :ff_cols]
    up = gate_up[:, ff_cols:]
    sigma_gate = jax.nn.sigmoid(gate)
    silu_gate = gate * sigma_gate
    act = (silu_gate * up).astype(jnp.bfloat16)
    down = lax.psum_scatter(
        jnp.dot(act, w_down, preferred_element_type=jnp.float32).astype(jnp.bfloat16),
        "tensor",
        scatter_dimension=0,
        tiled=True,
    ).astype(jnp.float32)
    f_inverse = lax.rsqrt(jnp.mean(down * down, axis=1, keepdims=True) + EPS)
    f_unit = down * f_inverse
    block_out = (hidden + f_unit * ffn_gain).astype(jnp.bfloat16)
    grad_out = cotangent.astype(jnp.float32)
    grad_ffn_part = jnp.sum(grad_out * f_unit, axis=0)
    grad_down = norm_back(grad_out, f_unit, f_inverse, ffn_gain).astype(jnp.bfloat16)
    grad_down_all = lax.all_gather(grad_down, "tensor", axis=0, tiled=True)
    grad_act = dot_last(grad_down_all, w_down)
    grad_w_down = dot_first(act, grad_down_all)
    grad_gate = grad_act * up * sigma_gate * (1.0 + gate * (1.0 - sigma_gate))
    grad_up = grad_act * silu_gate
    grad_gate_up = jnp.concatenate([grad_gate, grad_up], axis=1).astype(jnp.bfloat16)
    grad_w_gate_up = dot_first(h_low, grad_gate_up)
    grad_hidden = grad_out + lax.psum_scatter(
        dot_last(grad_gate_up, w_gate_up).astype(jnp.bfloat16), "tensor", scatter_dimension=0, tiled=True
    ).astype(jnp.float32)
    grad_attn_part = jnp.sum(grad_hidden * a_unit, axis=0)
    grad_branch = norm_back(grad_hidden, a_unit, a_inverse, attn_gain).astype(jnp.bfloat16)
    grad_branch_all = lax.all_gather(grad_branch, "tensor", axis=0, tiled=True)
    grad_w_out = dot_first(mixed, grad_branch_all)
    grad_mixed = dot_last(grad_branch_all, w_out).astype(jnp.bfloat16).reshape(shaped)

    def attend_back(pieces):
        query_block, key_block, value_block, seg_row, log_block, grad_block = pieces
        scores = scores_of(query_block, key_block, seg_row)
        probs = jnp.exp(scores - log_block[..., None])
        grad_probs = jnp.einsum(
            "qhd,khd->hqk", grad_block, value_block, preferred_element_type=jnp.float32
        )
        grad_scores = (
            probs * (grad_probs - jnp.sum(probs * grad_probs, axis=-1, keepdims=True))
        ).astype(jnp.bfloat16)
        grad_query = (
            jnp.einsum("hqk,khd->qhd", grad_scores, key_block, preferred_element_type=jnp.float32)
            * att_scale
        )
        grad_key = (
            jnp.einsum("hqk,qhd->khd", grad_scores, query_block, preferred_element_type=jnp.float32)
            * att_scale
        )
        grad_value = jnp.einsum(
            "hqk,qhd->khd",
            probs.astype(jnp.bfloat16),
            grad_block,
            preferred_element_type=jnp.float32,
        )
        return (grad_query, grad_key, grad_value.astype(jnp.bfloat16))

    grad_query, grad_key, grad_value = lax.map(
        attend_back, (query_seqs, key_seqs, value_seqs, segment_ids, log_total, grad_mixed)
    )
    grad_q_normed = rotate_back(
        rounded(grad_query.reshape(token_count, heads_here, HD)), cosine, sine
    ).reshape(token_count, head_cols)
    grad_k_normed = rotate_back(
        rounded(grad_key.reshape(token_count, heads_here, HD)), cosine, sine
    ).reshape(token_count, head_cols)
    grad_q_gain = jnp.sum(grad_q_normed * q_unit, axis=0)
    grad_k_gain = jnp.sum(grad_k_normed * k_unit, axis=0)
    inner_q = grad_q_normed * q_gain
    inner_k = grad_k_normed * k_gain
    q_inner_sum, k_inner_sum = lax.psum(
        (jnp.sum(inner_q * q_unit, axis=1), jnp.sum(inner_k * k_unit, axis=1)), "tensor"
    )
    grad_q_raw = q_inverse * (inner_q - q_unit * (q_inner_sum / full_width)[:, None])
    grad_k_raw = k_inverse * (inner_k - k_unit * (k_inner_sum / full_width)[:, None])
    grad_qkv = jnp.concatenate(
        [
            grad_q_raw.astype(jnp.bfloat16),
            grad_k_raw.astype(jnp.bfloat16),
            grad_value.reshape(token_count, head_cols),
        ],
        axis=1,
    )
    grad_w_qkv = dot_first(whole_x, grad_qkv)
    grad_tokens = grad_hidden + lax.psum_scatter(
        dot_last(grad_qkv, w_qkv).astype(jnp.bfloat16), "tensor", scatter_dimension=0, tiled=True
    ).astype(jnp.float32)
    grad_w_qkv, grad_w_out, grad_w_gate_up, grad_w_down = [
        lax.psum(part.astype(jnp.bfloat16), "dp").astype(jnp.float32)
        for part in (grad_w_qkv, grad_w_out, grad_w_gate_up, grad_w_down)
    ]
    grad_q_gain, grad_k_gain = lax.psum((grad_q_gain, grad_k_gain), "dp")
    grad_attn_gain, grad_ffn_gain = lax.psum((grad_attn_part, grad_ffn_part), ("dp", "tensor"))
    return (
        block_out,
        grad_tokens,
        grad_w_qkv[:, :head_cols],
        grad_w_qkv[:, head_cols : 2 * head_cols],
        grad_w_qkv[:, 2 * head_cols :],
        grad_w_out,
        grad_w_gate_up[:, :ff_cols],
        grad_w_gate_up[:, ff_cols:],
        grad_w_down,
        grad_q_gain,
        grad_k_gain,
        grad_attn_gain,
        grad_ffn_gain,
    )


MESH = pl.DeviceIdType.MESH
LANES = 2


def places_of():
    d = lax.axis_index("dp")
    t = lax.axis_index("tensor")
    z, c = lax.div(t, 2), lax.rem(t, 2)
    dx = d + 1 - 2 * lax.rem(d, 2)
    dy = lax.rem(d + 2, 4)
    zs = (z, z + 1 - 2 * lax.rem(z, 2), lax.rem(z + 2, 4), 3 - z)
    inner = lax.rem(z + 1, 4) >= 2
    return d, dx, dy, zs, c, inner


def remote(src, dst, send, recv, dp, tensor):
    return pltpu.make_async_remote_copy(
        src_ref=src, dst_ref=dst, send_sem=send, recv_sem=recv, device_id=(dp, tensor), device_id_type=MESH
    )


def enter(d, zs, c, dx=None, dy=None):
    barrier = pltpu.get_barrier_semaphore()
    peers = [(d, 2 * zs[r] + c) for r in (1, 2, 3)] + [(d, 2 * zs[0] + 1 - c)]
    if dx is not None:
        peers += [(dx, 2 * zs[0] + c), (dy, 2 * zs[0] + c)]
    for peer in peers:
        pl.semaphore_signal(barrier, inc=1, device_id=peer, device_id_type=MESH)
    pl.semaphore_wait(barrier, len(peers))


class Gather:
    def __init__(self, full, send, recv, place):
        self.full, self.send, self.recv = full, send, recv
        self.d, _, _, self.zs, self.c, self.inner = place
        self.t = 2 * self.zs[0] + self.c

    def lane(self, r):
        return self.full.at[2 * self.zs[r] + self.c]

    def other(self, r):
        return self.full.at[2 * self.zs[r] + 1 - self.c]

    def to_z(self, r, k, via):
        return remote(self.lane(r), self.lane(r), self.send.at[via if r == 0 else 7], self.recv.at[k], self.d, 2 * self.zs[via] + self.c)

    def to_core(self, r):
        return remote(self.lane(r), self.lane(r), self.send.at[0 if r == 0 else 3 + r], self.recv.at[4 + r], self.d, 2 * self.zs[0] + 1 - self.c)

    def start(self):
        self.to_z(0, 2, 2).start()
        self.to_z(0, 1, 1).start()
        self.to_core(0).start()

    def start_inner(self):
        @pl.when(self.inner)
        def _():
            self.to_z(0, 2, 2).wait_send()
            self.to_z(0, 3, 3).start()

    def arrive(self, r):
        self.to_z(r, r, r).wait_recv()
        if r == 2:
            @pl.when(self.inner)
            def _():
                self.to_z(2, 3, 1).start()
        self.to_core(r).start()

    def ready(self, r):
        remote(self.other(r), self.other(r), self.send.at[0], self.recv.at[4 + r], self.d, self.t).wait_recv()

    def finish(self):
        @pl.when(jnp.logical_not(self.inner))
        def _():
            self.to_z(0, 2, 2).wait_send()

        @pl.when(self.inner)
        def _():
            self.to_z(0, 3, 3).wait_send()
            self.to_z(2, 3, 1).wait_send()

        self.to_z(0, 1, 1).wait_send()
        for r in range(4):
            self.to_core(r).wait_send()


class Scatter:
    def __init__(self, parts, pair, land, send, recv, place):
        self.parts, self.pair, self.land, self.send, self.recv = parts, pair, land, send, recv
        self.d, _, _, self.zs, self.c, self.inner = place
        self.t = 2 * self.zs[0] + self.c

    def mine(self, r):
        return self.parts.at[2 * self.zs[r] + self.c]

    def to_core(self, r):
        src = self.parts.at[2 * self.zs[r] + 1 - self.c]
        return remote(src, self.pair.at[r], self.send.at[r], self.recv.at[r], self.d, 2 * self.zs[0] + 1 - self.c)

    def to_z(self, r, k, via):
        return remote(self.mine(r), self.land.at[k], self.send.at[4 + r], self.recv.at[4 + k], self.d, 2 * self.zs[via] + self.c)

    def add_pair(self, r):
        self.to_core(r).wait_recv()
        add_into(self.mine(r), self.pair.at[r])

    def pass_on(self, r):
        if r == 1:
            self.to_z(1, 1, 1).start()
        if r == 2:
            @pl.when(jnp.logical_not(self.inner))
            def _():
                self.to_z(2, 2, 2).start()
        if r == 3:
            @pl.when(self.inner)
            def _():
                self.to_z(3, 3, 3).start()

            @pl.when(jnp.logical_not(self.inner))
            def _():
                self.to_z(3, 0, 1).start()

    def relay(self):
        @pl.when(self.inner)
        def _():
            self.to_z(3, 0, 1).wait_recv()
            add_into(self.mine(2), self.land.at[0])
            self.to_z(2, 2, 2).start()

    def arrived(self):
        self.to_z(1, 1, 1).wait_recv()
        self.to_z(2, 2, 2).wait_recv()

        @pl.when(self.inner)
        def _():
            self.to_z(3, 3, 3).wait_recv()

        @pl.when(jnp.logical_not(self.inner))
        def _():
            self.land[3] = jnp.zeros(self.land.shape[1:], self.land.dtype)

    def total(self, rows):
        own = self.parts[2 * self.zs[0] + self.c, rows, :].astype(jnp.float32)
        return own + self.land[1, rows, :].astype(jnp.float32) + self.land[2, rows, :].astype(jnp.float32) + self.land[3, rows, :].astype(jnp.float32)

    def finish(self):
        for r in range(4):
            self.to_core(r).wait_send()
        for r in (1, 2, 3):
            self.to_z(r, 1, 1).wait_send()


def add_into(into, other):
    rows = into.shape[0]

    def step(i, carry):
        at = pl.ds(pl.multiple_of(i * 32, 32), 32)
        into[at, :] = (into[at, :].astype(jnp.float32) + other[at, :].astype(jnp.float32)).astype(into.dtype)
        return carry

    lax.fori_loop(0, rows // 32, step, 0)


class Spread:
    def __init__(self, full, whole, send, recv, own_sem, place):
        self.full, self.whole, self.send, self.recv, self.own_sem = full, whole, send, recv, own_sem
        self.d, self.dx, self.dy, self.zs, self.c, _ = place
        self.t = 2 * self.zs[0] + self.c

    def slot(self, g, r):
        return self.whole.at[g, 2 * self.zs[r] + self.c]

    def own(self, r, k):
        src = self.full.at[2 * self.zs[r] + self.c]
        return remote(src, self.slot(1 + k, r), self.send.at[k * 4 + r], self.recv.at[k * 4 + r], (self.dx, self.dy)[k], self.t)

    def start(self, r):
        self.own(r, 0).start()
        self.own(r, 1).start()

    def hop(self, r):
        group, target = (1, self.dy) if r in (0, 3) else (2, self.dx)
        return remote(self.slot(group, r), self.slot(3, r), self.send.at[8 + r], self.recv.at[8 + r], target, self.t)

    def to_core(self, r, k):
        return remote(self.slot(1 + k, r), self.slot(1 + k, r), self.send.at[12 + k * 4 + r], self.recv.at[12 + k * 4 + r], self.d, 2 * self.zs[0] + 1 - self.c)

    def pass_on(self, r):
        self.own(r, 0).wait_recv()
        self.own(r, 1).wait_recv()
        self.hop(r).start()
        self.to_core(r, 0).start()
        self.to_core(r, 1).start()

    def last(self, r):
        self.hop(r).wait_recv()
        self.to_core(r, 2).start()

    def keep(self):
        return pltpu.make_async_copy(self.full, self.whole.at[0], self.own_sem)

    def finish(self):
        for r in range(4):
            self.own(r, 0).wait_send()
            self.own(r, 1).wait_send()
            self.hop(r).wait_send()
            for k in range(3):
                self.to_core(r, k).wait()
        self.keep().wait()


def dot_nt(left, right):
    return lax.dot_general(left, right, (((1,), (1,)), ((), ())), preferred_element_type=jnp.float32)


def ffn_kernel(
    x_ref, br_ref, cot_ref, again_ref, gain_ref, wg_ref, wu_ref, wd_ref,
    bo_ref, gh_ref, gb_ref, gains_ref, act, gg, gu, hall_ref, gdall_ref,
    hfull, gfull, hid_ref, sums, gate, up, parts, pair, land,
    ag_send, ag_recv, rs_send, rs_recv, xy_send, xy_recv, own_sem,
):
    place = places_of()
    d, dx, dy, zs, c, inner = place
    t = 2 * zs[0] + c
    width = wg_ref.shape[1]
    rows, wide = x_ref.shape
    ft, dt = 512, 1024
    step_rows = 32
    a_gain, gain = again_ref[...], gain_ref[...]

    def opening(i, carry):
        at = pl.ds(pl.multiple_of(i * step_rows, step_rows), step_rows)
        branch = br_ref[at, :]
        inverse = lax.rsqrt(jnp.mean(branch * branch, axis=1, keepdims=True) + EPS)
        hidden = x_ref[at, :].astype(jnp.float32) + branch * inverse * a_gain
        hid_ref[at, :] = hidden
        hfull[t, at, :] = hidden.astype(jnp.bfloat16)
        return carry

    lax.fori_loop(0, rows // step_rows, opening, 0)
    enter(d, zs, c, dx, dy)

    def unit_forward(zz):
        both = pl.ds(2 * zz, 2)
        at = pl.ds(pl.multiple_of(zz * 2 * rows, 2 * rows), 2 * rows)

        def mid(j, carry):
            cols = pl.ds(pl.multiple_of(j * ft, ft), ft)
            block = hfull[both].reshape(2 * rows, wide)
            g = jnp.dot(block, wg_ref[:, cols], preferred_element_type=jnp.float32)
            u = jnp.dot(block, wu_ref[:, cols], preferred_element_type=jnp.float32)
            gate[at, cols] = g
            up[at, cols] = u
            act[at, cols] = (g * jax.nn.sigmoid(g) * u).astype(jnp.bfloat16)
            return carry

        lax.fori_loop(0, width // ft, mid, 0)

        def out(j, carry):
            cols = pl.ds(pl.multiple_of(j * dt, dt), dt)
            p = jnp.dot(act[at, :], wd_ref[:, cols], preferred_element_type=jnp.float32)
            parts[both, :, cols] = p.astype(jnp.bfloat16).reshape(2, rows, dt)
            return carry

        lax.fori_loop(0, wide // dt, out, 0)

    def unit_backward(zz):
        both = pl.ds(2 * zz, 2)
        at = pl.ds(pl.multiple_of(zz * 2 * rows, 2 * rows), 2 * rows)

        def mid(j, carry):
            cols = pl.ds(pl.multiple_of(j * ft, ft), ft)
            block = gfull[both].reshape(2 * rows, wide)
            ga = dot_nt(block, wd_ref[cols, :])
            g, u = gate[at, cols], up[at, cols]
            s = jax.nn.sigmoid(g)
            gg[at, cols] = (ga * u * s * (1.0 + g * (1.0 - s))).astype(jnp.bfloat16)
            gu[at, cols] = (ga * (g * s)).astype(jnp.bfloat16)
            return carry

        lax.fori_loop(0, width // ft, mid, 0)

        def out(j, carry):
            cols = pl.ds(pl.multiple_of(j * dt, dt), dt)
            p = dot_nt(gg[at, :], wg_ref[cols, :]) + dot_nt(gu[at, :], wu_ref[cols, :])
            parts[both, :, cols] = p.astype(jnp.bfloat16).reshape(2, rows, dt)
            return carry

        lax.fori_loop(0, wide // dt, out, 0)

    def phase(p, full, whole, unit):
        ag = Gather(full, ag_send.at[p], ag_recv.at[p], place)
        rs = Scatter(parts, pair.at[p], land.at[p], rs_send.at[p], rs_recv.at[p], place)
        xy = Spread(full, whole, xy_send.at[p], xy_recv.at[p], own_sem.at[p], place)
        ag.start()
        xy.start(0)
        ag.ready(0)
        unit(zs[0])
        rs.to_core(0).start()
        ag.start_inner()
        ag.arrive(2)
        xy.start(2)
        ag.arrive(1)
        xy.start(1)
        ag.ready(2)
        unit(zs[2])
        rs.to_core(2).start()
        ag.ready(1)
        unit(zs[1])
        rs.to_core(1).start()
        rs.add_pair(2)
        rs.pass_on(2)
        rs.add_pair(1)
        rs.pass_on(1)
        ag.arrive(3)
        xy.start(3)
        ag.ready(3)
        unit(zs[3])
        rs.to_core(3).start()
        xy.keep().start()
        rs.add_pair(3)
        rs.pass_on(3)
        rs.add_pair(0)
        xy.pass_on(0)
        xy.pass_on(2)
        xy.pass_on(1)
        rs.relay()
        rs.arrived()
        return ag, rs, xy

    ag, rs, xy_h = phase(0, hfull, hall_ref, unit_forward)
    sums[...] = jnp.zeros_like(sums)

    def middle(i, carry):
        at = pl.ds(pl.multiple_of(i * step_rows, step_rows), step_rows)
        down = rs.total(at)
        inverse = lax.rsqrt(jnp.mean(down * down, axis=1, keepdims=True) + EPS)
        unit = down * inverse
        bo_ref[at, :] = (hid_ref[at, :] + unit * gain).astype(jnp.bfloat16)
        grad = cot_ref[at, :].astype(jnp.float32)
        sums[0:1, :] += jnp.sum(grad * unit, axis=0, keepdims=True)
        inner_grad = grad * gain
        gfull[t, at, :] = (inverse * (inner_grad - unit * jnp.mean(inner_grad * unit, axis=1, keepdims=True))).astype(jnp.bfloat16)
        return carry

    lax.fori_loop(0, rows // step_rows, middle, 0)
    ag.finish()
    rs.finish()
    xy_h.pass_on(3)
    for r in range(4):
        xy_h.last(r)
    ag, rs, xy = phase(1, gfull, gdall_ref, unit_backward)

    def ending(i, carry):
        at = pl.ds(pl.multiple_of(i * step_rows, step_rows), step_rows)
        grad = cot_ref[at, :].astype(jnp.float32) + rs.total(at)
        gh_ref[at, :] = grad
        branch = br_ref[at, :]
        inverse = lax.rsqrt(jnp.mean(branch * branch, axis=1, keepdims=True) + EPS)
        unit = branch * inverse
        sums[1:2, :] += jnp.sum(grad * unit, axis=0, keepdims=True)
        inner_grad = grad * a_gain
        gb_ref[at, :] = (inverse * (inner_grad - unit * jnp.mean(inner_grad * unit, axis=1, keepdims=True))).astype(jnp.bfloat16)
        return carry

    lax.fori_loop(0, rows // step_rows, ending, 0)
    for i in range(wide // HD):
        gains_ref[i : i + 1, :] = sums[0:1, i * HD : (i + 1) * HD]
        gains_ref[wide // HD + i : wide // HD + i + 1, :] = sums[1:2, i * HD : (i + 1) * HD]
    ag.finish()
    rs.finish()
    xy.pass_on(3)
    for r in range(4):
        xy.last(r)
    xy_h.finish()
    xy.finish()


def ffn(x_own, branch, cot, attn_gain, ffn_gain, w_gate, w_up, w_down):
    rows, wide = x_own.shape
    width = w_gate.shape[1]
    groups, world = 4, 8
    vmem = pl.BlockSpec(memory_space=pltpu.VMEM)
    anywhere = pl.BlockSpec(memory_space=pl.ANY)
    bf, f32 = jnp.bfloat16, jnp.float32
    whole = jax.ShapeDtypeStruct((groups, world, rows, wide), bf)
    units = jax.ShapeDtypeStruct((world * rows, width), bf)
    dma = pltpu.SemaphoreType.DMA
    return pl.pallas_call(
        ffn_kernel,
        out_shape=(
            jax.ShapeDtypeStruct((rows, wide), bf),
            jax.ShapeDtypeStruct((rows, wide), f32),
            jax.ShapeDtypeStruct((rows, wide), bf),
            jax.ShapeDtypeStruct((2 * wide // HD, HD), f32),
            units, units, units,
            whole,
            whole,
        ),
        in_specs=[vmem] * 8,
        out_specs=(vmem,) * 7 + (anywhere, anywhere),
        scratch_shapes=[
            pltpu.VMEM((world, rows, wide), bf),
            pltpu.VMEM((world, rows, wide), bf),
            pltpu.VMEM((rows, wide), f32),
            pltpu.VMEM((8, wide), f32),
            pltpu.VMEM((world * rows, width), f32),
            pltpu.VMEM((world * rows, width), f32),
            pltpu.VMEM((world, rows, wide), bf),
            pltpu.VMEM((2, 4, rows, wide), bf),
            pltpu.VMEM((2, 4, rows, wide), bf),
            dma((2, 8)),
            dma((2, 8)),
            dma((2, 8)),
            dma((2, 8)),
            dma((2, 24)),
            dma((2, 24)),
            dma((2,)),
        ],
        compiler_params=pltpu.CompilerParams(
            collective_id=2, has_side_effects=True, vmem_limit_bytes=60 * 2**20
        ),
        name="ffn",
    )(x_own, branch, cot, attn_gain.reshape(1, wide), ffn_gain.reshape(1, wide), w_gate, w_up, w_down)


WINDOW = 3


class Exchange:
    def __init__(self, block, land, send, recv, place):
        self.block, self.land, self.send, self.recv = block, land, send, recv
        self.d, _, _, self.zs, self.c, _ = place
        self.t = 2 * self.zs[0] + self.c

    def copies(self):
        out = []
        for r in range(4):
            for k in range(2):
                if r == 0 and k == 0:
                    continue
                at = 4 * k + r
                core = self.c if k == 0 else 1 - self.c
                out.append((2 * self.zs[r] + core, at))
        return out

    def start(self):
        for peer, at in self.copies():
            remote(self.block, self.land.at[self.t], self.send.at[at], self.recv.at[at], self.d, peer).start()

    def wait(self):
        for peer, at in self.copies():
            remote(self.block, self.land.at[peer], self.send.at[at], self.recv.at[at], self.d, peer).wait()


def enter_all(d, zs, c, dx, dy):
    barrier = pltpu.get_barrier_semaphore()
    peers = [(d, 2 * zs[r] + c) for r in (1, 2, 3)] + [(d, 2 * zs[r] + 1 - c) for r in range(4)]
    peers += [(dx, 2 * zs[0] + c), (dy, 2 * zs[0] + c)]
    for peer in peers:
        pl.semaphore_signal(barrier, inc=1, device_id=peer, device_id_type=MESH)
    pl.semaphore_wait(barrier, len(peers))


def put_column(stat, base, zz, square):
    rows = square.shape[0]
    folded = square[:, :HD]
    for h in range(1, square.shape[1] // HD):
        folded = folded + square[:, h * HD : (h + 1) * HD]
    line = jnp.sum(folded.T, axis=0, keepdims=True)
    for i in range(rows // HD):
        stat[pl.ds(base + 2 * zz + i, 1), :] = line[:, i * HD : (i + 1) * HD]


def get_column(stat_row, count):
    return jnp.broadcast_to(stat_row, (count, HD)).T


def attn_kernel(
    x_ref, wq_ref, wk_ref, wv_ref, wo_ref, qg_ref, kg_ref, cos_ref, sin_ref, first_ref,
    br_ref, q_out, k_out, v_out, qu_out, ku_out, rq_out, rk_out, mixed_out, xall_ref,
    xfull, parts, pair, land, stat, stats,
    ag_send, ag_recv, rs_send, rs_recv, xy_send, xy_recv, st_send, st_recv, own_sem,
):
    place = places_of()
    d, dx, dy, zs, c, inner = place
    t = 2 * zs[0] + c
    rows, wide = x_ref.shape
    span = 2 * rows
    heads = wq_ref.shape[1] // HD
    xfull[t] = x_ref[...]
    enter_all(d, zs, c, dx, dy)
    ag = Gather(xfull, ag_send, ag_recv, place)
    rs = Scatter(parts, pair, land, rs_send, rs_recv, place)
    xy = Spread(xfull, xall_ref, xy_send, xy_recv, own_sem, place)
    ex = Exchange(stat, stats, st_send, st_recv, place)

    def at_of(zz):
        return pl.ds(pl.multiple_of(zz * span, span), span)

    def project_qk(zz):
        block = xfull[pl.ds(2 * zz, 2)].reshape(span, wide)
        for w_ref, out, base in ((wq_ref, qu_out, 0), (wk_ref, ku_out, 8)):
            raw = jnp.dot(block, w_ref[...], preferred_element_type=jnp.float32)
            out[at_of(zz), :] = raw
            put_column(stat, base, zz, raw * raw)

    def project_v(zz):
        block = xfull[pl.ds(2 * zz, 2)].reshape(span, wide)
        v_out[at_of(zz), :] = jnp.dot(block, wv_ref[...], preferred_element_type=jnp.float32).astype(jnp.bfloat16)

    ag.start()
    xy.start(0)
    ag.ready(0)
    project_qk(zs[0])
    project_v(zs[0])
    ag.start_inner()
    ag.arrive(2)
    xy.start(2)
    ag.arrive(1)
    xy.start(1)
    ag.ready(2)
    project_qk(zs[2])
    ag.ready(1)
    project_qk(zs[1])
    project_v(zs[2])
    ag.arrive(3)
    xy.start(3)
    ag.ready(3)
    project_qk(zs[3])
    ex.start()
    project_v(zs[1])
    project_v(zs[3])
    xy.keep().start()
    ex.wait()
    total = stat[...]
    for r in range(4):
        for k in range(2):
            if r or k:
                total = total + stats[2 * zs[r] + (c if k == 0 else 1 - c)]
    inverse = lax.rsqrt(total / (8 * wq_ref.shape[1]) + EPS)
    rq_out[...] = inverse[:8]
    rk_out[...] = inverse[8:]

    def norm_rope(i, carry):
        at = pl.ds(pl.multiple_of(i * HD, HD), HD)
        cosine, sine = cos_ref[at, :], sin_ref[at, :]
        for line, raw, out, gain in ((rq_out, qu_out, q_out, qg_ref), (rk_out, ku_out, k_out, kg_ref)):
            scale = get_column(line[pl.ds(i, 1), :], HD)
            for h in range(heads):
                cols = slice(h * HD, (h + 1) * HD)
                unit = raw[at, cols] * scale
                raw[at, cols] = unit
                normed = unit * gain[:, cols]
                out[at, cols] = (normed * cosine + pltpu.roll(normed, HD // 2, 1) * sine).astype(jnp.bfloat16)
        return carry

    lax.fori_loop(0, 8, norm_rope, 0)

    def attend(zz):
        at = at_of(zz)
        low = jnp.maximum(zz - (WINDOW - 1), 0) * span
        keys_at = pl.ds(pl.multiple_of(low, span), WINDOW * span)
        key_place = low + lax.broadcasted_iota(jnp.int32, (span, WINDOW * span), 1)
        query_place = zz * span + lax.broadcasted_iota(jnp.int32, (span, WINDOW * span), 0)
        allowed = (key_place <= query_place) & (key_place >= first_ref[at, :])
        for h in range(heads):
            cols = slice(h * HD, (h + 1) * HD)
            scores = dot_nt(q_out[at, cols], k_out[keys_at, cols]) * HD**-0.5
            scores = jnp.where(allowed, scores, -1e30)
            top = jnp.max(scores, axis=1, keepdims=True)
            expo = jnp.exp(scores - top)
            probs = expo * (1.0 / jnp.sum(expo, axis=1, keepdims=True))
            mixed_out[at, cols] = jnp.dot(probs.astype(jnp.bfloat16), v_out[keys_at, cols], preferred_element_type=jnp.float32).astype(jnp.bfloat16)
        dt = 1024

        def out(j, carry):
            to = pl.ds(pl.multiple_of(j * dt, dt), dt)
            p = jnp.dot(mixed_out[at, :], wo_ref[:, to], preferred_element_type=jnp.float32)
            parts[pl.ds(2 * zz, 2), :, to] = p.astype(jnp.bfloat16).reshape(2, rows, dt)
            return carry

        lax.fori_loop(0, wide // dt, out, 0)

    attend(zs[3])
    rs.to_core(3).start()
    attend(zs[2])
    rs.to_core(2).start()
    rs.add_pair(3)
    rs.pass_on(3)
    attend(zs[1])
    rs.to_core(1).start()
    rs.add_pair(2)
    rs.pass_on(2)
    rs.add_pair(1)
    rs.pass_on(1)
    attend(zs[0])
    rs.to_core(0).start()
    rs.add_pair(0)
    xy.pass_on(0)
    xy.pass_on(2)
    xy.pass_on(1)
    rs.relay()
    xy.pass_on(3)
    for r in range(4):
        xy.last(r)
    rs.arrived()

    def ending(i, carry):
        at = pl.ds(pl.multiple_of(i * 32, 32), 32)
        br_ref[at, :] = rs.total(at)
        return carry

    lax.fori_loop(0, rows // 32, ending, 0)
    ag.finish()
    rs.finish()
    xy.finish()


def attention(x_own, w_query, w_key, w_value, w_out, q_gain, k_gain, cosine, sine, first):
    rows, wide = x_own.shape
    head_cols = w_query.shape[1]
    groups, world = 4, 8
    count = world * rows
    vmem = pl.BlockSpec(memory_space=pltpu.VMEM)
    bf, f32 = jnp.bfloat16, jnp.float32
    dma = pltpu.SemaphoreType.DMA
    cols = jax.ShapeDtypeStruct((count, head_cols), bf)
    wide_cols = jax.ShapeDtypeStruct((count, head_cols), f32)
    line = jax.ShapeDtypeStruct((8, HD), f32)
    return pl.pallas_call(
        attn_kernel,
        out_shape=(
            jax.ShapeDtypeStruct((rows, wide), f32),
            cols, cols, cols, wide_cols, wide_cols, line, line, cols,
            jax.ShapeDtypeStruct((groups, world, rows, wide), bf),
        ),
        in_specs=[vmem] * 10,
        out_specs=(vmem,) * 9 + (pl.BlockSpec(memory_space=pl.ANY),),
        scratch_shapes=[
            pltpu.VMEM((world, rows, wide), bf),
            pltpu.VMEM((world, rows, wide), bf),
            pltpu.VMEM((4, rows, wide), bf),
            pltpu.VMEM((4, rows, wide), bf),
            pltpu.VMEM((16, HD), f32),
            pltpu.VMEM((world, 16, HD), f32),
            dma((8,)), dma((8,)), dma((8,)), dma((8,)), dma((24,)), dma((24,)), dma((8,)), dma((8,)),
            pltpu.SemaphoreType.DMA,
        ],
        compiler_params=pltpu.CompilerParams(
            collective_id=1, has_side_effects=True, vmem_limit_bytes=60 * 2**20
        ),
        name="attn",
    )(x_own, w_query, w_key, w_value, w_out, q_gain.reshape(1, -1), k_gain.reshape(1, -1), cosine, sine, first)


def dot_tn(left, right):
    return lax.dot_general(left, right, (((0,), (0,)), ((), ())), preferred_element_type=jnp.float32)


class Background:
    tokens, units = 512, 512

    def __init__(self, hall, gdall, weights, outs, hbuf, gbuf, tiles, sums, mids, load_sem, tile_sem, out_sem):
        self.hall, self.gdall, self.weights, self.outs = hall, gdall, weights, outs
        self.hbuf, self.gbuf, self.tiles, self.sums, self.mids = hbuf, gbuf, tiles, sums, mids
        self.load_sem, self.tile_sem, self.out_sem = load_sem, tile_sem, out_sem
        self.blocks = self.tokens // hall.shape[2]
        self.per_group = hall.shape[1] // self.blocks
        self.per_tile = 3 * self.per_group
        self.tile_count = weights[0].shape[1] // self.units
        self.count = self.tile_count * self.per_tile

    def loads(self, n):
        slot, m = n % 2, n % self.per_tile
        group, part = 1 + m // self.per_group, m % self.per_group
        blocks = pl.ds(part * self.blocks, self.blocks)
        return (
            pltpu.make_async_copy(self.hall.at[group, blocks], self.hbuf.at[slot], self.load_sem.at[0, slot]),
            pltpu.make_async_copy(self.gdall.at[group, blocks], self.gbuf.at[slot], self.load_sem.at[1, slot]),
        )

    def tile_loads(self, tile):
        at = pl.ds(tile * self.units, self.units)
        wg, wu, wd = self.weights
        return (
            pltpu.make_async_copy(wg.at[:, at], self.tiles[0], self.tile_sem.at[0]),
            pltpu.make_async_copy(wu.at[:, at], self.tiles[1], self.tile_sem.at[1]),
            pltpu.make_async_copy(wd.at[at, :], self.tiles[2], self.tile_sem.at[2]),
        )

    def stores(self, tile):
        at = pl.ds(tile * self.units, self.units)
        og, ou, od = self.outs
        return (
            pltpu.make_async_copy(self.sums[0], og.at[:, at], self.out_sem.at[0]),
            pltpu.make_async_copy(self.sums[1], ou.at[:, at], self.out_sem.at[1]),
            pltpu.make_async_copy(self.sums[2], od.at[at, :], self.out_sem.at[2]),
        )

    def begin(self):
        for copy in self.tile_loads(0) + self.loads(0):
            copy.start()

    def step(self, n):
        slot, tile, m = n % 2, n // self.per_tile, n % self.per_tile
        if n + 1 < self.count:
            for copy in self.loads(n + 1):
                copy.start()
        if m == 0:
            for copy in self.tile_loads(tile):
                copy.wait()
            if tile:
                for copy in self.stores(tile - 1):
                    copy.wait()
        for copy in self.loads(n):
            copy.wait()
        hbuf, gbuf = self.hbuf.at[slot], self.gbuf.at[slot]
        wg, wu, wd = self.tiles
        act, gg, gu = self.mids
        rows, wide = hbuf.shape[1:]
        half = self.tokens // 2

        def mid(i, carry):
            blocks = pl.ds(i * (self.blocks // 2), self.blocks // 2)
            at = pl.ds(pl.multiple_of(i * half, half), half)
            h = hbuf[blocks].reshape(half, wide)
            g = jnp.dot(h, wg[...], preferred_element_type=jnp.float32)
            u = jnp.dot(h, wu[...], preferred_element_type=jnp.float32)
            ga = dot_nt(gbuf[blocks].reshape(half, wide), wd[...])
            s = jax.nn.sigmoid(g)
            gs = g * s
            act[at, :] = (gs * u).astype(jnp.bfloat16)
            gg[at, :] = (ga * u * s * (1.0 + g * (1.0 - s))).astype(jnp.bfloat16)
            gu[at, :] = (ga * gs).astype(jnp.bfloat16)
            return carry

        lax.fori_loop(0, 2, mid, 0)
        span = 512

        def into(i, carry):
            at = pl.ds(pl.multiple_of(i * span, span), span)
            h = hbuf[:, :, at].reshape(self.tokens, span)
            pg = dot_tn(h, gg[...])
            pu = dot_tn(h, gu[...])
            pd = dot_tn(act[...], gbuf[:, :, at].reshape(self.tokens, span))
            if m == 0:
                self.sums[0][at, :], self.sums[1][at, :], self.sums[2][:, at] = pg, pu, pd
            else:
                self.sums[0][at, :] += pg
                self.sums[1][at, :] += pu
                self.sums[2][:, at] += pd
            return carry

        lax.fori_loop(0, wide // span, into, 0)
        if m == self.per_tile - 1:
            for copy in self.stores(tile):
                copy.start()
            if tile + 1 < self.tile_count:
                for copy in self.tile_loads(tile + 1):
                    copy.start()

    def finish(self):
        for copy in self.stores(self.tile_count - 1):
            copy.wait()


class SpreadColumns:
    def __init__(self, own, whole, send, recv, own_sem, place):
        self.src, self.whole, self.send, self.recv, self.own_sem = own, whole, send, recv, own_sem
        self.d, self.dx, self.dy, self.zs, self.c, _ = place
        self.t = 2 * self.zs[0] + self.c

    def own(self, p, k):
        return remote(self.src.at[p], self.whole.at[1 + k, p], self.send.at[k * 3 + p], self.recv.at[k * 3 + p], (self.dx, self.dy)[k], self.t)

    def hop(self, p, b):
        half = self.src.shape[1] // 2
        at = pl.ds(b * half, half)
        return remote(self.whole.at[1 + b, p, at], self.whole.at[3, p, at], self.send.at[6 + 2 * p + b], self.recv.at[6 + 2 * p + b], (self.dy, self.dx)[b], self.t)

    def start(self, p):
        self.own(p, 0).start()
        self.own(p, 1).start()

    def pass_on(self, p):
        for b in range(2):
            self.own(p, b).wait_recv()
            self.hop(p, b).start()

    def keep(self):
        return pltpu.make_async_copy(self.src, self.whole.at[0], self.own_sem)

    def finish(self):
        for p in range(3):
            for b in range(2):
                self.own(p, b).wait_send()
                self.hop(p, b).wait()
        self.keep().wait()


class SumHalves:
    def __init__(self, buf, once, twice, send, recv, place):
        self.buf, self.land, self.send, self.recv = buf, (once, twice), send, recv
        self.d, self.dx, self.dy, self.zs, self.c, _ = place
        self.t = 2 * self.zs[0] + self.c

    def move(self, stage, b):
        at = 2 * stage + b
        return remote(self.buf.at[b], self.land[stage].at[b], self.send.at[at], self.recv.at[at], (self.dx, self.dy)[(stage + b) % 2], self.t)

    def start(self, stage):
        for b in range(2):
            self.move(stage, b).start()

    def add(self, stage):
        for b in range(2):
            self.move(stage, b).wait()
            add_into(self.buf.at[b], self.land[stage].at[b])


class ExchangeGroups:
    def __init__(self, block, land, send, recv, place):
        self.block, self.land, self.send, self.recv = block, land, send, recv
        d, dx, dy, zs, c, _ = place
        self.peers, self.t = (dx, dy, 3 - d), 2 * zs[0] + c

    def copies(self):
        return [remote(self.block, self.land.at[k], self.send.at[k], self.recv.at[k], peer, self.t) for k, peer in enumerate(self.peers)]

    def start(self):
        for copy in self.copies():
            copy.start()

    def wait(self):
        for copy in self.copies():
            copy.wait()


def back_kernel(
    gb_ref, gh_ref, q_ref, k_ref, v_ref, mixed_ref, qu_ref, ku_ref, rq_ref, rk_ref, first_ref, cos_ref, sin_ref,
    qg_ref, kg_ref, wq_ref, wk_ref, wv_ref, wo_ref, gains_ref, hall, gdall, wg, wu, wd,
    gt_ref, gains_out, dwo_ref, gall_ref, dwg, dwu, dwd,
    full, pair, land, gm, dq, dk, dv, own, wo_once, wo_twice, stat, stats, gland, block, blocks, gacc,
    hbuf, gbuf, tg, tu, td, sg, su, sd, act, gg, gu,
    ag_send, ag_recv, rs_send, rs_recv, st_send, st_recv, ga_send, ga_recv, gr_send, gr_recv,
    co_send, co_recv, wo_send, wo_recv, own_sem, load_sem, tile_sem, out_sem,
):
    place = places_of()
    d, dx, dy, zs, c, inner = place
    t = 2 * zs[0] + c
    rows, wide = gb_ref.shape
    span = 2 * rows
    heads = wq_ref.shape[1] // HD
    count = q_ref.shape[0]
    scale = HD**-0.5
    full[t] = gb_ref[...]
    barrier = pltpu.get_barrier_semaphore()
    peers = [(d, 2 * zs[r] + c) for r in (1, 2, 3)] + [(d, 2 * zs[r] + 1 - c) for r in range(4)]
    peers += [(dx, t), (dy, t), (3 - d, t)]
    for peer in peers:
        pl.semaphore_signal(barrier, inc=1, device_id=peer, device_id_type=MESH)
    pl.semaphore_wait(barrier, len(peers))
    ag = Gather(full, ag_send, ag_recv, place)
    rs = Scatter(full, pair, land, rs_send, rs_recv, place)
    ex = Exchange(stat, stats, st_send, st_recv, place)
    gains = Exchange(gains_ref, gland, ga_send, ga_recv, place)
    groups = ExchangeGroups(block, blocks, gr_send, gr_recv, place)
    cols_all = SpreadColumns(own, gall_ref, co_send, co_recv, own_sem, place)
    wo_sum = SumHalves(dwo_ref, wo_once, wo_twice, wo_send, wo_recv, place)
    work = Background(hall, gdall, (wg, wu, wd), (dwg, dwu, dwd), hbuf, gbuf, (tg, tu, td), (sg, su, sd), (act, gg, gu), load_sem, tile_sem, out_sem)

    def at_of(zz):
        return pl.ds(pl.multiple_of(zz * span, span), span)

    ag.start()
    gains.start()
    work.begin()
    work.step(0)
    work.step(1)
    ag.ready(0)
    ag.start_inner()
    ag.arrive(2)
    ag.arrive(1)
    work.step(2)
    work.step(3)
    ag.ready(2)
    ag.ready(1)
    ag.arrive(3)
    work.step(4)
    work.step(5)
    ag.ready(3)

    def mixed_back(zz, carry):
        part = full[pl.ds(2 * zz, 2)].reshape(span, wide)
        gm[at_of(zz), :] = dot_nt(part, wo_ref[...]).astype(jnp.bfloat16)
        return carry

    lax.fori_loop(0, 4, mixed_back, 0)

    def out_back(j, carry):
        to = pl.ds(pl.multiple_of(j * 512, 512), 512)
        p = dot_tn(mixed_ref[...], full[:, :, to].reshape(count, 512))
        dwo_ref[:, :, to] = p.astype(jnp.bfloat16).reshape(2, p.shape[0] // 2, 512)
        return carry

    lax.fori_loop(0, wide // 512, out_back, 0)
    wo_sum.start(0)
    ag.finish()
    dk[...] = jnp.zeros_like(dk)
    dv[...] = jnp.zeros_like(dv)

    def attend_back(zz, carry):
        at = at_of(zz)
        low = jnp.maximum(zz - (WINDOW - 1), 0) * span
        keys_at = pl.ds(pl.multiple_of(low, span), WINDOW * span)
        key_place = low + lax.broadcasted_iota(jnp.int32, (span, WINDOW * span), 1)
        query_place = zz * span + lax.broadcasted_iota(jnp.int32, (span, WINDOW * span), 0)
        allowed = (key_place <= query_place) & (key_place >= first_ref[at, :])
        for h in range(heads):
            cols = slice(h * HD, (h + 1) * HD)
            scores = dot_nt(q_ref[at, cols], k_ref[keys_at, cols]) * scale
            scores = jnp.where(allowed, scores, -1e30)
            top = jnp.max(scores, axis=1, keepdims=True)
            expo = jnp.exp(scores - top)
            probs = expo * (1.0 / jnp.sum(expo, axis=1, keepdims=True))
            grad = gm[at, cols]
            gp = dot_nt(grad, v_ref[keys_at, cols])
            gs = (probs * (gp - jnp.sum(probs * gp, axis=1, keepdims=True))).astype(jnp.bfloat16)
            dq[at, cols] = jnp.dot(gs, k_ref[keys_at, cols], preferred_element_type=jnp.float32) * scale
            dk[keys_at, cols] += dot_tn(gs, q_ref[at, cols]) * scale
            dv[keys_at, cols] += dot_tn(probs.astype(jnp.bfloat16), grad)
        return carry

    lax.fori_loop(0, 4, attend_back, 0)
    own[2] = dv[...].astype(jnp.bfloat16)
    cols_all.start(2)
    wo_sum.add(0)
    wo_sum.start(1)
    gacc[...] = jnp.zeros_like(gacc)

    def unrope(i, carry):
        at = pl.ds(pl.multiple_of(i * HD, HD), HD)
        cosine, sine = cos_ref[at, :], sin_ref[at, :]
        for n, (grad, unit_ref, gain) in enumerate(((dq, qu_ref, qg_ref), (dk, ku_ref, kg_ref))):
            total = jnp.zeros((HD, HD), jnp.float32)
            for h in range(heads):
                cols = slice(h * HD, (h + 1) * HD)
                value = grad[at, cols].astype(jnp.bfloat16).astype(jnp.float32)
                value = value * cosine - pltpu.roll(value, HD // 2, 1) * sine
                unit = unit_ref[at, cols]
                row = n * heads + h
                gacc[row : row + 1, :] += jnp.sum(value * unit, axis=0, keepdims=True)
                value = value * gain[:, cols]
                grad[at, cols] = value
                total = total + value * unit
            stat[pl.ds(8 * n + i, 1), :] = jnp.sum(total.T, axis=0, keepdims=True)
        return carry

    lax.fori_loop(0, count // HD, unrope, 0)
    ex.start()
    gains.wait()
    total = gains_ref[...]
    for r in range(4):
        for k in range(2):
            if r or k:
                total = total + gland[2 * zs[r] + (c if k == 0 else 1 - c)]
    lines = gains_ref.shape[0]
    block[:lines, :] = total
    block[lines:, :] = gacc[...]
    groups.start()
    work.step(6)
    ex.wait()
    total = stat[...]
    for r in range(4):
        for k in range(2):
            if r or k:
                total = total + stats[2 * zs[r] + (c if k == 0 else 1 - c)]
    stat[...] = total * (1.0 / (8 * wq_ref.shape[1]))

    def norm_back_rows(i, carry):
        at = pl.ds(pl.multiple_of(i * HD, HD), HD)
        for n, (grad, unit_ref, inv_ref) in enumerate(((dq, qu_ref, rq_ref), (dk, ku_ref, rk_ref))):
            mean = get_column(stat[pl.ds(8 * n + i, 1), :], HD)
            inverse = get_column(inv_ref[pl.ds(i, 1), :], HD)
            for h in range(heads):
                cols = slice(h * HD, (h + 1) * HD)
                own[n, at, cols] = (inverse * (grad[at, cols] - unit_ref[at, cols] * mean)).astype(jnp.bfloat16)
        return carry

    lax.fori_loop(0, count // HD, norm_back_rows, 0)
    cols_all.start(0)
    cols_all.start(1)
    cols_all.keep().start()

    def tokens_back(zz):
        at = at_of(zz)
        dt = 1024

        def out(j, carry):
            to = pl.ds(pl.multiple_of(j * dt, dt), dt)
            p = dot_nt(own[0, at, :], wq_ref[to, :]) + dot_nt(own[1, at, :], wk_ref[to, :]) + dot_nt(own[2, at, :], wv_ref[to, :])
            full[pl.ds(2 * zz, 2), :, to] = p.astype(jnp.bfloat16).reshape(2, rows, dt)
            return carry

        lax.fori_loop(0, wide // dt, out, 0)

    tokens_back(zs[3])
    rs.to_core(3).start()
    tokens_back(zs[2])
    rs.to_core(2).start()
    rs.add_pair(3)
    rs.pass_on(3)
    tokens_back(zs[1])
    rs.to_core(1).start()
    rs.add_pair(2)
    rs.pass_on(2)
    rs.add_pair(1)
    rs.pass_on(1)
    tokens_back(zs[0])
    rs.to_core(0).start()
    rs.add_pair(0)
    cols_all.pass_on(2)
    wo_sum.add(1)
    work.step(7)
    rs.relay()
    work.step(8)
    work.step(9)
    cols_all.pass_on(0)
    cols_all.pass_on(1)
    work.step(10)
    work.step(11)
    rs.arrived()

    def ending(i, carry):
        at = pl.ds(pl.multiple_of(i * 32, 32), 32)
        gt_ref[at, :] = gh_ref[at, :] + rs.total(at)
        return carry

    lax.fori_loop(0, rows // 32, ending, 0)
    groups.wait()
    gains_out[...] = block[...] + blocks[0] + blocks[1] + blocks[2]
    rs.finish()
    cols_all.finish()
    work.finish()


def backward(grad_branch, grad_hidden, kept, first, cosine, signed, q_gain, k_gain, weights, gains, h_all, gd_all, ffn_weights):
    queries, keys, values, mixed, q_unit, k_unit, q_inverse, k_inverse = kept
    rows, wide = grad_branch.shape
    count, head_cols = queries.shape
    heads = head_cols // HD
    world = 8
    width = ffn_weights[0].shape[1]
    lines = gains.shape[0]
    vmem = pl.BlockSpec(memory_space=pltpu.VMEM)
    anywhere = pl.BlockSpec(memory_space=pl.ANY)
    bf, f32 = jnp.bfloat16, jnp.float32
    dma = pltpu.SemaphoreType.DMA
    tok, unit = Background.tokens, Background.units
    return pl.pallas_call(
        back_kernel,
        out_shape=(
            jax.ShapeDtypeStruct((rows, wide), f32),
            jax.ShapeDtypeStruct((lines + 8, HD), f32),
            jax.ShapeDtypeStruct((2, head_cols // 2, wide), bf),
            jax.ShapeDtypeStruct((4, 3, count, head_cols), bf),
            jax.ShapeDtypeStruct((wide, width), f32),
            jax.ShapeDtypeStruct((wide, width), f32),
            jax.ShapeDtypeStruct((width, wide), f32),
        ),
        in_specs=[vmem] * 20 + [anywhere] * 5,
        out_specs=(vmem, vmem, vmem) + (anywhere,) * 4,
        scratch_shapes=[
            pltpu.VMEM((world, rows, wide), bf),
            pltpu.VMEM((4, rows, wide), bf),
            pltpu.VMEM((4, rows, wide), bf),
            pltpu.VMEM((count, head_cols), bf),
            pltpu.VMEM((count, head_cols), f32),
            pltpu.VMEM((count, head_cols), f32),
            pltpu.VMEM((count, head_cols), f32),
            pltpu.VMEM((3, count, head_cols), bf),
            pltpu.VMEM((2, head_cols // 2, wide), bf),
            pltpu.VMEM((2, head_cols // 2, wide), bf),
            pltpu.VMEM((16, HD), f32),
            pltpu.VMEM((world, 16, HD), f32),
            pltpu.VMEM((world, lines, HD), f32),
            pltpu.VMEM((lines + 8, HD), f32),
            pltpu.VMEM((3, lines + 8, HD), f32),
            pltpu.VMEM((8, HD), f32),
            pltpu.VMEM((2, tok // rows, rows, wide), bf),
            pltpu.VMEM((2, tok // rows, rows, wide), bf),
            pltpu.VMEM((wide, unit), bf),
            pltpu.VMEM((wide, unit), bf),
            pltpu.VMEM((unit, wide), bf),
            pltpu.VMEM((wide, unit), f32),
            pltpu.VMEM((wide, unit), f32),
            pltpu.VMEM((unit, wide), f32),
            pltpu.VMEM((tok, unit), bf),
            pltpu.VMEM((tok, unit), bf),
            pltpu.VMEM((tok, unit), bf),
            dma((8,)), dma((8,)), dma((8,)), dma((8,)), dma((8,)), dma((8,)), dma((8,)), dma((8,)), dma((3,)), dma((3,)),
            dma((12,)), dma((12,)), dma((4,)), dma((4,)), pltpu.SemaphoreType.DMA, dma((2, 2)), dma((3,)), dma((3,)),
        ],
        compiler_params=pltpu.CompilerParams(
            collective_id=3, has_side_effects=True, vmem_limit_bytes=62 * 2**20
        ),
        name="back",
    )(
        grad_branch, grad_hidden, queries, keys, values, mixed, q_unit, k_unit, q_inverse, k_inverse, first, cosine, signed,
        q_gain.reshape(1, -1), k_gain.reshape(1, -1), *weights, gains, h_all, gd_all, *ffn_weights,
    )


def on_device_fused(
    tokens,
    segment_ids,
    w_query,
    w_key,
    w_value,
    w_out,
    w_gate,
    w_up,
    w_down,
    q_gain,
    k_gain,
    attn_gain,
    ffn_gain,
    cotangent,
):
    wide = tokens.shape[1]
    token_count = segment_ids.shape[0] * segment_ids.shape[1]
    head_cols = w_query.shape[1]
    positions = positions_of(segment_ids).reshape(token_count)
    cosine, sine = rotary_tables(positions)
    first = (jnp.arange(token_count, dtype=jnp.int32) - positions)[:, None]
    signed = jnp.where(jnp.arange(HD) < HD // 2, -sine, sine)
    branch, queries, keys, values, q_unit, k_unit, q_inverse, k_inverse, mixed, x_all = attention(
        tokens, w_query, w_key, w_value, w_out, q_gain, k_gain, cosine, signed, first
    )
    block_out, grad_hidden, grad_branch, gains, act, grad_gate, grad_up, h_all, gd_all = ffn(
        tokens, branch, cotangent, attn_gain, ffn_gain, w_gate, w_up, w_down
    )
    grad_tokens, gains, grad_w_out, grad_qkv, part_gate, part_up, part_down = backward(
        grad_branch, grad_hidden, (queries, keys, values, mixed, q_unit, k_unit, q_inverse, k_inverse),
        first, cosine, signed, q_gain, k_gain, (w_query, w_key, w_value, w_out), gains, h_all, gd_all, (w_gate, w_up, w_down),
    )
    h_own = h_all[0].reshape(token_count, wide)
    gd_own = gd_all[0].reshape(token_count, wide)
    grad_w_gate = part_gate + dot_first(h_own, grad_gate)
    grad_w_up = part_up + dot_first(h_own, grad_up)
    grad_w_down = part_down + dot_first(act, gd_own)
    x_all = x_all.reshape(4 * token_count, wide)

    def over_all(part):
        return dot_first(x_all, grad_qkv[:, part].reshape(4 * token_count, head_cols))

    lines = wide // HD
    gain_rows = head_cols // HD
    return (
        block_out,
        grad_tokens,
        over_all(0),
        over_all(1),
        over_all(2),
        grad_w_out.reshape(head_cols, wide).astype(jnp.float32),
        grad_w_gate,
        grad_w_up,
        grad_w_down,
        gains[2 * lines : 2 * lines + gain_rows].reshape(head_cols),
        gains[2 * lines + gain_rows : 2 * lines + 2 * gain_rows].reshape(head_cols),
        gains[lines : 2 * lines].reshape(wide),
        gains[:lines].reshape(wide),
    )


def solution(mesh):
    placed = (
        P(("dp", "tensor"), None),
        P("dp", None),
        P(None, "tensor"),
        P(None, "tensor"),
        P(None, "tensor"),
        P("tensor", None),
        P(None, "tensor"),
        P(None, "tensor"),
        P("tensor", None),
        P("tensor"),
        P("tensor"),
        P(),
        P(),
        P(("dp", "tensor"), None),
    )
    return jax.shard_map(
        on_device_fused if dict(mesh.shape) == {"dp": 4, "tensor": 8} else on_device,
        mesh=mesh,
        in_specs=placed,
        out_specs=(
            P(("dp", "tensor"), None),
            P(("dp", "tensor"), None),
            P(None, "tensor"),
            P(None, "tensor"),
            P(None, "tensor"),
            P("tensor", None),
            P(None, "tensor"),
            P(None, "tensor"),
            P("tensor", None),
            P("tensor"),
            P("tensor"),
            P(),
            P(),
        ),
        check_vma=False,
    )
```

```python
import jax
import jax.numpy as jnp
from jax import lax
from jax.experimental import pallas as pl
from jax.experimental.pallas import tpu as pltpu
from jax.sharding import PartitionSpec as P

HD = 128


EPS = 1e-06
THETA = 500000.0


def rounded(value):
    return lax.optimization_barrier(value.astype(jnp.bfloat16)).astype(jnp.float32)


def dot_last(left, right):
    return lax.dot_general(
        left, right, (((1,), (1,)), ((), ())), preferred_element_type=jnp.float32
    )


def dot_first(left, right):
    return lax.dot_general(
        left, right, (((0,), (0,)), ((), ())), preferred_element_type=jnp.float32
    )


def positions_of(segment_ids):
    length = segment_ids.shape[-1]
    places = jnp.arange(length, dtype=jnp.int32)
    below = (segment_ids[:, None, :] < segment_ids[:, :, None]).astype(jnp.int32)
    return places[None, :] - jnp.sum(below, axis=2)


def rotary_tables(positions):
    half = HD // 2
    freq = THETA ** (-(jnp.arange(half, dtype=jnp.float32) * 2.0 / HD))
    angle = positions.astype(jnp.float32)[:, None] * freq[None, :]
    cosine = jnp.concatenate([jnp.cos(angle), jnp.cos(angle)], axis=1)
    sine = jnp.concatenate([jnp.sin(angle), jnp.sin(angle)], axis=1)
    return (cosine, sine)


def rotate(value, cosine, sine):
    half = value.shape[-1] // 2
    turned = jnp.concatenate([-value[..., half:], value[..., :half]], axis=-1)
    return value * cosine[:, None, :] + turned * sine[:, None, :]


def rotate_back(grad, cosine, sine):
    half = grad.shape[-1] // 2
    scaled = grad * sine[:, None, :]
    unturned = jnp.concatenate([scaled[..., half:], -scaled[..., :half]], axis=-1)
    return grad * cosine[:, None, :] + unturned


def norm_back(grad_out, unit, inverse, gain):
    inner = grad_out * gain
    return inverse * (inner - unit * jnp.mean(inner * unit, axis=1, keepdims=True))


def on_device(
    tokens,
    segment_ids,
    w_query,
    w_key,
    w_value,
    w_out,
    w_gate,
    w_up,
    w_down,
    q_gain,
    k_gain,
    attn_gain,
    ffn_gain,
    cotangent,
):
    row_count, full_width = tokens.shape
    head_cols = w_query.shape[1]
    heads_here = head_cols // HD
    ff_cols = w_gate.shape[1]
    seqs_here, seq_len = segment_ids.shape
    token_count = seqs_here * seq_len
    att_scale = HD ** (-0.5)
    whole_x = lax.all_gather(tokens, "tensor", axis=0, tiled=True)
    w_qkv = jnp.concatenate([w_query, w_key, w_value], axis=1)
    projected = jnp.dot(whole_x, w_qkv, preferred_element_type=jnp.float32)
    q_raw = projected[:, :head_cols]
    k_raw = projected[:, head_cols : 2 * head_cols]
    values = projected[:, 2 * head_cols :].astype(jnp.bfloat16)
    q_total, k_total = lax.psum(
        (jnp.sum(q_raw * q_raw, axis=1), jnp.sum(k_raw * k_raw, axis=1)), "tensor"
    )
    q_inverse = lax.rsqrt(q_total / full_width + EPS)[:, None]
    k_inverse = lax.rsqrt(k_total / full_width + EPS)[:, None]
    q_unit = q_raw * q_inverse
    k_unit = k_raw * k_inverse
    cosine, sine = rotary_tables(positions_of(segment_ids).reshape(token_count))
    queries = rotate((q_unit * q_gain).reshape(token_count, heads_here, HD), cosine, sine).astype(
        jnp.bfloat16
    )
    keys = rotate((k_unit * k_gain).reshape(token_count, heads_here, HD), cosine, sine).astype(
        jnp.bfloat16
    )
    shaped = (seqs_here, seq_len, heads_here, HD)
    query_seqs = queries.reshape(shaped)
    key_seqs = keys.reshape(shaped)
    value_seqs = values.reshape(shaped)
    places = jnp.arange(seq_len, dtype=jnp.int32)
    causal = places[:, None] >= places[None, :]

    def scores_of(query_block, key_block, seg_row):
        raw = (
            jnp.einsum("qhd,khd->hqk", query_block, key_block, preferred_element_type=jnp.float32)
            * att_scale
        )
        allowed = causal & (seg_row[:, None] == seg_row[None, :])
        return jnp.where(allowed[None], raw, -1e30)

    def attend(pieces):
        query_block, key_block, value_block, seg_row = pieces
        scores = scores_of(query_block, key_block, seg_row)
        top = jnp.max(scores, axis=-1, keepdims=True)
        expo = jnp.exp(scores - top)
        total = jnp.sum(expo, axis=-1, keepdims=True)
        probs = (expo / total).astype(jnp.bfloat16)
        mixed_block = jnp.einsum(
            "hqk,khd->qhd", probs, value_block, preferred_element_type=jnp.float32
        )
        return (mixed_block.astype(jnp.bfloat16), (top + jnp.log(total))[..., 0])

    mixed, log_total = lax.map(attend, (query_seqs, key_seqs, value_seqs, segment_ids))
    mixed = mixed.reshape(token_count, head_cols)
    x_rows = tokens.astype(jnp.float32)
    branch = lax.psum_scatter(
        jnp.dot(mixed, w_out, preferred_element_type=jnp.float32).astype(jnp.bfloat16),
        "tensor",
        scatter_dimension=0,
        tiled=True,
    ).astype(jnp.float32)
    a_inverse = lax.rsqrt(jnp.mean(branch * branch, axis=1, keepdims=True) + EPS)
    hidden = x_rows + branch * a_inverse * attn_gain
    h_low = lax.all_gather(hidden.astype(jnp.bfloat16), "tensor", axis=0, tiled=True)
    a_unit = branch * a_inverse
    w_gate_up = jnp.concatenate([w_gate, w_up], axis=1)
    gate_up = jnp.dot(h_low, w_gate_up, preferred_element_type=jnp.float32)
    gate = gate_up[:, :ff_cols]
    up = gate_up[:, ff_cols:]
    sigma_gate = jax.nn.sigmoid(gate)
    silu_gate = gate * sigma_gate
    act = (silu_gate * up).astype(jnp.bfloat16)
    down = lax.psum_scatter(
        jnp.dot(act, w_down, preferred_element_type=jnp.float32).astype(jnp.bfloat16),
        "tensor",
        scatter_dimension=0,
        tiled=True,
    ).astype(jnp.float32)
    f_inverse = lax.rsqrt(jnp.mean(down * down, axis=1, keepdims=True) + EPS)
    f_unit = down * f_inverse
    block_out = (hidden + f_unit * ffn_gain).astype(jnp.bfloat16)
    grad_out = cotangent.astype(jnp.float32)
    grad_ffn_part = jnp.sum(grad_out * f_unit, axis=0)
    grad_down = norm_back(grad_out, f_unit, f_inverse, ffn_gain).astype(jnp.bfloat16)
    grad_down_all = lax.all_gather(grad_down, "tensor", axis=0, tiled=True)
    grad_act = dot_last(grad_down_all, w_down)
    grad_w_down = dot_first(act, grad_down_all)
    grad_gate = grad_act * up * sigma_gate * (1.0 + gate * (1.0 - sigma_gate))
    grad_up = grad_act * silu_gate
    grad_gate_up = jnp.concatenate([grad_gate, grad_up], axis=1).astype(jnp.bfloat16)
    grad_w_gate_up = dot_first(h_low, grad_gate_up)
    grad_hidden = grad_out + lax.psum_scatter(
        dot_last(grad_gate_up, w_gate_up).astype(jnp.bfloat16), "tensor", scatter_dimension=0, tiled=True
    ).astype(jnp.float32)
    grad_attn_part = jnp.sum(grad_hidden * a_unit, axis=0)
    grad_branch = norm_back(grad_hidden, a_unit, a_inverse, attn_gain).astype(jnp.bfloat16)
    grad_branch_all = lax.all_gather(grad_branch, "tensor", axis=0, tiled=True)
    grad_w_out = dot_first(mixed, grad_branch_all)
    grad_mixed = dot_last(grad_branch_all, w_out).astype(jnp.bfloat16).reshape(shaped)

    def attend_back(pieces):
        query_block, key_block, value_block, seg_row, log_block, grad_block = pieces
        scores = scores_of(query_block, key_block, seg_row)
        probs = jnp.exp(scores - log_block[..., None])
        grad_probs = jnp.einsum(
            "qhd,khd->hqk", grad_block, value_block, preferred_element_type=jnp.float32
        )
        grad_scores = (
            probs * (grad_probs - jnp.sum(probs * grad_probs, axis=-1, keepdims=True))
        ).astype(jnp.bfloat16)
        grad_query = (
            jnp.einsum("hqk,khd->qhd", grad_scores, key_block, preferred_element_type=jnp.float32)
            * att_scale
        )
        grad_key = (
            jnp.einsum("hqk,qhd->khd", grad_scores, query_block, preferred_element_type=jnp.float32)
            * att_scale
        )
        grad_value = jnp.einsum(
            "hqk,qhd->khd",
            probs.astype(jnp.bfloat16),
            grad_block,
            preferred_element_type=jnp.float32,
        )
        return (grad_query, grad_key, grad_value.astype(jnp.bfloat16))

    grad_query, grad_key, grad_value = lax.map(
        attend_back, (query_seqs, key_seqs, value_seqs, segment_ids, log_total, grad_mixed)
    )
    grad_q_normed = rotate_back(
        rounded(grad_query.reshape(token_count, heads_here, HD)), cosine, sine
    ).reshape(token_count, head_cols)
    grad_k_normed = rotate_back(
        rounded(grad_key.reshape(token_count, heads_here, HD)), cosine, sine
    ).reshape(token_count, head_cols)
    grad_q_gain = jnp.sum(grad_q_normed * q_unit, axis=0)
    grad_k_gain = jnp.sum(grad_k_normed * k_unit, axis=0)
    inner_q = grad_q_normed * q_gain
    inner_k = grad_k_normed * k_gain
    q_inner_sum, k_inner_sum = lax.psum(
        (jnp.sum(inner_q * q_unit, axis=1), jnp.sum(inner_k * k_unit, axis=1)), "tensor"
    )
    grad_q_raw = q_inverse * (inner_q - q_unit * (q_inner_sum / full_width)[:, None])
    grad_k_raw = k_inverse * (inner_k - k_unit * (k_inner_sum / full_width)[:, None])
    grad_qkv = jnp.concatenate(
        [
            grad_q_raw.astype(jnp.bfloat16),
            grad_k_raw.astype(jnp.bfloat16),
            grad_value.reshape(token_count, head_cols),
        ],
        axis=1,
    )
    grad_w_qkv = dot_first(whole_x, grad_qkv)
    grad_tokens = grad_hidden + lax.psum_scatter(
        dot_last(grad_qkv, w_qkv).astype(jnp.bfloat16), "tensor", scatter_dimension=0, tiled=True
    ).astype(jnp.float32)
    grad_w_qkv, grad_w_out, grad_w_gate_up, grad_w_down = [
        lax.psum(part.astype(jnp.bfloat16), "dp").astype(jnp.float32)
        for part in (grad_w_qkv, grad_w_out, grad_w_gate_up, grad_w_down)
    ]
    grad_q_gain, grad_k_gain = lax.psum((grad_q_gain, grad_k_gain), "dp")
    grad_attn_gain, grad_ffn_gain = lax.psum((grad_attn_part, grad_ffn_part), ("dp", "tensor"))
    return (
        block_out,
        grad_tokens,
        grad_w_qkv[:, :head_cols],
        grad_w_qkv[:, head_cols : 2 * head_cols],
        grad_w_qkv[:, 2 * head_cols :],
        grad_w_out,
        grad_w_gate_up[:, :ff_cols],
        grad_w_gate_up[:, ff_cols:],
        grad_w_down,
        grad_q_gain,
        grad_k_gain,
        grad_attn_gain,
        grad_ffn_gain,
    )


MESH = pl.DeviceIdType.MESH
LANES = 2


def places_of():
    d = lax.axis_index("dp")
    t = lax.axis_index("tensor")
    z, c = lax.div(t, 2), lax.rem(t, 2)
    dx = d + 1 - 2 * lax.rem(d, 2)
    dy = lax.rem(d + 2, 4)
    zs = (z, z + 1 - 2 * lax.rem(z, 2), lax.rem(z + 2, 4), 3 - z)
    inner = lax.rem(z + 1, 4) >= 2
    return d, dx, dy, zs, c, inner


def remote(src, dst, send, recv, dp, tensor):
    return pltpu.make_async_remote_copy(
        src_ref=src, dst_ref=dst, send_sem=send, recv_sem=recv, device_id=(dp, tensor), device_id_type=MESH
    )


def enter(d, zs, c, dx=None, dy=None):
    barrier = pltpu.get_barrier_semaphore()
    peers = [(d, 2 * zs[r] + c) for r in (1, 2, 3)] + [(d, 2 * zs[0] + 1 - c)]
    if dx is not None:
        peers += [(dx, 2 * zs[0] + c), (dy, 2 * zs[0] + c)]
    for peer in peers:
        pl.semaphore_signal(barrier, inc=1, device_id=peer, device_id_type=MESH)
    pl.semaphore_wait(barrier, len(peers))


class Gather:
    def __init__(self, full, send, recv, place):
        self.full, self.send, self.recv = full, send, recv
        self.d, _, _, self.zs, self.c, self.inner = place
        self.t = 2 * self.zs[0] + self.c

    def lane(self, r):
        return self.full.at[2 * self.zs[r] + self.c]

    def other(self, r):
        return self.full.at[2 * self.zs[r] + 1 - self.c]

    def to_z(self, r, k, via):
        return remote(self.lane(r), self.lane(r), self.send.at[via if r == 0 else 7], self.recv.at[k], self.d, 2 * self.zs[via] + self.c)

    def to_core(self, r):
        return remote(self.lane(r), self.lane(r), self.send.at[0 if r == 0 else 3 + r], self.recv.at[4 + r], self.d, 2 * self.zs[0] + 1 - self.c)

    def start(self):
        self.to_z(0, 2, 2).start()
        self.to_z(0, 1, 1).start()
        self.to_core(0).start()

    def start_inner(self):
        @pl.when(self.inner)
        def _():
            self.to_z(0, 2, 2).wait_send()
            self.to_z(0, 3, 3).start()

    def arrive(self, r):
        self.to_z(r, r, r).wait_recv()
        if r == 2:
            @pl.when(self.inner)
            def _():
                self.to_z(2, 3, 1).start()
        self.to_core(r).start()

    def ready(self, r):
        remote(self.other(r), self.other(r), self.send.at[0], self.recv.at[4 + r], self.d, self.t).wait_recv()

    def finish(self):
        @pl.when(jnp.logical_not(self.inner))
        def _():
            self.to_z(0, 2, 2).wait_send()

        @pl.when(self.inner)
        def _():
            self.to_z(0, 3, 3).wait_send()
            self.to_z(2, 3, 1).wait_send()

        self.to_z(0, 1, 1).wait_send()
        for r in range(4):
            self.to_core(r).wait_send()


class Scatter:
    def __init__(self, parts, pair, land, send, recv, place):
        self.parts, self.pair, self.land, self.send, self.recv = parts, pair, land, send, recv
        self.d, _, _, self.zs, self.c, self.inner = place
        self.t = 2 * self.zs[0] + self.c

    def mine(self, r):
        return self.parts.at[2 * self.zs[r] + self.c]

    def to_core(self, r):
        src = self.parts.at[2 * self.zs[r] + 1 - self.c]
        return remote(src, self.pair.at[r], self.send.at[r], self.recv.at[r], self.d, 2 * self.zs[0] + 1 - self.c)

    def to_z(self, r, k, via):
        return remote(self.mine(r), self.land.at[k], self.send.at[4 + r], self.recv.at[4 + k], self.d, 2 * self.zs[via] + self.c)

    def add_pair(self, r):
        self.to_core(r).wait_recv()
        add_into(self.mine(r), self.pair.at[r])

    def pass_on(self, r):
        if r == 1:
            self.to_z(1, 1, 1).start()
        if r == 2:
            @pl.when(jnp.logical_not(self.inner))
            def _():
                self.to_z(2, 2, 2).start()
        if r == 3:
            @pl.when(self.inner)
            def _():
                self.to_z(3, 3, 3).start()

            @pl.when(jnp.logical_not(self.inner))
            def _():
                self.to_z(3, 0, 1).start()

    def relay(self):
        @pl.when(self.inner)
        def _():
            self.to_z(3, 0, 1).wait_recv()
            add_into(self.mine(2), self.land.at[0])
            self.to_z(2, 2, 2).start()

    def arrived(self):
        self.to_z(1, 1, 1).wait_recv()
        self.to_z(2, 2, 2).wait_recv()

        @pl.when(self.inner)
        def _():
            self.to_z(3, 3, 3).wait_recv()

        @pl.when(jnp.logical_not(self.inner))
        def _():
            self.land[3] = jnp.zeros(self.land.shape[1:], self.land.dtype)

    def total(self, rows):
        own = self.parts[2 * self.zs[0] + self.c, rows, :].astype(jnp.float32)
        return own + self.land[1, rows, :].astype(jnp.float32) + self.land[2, rows, :].astype(jnp.float32) + self.land[3, rows, :].astype(jnp.float32)

    def finish(self):
        for r in range(4):
            self.to_core(r).wait_send()
        for r in (1, 2, 3):
            self.to_z(r, 1, 1).wait_send()


def add_into(into, other):
    rows = into.shape[0]

    def step(i, carry):
        at = pl.ds(pl.multiple_of(i * 32, 32), 32)
        into[at, :] = (into[at, :].astype(jnp.float32) + other[at, :].astype(jnp.float32)).astype(into.dtype)
        return carry

    lax.fori_loop(0, rows // 32, step, 0)


class Spread:
    def __init__(self, full, whole, send, recv, own_sem, place):
        self.full, self.whole, self.send, self.recv, self.own_sem = full, whole, send, recv, own_sem
        self.d, self.dx, self.dy, self.zs, self.c, _ = place
        self.t = 2 * self.zs[0] + self.c
        self.seen = set()

    def ready(self, k, r):
        other = self.whole.at[1 + k, 2 * self.zs[r] + 1 - self.c]
        remote(other, other, self.send.at[0], self.recv.at[12 + k * 4 + r], self.d, self.t).wait_recv()
        self.seen.add((k, r))

    def slot(self, g, r):
        return self.whole.at[g, 2 * self.zs[r] + self.c]

    def own(self, r, k):
        src = self.full.at[2 * self.zs[r] + self.c]
        return remote(src, self.slot(1 + k, r), self.send.at[k * 4 + r], self.recv.at[k * 4 + r], (self.dx, self.dy)[k], self.t)

    def start(self, r):
        self.own(r, 0).start()
        self.own(r, 1).start()

    def hop(self, r):
        group, target = (1, self.dy) if r in (0, 3) else (2, self.dx)
        return remote(self.slot(group, r), self.slot(3, r), self.send.at[8 + r], self.recv.at[8 + r], target, self.t)

    def to_core(self, r, k):
        return remote(self.slot(1 + k, r), self.slot(1 + k, r), self.send.at[12 + k * 4 + r], self.recv.at[12 + k * 4 + r], self.d, 2 * self.zs[0] + 1 - self.c)

    def pass_on(self, r):
        self.own(r, 0).wait_recv()
        self.own(r, 1).wait_recv()
        self.hop(r).start()
        self.to_core(r, 0).start()
        self.to_core(r, 1).start()

    def last(self, r):
        self.hop(r).wait_recv()
        self.to_core(r, 2).start()

    def keep(self):
        return pltpu.make_async_copy(self.full, self.whole.at[0], self.own_sem)

    def finish(self):
        for r in range(4):
            self.own(r, 0).wait_send()
            self.own(r, 1).wait_send()
            self.hop(r).wait_send()
            for k in range(3):
                self.to_core(r, k).wait_send()
                if (k, r) not in self.seen:
                    self.to_core(r, k).wait_recv()
        self.keep().wait()


def dot_tn(left, right):
    return lax.dot_general(left, right, (((0,), (0,)), ((), ())), preferred_element_type=jnp.float32)


def dot_nt(left, right):
    return lax.dot_general(left, right, (((1,), (1,)), ((), ())), preferred_element_type=jnp.float32)


def ffn_kernel(
    x_ref, br_ref, cot_ref, again_ref, gain_ref, wg_ref, wu_ref, wd_ref,
    bo_ref, gh_ref, gb_ref, gains_ref, hall_ref, gdall_ref, og_ref, ou_ref, od_ref, gate_all, up_all,
    hfull, gfull, hid_ref, sums, gate, up, act, gg, gu, parts, pair, land, hbuf, gbuf, ubuf,
    ag_send, ag_recv, rs_send, rs_recv, xy_send, xy_recv, own_sem, load_sem, store_sem, out_sem,
):
    place = places_of()
    d, dx, dy, zs, c, inner = place
    t = 2 * zs[0] + c
    width = wg_ref.shape[1]
    rows, wide = x_ref.shape
    ft, dt = 512, 1024
    step_rows = 32
    a_gain, gain = again_ref[...], gain_ref[...]

    def opening(i, carry):
        at = pl.ds(pl.multiple_of(i * step_rows, step_rows), step_rows)
        branch = br_ref[at, :]
        inverse = lax.rsqrt(jnp.mean(branch * branch, axis=1, keepdims=True) + EPS)
        hidden = x_ref[at, :].astype(jnp.float32) + branch * inverse * a_gain
        hid_ref[at, :] = hidden
        hfull[t, at, :] = hidden.astype(jnp.bfloat16)
        return carry

    lax.fori_loop(0, rows // step_rows, opening, 0)
    enter(d, zs, c, dx, dy)

    def unit_forward(zz):
        both = pl.ds(2 * zz, 2)
        at = pl.ds(pl.multiple_of(zz * 2 * rows, 2 * rows), 2 * rows)

        def mid(j, carry):
            cols = pl.ds(pl.multiple_of(j * ft, ft), ft)
            block = hfull[both].reshape(2 * rows, wide)
            g = jnp.dot(block, wg_ref[:, cols], preferred_element_type=jnp.float32)
            u = jnp.dot(block, wu_ref[:, cols], preferred_element_type=jnp.float32)
            gate[at, cols] = g
            up[at, cols] = u
            act[at, cols] = (g * jax.nn.sigmoid(g) * u).astype(jnp.bfloat16)
            return carry

        lax.fori_loop(0, width // ft, mid, 0)

        def out(j, carry):
            cols = pl.ds(pl.multiple_of(j * dt, dt), dt)
            p = jnp.dot(act[at, :], wd_ref[:, cols], preferred_element_type=jnp.float32)
            parts[both, :, cols] = p.astype(jnp.bfloat16).reshape(2, rows, dt)
            return carry

        lax.fori_loop(0, wide // dt, out, 0)

    def unit_backward(zz):
        both = pl.ds(2 * zz, 2)
        at = pl.ds(pl.multiple_of(zz * 2 * rows, 2 * rows), 2 * rows)

        def mid(j, carry):
            cols = pl.ds(pl.multiple_of(j * ft, ft), ft)
            block = gfull[both].reshape(2 * rows, wide)
            ga = dot_nt(block, wd_ref[cols, :])
            g, u = gate[at, cols], up[at, cols]
            s = jax.nn.sigmoid(g)
            gg[at, cols] = (ga * u * s * (1.0 + g * (1.0 - s))).astype(jnp.bfloat16)
            gu[at, cols] = (ga * (g * s)).astype(jnp.bfloat16)
            return carry

        lax.fori_loop(0, width // ft, mid, 0)

        def out(j, carry):
            cols = pl.ds(pl.multiple_of(j * dt, dt), dt)
            p = dot_nt(gg[at, :], wg_ref[cols, :]) + dot_nt(gu[at, :], wu_ref[cols, :])
            parts[both, :, cols] = p.astype(jnp.bfloat16).reshape(2, rows, dt)
            return carry

        lax.fori_loop(0, wide // dt, out, 0)

    def own_copies(i, down):
        slot = pl.ds(pl.multiple_of(lax.rem(i, 4) * 256, 256), 256)
        at = pl.ds(pl.multiple_of(i * 256, 256), 256)
        outs = (od_ref.at[at, pl.ds(0, width)], od_ref.at[at, pl.ds(width, width)]) if down else (og_ref.at[at, :], ou_ref.at[at, :])
        return [
            pltpu.make_async_copy(buf.at[slot, :], out, out_sem.at[n, lax.rem(i, 4)])
            for n, (buf, out) in enumerate(zip((gate, up), outs))
        ]

    def own_in(i, carry):
        slot = pl.ds(pl.multiple_of(lax.rem(i, 4) * 256, 256), 256)
        at = pl.ds(pl.multiple_of(i * 256, 256), 256)

        @pl.when(i >= 4)
        def _():
            for copy in own_copies(i - 4, False):
                copy.wait()

        h = hfull[:, :, at].reshape(8 * rows, 256)
        gate[slot, :] = dot_tn(h, gg[...])
        up[slot, :] = dot_tn(h, gu[...])
        for copy in own_copies(i, False):
            copy.start()
        return carry

    def own_down(i, carry):
        at = pl.ds(pl.multiple_of(i * 256, 256), 256)
        for copy in own_copies(i + 4, False):
            copy.wait()
        left = act[:, at]
        for n, buf in enumerate((gate, up)):
            buf[at, :] = dot_tn(left, gfull[:, :, n * width : (n + 1) * width].reshape(8 * rows, width))
        for copy in own_copies(i, True):
            copy.start()
        return carry

    done = []

    def fill(chunks):
        def load(n):
            k, r = chunks[n]
            slot = (base + n) % 2
            return pltpu.make_async_copy(hall_ref.at[1 + k, pl.ds(2 * zs[r], 2)], hbuf.at[slot], load_sem.at[slot])

        base = len(done)
        for n, (k, r) in enumerate(chunks):
            slot = len(done) % 2
            if n == 0:
                xy_h.ready(k, r)
                load(0).start()
            load(n).wait()
            if n + 1 < len(chunks):
                xy_h.ready(*chunks[n + 1])
                load(n + 1).start()
            if len(done) >= 2:
                for copy in stores(len(done) - 2):
                    copy.wait()

            def tile(j, carry):
                cols = pl.ds(pl.multiple_of(j * ft, ft), ft)
                block = hbuf[slot].reshape(2 * rows, wide)
                gbuf[slot, :, cols] = jnp.dot(block, wg_ref[:, cols], preferred_element_type=jnp.float32).astype(jnp.bfloat16)
                ubuf[slot, :, cols] = jnp.dot(block, wu_ref[:, cols], preferred_element_type=jnp.float32).astype(jnp.bfloat16)
                return carry

            lax.fori_loop(0, width // ft, tile, 0)
            done.append((k, r))
            for copy in stores(len(done) - 1):
                copy.start()

    def stores(n):
        k, r = done[n]
        at = pl.ds(pl.multiple_of(zs[r] * 2 * rows, 2 * rows), 2 * rows)
        return [
            pltpu.make_async_copy(buf.at[n % 2], out.at[k, at, :], store_sem.at[m, n % 2])
            for m, (buf, out) in enumerate(((gbuf, gate_all), (ubuf, up_all)))
        ]

    def phase(p, full, whole, unit):
        ag = Gather(full, ag_send.at[p], ag_recv.at[p], place)
        rs = Scatter(parts, pair.at[p], land.at[p], rs_send.at[p], rs_recv.at[p], place)
        xy = xy_h if p == 0 else xy_g
        ag.start()
        xy.start(0)
        ag.ready(0)
        unit(zs[0])
        rs.to_core(0).start()
        if p == 1:
            fill([(0, 3), (1, 3), (2, 0), (2, 2)])
        ag.start_inner()
        ag.arrive(2)
        xy.start(2)
        ag.arrive(1)
        xy.start(1)
        ag.ready(2)
        unit(zs[2])
        rs.to_core(2).start()
        ag.ready(1)
        unit(zs[1])
        rs.to_core(1).start()
        rs.add_pair(2)
        rs.pass_on(2)
        rs.add_pair(1)
        rs.pass_on(1)
        ag.arrive(3)
        xy.start(3)
        ag.ready(3)
        unit(zs[3])
        rs.to_core(3).start()
        xy.keep().start()
        rs.add_pair(3)
        rs.pass_on(3)
        rs.add_pair(0)
        xy.pass_on(0)
        xy.pass_on(2)
        xy.pass_on(1)
        if p == 0:
            fill([(0, 0), (1, 0), (0, 2)])
        else:
            lax.fori_loop(0, 8, own_in, 0)
        rs.relay()
        if p == 0:
            fill([(1, 2), (0, 1), (1, 1)])
        else:
            lax.fori_loop(0, 4, own_down, 0)
            fill([(2, 1), (2, 3)])
        rs.arrived()
        return ag, rs

    xy_h = Spread(hfull, hall_ref, xy_send.at[0], xy_recv.at[0], own_sem.at[0], place)
    xy_g = Spread(gfull, gdall_ref, xy_send.at[1], xy_recv.at[1], own_sem.at[1], place)
    ag, rs = phase(0, hfull, hall_ref, unit_forward)
    sums[...] = jnp.zeros_like(sums)

    def middle(i, carry):
        at = pl.ds(pl.multiple_of(i * step_rows, step_rows), step_rows)
        down = rs.total(at)
        inverse = lax.rsqrt(jnp.mean(down * down, axis=1, keepdims=True) + EPS)
        unit = down * inverse
        bo_ref[at, :] = (hid_ref[at, :] + unit * gain).astype(jnp.bfloat16)
        grad = cot_ref[at, :].astype(jnp.float32)
        sums[0:1, :] += jnp.sum(grad * unit, axis=0, keepdims=True)
        inner_grad = grad * gain
        gfull[t, at, :] = (inverse * (inner_grad - unit * jnp.mean(inner_grad * unit, axis=1, keepdims=True))).astype(jnp.bfloat16)
        return carry

    lax.fori_loop(0, rows // step_rows, middle, 0)
    ag.finish()
    rs.finish()
    xy_h.pass_on(3)
    for r in range(4):
        xy_h.last(r)
    ag, rs = phase(1, gfull, gdall_ref, unit_backward)

    def ending(i, carry):
        at = pl.ds(pl.multiple_of(i * step_rows, step_rows), step_rows)
        grad = cot_ref[at, :].astype(jnp.float32) + rs.total(at)
        gh_ref[at, :] = grad
        branch = br_ref[at, :]
        inverse = lax.rsqrt(jnp.mean(branch * branch, axis=1, keepdims=True) + EPS)
        unit = branch * inverse
        sums[1:2, :] += jnp.sum(grad * unit, axis=0, keepdims=True)
        inner_grad = grad * a_gain
        gb_ref[at, :] = (inverse * (inner_grad - unit * jnp.mean(inner_grad * unit, axis=1, keepdims=True))).astype(jnp.bfloat16)
        return carry

    lax.fori_loop(0, rows // step_rows, ending, 0)
    for i in range(wide // HD):
        gains_ref[i : i + 1, :] = sums[0:1, i * HD : (i + 1) * HD]
        gains_ref[wide // HD + i : wide // HD + i + 1, :] = sums[1:2, i * HD : (i + 1) * HD]
    ag.finish()
    rs.finish()
    xy_g.pass_on(3)
    for r in range(4):
        xy_g.last(r)
    xy_h.finish()
    for i in range(4):
        for copy in own_copies(i, True):
            copy.wait()
    for n in (len(done) - 2, len(done) - 1):
        for copy in stores(n):
            copy.wait()
    xy_g.finish()


def ffn(x_own, branch, cot, attn_gain, ffn_gain, w_gate, w_up, w_down):
    rows, wide = x_own.shape
    width = w_gate.shape[1]
    groups, world = 4, 8
    vmem = pl.BlockSpec(memory_space=pltpu.VMEM)
    anywhere = pl.BlockSpec(memory_space=pl.ANY)
    bf, f32 = jnp.bfloat16, jnp.float32
    whole = jax.ShapeDtypeStruct((groups, world, rows, wide), bf)
    others = jax.ShapeDtypeStruct((groups - 1, world * rows, width), bf)
    dma = pltpu.SemaphoreType.DMA
    return pl.pallas_call(
        ffn_kernel,
        out_shape=(
            jax.ShapeDtypeStruct((rows, wide), bf),
            jax.ShapeDtypeStruct((rows, wide), f32),
            jax.ShapeDtypeStruct((rows, wide), bf),
            jax.ShapeDtypeStruct((2 * wide // HD, HD), f32),
            whole,
            whole,
            jax.ShapeDtypeStruct((wide, width), f32),
            jax.ShapeDtypeStruct((wide, width), f32),
            jax.ShapeDtypeStruct((width, wide), f32),
            others,
            others,
        ),
        in_specs=[vmem] * 8,
        out_specs=(vmem,) * 4 + (anywhere,) * 7,
        scratch_shapes=[
            pltpu.VMEM((world, rows, wide), bf),
            pltpu.VMEM((world, rows, wide), bf),
            pltpu.VMEM((rows, wide), f32),
            pltpu.VMEM((8, wide), f32),
            pltpu.VMEM((world * rows, width), f32),
            pltpu.VMEM((world * rows, width), f32),
            pltpu.VMEM((world * rows, width), bf),
            pltpu.VMEM((world * rows, width), bf),
            pltpu.VMEM((world * rows, width), bf),
            pltpu.VMEM((world, rows, wide), bf),
            pltpu.VMEM((2, 4, rows, wide), bf),
            pltpu.VMEM((2, 4, rows, wide), bf),
            pltpu.VMEM((2, 2, rows, wide), bf),
            pltpu.VMEM((2, 2 * rows, width), bf),
            pltpu.VMEM((2, 2 * rows, width), bf),
            dma((2, 8)),
            dma((2, 8)),
            dma((2, 8)),
            dma((2, 8)),
            dma((2, 24)),
            dma((2, 24)),
            dma((2,)),
            dma((2,)),
            dma((2, 2)),
            dma((2, 4)),
        ],
        compiler_params=pltpu.CompilerParams(
            collective_id=2, has_side_effects=True, vmem_limit_bytes=60 * 2**20
        ),
        name="ffn",
    )(x_own, branch, cot, attn_gain.reshape(1, wide), ffn_gain.reshape(1, wide), w_gate, w_up, w_down)


WINDOW = 3


class Exchange:
    def __init__(self, block, land, send, recv, place):
        self.block, self.land, self.send, self.recv = block, land, send, recv
        self.d, _, _, self.zs, self.c, _ = place
        self.t = 2 * self.zs[0] + self.c

    def copies(self):
        out = []
        for r in range(4):
            for k in range(2):
                if r == 0 and k == 0:
                    continue
                at = 4 * k + r
                core = self.c if k == 0 else 1 - self.c
                out.append((2 * self.zs[r] + core, at))
        return out

    def start(self):
        for peer, at in self.copies():
            remote(self.block, self.land.at[self.t], self.send.at[at], self.recv.at[at], self.d, peer).start()

    def wait(self):
        for peer, at in self.copies():
            remote(self.block, self.land.at[peer], self.send.at[at], self.recv.at[at], self.d, peer).wait()


def enter_all(d, zs, c, dx, dy):
    barrier = pltpu.get_barrier_semaphore()
    peers = [(d, 2 * zs[r] + c) for r in (1, 2, 3)] + [(d, 2 * zs[r] + 1 - c) for r in range(4)]
    peers += [(dx, 2 * zs[0] + c), (dy, 2 * zs[0] + c)]
    for peer in peers:
        pl.semaphore_signal(barrier, inc=1, device_id=peer, device_id_type=MESH)
    pl.semaphore_wait(barrier, len(peers))


def put_column(stat, base, zz, square):
    rows = square.shape[0]
    folded = square[:, :HD]
    for h in range(1, square.shape[1] // HD):
        folded = folded + square[:, h * HD : (h + 1) * HD]
    line = jnp.sum(folded.T, axis=0, keepdims=True)
    for i in range(rows // HD):
        stat[pl.ds(base + 2 * zz + i, 1), :] = line[:, i * HD : (i + 1) * HD]


def get_column(stat_row, count):
    return jnp.broadcast_to(stat_row, (count, HD)).T


def attn_kernel(
    x_ref, wq_ref, wk_ref, wv_ref, wo_ref, qg_ref, kg_ref, cos_ref, sin_ref, first_ref,
    br_ref, q_out, k_out, v_out, qu_out, ku_out, rq_out, rk_out, mixed_out, xall_ref,
    xfull, parts, pair, land, stat, stats,
    ag_send, ag_recv, rs_send, rs_recv, xy_send, xy_recv, st_send, st_recv, own_sem,
):
    place = places_of()
    d, dx, dy, zs, c, inner = place
    t = 2 * zs[0] + c
    rows, wide = x_ref.shape
    span = 2 * rows
    heads = wq_ref.shape[1] // HD
    xfull[t] = x_ref[...]
    enter_all(d, zs, c, dx, dy)
    ag = Gather(xfull, ag_send, ag_recv, place)
    rs = Scatter(parts, pair, land, rs_send, rs_recv, place)
    xy = Spread(xfull, xall_ref, xy_send, xy_recv, own_sem, place)
    ex = Exchange(stat, stats, st_send, st_recv, place)

    def at_of(zz):
        return pl.ds(pl.multiple_of(zz * span, span), span)

    def project_qk(zz):
        block = xfull[pl.ds(2 * zz, 2)].reshape(span, wide)
        for w_ref, out, base in ((wq_ref, qu_out, 0), (wk_ref, ku_out, 8)):
            raw = jnp.dot(block, w_ref[...], preferred_element_type=jnp.float32)
            out[at_of(zz), :] = raw
            put_column(stat, base, zz, raw * raw)

    def project_v(zz):
        block = xfull[pl.ds(2 * zz, 2)].reshape(span, wide)
        v_out[at_of(zz), :] = jnp.dot(block, wv_ref[...], preferred_element_type=jnp.float32).astype(jnp.bfloat16)

    ag.start()
    xy.start(0)
    ag.ready(0)
    project_qk(zs[0])
    project_v(zs[0])
    ag.start_inner()
    ag.arrive(2)
    xy.start(2)
    ag.arrive(1)
    xy.start(1)
    ag.ready(2)
    project_qk(zs[2])
    ag.ready(1)
    project_qk(zs[1])
    project_v(zs[2])
    ag.arrive(3)
    xy.start(3)
    ag.ready(3)
    project_qk(zs[3])
    ex.start()
    project_v(zs[1])
    project_v(zs[3])
    xy.keep().start()
    ex.wait()
    total = stat[...]
    for r in range(4):
        for k in range(2):
            if r or k:
                total = total + stats[2 * zs[r] + (c if k == 0 else 1 - c)]
    inverse = lax.rsqrt(total / (8 * wq_ref.shape[1]) + EPS)
    rq_out[...] = inverse[:8]
    rk_out[...] = inverse[8:]

    def norm_rope(i, carry):
        at = pl.ds(pl.multiple_of(i * HD, HD), HD)
        cosine, sine = cos_ref[at, :], sin_ref[at, :]
        for line, raw, out, gain in ((rq_out, qu_out, q_out, qg_ref), (rk_out, ku_out, k_out, kg_ref)):
            scale = get_column(line[pl.ds(i, 1), :], HD)
            for h in range(heads):
                cols = slice(h * HD, (h + 1) * HD)
                unit = raw[at, cols] * scale
                raw[at, cols] = unit
                normed = unit * gain[:, cols]
                out[at, cols] = (normed * cosine + pltpu.roll(normed, HD // 2, 1) * sine).astype(jnp.bfloat16)
        return carry

    lax.fori_loop(0, 8, norm_rope, 0)

    def attend(zz):
        at = at_of(zz)
        low = jnp.maximum(zz - (WINDOW - 1), 0) * span
        keys_at = pl.ds(pl.multiple_of(low, span), WINDOW * span)
        key_place = low + lax.broadcasted_iota(jnp.int32, (span, WINDOW * span), 1)
        query_place = zz * span + lax.broadcasted_iota(jnp.int32, (span, WINDOW * span), 0)
        allowed = (key_place <= query_place) & (key_place >= first_ref[at, :])
        for h in range(heads):
            cols = slice(h * HD, (h + 1) * HD)
            scores = dot_nt(q_out[at, cols], k_out[keys_at, cols]) * HD**-0.5
            scores = jnp.where(allowed, scores, -1e30)
            top = jnp.max(scores, axis=1, keepdims=True)
            expo = jnp.exp(scores - top)
            probs = expo * (1.0 / jnp.sum(expo, axis=1, keepdims=True))
            mixed_out[at, cols] = jnp.dot(probs.astype(jnp.bfloat16), v_out[keys_at, cols], preferred_element_type=jnp.float32).astype(jnp.bfloat16)
        dt = 1024

        def out(j, carry):
            to = pl.ds(pl.multiple_of(j * dt, dt), dt)
            p = jnp.dot(mixed_out[at, :], wo_ref[:, to], preferred_element_type=jnp.float32)
            parts[pl.ds(2 * zz, 2), :, to] = p.astype(jnp.bfloat16).reshape(2, rows, dt)
            return carry

        lax.fori_loop(0, wide // dt, out, 0)

    attend(zs[3])
    rs.to_core(3).start()
    attend(zs[2])
    rs.to_core(2).start()
    rs.add_pair(3)
    rs.pass_on(3)
    attend(zs[1])
    rs.to_core(1).start()
    rs.add_pair(2)
    rs.pass_on(2)
    rs.add_pair(1)
    rs.pass_on(1)
    attend(zs[0])
    rs.to_core(0).start()
    rs.add_pair(0)
    xy.pass_on(0)
    xy.pass_on(2)
    xy.pass_on(1)
    rs.relay()
    xy.pass_on(3)
    for r in range(4):
        xy.last(r)
    rs.arrived()

    def ending(i, carry):
        at = pl.ds(pl.multiple_of(i * 32, 32), 32)
        br_ref[at, :] = rs.total(at)
        return carry

    lax.fori_loop(0, rows // 32, ending, 0)
    ag.finish()
    rs.finish()
    xy.finish()


def attention(x_own, w_query, w_key, w_value, w_out, q_gain, k_gain, cosine, sine, first):
    rows, wide = x_own.shape
    head_cols = w_query.shape[1]
    groups, world = 4, 8
    count = world * rows
    vmem = pl.BlockSpec(memory_space=pltpu.VMEM)
    bf, f32 = jnp.bfloat16, jnp.float32
    dma = pltpu.SemaphoreType.DMA
    cols = jax.ShapeDtypeStruct((count, head_cols), bf)
    wide_cols = jax.ShapeDtypeStruct((count, head_cols), f32)
    line = jax.ShapeDtypeStruct((8, HD), f32)
    return pl.pallas_call(
        attn_kernel,
        out_shape=(
            jax.ShapeDtypeStruct((rows, wide), f32),
            cols, cols, cols, wide_cols, wide_cols, line, line, cols,
            jax.ShapeDtypeStruct((groups, world, rows, wide), bf),
        ),
        in_specs=[vmem] * 10,
        out_specs=(vmem,) * 9 + (pl.BlockSpec(memory_space=pl.ANY),),
        scratch_shapes=[
            pltpu.VMEM((world, rows, wide), bf),
            pltpu.VMEM((world, rows, wide), bf),
            pltpu.VMEM((4, rows, wide), bf),
            pltpu.VMEM((4, rows, wide), bf),
            pltpu.VMEM((16, HD), f32),
            pltpu.VMEM((world, 16, HD), f32),
            dma((8,)), dma((8,)), dma((8,)), dma((8,)), dma((24,)), dma((24,)), dma((8,)), dma((8,)),
            pltpu.SemaphoreType.DMA,
        ],
        compiler_params=pltpu.CompilerParams(
            collective_id=1, has_side_effects=True, vmem_limit_bytes=60 * 2**20
        ),
        name="attn",
    )(x_own, w_query, w_key, w_value, w_out, q_gain.reshape(1, -1), k_gain.reshape(1, -1), cosine, sine, first)


class Background:
    tokens, units = 512, 512

    def __init__(self, hall, gdall, gate_all, up_all, w_down, starts, outs, hbuf, gbuf, gate, up, tile, sums, mids, load_sem, tile_sem, start_sem, out_sem):
        self.hall, self.gdall, self.gate_all, self.up_all, self.w_down, self.starts, self.outs = hall, gdall, gate_all, up_all, w_down, starts, outs
        self.hbuf, self.gbuf, self.gate, self.up, self.tile, self.sums, self.mids = hbuf, gbuf, gate, up, tile, sums, mids
        self.load_sem, self.tile_sem, self.start_sem, self.out_sem = load_sem, tile_sem, start_sem, out_sem
        self.blocks = self.tokens // hall.shape[2]
        self.per_group = hall.shape[1] // self.blocks
        self.per_tile = 3 * self.per_group
        self.tile_count = w_down.shape[0] // self.units
        self.count = self.tile_count * self.per_tile

    def loads(self, n):
        slot, m = n % 2, n % self.per_tile
        group, part = 1 + m // self.per_group, m % self.per_group
        blocks = pl.ds(part * self.blocks, self.blocks)
        rows = pl.ds(part * self.tokens, self.tokens)
        units = pl.ds(n // self.per_tile * self.units, self.units)
        return (
            pltpu.make_async_copy(self.hall.at[group, blocks], self.hbuf.at[slot], self.load_sem.at[0, slot]),
            pltpu.make_async_copy(self.gdall.at[group, blocks], self.gbuf.at[slot], self.load_sem.at[1, slot]),
            pltpu.make_async_copy(self.gate_all.at[group - 1, rows, units], self.gate.at[slot], self.load_sem.at[2, slot]),
            pltpu.make_async_copy(self.up_all.at[group - 1, rows, units], self.up.at[slot], self.load_sem.at[3, slot]),
        )

    def tile_load(self, tile):
        return pltpu.make_async_copy(self.w_down.at[pl.ds(tile * self.units, self.units), :], self.tile, self.tile_sem)

    def moves(self, tile, refs, sem, inward):
        at = pl.ds(tile * self.units, self.units)
        g, u, d = refs
        pairs = zip(self.sums, (g.at[:, at], u.at[:, at], d.at[at, :]))
        return [
            pltpu.make_async_copy(far, near, sem.at[n]) if inward else pltpu.make_async_copy(near, far, sem.at[n])
            for n, (near, far) in enumerate(pairs)
        ]

    def stores(self, tile):
        return self.moves(tile, self.outs, self.out_sem, False)

    def sums_in(self, tile):
        return self.moves(tile, self.starts, self.start_sem, True)

    def begin(self):
        for copy in self.loads(0) + (self.tile_load(0),) + tuple(self.sums_in(0)):
            copy.start()

    def turn(self, tile):
        for copy in self.stores(tile):
            copy.wait()
        for copy in self.sums_in(tile + 1):
            copy.start()

    def step(self, n):
        slot, tile, m = n % 2, n // self.per_tile, n % self.per_tile
        if n + 1 < self.count:
            for copy in self.loads(n + 1):
                copy.start()
        if m == 0:
            self.tile_load(tile).wait()
            for copy in self.sums_in(tile):
                copy.wait()
        for copy in self.loads(n):
            copy.wait()
        hbuf, gbuf, gate, up = self.hbuf.at[slot], self.gbuf.at[slot], self.gate.at[slot], self.up.at[slot]
        wd = self.tile
        act, gg, gu = self.mids
        rows, wide = hbuf.shape[1:]
        half = self.tokens // 2

        def mid(i, carry):
            blocks = pl.ds(i * (self.blocks // 2), self.blocks // 2)
            at = pl.ds(pl.multiple_of(i * half, half), half)
            g, u = gate[at, :].astype(jnp.float32), up[at, :].astype(jnp.float32)
            ga = dot_nt(gbuf[blocks].reshape(half, wide), wd[...])
            s = jax.nn.sigmoid(g)
            gs = g * s
            act[at, :] = (gs * u).astype(jnp.bfloat16)
            gg[at, :] = (ga * u * s * (1.0 + g * (1.0 - s))).astype(jnp.bfloat16)
            gu[at, :] = (ga * gs).astype(jnp.bfloat16)
            return carry

        lax.fori_loop(0, 2, mid, 0)
        span = 512

        def into(i, carry):
            at = pl.ds(pl.multiple_of(i * span, span), span)
            h = hbuf[:, :, at].reshape(self.tokens, span)
            pg = dot_tn(h, gg[...])
            pu = dot_tn(h, gu[...])
            pd = dot_tn(act[...], gbuf[:, :, at].reshape(self.tokens, span))
            self.sums[0][at, :] += pg
            self.sums[1][at, :] += pu
            self.sums[2][:, at] += pd
            return carry

        lax.fori_loop(0, wide // span, into, 0)
        if m == self.per_tile - 1:
            for copy in self.stores(tile):
                copy.start()
            if tile + 1 < self.tile_count:
                self.tile_load(tile + 1).start()

    def finish(self):
        for copy in self.stores(self.tile_count - 1):
            copy.wait()


class SpreadColumns:
    def __init__(self, own, whole, send, recv, own_sem, place):
        self.src, self.whole, self.send, self.recv, self.own_sem = own, whole, send, recv, own_sem
        self.d, self.dx, self.dy, self.zs, self.c, _ = place
        self.t = 2 * self.zs[0] + self.c

    def own(self, p, k):
        return remote(self.src.at[p], self.whole.at[1 + k, p], self.send.at[k * 3 + p], self.recv.at[k * 3 + p], (self.dx, self.dy)[k], self.t)

    def hop(self, p, b):
        half = self.src.shape[1] // 2
        at = pl.ds(b * half, half)
        return remote(self.whole.at[1 + b, p, at], self.whole.at[3, p, at], self.send.at[6 + 2 * p + b], self.recv.at[6 + 2 * p + b], (self.dy, self.dx)[b], self.t)

    def start(self, p):
        self.own(p, 0).start()
        self.own(p, 1).start()

    def pass_on(self, p):
        for b in range(2):
            self.own(p, b).wait_recv()
            self.hop(p, b).start()

    def keep(self):
        return pltpu.make_async_copy(self.src, self.whole.at[0], self.own_sem)

    def finish(self):
        for p in range(3):
            for b in range(2):
                self.own(p, b).wait_send()
                self.hop(p, b).wait()
        self.keep().wait()


class SumHalves:
    def __init__(self, buf, once, twice, send, recv, place):
        self.buf, self.land, self.send, self.recv = buf, (once, twice), send, recv
        self.d, self.dx, self.dy, self.zs, self.c, _ = place
        self.t = 2 * self.zs[0] + self.c

    def move(self, stage, b):
        at = 2 * stage + b
        return remote(self.buf.at[b], self.land[stage].at[b], self.send.at[at], self.recv.at[at], (self.dx, self.dy)[(stage + b) % 2], self.t)

    def start(self, stage):
        for b in range(2):
            self.move(stage, b).start()

    def add(self, stage):
        for b in range(2):
            self.move(stage, b).wait()
            add_into(self.buf.at[b], self.land[stage].at[b])


class ExchangeGroups:
    def __init__(self, block, land, send, recv, place):
        self.block, self.land, self.send, self.recv = block, land, send, recv
        d, dx, dy, zs, c, _ = place
        self.peers, self.t = (dx, dy, 3 - d), 2 * zs[0] + c

    def copies(self):
        return [remote(self.block, self.land.at[k], self.send.at[k], self.recv.at[k], peer, self.t) for k, peer in enumerate(self.peers)]

    def start(self):
        for copy in self.copies():
            copy.start()

    def wait(self):
        for copy in self.copies():
            copy.wait()


def back_kernel(
    gb_ref, gh_ref, q_ref, k_ref, v_ref, mixed_ref, qu_ref, ku_ref, rq_ref, rk_ref, first_ref, cos_ref, sin_ref,
    qg_ref, kg_ref, wq_ref, wk_ref, wv_ref, wo_ref, gains_ref, hall, gdall, gate_all, up_all, w_down, own_g, own_u, own_d,
    gt_ref, gains_out, dwo_ref, gall_ref, dwg, dwu, dwd,
    full, pair, land, gm, dq, dk, dv, own, wo_once, wo_twice, stat, stats, gland, block, blocks, gacc,
    hbuf, gbuf, gbf, ubf, td, sg, su, sd, act, gg, gu,
    ag_send, ag_recv, rs_send, rs_recv, st_send, st_recv, ga_send, ga_recv, gr_send, gr_recv,
    co_send, co_recv, wo_send, wo_recv, own_sem, load_sem, tile_sem, start_sem, out_sem,
):
    place = places_of()
    d, dx, dy, zs, c, inner = place
    t = 2 * zs[0] + c
    rows, wide = gb_ref.shape
    span = 2 * rows
    heads = wq_ref.shape[1] // HD
    count = q_ref.shape[0]
    scale = HD**-0.5
    full[t] = gb_ref[...]
    barrier = pltpu.get_barrier_semaphore()
    peers = [(d, 2 * zs[r] + c) for r in (1, 2, 3)] + [(d, 2 * zs[r] + 1 - c) for r in range(4)]
    peers += [(dx, t), (dy, t), (3 - d, t)]
    for peer in peers:
        pl.semaphore_signal(barrier, inc=1, device_id=peer, device_id_type=MESH)
    pl.semaphore_wait(barrier, len(peers))
    ag = Gather(full, ag_send, ag_recv, place)
    rs = Scatter(full, pair, land, rs_send, rs_recv, place)
    ex = Exchange(stat, stats, st_send, st_recv, place)
    gains = Exchange(gains_ref, gland, ga_send, ga_recv, place)
    groups = ExchangeGroups(block, blocks, gr_send, gr_recv, place)
    cols_all = SpreadColumns(own, gall_ref, co_send, co_recv, own_sem, place)
    wo_sum = SumHalves(dwo_ref, wo_once, wo_twice, wo_send, wo_recv, place)
    work = Background(
        hall, gdall, gate_all, up_all, w_down, (own_g, own_u, own_d), (dwg, dwu, dwd), hbuf, gbuf, gbf, ubf, td, (sg, su, sd), (act, gg, gu),
        load_sem, tile_sem, start_sem, out_sem,
    )

    def at_of(zz):
        return pl.ds(pl.multiple_of(zz * span, span), span)

    ag.start()
    gains.start()
    work.begin()
    work.step(0)
    work.step(1)
    ag.ready(0)
    ag.start_inner()
    ag.arrive(2)
    ag.arrive(1)
    work.step(2)
    work.step(3)
    ag.ready(2)
    ag.ready(1)
    ag.arrive(3)
    work.step(4)
    work.step(5)
    ag.ready(3)

    def mixed_back(zz, carry):
        part = full[pl.ds(2 * zz, 2)].reshape(span, wide)
        gm[at_of(zz), :] = dot_nt(part, wo_ref[...]).astype(jnp.bfloat16)
        return carry

    lax.fori_loop(0, 4, mixed_back, 0)

    def out_back(j, carry):
        to = pl.ds(pl.multiple_of(j * 512, 512), 512)
        p = dot_tn(mixed_ref[...], full[:, :, to].reshape(count, 512))
        dwo_ref[:, :, to] = p.astype(jnp.bfloat16).reshape(2, p.shape[0] // 2, 512)
        return carry

    lax.fori_loop(0, wide // 512, out_back, 0)
    wo_sum.start(0)
    ag.finish()
    dk[...] = jnp.zeros_like(dk)
    dv[...] = jnp.zeros_like(dv)

    def attend_back(zz, carry):
        at = at_of(zz)
        low = jnp.maximum(zz - (WINDOW - 1), 0) * span
        keys_at = pl.ds(pl.multiple_of(low, span), WINDOW * span)
        key_place = low + lax.broadcasted_iota(jnp.int32, (span, WINDOW * span), 1)
        query_place = zz * span + lax.broadcasted_iota(jnp.int32, (span, WINDOW * span), 0)
        allowed = (key_place <= query_place) & (key_place >= first_ref[at, :])
        for h in range(heads):
            cols = slice(h * HD, (h + 1) * HD)
            scores = dot_nt(q_ref[at, cols], k_ref[keys_at, cols]) * scale
            scores = jnp.where(allowed, scores, -1e30)
            top = jnp.max(scores, axis=1, keepdims=True)
            expo = jnp.exp(scores - top)
            probs = expo * (1.0 / jnp.sum(expo, axis=1, keepdims=True))
            grad = gm[at, cols]
            gp = dot_nt(grad, v_ref[keys_at, cols])
            gs = (probs * (gp - jnp.sum(probs * gp, axis=1, keepdims=True))).astype(jnp.bfloat16)
            dq[at, cols] = jnp.dot(gs, k_ref[keys_at, cols], preferred_element_type=jnp.float32) * scale
            dk[keys_at, cols] += dot_tn(gs, q_ref[at, cols]) * scale
            dv[keys_at, cols] += dot_tn(probs.astype(jnp.bfloat16), grad)
        return carry

    lax.fori_loop(0, 2, attend_back, 0)
    wo_sum.add(0)
    wo_sum.start(1)
    work.turn(0)
    lax.fori_loop(2, 4, attend_back, 0)
    own[2] = dv[...].astype(jnp.bfloat16)
    cols_all.start(2)
    gacc[...] = jnp.zeros_like(gacc)

    def unrope(i, carry):
        at = pl.ds(pl.multiple_of(i * HD, HD), HD)
        cosine, sine = cos_ref[at, :], sin_ref[at, :]
        for n, (grad, unit_ref, gain) in enumerate(((dq, qu_ref, qg_ref), (dk, ku_ref, kg_ref))):
            total = jnp.zeros((HD, HD), jnp.float32)
            for h in range(heads):
                cols = slice(h * HD, (h + 1) * HD)
                value = grad[at, cols].astype(jnp.bfloat16).astype(jnp.float32)
                value = value * cosine - pltpu.roll(value, HD // 2, 1) * sine
                unit = unit_ref[at, cols]
                row = n * heads + h
                gacc[row : row + 1, :] += jnp.sum(value * unit, axis=0, keepdims=True)
                value = value * gain[:, cols]
                grad[at, cols] = value
                total = total + value * unit
            stat[pl.ds(8 * n + i, 1), :] = jnp.sum(total.T, axis=0, keepdims=True)
        return carry

    lax.fori_loop(0, count // HD, unrope, 0)
    ex.start()
    gains.wait()
    total = gains_ref[...]
    for r in range(4):
        for k in range(2):
            if r or k:
                total = total + gland[2 * zs[r] + (c if k == 0 else 1 - c)]
    lines = gains_ref.shape[0]
    block[:lines, :] = total
    block[lines:, :] = gacc[...]
    groups.start()
    work.step(6)
    ex.wait()
    total = stat[...]
    for r in range(4):
        for k in range(2):
            if r or k:
                total = total + stats[2 * zs[r] + (c if k == 0 else 1 - c)]
    stat[...] = total * (1.0 / (8 * wq_ref.shape[1]))

    def norm_back_rows(i, carry):
        at = pl.ds(pl.multiple_of(i * HD, HD), HD)
        for n, (grad, unit_ref, inv_ref) in enumerate(((dq, qu_ref, rq_ref), (dk, ku_ref, rk_ref))):
            mean = get_column(stat[pl.ds(8 * n + i, 1), :], HD)
            inverse = get_column(inv_ref[pl.ds(i, 1), :], HD)
            for h in range(heads):
                cols = slice(h * HD, (h + 1) * HD)
                own[n, at, cols] = (inverse * (grad[at, cols] - unit_ref[at, cols] * mean)).astype(jnp.bfloat16)
        return carry

    lax.fori_loop(0, count // HD, norm_back_rows, 0)
    cols_all.start(0)
    cols_all.start(1)
    cols_all.keep().start()

    def tokens_back(zz):
        at = at_of(zz)
        dt = 1024

        def out(j, carry):
            to = pl.ds(pl.multiple_of(j * dt, dt), dt)
            p = dot_nt(own[0, at, :], wq_ref[to, :]) + dot_nt(own[1, at, :], wk_ref[to, :]) + dot_nt(own[2, at, :], wv_ref[to, :])
            full[pl.ds(2 * zz, 2), :, to] = p.astype(jnp.bfloat16).reshape(2, rows, dt)
            return carry

        lax.fori_loop(0, wide // dt, out, 0)

    tokens_back(zs[3])
    rs.to_core(3).start()
    tokens_back(zs[2])
    rs.to_core(2).start()
    rs.add_pair(3)
    rs.pass_on(3)
    tokens_back(zs[1])
    rs.to_core(1).start()
    rs.add_pair(2)
    rs.pass_on(2)
    rs.add_pair(1)
    rs.pass_on(1)
    tokens_back(zs[0])
    rs.to_core(0).start()
    rs.add_pair(0)
    cols_all.pass_on(2)
    wo_sum.add(1)
    work.step(7)
    rs.relay()
    work.step(8)
    work.step(9)
    cols_all.pass_on(0)
    cols_all.pass_on(1)
    work.step(10)
    work.step(11)
    rs.arrived()

    def ending(i, carry):
        at = pl.ds(pl.multiple_of(i * 32, 32), 32)
        gt_ref[at, :] = gh_ref[at, :] + rs.total(at)
        return carry

    lax.fori_loop(0, rows // 32, ending, 0)
    groups.wait()
    gains_out[...] = block[...] + blocks[0] + blocks[1] + blocks[2]
    rs.finish()
    cols_all.finish()
    work.finish()


def backward(grad_branch, grad_hidden, kept, first, cosine, signed, q_gain, k_gain, weights, gains, h_all, gd_all, gate_all, up_all, w_down, own_parts):
    queries, keys, values, mixed, q_unit, k_unit, q_inverse, k_inverse = kept
    rows, wide = grad_branch.shape
    count, head_cols = queries.shape
    heads = head_cols // HD
    world = 8
    width = w_down.shape[0]
    lines = gains.shape[0]
    vmem = pl.BlockSpec(memory_space=pltpu.VMEM)
    anywhere = pl.BlockSpec(memory_space=pl.ANY)
    bf, f32 = jnp.bfloat16, jnp.float32
    dma = pltpu.SemaphoreType.DMA
    tok, unit = Background.tokens, Background.units
    return pl.pallas_call(
        back_kernel,
        out_shape=(
            jax.ShapeDtypeStruct((rows, wide), f32),
            jax.ShapeDtypeStruct((lines + 8, HD), f32),
            jax.ShapeDtypeStruct((2, head_cols // 2, wide), bf),
            jax.ShapeDtypeStruct((4, 3, count, head_cols), bf),
            jax.ShapeDtypeStruct((wide, width), f32),
            jax.ShapeDtypeStruct((wide, width), f32),
            jax.ShapeDtypeStruct((width, wide), f32),
        ),
        in_specs=[vmem] * 20 + [anywhere] * 8,
        out_specs=(vmem, vmem, vmem) + (anywhere,) * 4,
        scratch_shapes=[
            pltpu.VMEM((world, rows, wide), bf),
            pltpu.VMEM((4, rows, wide), bf),
            pltpu.VMEM((4, rows, wide), bf),
            pltpu.VMEM((count, head_cols), bf),
            pltpu.VMEM((count, head_cols), f32),
            pltpu.VMEM((count, head_cols), f32),
            pltpu.VMEM((count, head_cols), f32),
            pltpu.VMEM((3, count, head_cols), bf),
            pltpu.VMEM((2, head_cols // 2, wide), bf),
            pltpu.VMEM((2, head_cols // 2, wide), bf),
            pltpu.VMEM((16, HD), f32),
            pltpu.VMEM((world, 16, HD), f32),
            pltpu.VMEM((world, lines, HD), f32),
            pltpu.VMEM((lines + 8, HD), f32),
            pltpu.VMEM((3, lines + 8, HD), f32),
            pltpu.VMEM((8, HD), f32),
            pltpu.VMEM((2, tok // rows, rows, wide), bf),
            pltpu.VMEM((2, tok // rows, rows, wide), bf),
            pltpu.VMEM((2, tok, unit), bf),
            pltpu.VMEM((2, tok, unit), bf),
            pltpu.VMEM((unit, wide), bf),
            pltpu.VMEM((wide, unit), f32),
            pltpu.VMEM((wide, unit), f32),
            pltpu.VMEM((unit, wide), f32),
            pltpu.VMEM((tok, unit), bf),
            pltpu.VMEM((tok, unit), bf),
            pltpu.VMEM((tok, unit), bf),
            dma((8,)), dma((8,)), dma((8,)), dma((8,)), dma((8,)), dma((8,)), dma((8,)), dma((8,)), dma((3,)), dma((3,)),
            dma((12,)), dma((12,)), dma((4,)), dma((4,)), pltpu.SemaphoreType.DMA, dma((4, 2)), pltpu.SemaphoreType.DMA, dma((3,)), dma((3,)),
        ],
        compiler_params=pltpu.CompilerParams(
            collective_id=3, has_side_effects=True, vmem_limit_bytes=62 * 2**20
        ),
        name="back",
    )(
        grad_branch, grad_hidden, queries, keys, values, mixed, q_unit, k_unit, q_inverse, k_inverse, first, cosine, signed,
        q_gain.reshape(1, -1), k_gain.reshape(1, -1), *weights, gains, h_all, gd_all, gate_all, up_all, w_down, *own_parts,
    )


def tail_kernel(pg_ref, pu_ref, pd_ref, x_ref, g_ref, og_ref, ou_ref, od_ref, oq_ref, ok_ref, ov_ref):
    count, cols = g_ref.shape[2], x_ref.shape[-1]
    og_ref[...] = pg_ref[...]
    ou_ref[...] = pu_ref[...]
    od_ref[...] = pd_ref[...]
    for p, out in enumerate((oq_ref, ok_ref, ov_ref)):
        total = jnp.zeros(out.shape, jnp.float32)
        for g in range(4):
            total = total + dot_tn(x_ref[g].reshape(count, cols), g_ref[g, p])
        out[...] = total


def weight_tail(parts, x_all, grad_qkv):
    groups, world, rows, wide = x_all.shape
    count, width = world * rows, parts[0].shape[1]
    head_cols = grad_qkv.shape[-1]
    cols = 256
    f32 = jnp.float32
    down = pl.BlockSpec((cols, width), lambda i: (i, 0))
    across = pl.BlockSpec((width, cols), lambda i: (0, i))
    heads = pl.BlockSpec((cols, head_cols), lambda i: (i, 0))
    return pl.pallas_call(
        tail_kernel,
        grid=(wide // cols,),
        in_specs=[
            down, down, across,
            pl.BlockSpec((groups, world, rows, cols), lambda i: (0, 0, 0, i)),
            pl.BlockSpec(grad_qkv.shape, lambda i: (0, 0, 0, 0)),
        ],
        out_specs=(down, down, across, heads, heads, heads),
        out_shape=(
            jax.ShapeDtypeStruct((wide, width), f32),
            jax.ShapeDtypeStruct((wide, width), f32),
            jax.ShapeDtypeStruct((width, wide), f32),
        )
        + (jax.ShapeDtypeStruct((wide, head_cols), f32),) * 3,
        compiler_params=pltpu.CompilerParams(vmem_limit_bytes=60 * 2**20),
        cost_estimate=pl.CostEstimate(
            flops=2 * count * wide * 3 * groups * head_cols, bytes_accessed=100 * 2**20, transcendentals=0
        ),
        name="tail",
    )(*parts, x_all, grad_qkv)


def on_device_fused(
    tokens,
    segment_ids,
    w_query,
    w_key,
    w_value,
    w_out,
    w_gate,
    w_up,
    w_down,
    q_gain,
    k_gain,
    attn_gain,
    ffn_gain,
    cotangent,
):
    wide = tokens.shape[1]
    token_count = segment_ids.shape[0] * segment_ids.shape[1]
    head_cols = w_query.shape[1]
    positions = positions_of(segment_ids).reshape(token_count)
    cosine, sine = rotary_tables(positions)
    first = (jnp.arange(token_count, dtype=jnp.int32) - positions)[:, None]
    signed = jnp.where(jnp.arange(HD) < HD // 2, -sine, sine)
    branch, queries, keys, values, q_unit, k_unit, q_inverse, k_inverse, mixed, x_all = attention(
        tokens, w_query, w_key, w_value, w_out, q_gain, k_gain, cosine, signed, first
    )
    block_out, grad_hidden, grad_branch, gains, h_all, gd_all, own_gate, own_up, own_down, gate_all, up_all = ffn(
        tokens, branch, cotangent, attn_gain, ffn_gain, w_gate, w_up, w_down
    )
    grad_tokens, gains, grad_w_out, grad_qkv, part_gate, part_up, part_down = backward(
        grad_branch, grad_hidden, (queries, keys, values, mixed, q_unit, k_unit, q_inverse, k_inverse),
        first, cosine, signed, q_gain, k_gain, (w_query, w_key, w_value, w_out), gains, h_all, gd_all, gate_all, up_all, w_down,
        (own_gate, own_up, own_down),
    )
    grad_w_gate, grad_w_up, grad_w_down, grad_w_query, grad_w_key, grad_w_value = weight_tail(
        (part_gate, part_up, part_down), x_all, grad_qkv
    )
    lines = wide // HD
    gain_rows = head_cols // HD
    return (
        block_out,
        grad_tokens,
        grad_w_query,
        grad_w_key,
        grad_w_value,
        grad_w_out.reshape(head_cols, wide).astype(jnp.float32),
        grad_w_gate,
        grad_w_up,
        grad_w_down,
        gains[2 * lines : 2 * lines + gain_rows].reshape(head_cols),
        gains[2 * lines + gain_rows : 2 * lines + 2 * gain_rows].reshape(head_cols),
        gains[lines : 2 * lines].reshape(wide),
        gains[:lines].reshape(wide),
    )


def solution(mesh):
    placed = (
        P(("dp", "tensor"), None),
        P("dp", None),
        P(None, "tensor"),
        P(None, "tensor"),
        P(None, "tensor"),
        P("tensor", None),
        P(None, "tensor"),
        P(None, "tensor"),
        P("tensor", None),
        P("tensor"),
        P("tensor"),
        P(),
        P(),
        P(("dp", "tensor"), None),
    )
    return jax.shard_map(
        on_device_fused if dict(mesh.shape) == {"dp": 4, "tensor": 8} else on_device,
        mesh=mesh,
        in_specs=placed,
        out_specs=(
            P(("dp", "tensor"), None),
            P(("dp", "tensor"), None),
            P(None, "tensor"),
            P(None, "tensor"),
            P(None, "tensor"),
            P("tensor", None),
            P(None, "tensor"),
            P(None, "tensor"),
            P("tensor", None),
            P("tensor"),
            P("tensor"),
            P(),
            P(),
        ),
        check_vma=False,
    )
```

```python
import jax
import jax.numpy as jnp
from jax import lax
from jax.experimental import pallas as pl
from jax.experimental.pallas import tpu as pltpu
from jax.sharding import PartitionSpec as P

HD = 128


EPS = 1e-06
THETA = 500000.0


def rounded(value):
    return lax.optimization_barrier(value.astype(jnp.bfloat16)).astype(jnp.float32)


def dot_last(left, right):
    return lax.dot_general(
        left, right, (((1,), (1,)), ((), ())), preferred_element_type=jnp.float32
    )


def dot_first(left, right):
    return lax.dot_general(
        left, right, (((0,), (0,)), ((), ())), preferred_element_type=jnp.float32
    )


def positions_of(segment_ids):
    length = segment_ids.shape[-1]
    places = jnp.arange(length, dtype=jnp.int32)
    below = (segment_ids[:, None, :] < segment_ids[:, :, None]).astype(jnp.int32)
    return places[None, :] - jnp.sum(below, axis=2)


def rotary_tables(positions):
    half = HD // 2
    freq = THETA ** (-(jnp.arange(half, dtype=jnp.float32) * 2.0 / HD))
    angle = positions.astype(jnp.float32)[:, None] * freq[None, :]
    cosine = jnp.concatenate([jnp.cos(angle), jnp.cos(angle)], axis=1)
    sine = jnp.concatenate([jnp.sin(angle), jnp.sin(angle)], axis=1)
    return (cosine, sine)


def rotate(value, cosine, sine):
    half = value.shape[-1] // 2
    turned = jnp.concatenate([-value[..., half:], value[..., :half]], axis=-1)
    return value * cosine[:, None, :] + turned * sine[:, None, :]


def rotate_back(grad, cosine, sine):
    half = grad.shape[-1] // 2
    scaled = grad * sine[:, None, :]
    unturned = jnp.concatenate([scaled[..., half:], -scaled[..., :half]], axis=-1)
    return grad * cosine[:, None, :] + unturned


def norm_back(grad_out, unit, inverse, gain):
    inner = grad_out * gain
    return inverse * (inner - unit * jnp.mean(inner * unit, axis=1, keepdims=True))


def on_device(
    tokens,
    segment_ids,
    w_query,
    w_key,
    w_value,
    w_out,
    w_gate,
    w_up,
    w_down,
    q_gain,
    k_gain,
    attn_gain,
    ffn_gain,
    cotangent,
):
    row_count, full_width = tokens.shape
    head_cols = w_query.shape[1]
    heads_here = head_cols // HD
    ff_cols = w_gate.shape[1]
    seqs_here, seq_len = segment_ids.shape
    token_count = seqs_here * seq_len
    att_scale = HD ** (-0.5)
    whole_x = lax.all_gather(tokens, "tensor", axis=0, tiled=True)
    w_qkv = jnp.concatenate([w_query, w_key, w_value], axis=1)
    projected = jnp.dot(whole_x, w_qkv, preferred_element_type=jnp.float32)
    q_raw = projected[:, :head_cols]
    k_raw = projected[:, head_cols : 2 * head_cols]
    values = projected[:, 2 * head_cols :].astype(jnp.bfloat16)
    q_total, k_total = lax.psum(
        (jnp.sum(q_raw * q_raw, axis=1), jnp.sum(k_raw * k_raw, axis=1)), "tensor"
    )
    q_inverse = lax.rsqrt(q_total / full_width + EPS)[:, None]
    k_inverse = lax.rsqrt(k_total / full_width + EPS)[:, None]
    q_unit = q_raw * q_inverse
    k_unit = k_raw * k_inverse
    cosine, sine = rotary_tables(positions_of(segment_ids).reshape(token_count))
    queries = rotate((q_unit * q_gain).reshape(token_count, heads_here, HD), cosine, sine).astype(
        jnp.bfloat16
    )
    keys = rotate((k_unit * k_gain).reshape(token_count, heads_here, HD), cosine, sine).astype(
        jnp.bfloat16
    )
    shaped = (seqs_here, seq_len, heads_here, HD)
    query_seqs = queries.reshape(shaped)
    key_seqs = keys.reshape(shaped)
    value_seqs = values.reshape(shaped)
    places = jnp.arange(seq_len, dtype=jnp.int32)
    causal = places[:, None] >= places[None, :]

    def scores_of(query_block, key_block, seg_row):
        raw = (
            jnp.einsum("qhd,khd->hqk", query_block, key_block, preferred_element_type=jnp.float32)
            * att_scale
        )
        allowed = causal & (seg_row[:, None] == seg_row[None, :])
        return jnp.where(allowed[None], raw, -1e30)

    def attend(pieces):
        query_block, key_block, value_block, seg_row = pieces
        scores = scores_of(query_block, key_block, seg_row)
        top = jnp.max(scores, axis=-1, keepdims=True)
        expo = jnp.exp(scores - top)
        total = jnp.sum(expo, axis=-1, keepdims=True)
        probs = (expo / total).astype(jnp.bfloat16)
        mixed_block = jnp.einsum(
            "hqk,khd->qhd", probs, value_block, preferred_element_type=jnp.float32
        )
        return (mixed_block.astype(jnp.bfloat16), (top + jnp.log(total))[..., 0])

    mixed, log_total = lax.map(attend, (query_seqs, key_seqs, value_seqs, segment_ids))
    mixed = mixed.reshape(token_count, head_cols)
    x_rows = tokens.astype(jnp.float32)
    branch = lax.psum_scatter(
        jnp.dot(mixed, w_out, preferred_element_type=jnp.float32).astype(jnp.bfloat16),
        "tensor",
        scatter_dimension=0,
        tiled=True,
    ).astype(jnp.float32)
    a_inverse = lax.rsqrt(jnp.mean(branch * branch, axis=1, keepdims=True) + EPS)
    hidden = x_rows + branch * a_inverse * attn_gain
    h_low = lax.all_gather(hidden.astype(jnp.bfloat16), "tensor", axis=0, tiled=True)
    a_unit = branch * a_inverse
    w_gate_up = jnp.concatenate([w_gate, w_up], axis=1)
    gate_up = jnp.dot(h_low, w_gate_up, preferred_element_type=jnp.float32)
    gate = gate_up[:, :ff_cols]
    up = gate_up[:, ff_cols:]
    sigma_gate = jax.nn.sigmoid(gate)
    silu_gate = gate * sigma_gate
    act = (silu_gate * up).astype(jnp.bfloat16)
    down = lax.psum_scatter(
        jnp.dot(act, w_down, preferred_element_type=jnp.float32).astype(jnp.bfloat16),
        "tensor",
        scatter_dimension=0,
        tiled=True,
    ).astype(jnp.float32)
    f_inverse = lax.rsqrt(jnp.mean(down * down, axis=1, keepdims=True) + EPS)
    f_unit = down * f_inverse
    block_out = (hidden + f_unit * ffn_gain).astype(jnp.bfloat16)
    grad_out = cotangent.astype(jnp.float32)
    grad_ffn_part = jnp.sum(grad_out * f_unit, axis=0)
    grad_down = norm_back(grad_out, f_unit, f_inverse, ffn_gain).astype(jnp.bfloat16)
    grad_down_all = lax.all_gather(grad_down, "tensor", axis=0, tiled=True)
    grad_act = dot_last(grad_down_all, w_down)
    grad_w_down = dot_first(act, grad_down_all)
    grad_gate = grad_act * up * sigma_gate * (1.0 + gate * (1.0 - sigma_gate))
    grad_up = grad_act * silu_gate
    grad_gate_up = jnp.concatenate([grad_gate, grad_up], axis=1).astype(jnp.bfloat16)
    grad_w_gate_up = dot_first(h_low, grad_gate_up)
    grad_hidden = grad_out + lax.psum_scatter(
        dot_last(grad_gate_up, w_gate_up).astype(jnp.bfloat16), "tensor", scatter_dimension=0, tiled=True
    ).astype(jnp.float32)
    grad_attn_part = jnp.sum(grad_hidden * a_unit, axis=0)
    grad_branch = norm_back(grad_hidden, a_unit, a_inverse, attn_gain).astype(jnp.bfloat16)
    grad_branch_all = lax.all_gather(grad_branch, "tensor", axis=0, tiled=True)
    grad_w_out = dot_first(mixed, grad_branch_all)
    grad_mixed = dot_last(grad_branch_all, w_out).astype(jnp.bfloat16).reshape(shaped)

    def attend_back(pieces):
        query_block, key_block, value_block, seg_row, log_block, grad_block = pieces
        scores = scores_of(query_block, key_block, seg_row)
        probs = jnp.exp(scores - log_block[..., None])
        grad_probs = jnp.einsum(
            "qhd,khd->hqk", grad_block, value_block, preferred_element_type=jnp.float32
        )
        grad_scores = (
            probs * (grad_probs - jnp.sum(probs * grad_probs, axis=-1, keepdims=True))
        ).astype(jnp.bfloat16)
        grad_query = (
            jnp.einsum("hqk,khd->qhd", grad_scores, key_block, preferred_element_type=jnp.float32)
            * att_scale
        )
        grad_key = (
            jnp.einsum("hqk,qhd->khd", grad_scores, query_block, preferred_element_type=jnp.float32)
            * att_scale
        )
        grad_value = jnp.einsum(
            "hqk,qhd->khd",
            probs.astype(jnp.bfloat16),
            grad_block,
            preferred_element_type=jnp.float32,
        )
        return (grad_query, grad_key, grad_value.astype(jnp.bfloat16))

    grad_query, grad_key, grad_value = lax.map(
        attend_back, (query_seqs, key_seqs, value_seqs, segment_ids, log_total, grad_mixed)
    )
    grad_q_normed = rotate_back(
        rounded(grad_query.reshape(token_count, heads_here, HD)), cosine, sine
    ).reshape(token_count, head_cols)
    grad_k_normed = rotate_back(
        rounded(grad_key.reshape(token_count, heads_here, HD)), cosine, sine
    ).reshape(token_count, head_cols)
    grad_q_gain = jnp.sum(grad_q_normed * q_unit, axis=0)
    grad_k_gain = jnp.sum(grad_k_normed * k_unit, axis=0)
    inner_q = grad_q_normed * q_gain
    inner_k = grad_k_normed * k_gain
    q_inner_sum, k_inner_sum = lax.psum(
        (jnp.sum(inner_q * q_unit, axis=1), jnp.sum(inner_k * k_unit, axis=1)), "tensor"
    )
    grad_q_raw = q_inverse * (inner_q - q_unit * (q_inner_sum / full_width)[:, None])
    grad_k_raw = k_inverse * (inner_k - k_unit * (k_inner_sum / full_width)[:, None])
    grad_qkv = jnp.concatenate(
        [
            grad_q_raw.astype(jnp.bfloat16),
            grad_k_raw.astype(jnp.bfloat16),
            grad_value.reshape(token_count, head_cols),
        ],
        axis=1,
    )
    grad_w_qkv = dot_first(whole_x, grad_qkv)
    grad_tokens = grad_hidden + lax.psum_scatter(
        dot_last(grad_qkv, w_qkv).astype(jnp.bfloat16), "tensor", scatter_dimension=0, tiled=True
    ).astype(jnp.float32)
    grad_w_qkv, grad_w_out, grad_w_gate_up, grad_w_down = [
        lax.psum(part.astype(jnp.bfloat16), "dp").astype(jnp.float32)
        for part in (grad_w_qkv, grad_w_out, grad_w_gate_up, grad_w_down)
    ]
    grad_q_gain, grad_k_gain = lax.psum((grad_q_gain, grad_k_gain), "dp")
    grad_attn_gain, grad_ffn_gain = lax.psum((grad_attn_part, grad_ffn_part), ("dp", "tensor"))
    return (
        block_out,
        grad_tokens,
        grad_w_qkv[:, :head_cols],
        grad_w_qkv[:, head_cols : 2 * head_cols],
        grad_w_qkv[:, 2 * head_cols :],
        grad_w_out,
        grad_w_gate_up[:, :ff_cols],
        grad_w_gate_up[:, ff_cols:],
        grad_w_down,
        grad_q_gain,
        grad_k_gain,
        grad_attn_gain,
        grad_ffn_gain,
    )


MESH = pl.DeviceIdType.MESH
LANES = 2


def places_of():
    d = lax.axis_index("dp")
    t = lax.axis_index("tensor")
    z, c = lax.div(t, 2), lax.rem(t, 2)
    dx = d + 1 - 2 * lax.rem(d, 2)
    dy = lax.rem(d + 2, 4)
    zs = (z, z + 1 - 2 * lax.rem(z, 2), lax.rem(z + 2, 4), 3 - z)
    inner = lax.rem(z + 1, 4) >= 2
    return d, dx, dy, zs, c, inner


def remote(src, dst, send, recv, dp, tensor):
    return pltpu.make_async_remote_copy(
        src_ref=src, dst_ref=dst, send_sem=send, recv_sem=recv, device_id=(dp, tensor), device_id_type=MESH
    )


def enter(d, zs, c, dx=None, dy=None):
    barrier = pltpu.get_barrier_semaphore()
    peers = [(d, 2 * zs[r] + c) for r in (1, 2, 3)] + [(d, 2 * zs[0] + 1 - c)]
    if dx is not None:
        peers += [(dx, 2 * zs[0] + c), (dy, 2 * zs[0] + c)]
    for peer in peers:
        pl.semaphore_signal(barrier, inc=1, device_id=peer, device_id_type=MESH)
    pl.semaphore_wait(barrier, len(peers))


class Gather:
    def __init__(self, full, send, recv, place):
        self.full, self.send, self.recv = full, send, recv
        self.d, _, _, self.zs, self.c, self.inner = place
        self.t = 2 * self.zs[0] + self.c

    def lane(self, r):
        return self.full.at[2 * self.zs[r] + self.c]

    def other(self, r):
        return self.full.at[2 * self.zs[r] + 1 - self.c]

    def to_z(self, r, k, via):
        return remote(self.lane(r), self.lane(r), self.send.at[via if r == 0 else 7], self.recv.at[k], self.d, 2 * self.zs[via] + self.c)

    def to_core(self, r):
        return remote(self.lane(r), self.lane(r), self.send.at[0 if r == 0 else 3 + r], self.recv.at[4 + r], self.d, 2 * self.zs[0] + 1 - self.c)

    def start(self):
        self.to_z(0, 2, 2).start()
        self.to_z(0, 1, 1).start()
        self.to_core(0).start()

    def start_inner(self):
        @pl.when(self.inner)
        def _():
            self.to_z(0, 2, 2).wait_send()
            self.to_z(0, 3, 3).start()

    def arrive(self, r):
        self.to_z(r, r, r).wait_recv()
        if r == 2:
            @pl.when(self.inner)
            def _():
                self.to_z(2, 3, 1).start()
        self.to_core(r).start()

    def ready(self, r):
        remote(self.other(r), self.other(r), self.send.at[0], self.recv.at[4 + r], self.d, self.t).wait_recv()

    def finish(self):
        @pl.when(jnp.logical_not(self.inner))
        def _():
            self.to_z(0, 2, 2).wait_send()

        @pl.when(self.inner)
        def _():
            self.to_z(0, 3, 3).wait_send()
            self.to_z(2, 3, 1).wait_send()

        self.to_z(0, 1, 1).wait_send()
        for r in range(4):
            self.to_core(r).wait_send()


class Scatter:
    def __init__(self, parts, pair, land, send, recv, place):
        self.parts, self.pair, self.land, self.send, self.recv = parts, pair, land, send, recv
        self.d, _, _, self.zs, self.c, self.inner = place
        self.t = 2 * self.zs[0] + self.c
        self.half = parts.shape[2] // 2

    def cut(self, ref, at, r, h):
        if h is None:
            return ref.at[at]
        return ref.at[at, :, pl.ds(h * self.half, self.half)]

    def mine(self, r, h=None):
        return self.cut(self.parts, 2 * self.zs[r] + self.c, r, h)

    def to_core(self, r, h=None):
        src = self.cut(self.parts, 2 * self.zs[r] + 1 - self.c, r, h)
        at = 8 if h == 1 else r
        return remote(src, self.cut(self.pair, r, r, h), self.send.at[at], self.recv.at[at], self.d, 2 * self.zs[0] + 1 - self.c)

    def start_core(self, r):
        for h in (0, 1) if r == 3 else (None,):
            self.to_core(r, h).start()

    def to_z(self, r, k, via, h=None):
        return remote(
            self.mine(r, h), self.cut(self.land, k, r, h), self.send.at[SENT[r, h]], self.recv.at[LANDED[k, h]], self.d,
            2 * self.zs[via] + self.c,
        )

    def add_pair(self, r, h=None):
        halves = (0, 1) if r == 3 and h is None else (h,)
        for h in halves:
            self.to_core(r, h).wait_recv()
            add_into(self.mine(r, h), self.cut(self.pair, r, r, h))

    def pass_on(self, r, h=None):
        if r == 1:
            self.to_z(1, 1, 1).start()
        if r == 2:
            @pl.when(jnp.logical_not(self.inner))
            def _():
                for h in range(2):
                    self.to_z(2, 2, 2, h).start()
        if r == 3:
            halves = (0, 1) if h is None else (h,)

            @pl.when(self.inner)
            def _():
                for h in halves:
                    self.to_z(3, 3, 3, h).start()

            @pl.when(jnp.logical_not(self.inner))
            def _():
                for h in halves:
                    self.to_z(3, 0, 1, h).start()

    def relay(self):
        @pl.when(self.inner)
        def _():
            for h in range(2):
                self.to_z(3, 0, 1, h).wait_recv()
                add_into(self.mine(2, h), self.cut(self.land, 0, 0, h))
                self.to_z(2, 2, 2, h).start()

    def arrived(self):
        self.to_z(1, 1, 1).wait_recv()

        @pl.when(self.inner)
        def _():
            for h in range(2):
                self.to_z(3, 3, 3, h).wait_recv()

        @pl.when(jnp.logical_not(self.inner))
        def _():
            self.land[3] = jnp.zeros(self.land.shape[1:], self.land.dtype)

        for h in range(2):
            self.to_z(2, 2, 2, h).wait_recv()

    def total(self, rows):
        own = self.parts[2 * self.zs[0] + self.c, rows, :].astype(jnp.float32)
        return own + self.land[1, rows, :].astype(jnp.float32) + self.land[2, rows, :].astype(jnp.float32) + self.land[3, rows, :].astype(jnp.float32)

    def finish(self):
        for r in range(3):
            self.to_core(r).wait_send()
        self.to_z(1, 1, 1).wait_send()
        for h in range(2):
            self.to_core(3, h).wait_send()
            self.to_z(2, 2, 2, h).wait_send()
            self.to_z(3, 3, 3, h).wait_send()


SENT = {(1, None): 5, (2, 0): 6, (2, 1): 9, (3, 0): 7, (3, 1): 10}
LANDED = {(1, None): 5, (2, 0): 6, (2, 1): 9, (3, 0): 7, (3, 1): 10, (0, 0): 4, (0, 1): 11}


def add_into(into, other):
    rows = into.shape[0]

    def step(i, carry):
        at = pl.ds(pl.multiple_of(i * 32, 32), 32)
        into[at, :] = (into[at, :].astype(jnp.float32) + other[at, :].astype(jnp.float32)).astype(into.dtype)
        return carry

    lax.fori_loop(0, rows // 32, step, 0)


class Loads:
    def __init__(self, pairs, sem):
        self.copies = [pltpu.make_async_copy(far, near, sem.at[n]) for n, (far, near) in enumerate(pairs)]

    def start(self):
        for copy in self.copies:
            copy.start()

    def wait(self, *which):
        for n in which:
            self.copies[n].wait()


class Spread:
    def __init__(self, full, whole, send, recv, own_sem, place):
        self.full, self.whole, self.send, self.recv, self.own_sem = full, whole, send, recv, own_sem
        self.d, self.dx, self.dy, self.zs, self.c, _ = place
        self.t = 2 * self.zs[0] + self.c
        self.seen = set()

    def ready(self, k, r):
        other = self.whole.at[1 + k, 2 * self.zs[r] + 1 - self.c]
        remote(other, other, self.send.at[0], self.recv.at[12 + k * 4 + r], self.d, self.t).wait_recv()
        self.seen.add((k, r))

    def slot(self, g, r):
        return self.whole.at[g, 2 * self.zs[r] + self.c]

    def own(self, r, k):
        src = self.full.at[2 * self.zs[r] + self.c]
        return remote(src, self.slot(1 + k, r), self.send.at[k * 4 + r], self.recv.at[k * 4 + r], (self.dx, self.dy)[k], self.t)

    def start(self, r):
        self.own(r, 0).start()
        self.own(r, 1).start()

    def hop(self, r):
        group, target = (1, self.dy) if r in (0, 3) else (2, self.dx)
        return remote(self.slot(group, r), self.slot(3, r), self.send.at[8 + r], self.recv.at[8 + r], target, self.t)

    def to_core(self, r, k):
        return remote(self.slot(1 + k, r), self.slot(1 + k, r), self.send.at[12 + k * 4 + r], self.recv.at[12 + k * 4 + r], self.d, 2 * self.zs[0] + 1 - self.c)

    def pass_on(self, r):
        self.own(r, 0).wait_recv()
        self.own(r, 1).wait_recv()
        self.hop(r).start()
        self.to_core(r, 0).start()
        self.to_core(r, 1).start()

    def last(self, r):
        self.hop(r).wait_recv()
        self.to_core(r, 2).start()

    def keep(self):
        return pltpu.make_async_copy(self.full, self.whole.at[0], self.own_sem)

    def finish(self):
        for r in range(4):
            self.own(r, 0).wait_send()
            self.own(r, 1).wait_send()
            self.hop(r).wait_send()
            for k in range(3):
                self.to_core(r, k).wait_send()
                if (k, r) not in self.seen:
                    self.to_core(r, k).wait_recv()
        self.keep().wait()


def dot_tn(left, right):
    return lax.dot_general(left, right, (((0,), (0,)), ((), ())), preferred_element_type=jnp.float32)


def dot_nt(left, right):
    return lax.dot_general(left, right, (((1,), (1,)), ((), ())), preferred_element_type=jnp.float32)


def ffn_kernel(
    x_ref, br_ref, cot_ref, again_ref, gain_ref, wg_hbm, wu_hbm, wd_hbm,
    bo_ref, gh_ref, gb_ref, gains_ref, hall_ref, gdall_ref, og_ref, ou_ref, od_ref, gate_all, up_all,
    hfull, gfull, hid_ref, sums, gate, up, act, gg, gu, parts, pair, land, hbuf, gbuf, ubuf, wg_ref, wu_ref, wd_ref,
    ag_send, ag_recv, rs_send, rs_recv, xy_send, xy_recv, own_sem, load_sem, store_sem, out_sem, weight_sem,
):
    place = places_of()
    d, dx, dy, zs, c, inner = place
    t = 2 * zs[0] + c
    weights = Loads(((wg_hbm, wg_ref), (wu_hbm, wu_ref), (wd_hbm, wd_ref)), weight_sem)
    weights.start()
    width = wg_ref.shape[1]
    rows, wide = x_ref.shape
    ft, dt = 512, 1024
    step_rows = 32
    a_gain, gain = again_ref[...], gain_ref[...]

    def opening(i, carry):
        at = pl.ds(pl.multiple_of(i * step_rows, step_rows), step_rows)
        branch = br_ref[at, :]
        inverse = lax.rsqrt(jnp.mean(branch * branch, axis=1, keepdims=True) + EPS)
        hidden = x_ref[at, :].astype(jnp.float32) + branch * inverse * a_gain
        hid_ref[at, :] = hidden
        hfull[t, at, :] = hidden.astype(jnp.bfloat16)
        return carry

    lax.fori_loop(0, rows // step_rows, opening, 0)
    enter(d, zs, c, dx, dy)

    def unit_forward(zz, after=None):
        both = pl.ds(2 * zz, 2)
        at = pl.ds(pl.multiple_of(zz * 2 * rows, 2 * rows), 2 * rows)

        def mid(j, carry):
            cols = pl.ds(pl.multiple_of(j * ft, ft), ft)
            block = hfull[both].reshape(2 * rows, wide)
            g = jnp.dot(block, wg_ref[:, cols], preferred_element_type=jnp.float32)
            u = jnp.dot(block, wu_ref[:, cols], preferred_element_type=jnp.float32)
            gate[at, cols] = g
            up[at, cols] = u
            act[at, cols] = (g * jax.nn.sigmoid(g) * u).astype(jnp.bfloat16)
            return carry

        lax.fori_loop(0, width // ft, mid, 0)

        def out(j, carry):
            cols = pl.ds(pl.multiple_of(j * dt, dt), dt)
            p = jnp.dot(act[at, :], wd_ref[:, cols], preferred_element_type=jnp.float32)
            parts[both, :, cols] = p.astype(jnp.bfloat16).reshape(2, rows, dt)
            return carry

        if after is None:
            lax.fori_loop(0, wide // dt, out, 0)
        else:
            for j in range(wide // dt):
                out(j, 0)
                after(j)

    def unit_backward(zz, after=None):
        both = pl.ds(2 * zz, 2)
        at = pl.ds(pl.multiple_of(zz * 2 * rows, 2 * rows), 2 * rows)

        def mid(j, carry):
            cols = pl.ds(pl.multiple_of(j * ft, ft), ft)
            block = gfull[both].reshape(2 * rows, wide)
            ga = dot_nt(block, wd_ref[cols, :])
            g, u = gate[at, cols], up[at, cols]
            s = jax.nn.sigmoid(g)
            gg[at, cols] = (ga * u * s * (1.0 + g * (1.0 - s))).astype(jnp.bfloat16)
            gu[at, cols] = (ga * (g * s)).astype(jnp.bfloat16)
            return carry

        lax.fori_loop(0, width // ft, mid, 0)

        def out(j, carry):
            cols = pl.ds(pl.multiple_of(j * dt, dt), dt)
            p = dot_nt(gg[at, :], wg_ref[cols, :]) + dot_nt(gu[at, :], wu_ref[cols, :])
            parts[both, :, cols] = p.astype(jnp.bfloat16).reshape(2, rows, dt)
            return carry

        if after is None:
            lax.fori_loop(0, wide // dt, out, 0)
        else:
            for j in range(wide // dt):
                out(j, 0)
                after(j)

    def own_copies(i, down):
        slot = pl.ds(pl.multiple_of(lax.rem(i, 4) * 256, 256), 256)
        at = pl.ds(pl.multiple_of(i * 256, 256), 256)
        outs = (od_ref.at[at, pl.ds(0, width)], od_ref.at[at, pl.ds(width, width)]) if down else (og_ref.at[at, :], ou_ref.at[at, :])
        return [
            pltpu.make_async_copy(buf.at[slot, :], out, out_sem.at[n, lax.rem(i, 4)])
            for n, (buf, out) in enumerate(zip((gate, up), outs))
        ]

    def own_in(i, carry):
        slot = pl.ds(pl.multiple_of(lax.rem(i, 4) * 256, 256), 256)
        at = pl.ds(pl.multiple_of(i * 256, 256), 256)

        @pl.when(i >= 4)
        def _():
            for copy in own_copies(i - 4, False):
                copy.wait()

        h = hfull[:, :, at].reshape(8 * rows, 256)
        gate[slot, :] = dot_tn(h, gg[...])
        up[slot, :] = dot_tn(h, gu[...])
        for copy in own_copies(i, False):
            copy.start()
        return carry

    def own_down(i, carry):
        at = pl.ds(pl.multiple_of(i * 256, 256), 256)
        for copy in own_copies(i + 4, False):
            copy.wait()
        left = act[:, at]
        for n, buf in enumerate((gate, up)):
            buf[at, :] = dot_tn(left, gfull[:, :, n * width : (n + 1) * width].reshape(8 * rows, width))
        for copy in own_copies(i, True):
            copy.start()
        return carry

    done = []

    def fill(chunks):
        def load(n):
            k, r = chunks[n]
            slot = (base + n) % 2
            return pltpu.make_async_copy(hall_ref.at[1 + k, pl.ds(2 * zs[r], 2)], hbuf.at[slot], load_sem.at[slot])

        base = len(done)
        for n, (k, r) in enumerate(chunks):
            slot = len(done) % 2
            if n == 0:
                xy_h.ready(k, r)
                load(0).start()
            load(n).wait()
            if n + 1 < len(chunks):
                xy_h.ready(*chunks[n + 1])
                load(n + 1).start()
            if len(done) >= 2:
                for copy in stores(len(done) - 2):
                    copy.wait()

            def tile(j, carry):
                cols = pl.ds(pl.multiple_of(j * ft, ft), ft)
                block = hbuf[slot].reshape(2 * rows, wide)
                gbuf[slot, :, cols] = jnp.dot(block, wg_ref[:, cols], preferred_element_type=jnp.float32).astype(jnp.bfloat16)
                ubuf[slot, :, cols] = jnp.dot(block, wu_ref[:, cols], preferred_element_type=jnp.float32).astype(jnp.bfloat16)
                return carry

            lax.fori_loop(0, width // ft, tile, 0)
            done.append((k, r))
            for copy in stores(len(done) - 1):
                copy.start()

    def stores(n):
        k, r = done[n]
        at = pl.ds(pl.multiple_of(zs[r] * 2 * rows, 2 * rows), 2 * rows)
        return [
            pltpu.make_async_copy(buf.at[n % 2], out.at[k, at, :], store_sem.at[m, n % 2])
            for m, (buf, out) in enumerate(((gbuf, gate_all), (ubuf, up_all)))
        ]

    def phase(p, full, whole, unit):
        ag = Gather(full, ag_send.at[p], ag_recv.at[p], place)
        rs = Scatter(parts, pair.at[p], land.at[p], rs_send.at[p], rs_recv.at[p], place)
        xy = xy_h if p == 0 else xy_g
        ag.start()
        xy.start(0)
        ag.ready(0)
        if p == 0:
            weights.wait(0, 1, 2)
        unit(zs[0])
        rs.start_core(0)
        if p == 1:
            fill([(0, 3), (1, 3), (2, 0), (2, 2)])
        xy.pass_on(0)
        ag.start_inner()
        ag.arrive(2)
        xy.start(2)
        ag.arrive(1)
        xy.start(1)
        ag.ready(2)
        unit(zs[2])
        rs.start_core(2)
        ag.ready(1)
        unit(zs[1])
        rs.start_core(1)
        rs.add_pair(2)
        rs.pass_on(2)
        rs.add_pair(1)
        rs.pass_on(1)
        ag.arrive(3)
        xy.start(3)
        ag.ready(3)
        unit(zs[3], lambda j: rs.to_core(3, j).start())
        for h in range(2):
            rs.add_pair(3, h)
            rs.pass_on(3, h)
        xy.keep().start()
        rs.add_pair(0)
        if p == 0:
            fill([(0, 0), (1, 0)])
            xy.pass_on(2)
            xy.pass_on(1)
            fill([(0, 2)])
        else:
            lax.fori_loop(0, 8, own_in, 0)
            xy.pass_on(2)
            xy.pass_on(1)
        rs.relay()
        if p == 0:
            fill([(1, 2), (0, 1), (1, 1)])
        else:
            lax.fori_loop(0, 4, own_down, 0)
            xy.pass_on(3)
            fill([(2, 1), (2, 3)])
        rs.arrived()
        return ag, rs

    xy_h = Spread(hfull, hall_ref, xy_send.at[0], xy_recv.at[0], own_sem.at[0], place)
    xy_g = Spread(gfull, gdall_ref, xy_send.at[1], xy_recv.at[1], own_sem.at[1], place)
    ag, rs = phase(0, hfull, hall_ref, unit_forward)
    sums[...] = jnp.zeros_like(sums)

    def middle(i, carry):
        at = pl.ds(pl.multiple_of(i * step_rows, step_rows), step_rows)
        down = rs.total(at)
        inverse = lax.rsqrt(jnp.mean(down * down, axis=1, keepdims=True) + EPS)
        unit = down * inverse
        bo_ref[at, :] = (hid_ref[at, :] + unit * gain).astype(jnp.bfloat16)
        grad = cot_ref[at, :].astype(jnp.float32)
        sums[0:1, :] += jnp.sum(grad * unit, axis=0, keepdims=True)
        inner_grad = grad * gain
        gfull[t, at, :] = (inverse * (inner_grad - unit * jnp.mean(inner_grad * unit, axis=1, keepdims=True))).astype(jnp.bfloat16)
        return carry

    lax.fori_loop(0, rows // step_rows, middle, 0)
    ag.finish()
    rs.finish()
    xy_h.pass_on(3)
    for r in range(4):
        xy_h.last(r)
    ag, rs = phase(1, gfull, gdall_ref, unit_backward)

    def ending(i, carry):
        at = pl.ds(pl.multiple_of(i * step_rows, step_rows), step_rows)
        grad = cot_ref[at, :].astype(jnp.float32) + rs.total(at)
        gh_ref[at, :] = grad
        branch = br_ref[at, :]
        inverse = lax.rsqrt(jnp.mean(branch * branch, axis=1, keepdims=True) + EPS)
        unit = branch * inverse
        sums[1:2, :] += jnp.sum(grad * unit, axis=0, keepdims=True)
        inner_grad = grad * a_gain
        gb_ref[at, :] = (inverse * (inner_grad - unit * jnp.mean(inner_grad * unit, axis=1, keepdims=True))).astype(jnp.bfloat16)
        return carry

    lax.fori_loop(0, rows // step_rows, ending, 0)
    for i in range(wide // HD):
        gains_ref[i : i + 1, :] = sums[0:1, i * HD : (i + 1) * HD]
        gains_ref[wide // HD + i : wide // HD + i + 1, :] = sums[1:2, i * HD : (i + 1) * HD]
    ag.finish()
    rs.finish()
    for r in range(4):
        xy_g.last(r)
    xy_h.finish()
    for i in range(4):
        for copy in own_copies(i, True):
            copy.wait()
    for n in (len(done) - 2, len(done) - 1):
        for copy in stores(n):
            copy.wait()
    xy_g.finish()


def ffn(x_own, branch, cot, attn_gain, ffn_gain, w_gate, w_up, w_down):
    rows, wide = x_own.shape
    width = w_gate.shape[1]
    groups, world = 4, 8
    vmem = pl.BlockSpec(memory_space=pltpu.VMEM)
    anywhere = pl.BlockSpec(memory_space=pl.ANY)
    bf, f32 = jnp.bfloat16, jnp.float32
    whole = jax.ShapeDtypeStruct((groups, world, rows, wide), bf)
    others = jax.ShapeDtypeStruct((groups - 1, world * rows, width), bf)
    dma = pltpu.SemaphoreType.DMA
    return pl.pallas_call(
        ffn_kernel,
        out_shape=(
            jax.ShapeDtypeStruct((rows, wide), bf),
            jax.ShapeDtypeStruct((rows, wide), f32),
            jax.ShapeDtypeStruct((rows, wide), bf),
            jax.ShapeDtypeStruct((2 * wide // HD, HD), f32),
            whole,
            whole,
            jax.ShapeDtypeStruct((wide, width), f32),
            jax.ShapeDtypeStruct((wide, width), f32),
            jax.ShapeDtypeStruct((width, wide), f32),
            others,
            others,
        ),
        in_specs=[vmem] * 5 + [anywhere] * 3,
        out_specs=(vmem,) * 4 + (anywhere,) * 7,
        scratch_shapes=[
            pltpu.VMEM((world, rows, wide), bf),
            pltpu.VMEM((world, rows, wide), bf),
            pltpu.VMEM((rows, wide), f32),
            pltpu.VMEM((8, wide), f32),
            pltpu.VMEM((world * rows, width), f32),
            pltpu.VMEM((world * rows, width), f32),
            pltpu.VMEM((world * rows, width), bf),
            pltpu.VMEM((world * rows, width), bf),
            pltpu.VMEM((world * rows, width), bf),
            pltpu.VMEM((world, rows, wide), bf),
            pltpu.VMEM((2, 4, rows, wide), bf),
            pltpu.VMEM((2, 4, rows, wide), bf),
            pltpu.VMEM((2, 2, rows, wide), bf),
            pltpu.VMEM((2, 2 * rows, width), bf),
            pltpu.VMEM((2, 2 * rows, width), bf),
            pltpu.VMEM((wide, width), bf),
            pltpu.VMEM((wide, width), bf),
            pltpu.VMEM((width, wide), bf),
            dma((2, 8)),
            dma((2, 8)),
            dma((2, 12)),
            dma((2, 12)),
            dma((2, 24)),
            dma((2, 24)),
            dma((2,)),
            dma((2,)),
            dma((2, 2)),
            dma((2, 4)),
            dma((3,)),
        ],
        compiler_params=pltpu.CompilerParams(
            collective_id=2, has_side_effects=True, vmem_limit_bytes=60 * 2**20
        ),
        name="ffn",
    )(x_own, branch, cot, attn_gain.reshape(1, wide), ffn_gain.reshape(1, wide), w_gate, w_up, w_down)


WINDOW = 3


class Exchange:
    def __init__(self, block, land, send, recv, place):
        self.block, self.land, self.send, self.recv = block, land, send, recv
        self.d, _, _, self.zs, self.c, _ = place
        self.t = 2 * self.zs[0] + self.c

    def copies(self):
        out = []
        for r in range(4):
            for k in range(2):
                if r == 0 and k == 0:
                    continue
                at = 4 * k + r
                core = self.c if k == 0 else 1 - self.c
                out.append((2 * self.zs[r] + core, at))
        return out

    def start(self):
        for peer, at in self.copies():
            remote(self.block, self.land.at[self.t], self.send.at[at], self.recv.at[at], self.d, peer).start()

    def wait(self):
        for peer, at in self.copies():
            remote(self.block, self.land.at[peer], self.send.at[at], self.recv.at[at], self.d, peer).wait()


def enter_all(d, zs, c, dx, dy):
    barrier = pltpu.get_barrier_semaphore()
    peers = [(d, 2 * zs[r] + c) for r in (1, 2, 3)] + [(d, 2 * zs[r] + 1 - c) for r in range(4)]
    peers += [(dx, 2 * zs[0] + c), (dy, 2 * zs[0] + c)]
    for peer in peers:
        pl.semaphore_signal(barrier, inc=1, device_id=peer, device_id_type=MESH)
    pl.semaphore_wait(barrier, len(peers))


def put_column(stat, base, zz, square):
    rows = square.shape[0]
    folded = square[:, :HD]
    for h in range(1, square.shape[1] // HD):
        folded = folded + square[:, h * HD : (h + 1) * HD]
    line = jnp.sum(folded.T, axis=0, keepdims=True)
    for i in range(rows // HD):
        stat[pl.ds(base + 2 * zz + i, 1), :] = line[:, i * HD : (i + 1) * HD]


def get_column(stat_row, count):
    return jnp.broadcast_to(stat_row, (count, HD)).T


def attn_kernel(
    x_ref, wq_hbm, wk_hbm, wv_hbm, wo_hbm, qg_ref, kg_ref, cos_ref, sin_ref, first_ref,
    br_ref, q_out, k_out, v_out, qu_out, ku_out, rq_out, rk_out, mixed_out, xall_ref,
    xfull, parts, pair, land, stat, stats, wq_ref, wk_ref, wv_ref, wo_ref,
    ag_send, ag_recv, rs_send, rs_recv, xy_send, xy_recv, st_send, st_recv, own_sem, weight_sem,
):
    place = places_of()
    d, dx, dy, zs, c, inner = place
    t = 2 * zs[0] + c
    rows, wide = x_ref.shape
    span = 2 * rows
    weights = Loads(((wq_hbm, wq_ref), (wk_hbm, wk_ref), (wv_hbm, wv_ref), (wo_hbm, wo_ref)), weight_sem)
    weights.start()
    heads = wq_ref.shape[1] // HD
    xfull[t] = x_ref[...]
    enter_all(d, zs, c, dx, dy)
    ag = Gather(xfull, ag_send, ag_recv, place)
    rs = Scatter(parts, pair, land, rs_send, rs_recv, place)
    xy = Spread(xfull, xall_ref, xy_send, xy_recv, own_sem, place)
    ex = Exchange(stat, stats, st_send, st_recv, place)

    def at_of(zz):
        return pl.ds(pl.multiple_of(zz * span, span), span)

    def project_qk(zz):
        block = xfull[pl.ds(2 * zz, 2)].reshape(span, wide)
        for w_ref, out, base in ((wq_ref, qu_out, 0), (wk_ref, ku_out, 8)):
            raw = jnp.dot(block, w_ref[...], preferred_element_type=jnp.float32)
            out[at_of(zz), :] = raw
            put_column(stat, base, zz, raw * raw)

    def project_v(zz):
        block = xfull[pl.ds(2 * zz, 2)].reshape(span, wide)
        v_out[at_of(zz), :] = jnp.dot(block, wv_ref[...], preferred_element_type=jnp.float32).astype(jnp.bfloat16)

    ag.start()
    xy.start(0)
    ag.ready(0)
    weights.wait(0, 1, 2, 3)
    project_qk(zs[0])
    project_v(zs[0])
    xy.pass_on(0)
    ag.start_inner()
    ag.arrive(2)
    xy.start(2)
    ag.arrive(1)
    xy.start(1)
    ag.ready(2)
    project_qk(zs[2])
    ag.ready(1)
    project_qk(zs[1])
    project_v(zs[2])
    ag.arrive(3)
    xy.start(3)
    ag.ready(3)
    project_qk(zs[3])
    ex.start()
    project_v(zs[1])
    project_v(zs[3])
    xy.keep().start()
    ex.wait()
    total = stat[...]
    for r in range(4):
        for k in range(2):
            if r or k:
                total = total + stats[2 * zs[r] + (c if k == 0 else 1 - c)]
    inverse = lax.rsqrt(total / (8 * wq_ref.shape[1]) + EPS)
    rq_out[...] = inverse[:8]
    rk_out[...] = inverse[8:]

    def norm_rope(i, carry):
        at = pl.ds(pl.multiple_of(i * HD, HD), HD)
        cosine, sine = cos_ref[at, :], sin_ref[at, :]
        for line, raw, out, gain in ((rq_out, qu_out, q_out, qg_ref), (rk_out, ku_out, k_out, kg_ref)):
            scale = get_column(line[pl.ds(i, 1), :], HD)
            for h in range(heads):
                cols = slice(h * HD, (h + 1) * HD)
                unit = raw[at, cols] * scale
                raw[at, cols] = unit
                normed = unit * gain[:, cols]
                out[at, cols] = (normed * cosine + pltpu.roll(normed, HD // 2, 1) * sine).astype(jnp.bfloat16)
        return carry

    lax.fori_loop(0, 8, norm_rope, 0)

    def attend(zz):
        at = at_of(zz)
        low = jnp.maximum(zz - (WINDOW - 1), 0) * span
        keys_at = pl.ds(pl.multiple_of(low, span), WINDOW * span)
        key_place = low + lax.broadcasted_iota(jnp.int32, (span, WINDOW * span), 1)
        query_place = zz * span + lax.broadcasted_iota(jnp.int32, (span, WINDOW * span), 0)
        allowed = (key_place <= query_place) & (key_place >= first_ref[at, :])
        for h in range(heads):
            cols = slice(h * HD, (h + 1) * HD)
            scores = dot_nt(q_out[at, cols], k_out[keys_at, cols]) * HD**-0.5
            scores = jnp.where(allowed, scores, -1e30)
            top = jnp.max(scores, axis=1, keepdims=True)
            expo = jnp.exp(scores - top)
            probs = expo * (1.0 / jnp.sum(expo, axis=1, keepdims=True))
            mixed_out[at, cols] = jnp.dot(probs.astype(jnp.bfloat16), v_out[keys_at, cols], preferred_element_type=jnp.float32).astype(jnp.bfloat16)
        dt = 1024

        def out(j, carry):
            to = pl.ds(pl.multiple_of(j * dt, dt), dt)
            p = jnp.dot(mixed_out[at, :], wo_ref[:, to], preferred_element_type=jnp.float32)
            parts[pl.ds(2 * zz, 2), :, to] = p.astype(jnp.bfloat16).reshape(2, rows, dt)
            return carry

        lax.fori_loop(0, wide // dt, out, 0)

    attend(zs[3])
    rs.start_core(3)
    attend(zs[2])
    rs.start_core(2)
    rs.add_pair(3)
    rs.pass_on(3)
    attend(zs[1])
    rs.start_core(1)
    rs.add_pair(2)
    rs.pass_on(2)
    rs.add_pair(1)
    rs.pass_on(1)
    attend(zs[0])
    rs.start_core(0)
    rs.add_pair(0)
    xy.pass_on(2)
    xy.pass_on(1)
    rs.relay()
    xy.pass_on(3)
    for r in range(4):
        xy.last(r)
    rs.arrived()

    def ending(i, carry):
        at = pl.ds(pl.multiple_of(i * 32, 32), 32)
        br_ref[at, :] = rs.total(at)
        return carry

    lax.fori_loop(0, rows // 32, ending, 0)
    ag.finish()
    rs.finish()
    xy.finish()


def attention(x_own, w_query, w_key, w_value, w_out, q_gain, k_gain, cosine, sine, first):
    rows, wide = x_own.shape
    head_cols = w_query.shape[1]
    groups, world = 4, 8
    count = world * rows
    vmem = pl.BlockSpec(memory_space=pltpu.VMEM)
    anywhere = pl.BlockSpec(memory_space=pl.ANY)
    bf, f32 = jnp.bfloat16, jnp.float32
    dma = pltpu.SemaphoreType.DMA
    cols = jax.ShapeDtypeStruct((count, head_cols), bf)
    wide_cols = jax.ShapeDtypeStruct((count, head_cols), f32)
    line = jax.ShapeDtypeStruct((8, HD), f32)
    return pl.pallas_call(
        attn_kernel,
        out_shape=(
            jax.ShapeDtypeStruct((rows, wide), f32),
            cols, cols, cols, wide_cols, wide_cols, line, line, cols,
            jax.ShapeDtypeStruct((groups, world, rows, wide), bf),
        ),
        in_specs=[vmem] + [anywhere] * 4 + [vmem] * 5,
        out_specs=(vmem,) * 9 + (pl.BlockSpec(memory_space=pl.ANY),),
        scratch_shapes=[
            pltpu.VMEM((world, rows, wide), bf),
            pltpu.VMEM((world, rows, wide), bf),
            pltpu.VMEM((4, rows, wide), bf),
            pltpu.VMEM((4, rows, wide), bf),
            pltpu.VMEM((16, HD), f32),
            pltpu.VMEM((world, 16, HD), f32),
            pltpu.VMEM((wide, head_cols), bf),
            pltpu.VMEM((wide, head_cols), bf),
            pltpu.VMEM((wide, head_cols), bf),
            pltpu.VMEM((head_cols, wide), bf),
            dma((8,)), dma((8,)), dma((12,)), dma((12,)), dma((24,)), dma((24,)), dma((8,)), dma((8,)),
            pltpu.SemaphoreType.DMA, dma((4,)),
        ],
        compiler_params=pltpu.CompilerParams(
            collective_id=1, has_side_effects=True, vmem_limit_bytes=60 * 2**20
        ),
        name="attn",
    )(x_own, w_query, w_key, w_value, w_out, q_gain.reshape(1, -1), k_gain.reshape(1, -1), cosine, sine, first)


class Background:
    tokens, units = 512, 512

    def __init__(self, hall, gdall, gate_all, up_all, w_down, starts, outs, hbuf, gbuf, gate, up, tile, sums, mids, load_sem, tile_sem, start_sem, out_sem):
        self.hall, self.gdall, self.gate_all, self.up_all, self.w_down, self.starts, self.outs = hall, gdall, gate_all, up_all, w_down, starts, outs
        self.hbuf, self.gbuf, self.gate, self.up, self.tile, self.sums, self.mids = hbuf, gbuf, gate, up, tile, sums, mids
        self.load_sem, self.tile_sem, self.start_sem, self.out_sem = load_sem, tile_sem, start_sem, out_sem
        self.blocks = self.tokens // hall.shape[2]
        self.per_group = hall.shape[1] // self.blocks
        self.per_tile = 3 * self.per_group
        self.tile_count = w_down.shape[0] // self.units
        self.count = self.tile_count * self.per_tile

    def loads(self, n):
        slot, m = n % 2, n % self.per_tile
        group, part = 1 + m // self.per_group, m % self.per_group
        blocks = pl.ds(part * self.blocks, self.blocks)
        rows = pl.ds(part * self.tokens, self.tokens)
        units = pl.ds(n // self.per_tile * self.units, self.units)
        return (
            pltpu.make_async_copy(self.hall.at[group, blocks], self.hbuf.at[slot], self.load_sem.at[0, slot]),
            pltpu.make_async_copy(self.gdall.at[group, blocks], self.gbuf.at[slot], self.load_sem.at[1, slot]),
            pltpu.make_async_copy(self.gate_all.at[group - 1, rows, units], self.gate.at[slot], self.load_sem.at[2, slot]),
            pltpu.make_async_copy(self.up_all.at[group - 1, rows, units], self.up.at[slot], self.load_sem.at[3, slot]),
        )

    def tile_load(self, tile):
        return pltpu.make_async_copy(self.w_down.at[pl.ds(tile * self.units, self.units), :], self.tile, self.tile_sem)

    def moves(self, tile, refs, sem, inward):
        at = pl.ds(tile * self.units, self.units)
        g, u, d = refs
        pairs = zip(self.sums, (g.at[:, at], u.at[:, at], d.at[at, :]))
        return [
            pltpu.make_async_copy(far, near, sem.at[n]) if inward else pltpu.make_async_copy(near, far, sem.at[n])
            for n, (near, far) in enumerate(pairs)
        ]

    def stores(self, tile):
        return self.moves(tile, self.outs, self.out_sem, False)

    def sums_in(self, tile):
        return self.moves(tile, self.starts, self.start_sem, True)

    def begin(self):
        for copy in self.loads(0) + (self.tile_load(0),) + tuple(self.sums_in(0)):
            copy.start()

    def turn(self, tile):
        for copy in self.stores(tile):
            copy.wait()
        for copy in self.sums_in(tile + 1):
            copy.start()

    def step(self, n):
        slot, tile, m = n % 2, n // self.per_tile, n % self.per_tile
        if n + 1 < self.count:
            for copy in self.loads(n + 1):
                copy.start()
        if m == 0:
            self.tile_load(tile).wait()
            for copy in self.sums_in(tile):
                copy.wait()
        for copy in self.loads(n):
            copy.wait()
        hbuf, gbuf, gate, up = self.hbuf.at[slot], self.gbuf.at[slot], self.gate.at[slot], self.up.at[slot]
        wd = self.tile
        act, gg, gu = self.mids
        rows, wide = hbuf.shape[1:]
        half = self.tokens // 2

        def mid(i, carry):
            blocks = pl.ds(i * (self.blocks // 2), self.blocks // 2)
            at = pl.ds(pl.multiple_of(i * half, half), half)
            g, u = gate[at, :].astype(jnp.float32), up[at, :].astype(jnp.float32)
            ga = dot_nt(gbuf[blocks].reshape(half, wide), wd[...])
            s = jax.nn.sigmoid(g)
            gs = g * s
            act[at, :] = (gs * u).astype(jnp.bfloat16)
            gg[at, :] = (ga * u * s * (1.0 + g * (1.0 - s))).astype(jnp.bfloat16)
            gu[at, :] = (ga * gs).astype(jnp.bfloat16)
            return carry

        lax.fori_loop(0, 2, mid, 0)
        span = 512

        def into(i, carry):
            at = pl.ds(pl.multiple_of(i * span, span), span)
            h = hbuf[:, :, at].reshape(self.tokens, span)
            pg = dot_tn(h, gg[...])
            pu = dot_tn(h, gu[...])
            pd = dot_tn(act[...], gbuf[:, :, at].reshape(self.tokens, span))
            self.sums[0][at, :] += pg
            self.sums[1][at, :] += pu
            self.sums[2][:, at] += pd
            return carry

        lax.fori_loop(0, wide // span, into, 0)
        if m == self.per_tile - 1:
            for copy in self.stores(tile):
                copy.start()
            if tile + 1 < self.tile_count:
                self.tile_load(tile + 1).start()

    def finish(self):
        for copy in self.stores(self.tile_count - 1):
            copy.wait()


class SpreadColumns:
    def __init__(self, own, whole, send, recv, own_sem, place):
        self.src, self.whole, self.send, self.recv, self.own_sem = own, whole, send, recv, own_sem
        self.d, self.dx, self.dy, self.zs, self.c, _ = place
        self.t = 2 * self.zs[0] + self.c

    def own(self, p, k):
        return remote(self.src.at[p], self.whole.at[1 + k, p], self.send.at[k * 3 + p], self.recv.at[k * 3 + p], (self.dx, self.dy)[k], self.t)

    def hop(self, p, b):
        half = self.src.shape[1] // 2
        at = pl.ds(b * half, half)
        return remote(self.whole.at[1 + b, p, at], self.whole.at[3, p, at], self.send.at[6 + 2 * p + b], self.recv.at[6 + 2 * p + b], (self.dy, self.dx)[b], self.t)

    def start(self, p):
        self.own(p, 0).start()
        self.own(p, 1).start()

    def pass_on(self, p):
        for b in range(2):
            self.own(p, b).wait_recv()
            self.hop(p, b).start()

    def keep(self):
        return pltpu.make_async_copy(self.src, self.whole.at[0], self.own_sem)

    def finish(self):
        for p in range(3):
            for b in range(2):
                self.own(p, b).wait_send()
                self.hop(p, b).wait()
        self.keep().wait()


class SumHalves:
    def __init__(self, buf, once, twice, send, recv, place):
        self.buf, self.land, self.send, self.recv = buf, (once, twice), send, recv
        self.d, self.dx, self.dy, self.zs, self.c, _ = place
        self.t = 2 * self.zs[0] + self.c

    def move(self, stage, b):
        at = 2 * stage + b
        return remote(self.buf.at[b], self.land[stage].at[b], self.send.at[at], self.recv.at[at], (self.dx, self.dy)[(stage + b) % 2], self.t)

    def start(self, stage):
        for b in range(2):
            self.move(stage, b).start()

    def add(self, stage):
        for b in range(2):
            self.move(stage, b).wait()
            add_into(self.buf.at[b], self.land[stage].at[b])


class ExchangeGroups:
    def __init__(self, block, land, send, recv, place):
        self.block, self.land, self.send, self.recv = block, land, send, recv
        d, dx, dy, zs, c, _ = place
        self.peers, self.t = (dx, dy, 3 - d), 2 * zs[0] + c

    def copies(self):
        return [remote(self.block, self.land.at[k], self.send.at[k], self.recv.at[k], peer, self.t) for k, peer in enumerate(self.peers)]

    def start(self):
        for copy in self.copies():
            copy.start()

    def wait(self):
        for copy in self.copies():
            copy.wait()


def back_kernel(
    gb_ref, gh_ref, q_hbm, k_hbm, v_hbm, mixed_hbm, qu_hbm, ku_hbm, rq_ref, rk_ref, first_ref, cos_ref, sin_ref,
    qg_ref, kg_ref, wq_hbm, wk_hbm, wv_hbm, wo_hbm, gains_ref, hall, gdall, gate_all, up_all, w_down, own_g, own_u, own_d,
    gt_ref, gains_out, dwo_ref, gall_ref, dwg, dwu, dwd,
    full, pair, land, gm, dq, dk, dv, own, wo_once, wo_twice, stat, stats, gland, block, blocks, gacc,
    hbuf, gbuf, gbf, ubf, td, sg, su, sd, act, gg, gu,
    q_ref, k_ref, v_ref, mixed_ref, qu_ref, ku_ref, wq_ref, wk_ref, wv_ref, wo_ref,
    ag_send, ag_recv, rs_send, rs_recv, st_send, st_recv, ga_send, ga_recv, gr_send, gr_recv,
    co_send, co_recv, wo_send, wo_recv, own_sem, load_sem, tile_sem, start_sem, out_sem, input_sem,
):
    place = places_of()
    d, dx, dy, zs, c, inner = place
    t = 2 * zs[0] + c
    rows, wide = gb_ref.shape
    span = 2 * rows
    heads = wq_ref.shape[1] // HD
    count = q_ref.shape[0]
    scale = HD**-0.5
    inputs = Loads(
        (
            (wo_hbm, wo_ref), (mixed_hbm, mixed_ref), (q_hbm, q_ref), (k_hbm, k_ref), (v_hbm, v_ref), (qu_hbm, qu_ref), (ku_hbm, ku_ref),
            (wq_hbm, wq_ref), (wk_hbm, wk_ref), (wv_hbm, wv_ref),
        ),
        input_sem,
    )
    full[t] = gb_ref[...]
    barrier = pltpu.get_barrier_semaphore()
    peers = [(d, 2 * zs[r] + c) for r in (1, 2, 3)] + [(d, 2 * zs[r] + 1 - c) for r in range(4)]
    peers += [(dx, t), (dy, t), (3 - d, t)]
    for peer in peers:
        pl.semaphore_signal(barrier, inc=1, device_id=peer, device_id_type=MESH)
    pl.semaphore_wait(barrier, len(peers))
    ag = Gather(full, ag_send, ag_recv, place)
    rs = Scatter(full, pair, land, rs_send, rs_recv, place)
    ex = Exchange(stat, stats, st_send, st_recv, place)
    gains = Exchange(gains_ref, gland, ga_send, ga_recv, place)
    groups = ExchangeGroups(block, blocks, gr_send, gr_recv, place)
    cols_all = SpreadColumns(own, gall_ref, co_send, co_recv, own_sem, place)
    wo_sum = SumHalves(dwo_ref, wo_once, wo_twice, wo_send, wo_recv, place)
    work = Background(
        hall, gdall, gate_all, up_all, w_down, (own_g, own_u, own_d), (dwg, dwu, dwd), hbuf, gbuf, gbf, ubf, td, (sg, su, sd), (act, gg, gu),
        load_sem, tile_sem, start_sem, out_sem,
    )

    def at_of(zz):
        return pl.ds(pl.multiple_of(zz * span, span), span)

    ag.start()
    gains.start()
    work.begin()
    inputs.start()
    work.step(0)
    work.step(1)
    ag.ready(0)
    ag.start_inner()
    ag.arrive(2)
    ag.arrive(1)
    work.step(2)
    work.step(3)
    ag.ready(2)
    ag.ready(1)
    ag.arrive(3)
    work.step(4)
    work.step(5)
    ag.ready(3)

    inputs.wait(*range(10))

    def mixed_back(zz, carry):
        part = full[pl.ds(2 * zz, 2)].reshape(span, wide)
        gm[at_of(zz), :] = dot_nt(part, wo_ref[...]).astype(jnp.bfloat16)
        return carry

    lax.fori_loop(0, 4, mixed_back, 0)

    def out_back(j, carry):
        to = pl.ds(pl.multiple_of(j * 512, 512), 512)
        p = dot_tn(mixed_ref[...], full[:, :, to].reshape(count, 512))
        dwo_ref[:, :, to] = p.astype(jnp.bfloat16).reshape(2, p.shape[0] // 2, 512)
        return carry

    lax.fori_loop(0, wide // 512, out_back, 0)
    wo_sum.start(0)
    ag.finish()
    dk[...] = jnp.zeros_like(dk)
    dv[...] = jnp.zeros_like(dv)

    def attend_back(zz, carry):
        at = at_of(zz)
        low = jnp.maximum(zz - (WINDOW - 1), 0) * span
        keys_at = pl.ds(pl.multiple_of(low, span), WINDOW * span)
        key_place = low + lax.broadcasted_iota(jnp.int32, (span, WINDOW * span), 1)
        query_place = zz * span + lax.broadcasted_iota(jnp.int32, (span, WINDOW * span), 0)
        allowed = (key_place <= query_place) & (key_place >= first_ref[at, :])
        for h in range(heads):
            cols = slice(h * HD, (h + 1) * HD)
            scores = dot_nt(q_ref[at, cols], k_ref[keys_at, cols]) * scale
            scores = jnp.where(allowed, scores, -1e30)
            top = jnp.max(scores, axis=1, keepdims=True)
            expo = jnp.exp(scores - top)
            probs = expo * (1.0 / jnp.sum(expo, axis=1, keepdims=True))
            grad = gm[at, cols]
            gp = dot_nt(grad, v_ref[keys_at, cols])
            gs = (probs * (gp - jnp.sum(probs * gp, axis=1, keepdims=True))).astype(jnp.bfloat16)
            dq[at, cols] = jnp.dot(gs, k_ref[keys_at, cols], preferred_element_type=jnp.float32) * scale
            dk[keys_at, cols] += dot_tn(gs, q_ref[at, cols]) * scale
            dv[keys_at, cols] += dot_tn(probs.astype(jnp.bfloat16), grad)
        return carry

    lax.fori_loop(0, 2, attend_back, 0)
    wo_sum.add(0)
    wo_sum.start(1)
    work.turn(0)
    lax.fori_loop(2, 4, attend_back, 0)
    own[2] = dv[...].astype(jnp.bfloat16)
    cols_all.start(2)
    gacc[...] = jnp.zeros_like(gacc)

    def unrope(i, carry):
        at = pl.ds(pl.multiple_of(i * HD, HD), HD)
        cosine, sine = cos_ref[at, :], sin_ref[at, :]
        for n, (grad, unit_ref, gain) in enumerate(((dq, qu_ref, qg_ref), (dk, ku_ref, kg_ref))):
            total = jnp.zeros((HD, HD), jnp.float32)
            for h in range(heads):
                cols = slice(h * HD, (h + 1) * HD)
                value = grad[at, cols].astype(jnp.bfloat16).astype(jnp.float32)
                value = value * cosine - pltpu.roll(value, HD // 2, 1) * sine
                unit = unit_ref[at, cols]
                row = n * heads + h
                gacc[row : row + 1, :] += jnp.sum(value * unit, axis=0, keepdims=True)
                value = value * gain[:, cols]
                grad[at, cols] = value
                total = total + value * unit
            stat[pl.ds(8 * n + i, 1), :] = jnp.sum(total.T, axis=0, keepdims=True)
        return carry

    lax.fori_loop(0, count // HD, unrope, 0)
    ex.start()
    gains.wait()
    total = gains_ref[...]
    for r in range(4):
        for k in range(2):
            if r or k:
                total = total + gland[2 * zs[r] + (c if k == 0 else 1 - c)]
    lines = gains_ref.shape[0]
    block[:lines, :] = total
    block[lines:, :] = gacc[...]
    groups.start()
    work.step(6)
    ex.wait()
    total = stat[...]
    for r in range(4):
        for k in range(2):
            if r or k:
                total = total + stats[2 * zs[r] + (c if k == 0 else 1 - c)]
    stat[...] = total * (1.0 / (8 * wq_ref.shape[1]))

    def norm_back_rows(i, carry):
        at = pl.ds(pl.multiple_of(i * HD, HD), HD)
        for n, (grad, unit_ref, inv_ref) in enumerate(((dq, qu_ref, rq_ref), (dk, ku_ref, rk_ref))):
            mean = get_column(stat[pl.ds(8 * n + i, 1), :], HD)
            inverse = get_column(inv_ref[pl.ds(i, 1), :], HD)
            for h in range(heads):
                cols = slice(h * HD, (h + 1) * HD)
                own[n, at, cols] = (inverse * (grad[at, cols] - unit_ref[at, cols] * mean)).astype(jnp.bfloat16)
        return carry

    lax.fori_loop(0, count // HD, norm_back_rows, 0)
    cols_all.start(0)
    cols_all.start(1)
    cols_all.keep().start()

    def tokens_back(zz):
        at = at_of(zz)
        dt = 1024

        def out(j, carry):
            to = pl.ds(pl.multiple_of(j * dt, dt), dt)
            p = dot_nt(own[0, at, :], wq_ref[to, :]) + dot_nt(own[1, at, :], wk_ref[to, :]) + dot_nt(own[2, at, :], wv_ref[to, :])
            full[pl.ds(2 * zz, 2), :, to] = p.astype(jnp.bfloat16).reshape(2, rows, dt)
            return carry

        lax.fori_loop(0, wide // dt, out, 0)

    tokens_back(zs[3])
    rs.start_core(3)
    tokens_back(zs[2])
    rs.start_core(2)
    rs.add_pair(3)
    rs.pass_on(3)
    tokens_back(zs[1])
    rs.start_core(1)
    rs.add_pair(2)
    rs.pass_on(2)
    rs.add_pair(1)
    rs.pass_on(1)
    tokens_back(zs[0])
    rs.start_core(0)
    rs.add_pair(0)
    cols_all.pass_on(2)
    wo_sum.add(1)
    work.step(7)
    rs.relay()
    work.step(8)
    work.step(9)
    cols_all.pass_on(0)
    cols_all.pass_on(1)
    work.step(10)
    work.step(11)
    rs.arrived()

    def ending(i, carry):
        at = pl.ds(pl.multiple_of(i * 32, 32), 32)
        gt_ref[at, :] = gh_ref[at, :] + rs.total(at)
        return carry

    lax.fori_loop(0, rows // 32, ending, 0)
    groups.wait()
    gains_out[...] = block[...] + blocks[0] + blocks[1] + blocks[2]
    rs.finish()
    cols_all.finish()
    work.finish()


def backward(grad_branch, grad_hidden, kept, first, cosine, signed, q_gain, k_gain, weights, gains, h_all, gd_all, gate_all, up_all, w_down, own_parts):
    queries, keys, values, mixed, q_unit, k_unit, q_inverse, k_inverse = kept
    rows, wide = grad_branch.shape
    count, head_cols = queries.shape
    heads = head_cols // HD
    world = 8
    width = w_down.shape[0]
    lines = gains.shape[0]
    vmem = pl.BlockSpec(memory_space=pltpu.VMEM)
    anywhere = pl.BlockSpec(memory_space=pl.ANY)
    bf, f32 = jnp.bfloat16, jnp.float32
    dma = pltpu.SemaphoreType.DMA
    tok, unit = Background.tokens, Background.units
    return pl.pallas_call(
        back_kernel,
        out_shape=(
            jax.ShapeDtypeStruct((rows, wide), f32),
            jax.ShapeDtypeStruct((lines + 8, HD), f32),
            jax.ShapeDtypeStruct((2, head_cols // 2, wide), bf),
            jax.ShapeDtypeStruct((4, 3, count, head_cols), bf),
            jax.ShapeDtypeStruct((wide, width), f32),
            jax.ShapeDtypeStruct((wide, width), f32),
            jax.ShapeDtypeStruct((width, wide), f32),
        ),
        in_specs=[vmem] * 2 + [anywhere] * 6 + [vmem] * 7 + [anywhere] * 4 + [vmem] + [anywhere] * 8,
        out_specs=(vmem, vmem, vmem) + (anywhere,) * 4,
        scratch_shapes=[
            pltpu.VMEM((world, rows, wide), bf),
            pltpu.VMEM((4, rows, wide), bf),
            pltpu.VMEM((4, rows, wide), bf),
            pltpu.VMEM((count, head_cols), bf),
            pltpu.VMEM((count, head_cols), f32),
            pltpu.VMEM((count, head_cols), f32),
            pltpu.VMEM((count, head_cols), f32),
            pltpu.VMEM((3, count, head_cols), bf),
            pltpu.VMEM((2, head_cols // 2, wide), bf),
            pltpu.VMEM((2, head_cols // 2, wide), bf),
            pltpu.VMEM((16, HD), f32),
            pltpu.VMEM((world, 16, HD), f32),
            pltpu.VMEM((world, lines, HD), f32),
            pltpu.VMEM((lines + 8, HD), f32),
            pltpu.VMEM((3, lines + 8, HD), f32),
            pltpu.VMEM((8, HD), f32),
            pltpu.VMEM((2, tok // rows, rows, wide), bf),
            pltpu.VMEM((2, tok // rows, rows, wide), bf),
            pltpu.VMEM((2, tok, unit), bf),
            pltpu.VMEM((2, tok, unit), bf),
            pltpu.VMEM((unit, wide), bf),
            pltpu.VMEM((wide, unit), f32),
            pltpu.VMEM((wide, unit), f32),
            pltpu.VMEM((unit, wide), f32),
            pltpu.VMEM((tok, unit), bf),
            pltpu.VMEM((tok, unit), bf),
            pltpu.VMEM((tok, unit), bf),
            pltpu.VMEM((count, head_cols), bf),
            pltpu.VMEM((count, head_cols), bf),
            pltpu.VMEM((count, head_cols), bf),
            pltpu.VMEM((count, head_cols), bf),
            pltpu.VMEM((count, head_cols), f32),
            pltpu.VMEM((count, head_cols), f32),
            pltpu.VMEM((wide, head_cols), bf),
            pltpu.VMEM((wide, head_cols), bf),
            pltpu.VMEM((wide, head_cols), bf),
            pltpu.VMEM((head_cols, wide), bf),
            dma((8,)), dma((8,)), dma((12,)), dma((12,)), dma((8,)), dma((8,)), dma((8,)), dma((8,)), dma((3,)), dma((3,)),
            dma((12,)), dma((12,)), dma((4,)), dma((4,)), pltpu.SemaphoreType.DMA, dma((4, 2)), pltpu.SemaphoreType.DMA, dma((3,)), dma((3,)), dma((10,)),
        ],
        compiler_params=pltpu.CompilerParams(
            collective_id=3, has_side_effects=True, vmem_limit_bytes=62 * 2**20
        ),
        name="back",
    )(
        grad_branch, grad_hidden, queries, keys, values, mixed, q_unit, k_unit, q_inverse, k_inverse, first, cosine, signed,
        q_gain.reshape(1, -1), k_gain.reshape(1, -1), *weights, gains, h_all, gd_all, gate_all, up_all, w_down, *own_parts,
    )


def tail_kernel(
    pg_ref, pu_ref, pd_ref, x_ref, g_ref, wo_ref, gains_ref, og_ref, ou_ref, od_ref, oq_ref, ok_ref, ov_ref, oo_ref, *gain_refs
):
    count, cols = g_ref.shape[2], x_ref.shape[-1]
    og_ref[...] = pg_ref[...]
    ou_ref[...] = pu_ref[...]
    od_ref[...] = pd_ref[...]
    oo_ref[...] = wo_ref[...].reshape(oo_ref.shape).astype(jnp.float32)
    row = 0
    for out in gain_refs:
        out[...] = gains_ref[row : row + out.shape[0], :]
        row += out.shape[0]
    for p, out in enumerate((oq_ref, ok_ref, ov_ref)):
        total = jnp.zeros(out.shape, jnp.float32)
        for g in range(4):
            total = total + dot_tn(x_ref[g].reshape(count, cols), g_ref[g, p])
        out[...] = total


def weight_tail(parts, x_all, grad_qkv, grad_out, gains):
    groups, world, rows, wide = x_all.shape
    count, width = world * rows, parts[0].shape[1]
    head_cols = grad_qkv.shape[-1]
    cols = 256
    f32 = jnp.float32
    down = pl.BlockSpec((cols, width), lambda i: (i, 0))
    across = pl.BlockSpec((width, cols), lambda i: (0, i))
    heads = pl.BlockSpec((cols, head_cols), lambda i: (i, 0))
    lines = [(wide // HD, HD)] * 2 + [(head_cols // HD, HD)] * 2
    return pl.pallas_call(
        tail_kernel,
        grid=(wide // cols,),
        in_specs=[
            down, down, across,
            pl.BlockSpec((groups, world, rows, cols), lambda i: (0, 0, 0, i)),
            pl.BlockSpec(grad_qkv.shape, lambda i: (0, 0, 0, 0)),
            pl.BlockSpec((2, head_cols // 2, cols), lambda i: (0, 0, i)),
            pl.BlockSpec(gains.shape, lambda i: (0, 0)),
        ],
        out_specs=(down, down, across, heads, heads, heads, pl.BlockSpec((head_cols, cols), lambda i: (0, i)))
        + tuple(pl.BlockSpec(shape, lambda i: (0, 0)) for shape in lines),
        out_shape=(
            jax.ShapeDtypeStruct((wide, width), f32),
            jax.ShapeDtypeStruct((wide, width), f32),
            jax.ShapeDtypeStruct((width, wide), f32),
        )
        + (jax.ShapeDtypeStruct((wide, head_cols), f32),) * 3
        + (jax.ShapeDtypeStruct((head_cols, wide), f32),)
        + tuple(jax.ShapeDtypeStruct(shape, f32) for shape in lines),
        compiler_params=pltpu.CompilerParams(vmem_limit_bytes=60 * 2**20),
        cost_estimate=pl.CostEstimate(
            flops=2 * count * wide * 3 * groups * head_cols, bytes_accessed=100 * 2**20, transcendentals=0
        ),
        name="tail",
    )(*parts, x_all, grad_qkv, grad_out, gains)


def on_device_fused(
    tokens,
    segment_ids,
    w_query,
    w_key,
    w_value,
    w_out,
    w_gate,
    w_up,
    w_down,
    q_gain,
    k_gain,
    attn_gain,
    ffn_gain,
    cotangent,
):
    wide = tokens.shape[1]
    token_count = segment_ids.shape[0] * segment_ids.shape[1]
    head_cols = w_query.shape[1]
    positions = positions_of(segment_ids).reshape(token_count)
    cosine, sine = rotary_tables(positions)
    first = (jnp.arange(token_count, dtype=jnp.int32) - positions)[:, None]
    signed = jnp.where(jnp.arange(HD) < HD // 2, -sine, sine)
    branch, queries, keys, values, q_unit, k_unit, q_inverse, k_inverse, mixed, x_all = attention(
        tokens, w_query, w_key, w_value, w_out, q_gain, k_gain, cosine, signed, first
    )
    block_out, grad_hidden, grad_branch, gains, h_all, gd_all, own_gate, own_up, own_down, gate_all, up_all = ffn(
        tokens, branch, cotangent, attn_gain, ffn_gain, w_gate, w_up, w_down
    )
    grad_tokens, gains, grad_w_out, grad_qkv, part_gate, part_up, part_down = backward(
        grad_branch, grad_hidden, (queries, keys, values, mixed, q_unit, k_unit, q_inverse, k_inverse),
        first, cosine, signed, q_gain, k_gain, (w_query, w_key, w_value, w_out), gains, h_all, gd_all, gate_all, up_all, w_down,
        (own_gate, own_up, own_down),
    )
    *grad_weights, grad_ffn_gain, grad_attn_gain, grad_q_gain, grad_k_gain = weight_tail(
        (part_gate, part_up, part_down), x_all, grad_qkv, grad_w_out, gains
    )
    grad_w_gate, grad_w_up, grad_w_down, grad_w_query, grad_w_key, grad_w_value, grad_w_out = grad_weights
    return (
        block_out,
        grad_tokens,
        grad_w_query,
        grad_w_key,
        grad_w_value,
        grad_w_out,
        grad_w_gate,
        grad_w_up,
        grad_w_down,
        grad_q_gain.reshape(head_cols),
        grad_k_gain.reshape(head_cols),
        grad_attn_gain.reshape(wide),
        grad_ffn_gain.reshape(wide),
    )


def solution(mesh):
    placed = (
        P(("dp", "tensor"), None),
        P("dp", None),
        P(None, "tensor"),
        P(None, "tensor"),
        P(None, "tensor"),
        P("tensor", None),
        P(None, "tensor"),
        P(None, "tensor"),
        P("tensor", None),
        P("tensor"),
        P("tensor"),
        P(),
        P(),
        P(("dp", "tensor"), None),
    )
    return jax.shard_map(
        on_device_fused if dict(mesh.shape) == {"dp": 4, "tensor": 8} else on_device,
        mesh=mesh,
        in_specs=placed,
        out_specs=(
            P(("dp", "tensor"), None),
            P(("dp", "tensor"), None),
            P(None, "tensor"),
            P(None, "tensor"),
            P(None, "tensor"),
            P("tensor", None),
            P(None, "tensor"),
            P(None, "tensor"),
            P("tensor", None),
            P("tensor"),
            P("tensor"),
            P(),
            P(),
        ),
        check_vma=False,
    )
```

```python
import jax
import jax.numpy as jnp
from jax import lax
from jax.experimental import pallas as pl
from jax.experimental.pallas import tpu as pltpu
from jax.sharding import PartitionSpec as P

HD = 128


EPS = 1e-06
THETA = 500000.0


def rounded(value):
    return lax.optimization_barrier(value.astype(jnp.bfloat16)).astype(jnp.float32)


def dot_last(left, right):
    return lax.dot_general(
        left, right, (((1,), (1,)), ((), ())), preferred_element_type=jnp.float32
    )


def dot_first(left, right):
    return lax.dot_general(
        left, right, (((0,), (0,)), ((), ())), preferred_element_type=jnp.float32
    )


def positions_of(segment_ids):
    length = segment_ids.shape[-1]
    places = jnp.arange(length, dtype=jnp.int32)
    below = (segment_ids[:, None, :] < segment_ids[:, :, None]).astype(jnp.int32)
    return places[None, :] - jnp.sum(below, axis=2)


def rotary_tables(positions):
    half = HD // 2
    freq = THETA ** (-(jnp.arange(half, dtype=jnp.float32) * 2.0 / HD))
    angle = positions.astype(jnp.float32)[:, None] * freq[None, :]
    cosine = jnp.concatenate([jnp.cos(angle), jnp.cos(angle)], axis=1)
    sine = jnp.concatenate([jnp.sin(angle), jnp.sin(angle)], axis=1)
    return (cosine, sine)


def rotate(value, cosine, sine):
    half = value.shape[-1] // 2
    turned = jnp.concatenate([-value[..., half:], value[..., :half]], axis=-1)
    return value * cosine[:, None, :] + turned * sine[:, None, :]


def rotate_back(grad, cosine, sine):
    half = grad.shape[-1] // 2
    scaled = grad * sine[:, None, :]
    unturned = jnp.concatenate([scaled[..., half:], -scaled[..., :half]], axis=-1)
    return grad * cosine[:, None, :] + unturned


def norm_back(grad_out, unit, inverse, gain):
    inner = grad_out * gain
    return inverse * (inner - unit * jnp.mean(inner * unit, axis=1, keepdims=True))


def on_device(
    tokens,
    segment_ids,
    w_query,
    w_key,
    w_value,
    w_out,
    w_gate,
    w_up,
    w_down,
    q_gain,
    k_gain,
    attn_gain,
    ffn_gain,
    cotangent,
):
    row_count, full_width = tokens.shape
    head_cols = w_query.shape[1]
    heads_here = head_cols // HD
    ff_cols = w_gate.shape[1]
    seqs_here, seq_len = segment_ids.shape
    token_count = seqs_here * seq_len
    att_scale = HD ** (-0.5)
    whole_x = lax.all_gather(tokens, "tensor", axis=0, tiled=True)
    w_qkv = jnp.concatenate([w_query, w_key, w_value], axis=1)
    projected = jnp.dot(whole_x, w_qkv, preferred_element_type=jnp.float32)
    q_raw = projected[:, :head_cols]
    k_raw = projected[:, head_cols : 2 * head_cols]
    values = projected[:, 2 * head_cols :].astype(jnp.bfloat16)
    q_total, k_total = lax.psum(
        (jnp.sum(q_raw * q_raw, axis=1), jnp.sum(k_raw * k_raw, axis=1)), "tensor"
    )
    q_inverse = lax.rsqrt(q_total / full_width + EPS)[:, None]
    k_inverse = lax.rsqrt(k_total / full_width + EPS)[:, None]
    q_unit = q_raw * q_inverse
    k_unit = k_raw * k_inverse
    cosine, sine = rotary_tables(positions_of(segment_ids).reshape(token_count))
    queries = rotate((q_unit * q_gain).reshape(token_count, heads_here, HD), cosine, sine).astype(
        jnp.bfloat16
    )
    keys = rotate((k_unit * k_gain).reshape(token_count, heads_here, HD), cosine, sine).astype(
        jnp.bfloat16
    )
    shaped = (seqs_here, seq_len, heads_here, HD)
    query_seqs = queries.reshape(shaped)
    key_seqs = keys.reshape(shaped)
    value_seqs = values.reshape(shaped)
    places = jnp.arange(seq_len, dtype=jnp.int32)
    causal = places[:, None] >= places[None, :]

    def scores_of(query_block, key_block, seg_row):
        raw = (
            jnp.einsum("qhd,khd->hqk", query_block, key_block, preferred_element_type=jnp.float32)
            * att_scale
        )
        allowed = causal & (seg_row[:, None] == seg_row[None, :])
        return jnp.where(allowed[None], raw, -1e30)

    def attend(pieces):
        query_block, key_block, value_block, seg_row = pieces
        scores = scores_of(query_block, key_block, seg_row)
        top = jnp.max(scores, axis=-1, keepdims=True)
        expo = jnp.exp(scores - top)
        total = jnp.sum(expo, axis=-1, keepdims=True)
        probs = (expo / total).astype(jnp.bfloat16)
        mixed_block = jnp.einsum(
            "hqk,khd->qhd", probs, value_block, preferred_element_type=jnp.float32
        )
        return (mixed_block.astype(jnp.bfloat16), (top + jnp.log(total))[..., 0])

    mixed, log_total = lax.map(attend, (query_seqs, key_seqs, value_seqs, segment_ids))
    mixed = mixed.reshape(token_count, head_cols)
    x_rows = tokens.astype(jnp.float32)
    branch = lax.psum_scatter(
        jnp.dot(mixed, w_out, preferred_element_type=jnp.float32).astype(jnp.bfloat16),
        "tensor",
        scatter_dimension=0,
        tiled=True,
    ).astype(jnp.float32)
    a_inverse = lax.rsqrt(jnp.mean(branch * branch, axis=1, keepdims=True) + EPS)
    hidden = x_rows + branch * a_inverse * attn_gain
    h_low = lax.all_gather(hidden.astype(jnp.bfloat16), "tensor", axis=0, tiled=True)
    a_unit = branch * a_inverse
    w_gate_up = jnp.concatenate([w_gate, w_up], axis=1)
    gate_up = jnp.dot(h_low, w_gate_up, preferred_element_type=jnp.float32)
    gate = gate_up[:, :ff_cols]
    up = gate_up[:, ff_cols:]
    sigma_gate = jax.nn.sigmoid(gate)
    silu_gate = gate * sigma_gate
    act = (silu_gate * up).astype(jnp.bfloat16)
    down = lax.psum_scatter(
        jnp.dot(act, w_down, preferred_element_type=jnp.float32).astype(jnp.bfloat16),
        "tensor",
        scatter_dimension=0,
        tiled=True,
    ).astype(jnp.float32)
    f_inverse = lax.rsqrt(jnp.mean(down * down, axis=1, keepdims=True) + EPS)
    f_unit = down * f_inverse
    block_out = (hidden + f_unit * ffn_gain).astype(jnp.bfloat16)
    grad_out = cotangent.astype(jnp.float32)
    grad_ffn_part = jnp.sum(grad_out * f_unit, axis=0)
    grad_down = norm_back(grad_out, f_unit, f_inverse, ffn_gain).astype(jnp.bfloat16)
    grad_down_all = lax.all_gather(grad_down, "tensor", axis=0, tiled=True)
    grad_act = dot_last(grad_down_all, w_down)
    grad_w_down = dot_first(act, grad_down_all)
    grad_gate = grad_act * up * sigma_gate * (1.0 + gate * (1.0 - sigma_gate))
    grad_up = grad_act * silu_gate
    grad_gate_up = jnp.concatenate([grad_gate, grad_up], axis=1).astype(jnp.bfloat16)
    grad_w_gate_up = dot_first(h_low, grad_gate_up)
    grad_hidden = grad_out + lax.psum_scatter(
        dot_last(grad_gate_up, w_gate_up).astype(jnp.bfloat16), "tensor", scatter_dimension=0, tiled=True
    ).astype(jnp.float32)
    grad_attn_part = jnp.sum(grad_hidden * a_unit, axis=0)
    grad_branch = norm_back(grad_hidden, a_unit, a_inverse, attn_gain).astype(jnp.bfloat16)
    grad_branch_all = lax.all_gather(grad_branch, "tensor", axis=0, tiled=True)
    grad_w_out = dot_first(mixed, grad_branch_all)
    grad_mixed = dot_last(grad_branch_all, w_out).astype(jnp.bfloat16).reshape(shaped)

    def attend_back(pieces):
        query_block, key_block, value_block, seg_row, log_block, grad_block = pieces
        scores = scores_of(query_block, key_block, seg_row)
        probs = jnp.exp(scores - log_block[..., None])
        grad_probs = jnp.einsum(
            "qhd,khd->hqk", grad_block, value_block, preferred_element_type=jnp.float32
        )
        grad_scores = (
            probs * (grad_probs - jnp.sum(probs * grad_probs, axis=-1, keepdims=True))
        ).astype(jnp.bfloat16)
        grad_query = (
            jnp.einsum("hqk,khd->qhd", grad_scores, key_block, preferred_element_type=jnp.float32)
            * att_scale
        )
        grad_key = (
            jnp.einsum("hqk,qhd->khd", grad_scores, query_block, preferred_element_type=jnp.float32)
            * att_scale
        )
        grad_value = jnp.einsum(
            "hqk,qhd->khd",
            probs.astype(jnp.bfloat16),
            grad_block,
            preferred_element_type=jnp.float32,
        )
        return (grad_query, grad_key, grad_value.astype(jnp.bfloat16))

    grad_query, grad_key, grad_value = lax.map(
        attend_back, (query_seqs, key_seqs, value_seqs, segment_ids, log_total, grad_mixed)
    )
    grad_q_normed = rotate_back(
        rounded(grad_query.reshape(token_count, heads_here, HD)), cosine, sine
    ).reshape(token_count, head_cols)
    grad_k_normed = rotate_back(
        rounded(grad_key.reshape(token_count, heads_here, HD)), cosine, sine
    ).reshape(token_count, head_cols)
    grad_q_gain = jnp.sum(grad_q_normed * q_unit, axis=0)
    grad_k_gain = jnp.sum(grad_k_normed * k_unit, axis=0)
    inner_q = grad_q_normed * q_gain
    inner_k = grad_k_normed * k_gain
    q_inner_sum, k_inner_sum = lax.psum(
        (jnp.sum(inner_q * q_unit, axis=1), jnp.sum(inner_k * k_unit, axis=1)), "tensor"
    )
    grad_q_raw = q_inverse * (inner_q - q_unit * (q_inner_sum / full_width)[:, None])
    grad_k_raw = k_inverse * (inner_k - k_unit * (k_inner_sum / full_width)[:, None])
    grad_qkv = jnp.concatenate(
        [
            grad_q_raw.astype(jnp.bfloat16),
            grad_k_raw.astype(jnp.bfloat16),
            grad_value.reshape(token_count, head_cols),
        ],
        axis=1,
    )
    grad_w_qkv = dot_first(whole_x, grad_qkv)
    grad_tokens = grad_hidden + lax.psum_scatter(
        dot_last(grad_qkv, w_qkv).astype(jnp.bfloat16), "tensor", scatter_dimension=0, tiled=True
    ).astype(jnp.float32)
    grad_w_qkv, grad_w_out, grad_w_gate_up, grad_w_down = [
        lax.psum(part.astype(jnp.bfloat16), "dp").astype(jnp.float32)
        for part in (grad_w_qkv, grad_w_out, grad_w_gate_up, grad_w_down)
    ]
    grad_q_gain, grad_k_gain = lax.psum((grad_q_gain, grad_k_gain), "dp")
    grad_attn_gain, grad_ffn_gain = lax.psum((grad_attn_part, grad_ffn_part), ("dp", "tensor"))
    return (
        block_out,
        grad_tokens,
        grad_w_qkv[:, :head_cols],
        grad_w_qkv[:, head_cols : 2 * head_cols],
        grad_w_qkv[:, 2 * head_cols :],
        grad_w_out,
        grad_w_gate_up[:, :ff_cols],
        grad_w_gate_up[:, ff_cols:],
        grad_w_down,
        grad_q_gain,
        grad_k_gain,
        grad_attn_gain,
        grad_ffn_gain,
    )


MESH = pl.DeviceIdType.MESH
LANES = 2


def places_of():
    d = lax.axis_index("dp")
    t = lax.axis_index("tensor")
    z, c = lax.div(t, 2), lax.rem(t, 2)
    dx = d + 1 - 2 * lax.rem(d, 2)
    dy = lax.rem(d + 2, 4)
    zs = (z, z + 1 - 2 * lax.rem(z, 2), lax.rem(z + 2, 4), 3 - z)
    inner = lax.rem(z + 1, 4) >= 2
    return d, dx, dy, zs, c, inner


def remote(src, dst, send, recv, dp, tensor):
    return pltpu.make_async_remote_copy(
        src_ref=src, dst_ref=dst, send_sem=send, recv_sem=recv, device_id=(dp, tensor), device_id_type=MESH
    )


def enter(d, zs, c, dx=None, dy=None):
    barrier = pltpu.get_barrier_semaphore()
    peers = [(d, 2 * zs[r] + c) for r in (1, 2, 3)] + [(d, 2 * zs[0] + 1 - c)]
    if dx is not None:
        peers += [(dx, 2 * zs[0] + c), (dy, 2 * zs[0] + c)]
    for peer in peers:
        pl.semaphore_signal(barrier, inc=1, device_id=peer, device_id_type=MESH)
    pl.semaphore_wait(barrier, len(peers))


class Gather:
    def __init__(self, full, send, recv, place):
        self.full, self.send, self.recv = full, send, recv
        self.d, _, _, self.zs, self.c, self.inner = place
        self.t = 2 * self.zs[0] + self.c

    def lane(self, r):
        return self.full.at[2 * self.zs[r] + self.c]

    def other(self, r):
        return self.full.at[2 * self.zs[r] + 1 - self.c]

    def to_z(self, r, k, via):
        return remote(self.lane(r), self.lane(r), self.send.at[via if r == 0 else 7], self.recv.at[k], self.d, 2 * self.zs[via] + self.c)

    def to_core(self, r):
        return remote(self.lane(r), self.lane(r), self.send.at[0 if r == 0 else 3 + r], self.recv.at[4 + r], self.d, 2 * self.zs[0] + 1 - self.c)

    def start(self):
        self.to_z(0, 2, 2).start()
        self.to_z(0, 1, 1).start()
        self.to_core(0).start()

    def start_inner(self):
        @pl.when(self.inner)
        def _():
            self.to_z(0, 2, 2).wait_send()
            self.to_z(0, 3, 3).start()

    def arrive(self, r):
        self.to_z(r, r, r).wait_recv()
        if r == 2:
            @pl.when(self.inner)
            def _():
                self.to_z(2, 3, 1).start()
        self.to_core(r).start()

    def ready(self, r):
        remote(self.other(r), self.other(r), self.send.at[0], self.recv.at[4 + r], self.d, self.t).wait_recv()

    def finish(self):
        @pl.when(jnp.logical_not(self.inner))
        def _():
            self.to_z(0, 2, 2).wait_send()

        @pl.when(self.inner)
        def _():
            self.to_z(0, 3, 3).wait_send()
            self.to_z(2, 3, 1).wait_send()

        self.to_z(0, 1, 1).wait_send()
        for r in range(4):
            self.to_core(r).wait_send()


class Scatter:
    def __init__(self, parts, pair, land, send, recv, place):
        self.parts, self.pair, self.land, self.send, self.recv = parts, pair, land, send, recv
        self.d, _, _, self.zs, self.c, self.inner = place
        self.t = 2 * self.zs[0] + self.c
        self.half = parts.shape[2] // 2

    def cut(self, ref, at, r, h):
        if h is None:
            return ref.at[at]
        return ref.at[at, :, pl.ds(h * self.half, self.half)]

    def mine(self, r, h=None):
        return self.cut(self.parts, 2 * self.zs[r] + self.c, r, h)

    def to_core(self, r, h=None):
        src = self.cut(self.parts, 2 * self.zs[r] + 1 - self.c, r, h)
        at = 8 if h == 1 else r
        return remote(src, self.cut(self.pair, r, r, h), self.send.at[at], self.recv.at[at], self.d, 2 * self.zs[0] + 1 - self.c)

    def start_core(self, r):
        for h in (0, 1) if r == 3 else (None,):
            self.to_core(r, h).start()

    def to_z(self, r, k, via, h=None):
        return remote(
            self.mine(r, h), self.cut(self.land, k, r, h), self.send.at[SENT[r, h]], self.recv.at[LANDED[k, h]], self.d,
            2 * self.zs[via] + self.c,
        )

    def add_pair(self, r, h=None):
        halves = (0, 1) if r == 3 and h is None else (h,)
        for h in halves:
            self.to_core(r, h).wait_recv()
            add_into(self.mine(r, h), self.cut(self.pair, r, r, h))

    def pass_on(self, r, h=None):
        if r == 1:
            self.to_z(1, 1, 1).start()
        if r == 2:
            @pl.when(jnp.logical_not(self.inner))
            def _():
                for h in range(2):
                    self.to_z(2, 2, 2, h).start()
        if r == 3:
            halves = (0, 1) if h is None else (h,)

            @pl.when(self.inner)
            def _():
                for h in halves:
                    self.to_z(3, 3, 3, h).start()

            @pl.when(jnp.logical_not(self.inner))
            def _():
                for h in halves:
                    self.to_z(3, 0, 1, h).start()

    def relay(self):
        @pl.when(self.inner)
        def _():
            for h in range(2):
                self.to_z(3, 0, 1, h).wait_recv()
                add_into(self.mine(2, h), self.cut(self.land, 0, 0, h))
                self.to_z(2, 2, 2, h).start()

    def arrived(self):
        self.to_z(1, 1, 1).wait_recv()

        @pl.when(self.inner)
        def _():
            for h in range(2):
                self.to_z(3, 3, 3, h).wait_recv()

        @pl.when(jnp.logical_not(self.inner))
        def _():
            self.land[3] = jnp.zeros(self.land.shape[1:], self.land.dtype)

        for h in range(2):
            self.to_z(2, 2, 2, h).wait_recv()

    def total(self, rows):
        own = self.parts[2 * self.zs[0] + self.c, rows, :].astype(jnp.float32)
        return own + self.land[1, rows, :].astype(jnp.float32) + self.land[2, rows, :].astype(jnp.float32) + self.land[3, rows, :].astype(jnp.float32)

    def finish(self):
        for r in range(3):
            self.to_core(r).wait_send()
        self.to_z(1, 1, 1).wait_send()
        for h in range(2):
            self.to_core(3, h).wait_send()
            self.to_z(2, 2, 2, h).wait_send()
            self.to_z(3, 3, 3, h).wait_send()


SENT = {(1, None): 5, (2, 0): 6, (2, 1): 9, (3, 0): 7, (3, 1): 10}
LANDED = {(1, None): 5, (2, 0): 6, (2, 1): 9, (3, 0): 7, (3, 1): 10, (0, 0): 4, (0, 1): 11}


def add_into(into, other):
    rows = into.shape[0]

    def step(i, carry):
        at = pl.ds(pl.multiple_of(i * 32, 32), 32)
        into[at, :] = (into[at, :].astype(jnp.float32) + other[at, :].astype(jnp.float32)).astype(into.dtype)
        return carry

    lax.fori_loop(0, rows // 32, step, 0)


class Loads:
    def __init__(self, pairs, sem):
        self.copies = [pltpu.make_async_copy(far, near, sem.at[n]) for n, (far, near) in enumerate(pairs)]

    def start(self):
        for copy in self.copies:
            copy.start()

    def wait(self, *which):
        for n in which:
            self.copies[n].wait()


class Spread:
    def __init__(self, full, whole, send, recv, own_sem, place):
        self.full, self.whole, self.send, self.recv, self.own_sem = full, whole, send, recv, own_sem
        self.d, self.dx, self.dy, self.zs, self.c, _ = place
        self.t = 2 * self.zs[0] + self.c
        self.seen = set()

    def ready(self, k, r):
        other = self.whole.at[1 + k, 2 * self.zs[r] + 1 - self.c]
        remote(other, other, self.send.at[0], self.recv.at[12 + k * 4 + r], self.d, self.t).wait_recv()
        self.seen.add((k, r))

    def slot(self, g, r):
        return self.whole.at[g, 2 * self.zs[r] + self.c]

    def own(self, r, k):
        src = self.full.at[2 * self.zs[r] + self.c]
        return remote(src, self.slot(1 + k, r), self.send.at[k * 4 + r], self.recv.at[k * 4 + r], (self.dx, self.dy)[k], self.t)

    def start(self, r):
        self.own(r, 0).start()
        self.own(r, 1).start()

    def hop(self, r):
        group, target = (1, self.dy) if r in (0, 3) else (2, self.dx)
        return remote(self.slot(group, r), self.slot(3, r), self.send.at[8 + r], self.recv.at[8 + r], target, self.t)

    def to_core(self, r, k):
        return remote(self.slot(1 + k, r), self.slot(1 + k, r), self.send.at[12 + k * 4 + r], self.recv.at[12 + k * 4 + r], self.d, 2 * self.zs[0] + 1 - self.c)

    def pass_on(self, r):
        self.own(r, 0).wait_recv()
        self.own(r, 1).wait_recv()
        self.hop(r).start()
        self.to_core(r, 0).start()
        self.to_core(r, 1).start()

    def last(self, r):
        self.hop(r).wait_recv()
        self.to_core(r, 2).start()

    def keep(self):
        return pltpu.make_async_copy(self.full, self.whole.at[0], self.own_sem)

    def finish(self):
        for r in range(4):
            self.own(r, 0).wait_send()
            self.own(r, 1).wait_send()
            self.hop(r).wait_send()
            for k in range(3):
                self.to_core(r, k).wait_send()
                if (k, r) not in self.seen:
                    self.to_core(r, k).wait_recv()
        self.keep().wait()


def dot_tn(left, right):
    return lax.dot_general(left, right, (((0,), (0,)), ((), ())), preferred_element_type=jnp.float32)


def dot_nt(left, right):
    return lax.dot_general(left, right, (((1,), (1,)), ((), ())), preferred_element_type=jnp.float32)


def ffn_kernel(
    x_ref, br_ref, cot_ref, again_ref, gain_ref, wg_hbm, wu_hbm, wd_hbm,
    bo_ref, gh_ref, gb_ref, gains_ref, hall_ref, gdall_ref, og_ref, ou_ref, od_ref, gate_all, up_all,
    hfull, gfull, hid_ref, sums, gate, up, act, gg, gu, parts, pair, land, hbuf, gbuf, ubuf, wg_ref, wu_ref, wd_ref,
    ag_send, ag_recv, rs_send, rs_recv, xy_send, xy_recv, own_sem, load_sem, store_sem, out_sem, weight_sem,
):
    place = places_of()
    d, dx, dy, zs, c, inner = place
    t = 2 * zs[0] + c
    weights = Loads(((wg_hbm, wg_ref), (wu_hbm, wu_ref), (wd_hbm, wd_ref)), weight_sem)
    weights.start()
    width = wg_ref.shape[1]
    rows, wide = x_ref.shape
    ft, dt = 512, 1024
    step_rows = 32
    a_gain, gain = again_ref[...], gain_ref[...]

    def opening(i, carry):
        at = pl.ds(pl.multiple_of(i * step_rows, step_rows), step_rows)
        branch = br_ref[at, :]
        inverse = lax.rsqrt(jnp.mean(branch * branch, axis=1, keepdims=True) + EPS)
        hidden = x_ref[at, :].astype(jnp.float32) + branch * inverse * a_gain
        hid_ref[at, :] = hidden
        hfull[t, at, :] = hidden.astype(jnp.bfloat16)
        return carry

    lax.fori_loop(0, rows // step_rows, opening, 0)
    enter(d, zs, c, dx, dy)

    def unit_forward(zz, after=None):
        both = pl.ds(2 * zz, 2)
        at = pl.ds(pl.multiple_of(zz * 2 * rows, 2 * rows), 2 * rows)

        def mid(j, carry):
            cols = pl.ds(pl.multiple_of(j * ft, ft), ft)
            block = hfull[both].reshape(2 * rows, wide)
            g = jnp.dot(block, wg_ref[:, cols], preferred_element_type=jnp.float32)
            u = jnp.dot(block, wu_ref[:, cols], preferred_element_type=jnp.float32)
            gate[at, cols] = g
            up[at, cols] = u
            act[at, cols] = (g * jax.nn.sigmoid(g) * u).astype(jnp.bfloat16)
            return carry

        lax.fori_loop(0, width // ft, mid, 0)

        def out(j, carry):
            cols = pl.ds(pl.multiple_of(j * dt, dt), dt)
            p = jnp.dot(act[at, :], wd_ref[:, cols], preferred_element_type=jnp.float32)
            parts[both, :, cols] = p.astype(jnp.bfloat16).reshape(2, rows, dt)
            return carry

        if after is None:
            lax.fori_loop(0, wide // dt, out, 0)
        else:
            for j in range(wide // dt):
                out(j, 0)
                after(j)

    def unit_backward(zz, after=None):
        both = pl.ds(2 * zz, 2)
        at = pl.ds(pl.multiple_of(zz * 2 * rows, 2 * rows), 2 * rows)

        def mid(j, carry):
            cols = pl.ds(pl.multiple_of(j * ft, ft), ft)
            block = gfull[both].reshape(2 * rows, wide)
            ga = dot_nt(block, wd_ref[cols, :])
            g, u = gate[at, cols], up[at, cols]
            s = jax.nn.sigmoid(g)
            gg[at, cols] = (ga * u * s * (1.0 + g * (1.0 - s))).astype(jnp.bfloat16)
            gu[at, cols] = (ga * (g * s)).astype(jnp.bfloat16)
            return carry

        lax.fori_loop(0, width // ft, mid, 0)

        def out(j, carry):
            cols = pl.ds(pl.multiple_of(j * dt, dt), dt)
            p = dot_nt(gg[at, :], wg_ref[cols, :]) + dot_nt(gu[at, :], wu_ref[cols, :])
            parts[both, :, cols] = p.astype(jnp.bfloat16).reshape(2, rows, dt)
            return carry

        if after is None:
            lax.fori_loop(0, wide // dt, out, 0)
        else:
            for j in range(wide // dt):
                out(j, 0)
                after(j)

    def own_copies(i, down):
        slot = pl.ds(pl.multiple_of(lax.rem(i, 4) * 256, 256), 256)
        at = pl.ds(pl.multiple_of(i * 256, 256), 256)
        outs = (od_ref.at[at, pl.ds(0, width)], od_ref.at[at, pl.ds(width, width)]) if down else (og_ref.at[at, :], ou_ref.at[at, :])
        return [
            pltpu.make_async_copy(buf.at[slot, :], out, out_sem.at[n, lax.rem(i, 4)])
            for n, (buf, out) in enumerate(zip((gate, up), outs))
        ]

    def own_in(i, carry):
        slot = pl.ds(pl.multiple_of(lax.rem(i, 4) * 256, 256), 256)
        at = pl.ds(pl.multiple_of(i * 256, 256), 256)

        @pl.when(i >= 4)
        def _():
            for copy in own_copies(i - 4, False):
                copy.wait()

        h = hfull[:, :, at].reshape(8 * rows, 256)
        gate[slot, :] = dot_tn(h, gg[...])
        up[slot, :] = dot_tn(h, gu[...])
        for copy in own_copies(i, False):
            copy.start()
        return carry

    def own_down(i, carry):
        at = pl.ds(pl.multiple_of(i * 256, 256), 256)
        for copy in own_copies(i + 4, False):
            copy.wait()
        left = act[:, at]
        for n, buf in enumerate((gate, up)):
            buf[at, :] = dot_tn(left, gfull[:, :, n * width : (n + 1) * width].reshape(8 * rows, width))
        for copy in own_copies(i, True):
            copy.start()
        return carry

    done = []

    def fill(chunks):
        def load(n):
            k, r = chunks[n]
            slot = (base + n) % 2
            return pltpu.make_async_copy(hall_ref.at[1 + k, pl.ds(2 * zs[r], 2)], hbuf.at[slot], load_sem.at[slot])

        base = len(done)
        for n, (k, r) in enumerate(chunks):
            slot = len(done) % 2
            if n == 0:
                xy_h.ready(k, r)
                load(0).start()
            load(n).wait()
            if n + 1 < len(chunks):
                xy_h.ready(*chunks[n + 1])
                load(n + 1).start()
            if len(done) >= 2:
                for copy in stores(len(done) - 2):
                    copy.wait()

            def tile(j, carry):
                cols = pl.ds(pl.multiple_of(j * ft, ft), ft)
                block = hbuf[slot].reshape(2 * rows, wide)
                gbuf[slot, :, cols] = jnp.dot(block, wg_ref[:, cols], preferred_element_type=jnp.float32).astype(jnp.bfloat16)
                ubuf[slot, :, cols] = jnp.dot(block, wu_ref[:, cols], preferred_element_type=jnp.float32).astype(jnp.bfloat16)
                return carry

            lax.fori_loop(0, width // ft, tile, 0)
            done.append((k, r))
            for copy in stores(len(done) - 1):
                copy.start()

    def stores(n):
        k, r = done[n]
        at = pl.ds(pl.multiple_of(zs[r] * 2 * rows, 2 * rows), 2 * rows)
        return [
            pltpu.make_async_copy(buf.at[n % 2], out.at[k, at, :], store_sem.at[m, n % 2])
            for m, (buf, out) in enumerate(((gbuf, gate_all), (ubuf, up_all)))
        ]

    def phase(p, full, whole, unit):
        ag = Gather(full, ag_send.at[p], ag_recv.at[p], place)
        rs = Scatter(parts, pair.at[p], land.at[p], rs_send.at[p], rs_recv.at[p], place)
        xy = xy_h if p == 0 else xy_g
        ag.start()
        xy.start(0)
        ag.ready(0)
        if p == 0:
            weights.wait(0, 1, 2)
        unit(zs[0])
        rs.start_core(0)
        if p == 1:
            fill([(0, 3), (1, 3), (2, 0), (2, 2)])
        xy.pass_on(0)
        ag.start_inner()
        ag.arrive(2)
        xy.start(2)
        ag.arrive(1)
        xy.start(1)
        ag.ready(2)
        unit(zs[2])
        rs.start_core(2)
        ag.ready(1)
        unit(zs[1])
        rs.start_core(1)
        rs.add_pair(2)
        rs.pass_on(2)
        rs.add_pair(1)
        rs.pass_on(1)
        ag.arrive(3)
        xy.start(3)
        ag.ready(3)
        unit(zs[3], lambda j: rs.to_core(3, j).start())
        for h in range(2):
            rs.add_pair(3, h)
            rs.pass_on(3, h)
        xy.keep().start()
        rs.add_pair(0)
        if p == 0:
            fill([(0, 0), (1, 0)])
            xy.pass_on(2)
            xy.pass_on(1)
            fill([(0, 2)])
        else:
            xy.pass_on(2)
            xy.pass_on(1)
            lax.fori_loop(0, 8, own_in, 0)
        rs.relay()
        if p == 0:
            fill([(1, 2), (0, 1), (1, 1)])
        else:
            xy.pass_on(3)
            lax.fori_loop(0, 4, own_down, 0)
            xy.last(0)
            fill([(2, 1), (2, 3)])
            xy.last(2)
            xy.last(1)
        rs.arrived()
        return ag, rs

    xy_h = Spread(hfull, hall_ref, xy_send.at[0], xy_recv.at[0], own_sem.at[0], place)
    xy_g = Spread(gfull, gdall_ref, xy_send.at[1], xy_recv.at[1], own_sem.at[1], place)
    ag, rs = phase(0, hfull, hall_ref, unit_forward)
    sums[...] = jnp.zeros_like(sums)

    def middle(i, carry):
        at = pl.ds(pl.multiple_of(i * step_rows, step_rows), step_rows)
        down = rs.total(at)
        inverse = lax.rsqrt(jnp.mean(down * down, axis=1, keepdims=True) + EPS)
        unit = down * inverse
        bo_ref[at, :] = (hid_ref[at, :] + unit * gain).astype(jnp.bfloat16)
        grad = cot_ref[at, :].astype(jnp.float32)
        sums[0:1, :] += jnp.sum(grad * unit, axis=0, keepdims=True)
        inner_grad = grad * gain
        gfull[t, at, :] = (inverse * (inner_grad - unit * jnp.mean(inner_grad * unit, axis=1, keepdims=True))).astype(jnp.bfloat16)
        return carry

    lax.fori_loop(0, rows // step_rows, middle, 0)
    ag.finish()
    rs.finish()
    xy_h.pass_on(3)
    for r in range(4):
        xy_h.last(r)
    ag, rs = phase(1, gfull, gdall_ref, unit_backward)

    def ending(i, carry):
        at = pl.ds(pl.multiple_of(i * step_rows, step_rows), step_rows)
        grad = cot_ref[at, :].astype(jnp.float32) + rs.total(at)
        gh_ref[at, :] = grad
        branch = br_ref[at, :]
        inverse = lax.rsqrt(jnp.mean(branch * branch, axis=1, keepdims=True) + EPS)
        unit = branch * inverse
        sums[1:2, :] += jnp.sum(grad * unit, axis=0, keepdims=True)
        inner_grad = grad * a_gain
        gb_ref[at, :] = (inverse * (inner_grad - unit * jnp.mean(inner_grad * unit, axis=1, keepdims=True))).astype(jnp.bfloat16)
        return carry

    lax.fori_loop(0, rows // step_rows, ending, 0)
    for i in range(wide // HD):
        gains_ref[i : i + 1, :] = sums[0:1, i * HD : (i + 1) * HD]
        gains_ref[wide // HD + i : wide // HD + i + 1, :] = sums[1:2, i * HD : (i + 1) * HD]
    ag.finish()
    rs.finish()
    xy_g.last(3)
    xy_h.finish()
    for i in range(4):
        for copy in own_copies(i, True):
            copy.wait()
    for n in (len(done) - 2, len(done) - 1):
        for copy in stores(n):
            copy.wait()
    xy_g.finish()


def ffn(x_own, branch, cot, attn_gain, ffn_gain, w_gate, w_up, w_down):
    rows, wide = x_own.shape
    width = w_gate.shape[1]
    groups, world = 4, 8
    vmem = pl.BlockSpec(memory_space=pltpu.VMEM)
    anywhere = pl.BlockSpec(memory_space=pl.ANY)
    bf, f32 = jnp.bfloat16, jnp.float32
    whole = jax.ShapeDtypeStruct((groups, world, rows, wide), bf)
    others = jax.ShapeDtypeStruct((groups - 1, world * rows, width), bf)
    dma = pltpu.SemaphoreType.DMA
    return pl.pallas_call(
        ffn_kernel,
        out_shape=(
            jax.ShapeDtypeStruct((rows, wide), bf),
            jax.ShapeDtypeStruct((rows, wide), f32),
            jax.ShapeDtypeStruct((rows, wide), bf),
            jax.ShapeDtypeStruct((2 * wide // HD, HD), f32),
            whole,
            whole,
            jax.ShapeDtypeStruct((wide, width), f32),
            jax.ShapeDtypeStruct((wide, width), f32),
            jax.ShapeDtypeStruct((width, wide), f32),
            others,
            others,
        ),
        in_specs=[vmem] * 5 + [anywhere] * 3,
        out_specs=(vmem,) * 4 + (anywhere,) * 7,
        scratch_shapes=[
            pltpu.VMEM((world, rows, wide), bf),
            pltpu.VMEM((world, rows, wide), bf),
            pltpu.VMEM((rows, wide), f32),
            pltpu.VMEM((8, wide), f32),
            pltpu.VMEM((world * rows, width), f32),
            pltpu.VMEM((world * rows, width), f32),
            pltpu.VMEM((world * rows, width), bf),
            pltpu.VMEM((world * rows, width), bf),
            pltpu.VMEM((world * rows, width), bf),
            pltpu.VMEM((world, rows, wide), bf),
            pltpu.VMEM((2, 4, rows, wide), bf),
            pltpu.VMEM((2, 4, rows, wide), bf),
            pltpu.VMEM((2, 2, rows, wide), bf),
            pltpu.VMEM((2, 2 * rows, width), bf),
            pltpu.VMEM((2, 2 * rows, width), bf),
            pltpu.VMEM((wide, width), bf),
            pltpu.VMEM((wide, width), bf),
            pltpu.VMEM((width, wide), bf),
            dma((2, 8)),
            dma((2, 8)),
            dma((2, 12)),
            dma((2, 12)),
            dma((2, 24)),
            dma((2, 24)),
            dma((2,)),
            dma((2,)),
            dma((2, 2)),
            dma((2, 4)),
            dma((3,)),
        ],
        compiler_params=pltpu.CompilerParams(
            collective_id=2, has_side_effects=True, vmem_limit_bytes=60 * 2**20
        ),
        name="ffn",
    )(x_own, branch, cot, attn_gain.reshape(1, wide), ffn_gain.reshape(1, wide), w_gate, w_up, w_down)


WINDOW = 3


class Exchange:
    def __init__(self, block, land, send, recv, place):
        self.block, self.land, self.send, self.recv = block, land, send, recv
        self.d, _, _, self.zs, self.c, _ = place
        self.t = 2 * self.zs[0] + self.c

    def copies(self):
        out = []
        for r in range(4):
            for k in range(2):
                if r == 0 and k == 0:
                    continue
                at = 4 * k + r
                core = self.c if k == 0 else 1 - self.c
                out.append((2 * self.zs[r] + core, at))
        return out

    def start(self):
        for peer, at in self.copies():
            remote(self.block, self.land.at[self.t], self.send.at[at], self.recv.at[at], self.d, peer).start()

    def wait(self):
        for peer, at in self.copies():
            remote(self.block, self.land.at[peer], self.send.at[at], self.recv.at[at], self.d, peer).wait()


def enter_all(d, zs, c, dx, dy):
    barrier = pltpu.get_barrier_semaphore()
    peers = [(d, 2 * zs[r] + c) for r in (1, 2, 3)] + [(d, 2 * zs[r] + 1 - c) for r in range(4)]
    peers += [(dx, 2 * zs[0] + c), (dy, 2 * zs[0] + c)]
    for peer in peers:
        pl.semaphore_signal(barrier, inc=1, device_id=peer, device_id_type=MESH)
    pl.semaphore_wait(barrier, len(peers))


def put_column(stat, base, zz, square):
    rows = square.shape[0]
    folded = square[:, :HD]
    for h in range(1, square.shape[1] // HD):
        folded = folded + square[:, h * HD : (h + 1) * HD]
    line = jnp.sum(folded.T, axis=0, keepdims=True)
    for i in range(rows // HD):
        stat[pl.ds(base + 2 * zz + i, 1), :] = line[:, i * HD : (i + 1) * HD]


def get_column(stat_row, count):
    return jnp.broadcast_to(stat_row, (count, HD)).T


def attn_kernel(
    x_ref, wq_hbm, wk_hbm, wv_hbm, wo_hbm, qg_ref, kg_ref, cos_ref, sin_ref, first_ref,
    br_ref, q_out, k_out, v_out, qu_out, ku_out, rq_out, rk_out, mixed_out, xall_ref,
    xfull, parts, pair, land, stat, stats, wq_ref, wk_ref, wv_ref, wo_ref,
    ag_send, ag_recv, rs_send, rs_recv, xy_send, xy_recv, st_send, st_recv, own_sem, weight_sem,
):
    place = places_of()
    d, dx, dy, zs, c, inner = place
    t = 2 * zs[0] + c
    rows, wide = x_ref.shape
    span = 2 * rows
    weights = Loads(((wq_hbm, wq_ref), (wk_hbm, wk_ref), (wv_hbm, wv_ref), (wo_hbm, wo_ref)), weight_sem)
    weights.start()
    heads = wq_ref.shape[1] // HD
    xfull[t] = x_ref[...]
    enter_all(d, zs, c, dx, dy)
    ag = Gather(xfull, ag_send, ag_recv, place)
    rs = Scatter(parts, pair, land, rs_send, rs_recv, place)
    xy = Spread(xfull, xall_ref, xy_send, xy_recv, own_sem, place)
    ex = Exchange(stat, stats, st_send, st_recv, place)

    def at_of(zz):
        return pl.ds(pl.multiple_of(zz * span, span), span)

    def project_qk(zz):
        block = xfull[pl.ds(2 * zz, 2)].reshape(span, wide)
        for w_ref, out, base in ((wq_ref, qu_out, 0), (wk_ref, ku_out, 8)):
            raw = jnp.dot(block, w_ref[...], preferred_element_type=jnp.float32)
            out[at_of(zz), :] = raw
            put_column(stat, base, zz, raw * raw)

    def project_v(zz):
        block = xfull[pl.ds(2 * zz, 2)].reshape(span, wide)
        v_out[at_of(zz), :] = jnp.dot(block, wv_ref[...], preferred_element_type=jnp.float32).astype(jnp.bfloat16)

    ag.start()
    xy.start(0)
    ag.ready(0)
    weights.wait(0, 1, 2, 3)
    project_qk(zs[0])
    project_v(zs[0])
    xy.pass_on(0)
    ag.start_inner()
    ag.arrive(2)
    xy.start(2)
    ag.arrive(1)
    xy.start(1)
    ag.ready(2)
    project_qk(zs[2])
    ag.ready(1)
    project_qk(zs[1])
    project_v(zs[2])
    ag.arrive(3)
    xy.start(3)
    ag.ready(3)
    project_qk(zs[3])
    ex.start()
    project_v(zs[1])
    project_v(zs[3])
    xy.keep().start()
    ex.wait()
    total = stat[...]
    for r in range(4):
        for k in range(2):
            if r or k:
                total = total + stats[2 * zs[r] + (c if k == 0 else 1 - c)]
    inverse = lax.rsqrt(total / (8 * wq_ref.shape[1]) + EPS)
    rq_out[...] = inverse[:8]
    rk_out[...] = inverse[8:]

    def norm_rope(i, carry):
        at = pl.ds(pl.multiple_of(i * HD, HD), HD)
        cosine, sine = cos_ref[at, :], sin_ref[at, :]
        for line, raw, out, gain in ((rq_out, qu_out, q_out, qg_ref), (rk_out, ku_out, k_out, kg_ref)):
            scale = get_column(line[pl.ds(i, 1), :], HD)
            for h in range(heads):
                cols = slice(h * HD, (h + 1) * HD)
                unit = raw[at, cols] * scale
                raw[at, cols] = unit
                normed = unit * gain[:, cols]
                out[at, cols] = (normed * cosine + pltpu.roll(normed, HD // 2, 1) * sine).astype(jnp.bfloat16)
        return carry

    lax.fori_loop(0, 8, norm_rope, 0)

    def attend(zz):
        at = at_of(zz)
        low = jnp.maximum(zz - (WINDOW - 1), 0) * span
        keys_at = pl.ds(pl.multiple_of(low, span), WINDOW * span)
        key_place = low + lax.broadcasted_iota(jnp.int32, (span, WINDOW * span), 1)
        query_place = zz * span + lax.broadcasted_iota(jnp.int32, (span, WINDOW * span), 0)
        allowed = (key_place <= query_place) & (key_place >= first_ref[at, :])
        for h in range(heads):
            cols = slice(h * HD, (h + 1) * HD)
            scores = dot_nt(q_out[at, cols], k_out[keys_at, cols]) * HD**-0.5
            scores = jnp.where(allowed, scores, -1e30)
            top = jnp.max(scores, axis=1, keepdims=True)
            expo = jnp.exp(scores - top)
            probs = expo * (1.0 / jnp.sum(expo, axis=1, keepdims=True))
            mixed_out[at, cols] = jnp.dot(probs.astype(jnp.bfloat16), v_out[keys_at, cols], preferred_element_type=jnp.float32).astype(jnp.bfloat16)
        dt = 1024

        def out(j, carry):
            to = pl.ds(pl.multiple_of(j * dt, dt), dt)
            p = jnp.dot(mixed_out[at, :], wo_ref[:, to], preferred_element_type=jnp.float32)
            parts[pl.ds(2 * zz, 2), :, to] = p.astype(jnp.bfloat16).reshape(2, rows, dt)
            return carry

        lax.fori_loop(0, wide // dt, out, 0)

    attend(zs[3])
    rs.start_core(3)
    attend(zs[2])
    rs.start_core(2)
    rs.add_pair(3)
    rs.pass_on(3)
    attend(zs[1])
    rs.start_core(1)
    rs.add_pair(2)
    rs.pass_on(2)
    rs.add_pair(1)
    rs.pass_on(1)
    attend(zs[0])
    rs.start_core(0)
    rs.add_pair(0)
    xy.pass_on(2)
    xy.pass_on(1)
    rs.relay()
    xy.pass_on(3)
    for r in range(4):
        xy.last(r)
    rs.arrived()

    def ending(i, carry):
        at = pl.ds(pl.multiple_of(i * 32, 32), 32)
        br_ref[at, :] = rs.total(at)
        return carry

    lax.fori_loop(0, rows // 32, ending, 0)
    ag.finish()
    rs.finish()
    xy.finish()


def attention(x_own, w_query, w_key, w_value, w_out, q_gain, k_gain, cosine, sine, first):
    rows, wide = x_own.shape
    head_cols = w_query.shape[1]
    groups, world = 4, 8
    count = world * rows
    vmem = pl.BlockSpec(memory_space=pltpu.VMEM)
    anywhere = pl.BlockSpec(memory_space=pl.ANY)
    bf, f32 = jnp.bfloat16, jnp.float32
    dma = pltpu.SemaphoreType.DMA
    cols = jax.ShapeDtypeStruct((count, head_cols), bf)
    wide_cols = jax.ShapeDtypeStruct((count, head_cols), f32)
    line = jax.ShapeDtypeStruct((8, HD), f32)
    return pl.pallas_call(
        attn_kernel,
        out_shape=(
            jax.ShapeDtypeStruct((rows, wide), f32),
            cols, cols, cols, wide_cols, wide_cols, line, line, cols,
            jax.ShapeDtypeStruct((groups, world, rows, wide), bf),
        ),
        in_specs=[vmem] + [anywhere] * 4 + [vmem] * 5,
        out_specs=(vmem,) * 9 + (pl.BlockSpec(memory_space=pl.ANY),),
        scratch_shapes=[
            pltpu.VMEM((world, rows, wide), bf),
            pltpu.VMEM((world, rows, wide), bf),
            pltpu.VMEM((4, rows, wide), bf),
            pltpu.VMEM((4, rows, wide), bf),
            pltpu.VMEM((16, HD), f32),
            pltpu.VMEM((world, 16, HD), f32),
            pltpu.VMEM((wide, head_cols), bf),
            pltpu.VMEM((wide, head_cols), bf),
            pltpu.VMEM((wide, head_cols), bf),
            pltpu.VMEM((head_cols, wide), bf),
            dma((8,)), dma((8,)), dma((12,)), dma((12,)), dma((24,)), dma((24,)), dma((8,)), dma((8,)),
            pltpu.SemaphoreType.DMA, dma((4,)),
        ],
        compiler_params=pltpu.CompilerParams(
            collective_id=1, has_side_effects=True, vmem_limit_bytes=60 * 2**20
        ),
        name="attn",
    )(x_own, w_query, w_key, w_value, w_out, q_gain.reshape(1, -1), k_gain.reshape(1, -1), cosine, sine, first)


class Background:
    tokens, units = 512, 512

    def __init__(self, hall, gdall, gate_all, up_all, w_down, starts, outs, hbuf, gbuf, gate, up, tile, sums, mids, load_sem, tile_sem, start_sem, out_sem):
        self.hall, self.gdall, self.gate_all, self.up_all, self.w_down, self.starts, self.outs = hall, gdall, gate_all, up_all, w_down, starts, outs
        self.hbuf, self.gbuf, self.gate, self.up, self.tile, self.sums, self.mids = hbuf, gbuf, gate, up, tile, sums, mids
        self.load_sem, self.tile_sem, self.start_sem, self.out_sem = load_sem, tile_sem, start_sem, out_sem
        self.blocks = self.tokens // hall.shape[2]
        self.per_group = hall.shape[1] // self.blocks
        self.per_tile = 3 * self.per_group
        self.tile_count = w_down.shape[0] // self.units
        self.count = self.tile_count * self.per_tile

    def loads(self, n):
        slot, m = n % 2, n % self.per_tile
        group, part = 1 + m // self.per_group, m % self.per_group
        blocks = pl.ds(part * self.blocks, self.blocks)
        rows = pl.ds(part * self.tokens, self.tokens)
        units = pl.ds(n // self.per_tile * self.units, self.units)
        return (
            pltpu.make_async_copy(self.hall.at[group, blocks], self.hbuf.at[slot], self.load_sem.at[0, slot]),
            pltpu.make_async_copy(self.gdall.at[group, blocks], self.gbuf.at[slot], self.load_sem.at[1, slot]),
            pltpu.make_async_copy(self.gate_all.at[group - 1, rows, units], self.gate.at[slot], self.load_sem.at[2, slot]),
            pltpu.make_async_copy(self.up_all.at[group - 1, rows, units], self.up.at[slot], self.load_sem.at[3, slot]),
        )

    def tile_load(self, tile):
        return pltpu.make_async_copy(self.w_down.at[pl.ds(tile * self.units, self.units), :], self.tile, self.tile_sem)

    def moves(self, tile, refs, sem, inward):
        at = pl.ds(tile * self.units, self.units)
        g, u, d = refs
        pairs = zip(self.sums, (g.at[:, at], u.at[:, at], d.at[at, :]))
        return [
            pltpu.make_async_copy(far, near, sem.at[n]) if inward else pltpu.make_async_copy(near, far, sem.at[n])
            for n, (near, far) in enumerate(pairs)
        ]

    def stores(self, tile):
        return self.moves(tile, self.outs, self.out_sem, False)

    def sums_in(self, tile):
        return self.moves(tile, self.starts, self.start_sem, True)

    def begin(self):
        for copy in self.loads(0) + (self.tile_load(0),) + tuple(self.sums_in(0)):
            copy.start()

    def turn(self, tile):
        for copy in self.stores(tile):
            copy.wait()
        for copy in self.sums_in(tile + 1):
            copy.start()

    def step(self, n):
        slot, tile, m = n % 2, n // self.per_tile, n % self.per_tile
        if n + 1 < self.count:
            for copy in self.loads(n + 1):
                copy.start()
        if m == 0:
            self.tile_load(tile).wait()
            for copy in self.sums_in(tile):
                copy.wait()
        for copy in self.loads(n):
            copy.wait()
        hbuf, gbuf, gate, up = self.hbuf.at[slot], self.gbuf.at[slot], self.gate.at[slot], self.up.at[slot]
        wd = self.tile
        act, gg, gu = self.mids
        rows, wide = hbuf.shape[1:]
        g, u = gate[...].astype(jnp.float32), up[...].astype(jnp.float32)
        ga = dot_nt(gbuf[...].reshape(self.tokens, wide), wd[...])
        s = jax.nn.sigmoid(g)
        gs = g * s
        act[...] = (gs * u).astype(jnp.bfloat16)
        gg[...] = (ga * u * s * (1.0 + g * (1.0 - s))).astype(jnp.bfloat16)
        gu[...] = (ga * gs).astype(jnp.bfloat16)
        span = 1024

        def into(i, carry):
            at = pl.ds(pl.multiple_of(i * span, span), span)
            h = hbuf[:, :, at].reshape(self.tokens, span)
            pg = dot_tn(h, gg[...])
            pu = dot_tn(h, gu[...])
            pd = dot_tn(act[...], gbuf[:, :, at].reshape(self.tokens, span))
            self.sums[0][at, :] += pg
            self.sums[1][at, :] += pu
            self.sums[2][:, at] += pd
            return carry

        lax.fori_loop(0, wide // span, into, 0)
        if m == self.per_tile - 1:
            for copy in self.stores(tile):
                copy.start()
            if tile + 1 < self.tile_count:
                self.tile_load(tile + 1).start()

    def finish(self):
        for copy in self.stores(self.tile_count - 1):
            copy.wait()


class SpreadColumns:
    def __init__(self, own, whole, send, recv, own_sem, place):
        self.src, self.whole, self.send, self.recv, self.own_sem = own, whole, send, recv, own_sem
        self.d, self.dx, self.dy, self.zs, self.c, _ = place
        self.t = 2 * self.zs[0] + self.c

    def own(self, p, k):
        return remote(self.src.at[p], self.whole.at[1 + k, p], self.send.at[k * 3 + p], self.recv.at[k * 3 + p], (self.dx, self.dy)[k], self.t)

    def hop(self, p, b):
        half = self.src.shape[1] // 2
        at = pl.ds(b * half, half)
        return remote(self.whole.at[1 + b, p, at], self.whole.at[3, p, at], self.send.at[6 + 2 * p + b], self.recv.at[6 + 2 * p + b], (self.dy, self.dx)[b], self.t)

    def start(self, p):
        self.own(p, 0).start()
        self.own(p, 1).start()

    def pass_on(self, p):
        for b in range(2):
            self.own(p, b).wait_recv()
            self.hop(p, b).start()

    def keep(self):
        return pltpu.make_async_copy(self.src, self.whole.at[0], self.own_sem)

    def finish(self):
        for p in range(3):
            for b in range(2):
                self.own(p, b).wait_send()
                self.hop(p, b).wait()
        self.keep().wait()


class SumHalves:
    def __init__(self, buf, once, twice, send, recv, place):
        self.buf, self.land, self.send, self.recv = buf, (once, twice), send, recv
        self.d, self.dx, self.dy, self.zs, self.c, _ = place
        self.t = 2 * self.zs[0] + self.c

    def move(self, stage, b):
        at = 2 * stage + b
        return remote(self.buf.at[b], self.land[stage].at[b], self.send.at[at], self.recv.at[at], (self.dx, self.dy)[(stage + b) % 2], self.t)

    def start(self, stage):
        for b in range(2):
            self.move(stage, b).start()

    def add(self, stage):
        for b in range(2):
            self.move(stage, b).wait()
            add_into(self.buf.at[b], self.land[stage].at[b])


class ExchangeGroups:
    def __init__(self, block, land, send, recv, place):
        self.block, self.land, self.send, self.recv = block, land, send, recv
        d, dx, dy, zs, c, _ = place
        self.peers, self.t = (dx, dy, 3 - d), 2 * zs[0] + c

    def copies(self):
        return [remote(self.block, self.land.at[k], self.send.at[k], self.recv.at[k], peer, self.t) for k, peer in enumerate(self.peers)]

    def start(self):
        for copy in self.copies():
            copy.start()

    def wait(self):
        for copy in self.copies():
            copy.wait()


def back_kernel(
    gb_ref, gh_ref, q_hbm, k_hbm, v_hbm, mixed_hbm, qu_hbm, ku_hbm, rq_ref, rk_ref, first_ref, cos_ref, sin_ref,
    qg_ref, kg_ref, wq_hbm, wk_hbm, wv_hbm, wo_hbm, gains_ref, hall, gdall, gate_all, up_all, w_down, own_g, own_u, own_d,
    gt_ref, gains_out, dwo_ref, gall_ref, dwg, dwu, dwd,
    full, pair, land, gm, dq, dk, dv, own, wo_once, wo_twice, stat, stats, gland, block, blocks, gacc,
    hbuf, gbuf, gbf, ubf, td, sg, su, sd, act, gg, gu,
    q_ref, k_ref, v_ref, mixed_ref, qu_ref, ku_ref, wq_ref, wk_ref, wv_ref, wo_ref,
    ag_send, ag_recv, rs_send, rs_recv, st_send, st_recv, ga_send, ga_recv, gr_send, gr_recv,
    co_send, co_recv, wo_send, wo_recv, own_sem, load_sem, tile_sem, start_sem, out_sem, input_sem,
):
    place = places_of()
    d, dx, dy, zs, c, inner = place
    t = 2 * zs[0] + c
    rows, wide = gb_ref.shape
    span = 2 * rows
    heads = wq_ref.shape[1] // HD
    count = q_ref.shape[0]
    scale = HD**-0.5
    inputs = Loads(
        (
            (wo_hbm, wo_ref), (mixed_hbm, mixed_ref), (q_hbm, q_ref), (k_hbm, k_ref), (v_hbm, v_ref), (qu_hbm, qu_ref), (ku_hbm, ku_ref),
            (wq_hbm, wq_ref), (wk_hbm, wk_ref), (wv_hbm, wv_ref),
        ),
        input_sem,
    )
    work = Background(
        hall, gdall, gate_all, up_all, w_down, (own_g, own_u, own_d), (dwg, dwu, dwd), hbuf, gbuf, gbf, ubf, td, (sg, su, sd), (act, gg, gu),
        load_sem, tile_sem, start_sem, out_sem,
    )
    work.begin()
    inputs.start()
    full[t] = gb_ref[...]
    barrier = pltpu.get_barrier_semaphore()
    peers = [(d, 2 * zs[r] + c) for r in (1, 2, 3)] + [(d, 2 * zs[r] + 1 - c) for r in range(4)]
    peers += [(dx, t), (dy, t), (3 - d, t)]
    for peer in peers:
        pl.semaphore_signal(barrier, inc=1, device_id=peer, device_id_type=MESH)
    pl.semaphore_wait(barrier, len(peers))
    ag = Gather(full, ag_send, ag_recv, place)
    rs = Scatter(full, pair, land, rs_send, rs_recv, place)
    ex = Exchange(stat, stats, st_send, st_recv, place)
    gains = Exchange(gains_ref, gland, ga_send, ga_recv, place)
    groups = ExchangeGroups(block, blocks, gr_send, gr_recv, place)
    cols_all = SpreadColumns(own, gall_ref, co_send, co_recv, own_sem, place)
    wo_sum = SumHalves(dwo_ref, wo_once, wo_twice, wo_send, wo_recv, place)
    def at_of(zz):
        return pl.ds(pl.multiple_of(zz * span, span), span)

    ag.start()
    gains.start()
    def out_back(j, carry):
        to = pl.ds(pl.multiple_of(j * 512, 512), 512)
        p = dot_tn(mixed_ref[...], full[:, :, to].reshape(count, 512))
        dwo_ref[:, :, to] = p.astype(jnp.bfloat16).reshape(2, p.shape[0] // 2, 512)
        return carry

    def attend_back(zz):
        at = at_of(zz)
        gm[at, :] = dot_nt(full[pl.ds(2 * zz, 2)].reshape(span, wide), wo_ref[...]).astype(jnp.bfloat16)
        low = jnp.maximum(zz - (WINDOW - 1), 0) * span
        keys_at = pl.ds(pl.multiple_of(low, span), WINDOW * span)
        key_place = low + lax.broadcasted_iota(jnp.int32, (span, WINDOW * span), 1)
        query_place = zz * span + lax.broadcasted_iota(jnp.int32, (span, WINDOW * span), 0)
        allowed = (key_place <= query_place) & (key_place >= first_ref[at, :])
        for h in range(heads):
            cols = slice(h * HD, (h + 1) * HD)
            scores = dot_nt(q_ref[at, cols], k_ref[keys_at, cols]) * scale
            scores = jnp.where(allowed, scores, -1e30)
            top = jnp.max(scores, axis=1, keepdims=True)
            expo = jnp.exp(scores - top)
            probs = expo * (1.0 / jnp.sum(expo, axis=1, keepdims=True))
            grad = gm[at, cols]
            gp = dot_nt(grad, v_ref[keys_at, cols])
            gs = (probs * (gp - jnp.sum(probs * gp, axis=1, keepdims=True))).astype(jnp.bfloat16)
            dq[at, cols] = jnp.dot(gs, k_ref[keys_at, cols], preferred_element_type=jnp.float32) * scale
            dk[keys_at, cols] += dot_tn(gs, q_ref[at, cols]) * scale
            dv[keys_at, cols] += dot_tn(probs.astype(jnp.bfloat16), grad)

    dk[...] = jnp.zeros_like(dk)
    dv[...] = jnp.zeros_like(dv)
    work.step(0)
    ag.ready(0)
    inputs.wait(*range(10))
    attend_back(zs[0])
    work.step(1)
    work.step(2)
    ag.start_inner()
    ag.arrive(2)
    ag.arrive(1)
    work.step(3)
    ag.ready(2)
    attend_back(zs[2])
    ag.ready(1)
    attend_back(zs[1])
    ag.arrive(3)
    work.step(4)
    ag.ready(3)
    attend_back(zs[3])
    own[2] = dv[...].astype(jnp.bfloat16)
    cols_all.start(2)
    gacc[...] = jnp.zeros_like(gacc)

    def unrope(i, carry):
        at = pl.ds(pl.multiple_of(i * HD, HD), HD)
        cosine, sine = cos_ref[at, :], sin_ref[at, :]
        for n, (grad, unit_ref, gain) in enumerate(((dq, qu_ref, qg_ref), (dk, ku_ref, kg_ref))):
            total = jnp.zeros((HD, HD), jnp.float32)
            for h in range(heads):
                cols = slice(h * HD, (h + 1) * HD)
                value = grad[at, cols].astype(jnp.bfloat16).astype(jnp.float32)
                value = value * cosine - pltpu.roll(value, HD // 2, 1) * sine
                unit = unit_ref[at, cols]
                row = n * heads + h
                gacc[row : row + 1, :] += jnp.sum(value * unit, axis=0, keepdims=True)
                value = value * gain[:, cols]
                grad[at, cols] = value
                total = total + value * unit
            stat[pl.ds(8 * n + i, 1), :] = jnp.sum(total.T, axis=0, keepdims=True)
        return carry

    lax.fori_loop(0, count // HD, unrope, 0)
    ex.start()
    gains.wait()
    total = gains_ref[...]
    for r in range(4):
        for k in range(2):
            if r or k:
                total = total + gland[2 * zs[r] + (c if k == 0 else 1 - c)]
    lines = gains_ref.shape[0]
    block[:lines, :] = total
    block[lines:, :] = gacc[...]
    groups.start()
    lax.fori_loop(0, wide // 512, out_back, 0)
    wo_sum.start(0)
    ag.finish()
    work.step(5)
    ex.wait()
    total = stat[...]
    for r in range(4):
        for k in range(2):
            if r or k:
                total = total + stats[2 * zs[r] + (c if k == 0 else 1 - c)]
    stat[...] = total * (1.0 / (8 * wq_ref.shape[1]))

    def norm_back_rows(i, carry):
        at = pl.ds(pl.multiple_of(i * HD, HD), HD)
        for n, (grad, unit_ref, inv_ref) in enumerate(((dq, qu_ref, rq_ref), (dk, ku_ref, rk_ref))):
            mean = get_column(stat[pl.ds(8 * n + i, 1), :], HD)
            inverse = get_column(inv_ref[pl.ds(i, 1), :], HD)
            for h in range(heads):
                cols = slice(h * HD, (h + 1) * HD)
                own[n, at, cols] = (inverse * (grad[at, cols] - unit_ref[at, cols] * mean)).astype(jnp.bfloat16)
        return carry

    lax.fori_loop(0, count // HD, norm_back_rows, 0)
    cols_all.start(0)
    cols_all.start(1)
    cols_all.keep().start()

    def tokens_back(zz):
        at = at_of(zz)
        dt = 1024

        def out(j, carry):
            to = pl.ds(pl.multiple_of(j * dt, dt), dt)
            p = dot_nt(own[0, at, :], wq_ref[to, :]) + dot_nt(own[1, at, :], wk_ref[to, :]) + dot_nt(own[2, at, :], wv_ref[to, :])
            full[pl.ds(2 * zz, 2), :, to] = p.astype(jnp.bfloat16).reshape(2, rows, dt)
            return carry

        lax.fori_loop(0, wide // dt, out, 0)

    tokens_back(zs[3])
    rs.start_core(3)
    work.turn(0)
    tokens_back(zs[2])
    rs.start_core(2)
    rs.add_pair(3)
    rs.pass_on(3)
    tokens_back(zs[1])
    rs.start_core(1)
    rs.add_pair(2)
    rs.pass_on(2)
    rs.add_pair(1)
    rs.pass_on(1)
    tokens_back(zs[0])
    rs.start_core(0)
    rs.add_pair(0)
    cols_all.pass_on(2)
    work.step(6)
    rs.relay()
    work.step(7)
    wo_sum.add(0)
    wo_sum.start(1)
    work.step(8)
    work.step(9)
    cols_all.pass_on(0)
    work.step(10)
    cols_all.pass_on(1)
    work.step(11)
    wo_sum.add(1)
    rs.arrived()

    def ending(i, carry):
        at = pl.ds(pl.multiple_of(i * 32, 32), 32)
        gt_ref[at, :] = gh_ref[at, :] + rs.total(at)
        return carry

    lax.fori_loop(0, rows // 32, ending, 0)
    groups.wait()
    gains_out[...] = block[...] + blocks[0] + blocks[1] + blocks[2]
    rs.finish()
    cols_all.finish()
    work.finish()


def backward(grad_branch, grad_hidden, kept, first, cosine, signed, q_gain, k_gain, weights, gains, h_all, gd_all, gate_all, up_all, w_down, own_parts):
    queries, keys, values, mixed, q_unit, k_unit, q_inverse, k_inverse = kept
    rows, wide = grad_branch.shape
    count, head_cols = queries.shape
    heads = head_cols // HD
    world = 8
    width = w_down.shape[0]
    lines = gains.shape[0]
    vmem = pl.BlockSpec(memory_space=pltpu.VMEM)
    anywhere = pl.BlockSpec(memory_space=pl.ANY)
    bf, f32 = jnp.bfloat16, jnp.float32
    dma = pltpu.SemaphoreType.DMA
    tok, unit = Background.tokens, Background.units
    return pl.pallas_call(
        back_kernel,
        out_shape=(
            jax.ShapeDtypeStruct((rows, wide), f32),
            jax.ShapeDtypeStruct((lines + 8, HD), f32),
            jax.ShapeDtypeStruct((2, head_cols // 2, wide), bf),
            jax.ShapeDtypeStruct((4, 3, count, head_cols), bf),
            jax.ShapeDtypeStruct((wide, width), f32),
            jax.ShapeDtypeStruct((wide, width), f32),
            jax.ShapeDtypeStruct((width, wide), f32),
        ),
        in_specs=[vmem] * 2 + [anywhere] * 6 + [vmem] * 7 + [anywhere] * 4 + [vmem] + [anywhere] * 8,
        out_specs=(vmem, vmem, vmem) + (anywhere,) * 4,
        scratch_shapes=[
            pltpu.VMEM((world, rows, wide), bf),
            pltpu.VMEM((4, rows, wide), bf),
            pltpu.VMEM((4, rows, wide), bf),
            pltpu.VMEM((count, head_cols), bf),
            pltpu.VMEM((count, head_cols), f32),
            pltpu.VMEM((count, head_cols), f32),
            pltpu.VMEM((count, head_cols), f32),
            pltpu.VMEM((3, count, head_cols), bf),
            pltpu.VMEM((2, head_cols // 2, wide), bf),
            pltpu.VMEM((2, head_cols // 2, wide), bf),
            pltpu.VMEM((16, HD), f32),
            pltpu.VMEM((world, 16, HD), f32),
            pltpu.VMEM((world, lines, HD), f32),
            pltpu.VMEM((lines + 8, HD), f32),
            pltpu.VMEM((3, lines + 8, HD), f32),
            pltpu.VMEM((8, HD), f32),
            pltpu.VMEM((2, tok // rows, rows, wide), bf),
            pltpu.VMEM((2, tok // rows, rows, wide), bf),
            pltpu.VMEM((2, tok, unit), bf),
            pltpu.VMEM((2, tok, unit), bf),
            pltpu.VMEM((unit, wide), bf),
            pltpu.VMEM((wide, unit), f32),
            pltpu.VMEM((wide, unit), f32),
            pltpu.VMEM((unit, wide), f32),
            pltpu.VMEM((tok, unit), bf),
            pltpu.VMEM((tok, unit), bf),
            pltpu.VMEM((tok, unit), bf),
            pltpu.VMEM((count, head_cols), bf),
            pltpu.VMEM((count, head_cols), bf),
            pltpu.VMEM((count, head_cols), bf),
            pltpu.VMEM((count, head_cols), bf),
            pltpu.VMEM((count, head_cols), f32),
            pltpu.VMEM((count, head_cols), f32),
            pltpu.VMEM((wide, head_cols), bf),
            pltpu.VMEM((wide, head_cols), bf),
            pltpu.VMEM((wide, head_cols), bf),
            pltpu.VMEM((head_cols, wide), bf),
            dma((8,)), dma((8,)), dma((12,)), dma((12,)), dma((8,)), dma((8,)), dma((8,)), dma((8,)), dma((3,)), dma((3,)),
            dma((12,)), dma((12,)), dma((4,)), dma((4,)), pltpu.SemaphoreType.DMA, dma((4, 2)), pltpu.SemaphoreType.DMA, dma((3,)), dma((3,)), dma((10,)),
        ],
        compiler_params=pltpu.CompilerParams(
            collective_id=3, has_side_effects=True, vmem_limit_bytes=62 * 2**20
        ),
        name="back",
    )(
        grad_branch, grad_hidden, queries, keys, values, mixed, q_unit, k_unit, q_inverse, k_inverse, first, cosine, signed,
        q_gain.reshape(1, -1), k_gain.reshape(1, -1), *weights, gains, h_all, gd_all, gate_all, up_all, w_down, *own_parts,
    )


def tail_kernel(
    pg_ref, pu_ref, pd_ref, x_ref, g_ref, wo_ref, gains_ref, og_ref, ou_ref, od_ref, oq_ref, ok_ref, ov_ref, oo_ref, *gain_refs
):
    count, cols = g_ref.shape[2], x_ref.shape[-1]
    og_ref[...] = pg_ref[...]
    ou_ref[...] = pu_ref[...]
    od_ref[...] = pd_ref[...]
    oo_ref[...] = wo_ref[...].reshape(oo_ref.shape).astype(jnp.float32)
    row = 0
    for out in gain_refs:
        out[...] = gains_ref[row : row + out.shape[0], :]
        row += out.shape[0]
    for p, out in enumerate((oq_ref, ok_ref, ov_ref)):
        total = jnp.zeros(out.shape, jnp.float32)
        for g in range(4):
            total = total + dot_tn(x_ref[g].reshape(count, cols), g_ref[g, p])
        out[...] = total


def weight_tail(parts, x_all, grad_qkv, grad_out, gains):
    groups, world, rows, wide = x_all.shape
    count, width = world * rows, parts[0].shape[1]
    head_cols = grad_qkv.shape[-1]
    cols = 512
    f32 = jnp.float32
    down = pl.BlockSpec((cols, width), lambda i: (i, 0))
    across = pl.BlockSpec((width, cols), lambda i: (0, i))
    heads = pl.BlockSpec((cols, head_cols), lambda i: (i, 0))
    lines = [(wide // HD, HD)] * 2 + [(head_cols // HD, HD)] * 2
    return pl.pallas_call(
        tail_kernel,
        grid=(wide // cols,),
        in_specs=[
            down, down, across,
            pl.BlockSpec((groups, world, rows, cols), lambda i: (0, 0, 0, i)),
            pl.BlockSpec(grad_qkv.shape, lambda i: (0, 0, 0, 0)),
            pl.BlockSpec((2, head_cols // 2, cols), lambda i: (0, 0, i)),
            pl.BlockSpec(gains.shape, lambda i: (0, 0)),
        ],
        out_specs=(down, down, across, heads, heads, heads, pl.BlockSpec((head_cols, cols), lambda i: (0, i)))
        + tuple(pl.BlockSpec(shape, lambda i: (0, 0)) for shape in lines),
        out_shape=(
            jax.ShapeDtypeStruct((wide, width), f32),
            jax.ShapeDtypeStruct((wide, width), f32),
            jax.ShapeDtypeStruct((width, wide), f32),
        )
        + (jax.ShapeDtypeStruct((wide, head_cols), f32),) * 3
        + (jax.ShapeDtypeStruct((head_cols, wide), f32),)
        + tuple(jax.ShapeDtypeStruct(shape, f32) for shape in lines),
        compiler_params=pltpu.CompilerParams(vmem_limit_bytes=60 * 2**20),
        cost_estimate=pl.CostEstimate(
            flops=2 * count * wide * 3 * groups * head_cols, bytes_accessed=100 * 2**20, transcendentals=0
        ),
        name="tail",
    )(*parts, x_all, grad_qkv, grad_out, gains)


def on_device_fused(
    tokens,
    segment_ids,
    w_query,
    w_key,
    w_value,
    w_out,
    w_gate,
    w_up,
    w_down,
    q_gain,
    k_gain,
    attn_gain,
    ffn_gain,
    cotangent,
):
    wide = tokens.shape[1]
    token_count = segment_ids.shape[0] * segment_ids.shape[1]
    head_cols = w_query.shape[1]
    positions = positions_of(segment_ids).reshape(token_count)
    cosine, sine = rotary_tables(positions)
    first = (jnp.arange(token_count, dtype=jnp.int32) - positions)[:, None]
    signed = jnp.where(jnp.arange(HD) < HD // 2, -sine, sine)
    branch, queries, keys, values, q_unit, k_unit, q_inverse, k_inverse, mixed, x_all = attention(
        tokens, w_query, w_key, w_value, w_out, q_gain, k_gain, cosine, signed, first
    )
    block_out, grad_hidden, grad_branch, gains, h_all, gd_all, own_gate, own_up, own_down, gate_all, up_all = ffn(
        tokens, branch, cotangent, attn_gain, ffn_gain, w_gate, w_up, w_down
    )
    grad_tokens, gains, grad_w_out, grad_qkv, part_gate, part_up, part_down = backward(
        grad_branch, grad_hidden, (queries, keys, values, mixed, q_unit, k_unit, q_inverse, k_inverse),
        first, cosine, signed, q_gain, k_gain, (w_query, w_key, w_value, w_out), gains, h_all, gd_all, gate_all, up_all, w_down,
        (own_gate, own_up, own_down),
    )
    *grad_weights, grad_ffn_gain, grad_attn_gain, grad_q_gain, grad_k_gain = weight_tail(
        (part_gate, part_up, part_down), x_all, grad_qkv, grad_w_out, gains
    )
    grad_w_gate, grad_w_up, grad_w_down, grad_w_query, grad_w_key, grad_w_value, grad_w_out = grad_weights
    return (
        block_out,
        grad_tokens,
        grad_w_query,
        grad_w_key,
        grad_w_value,
        grad_w_out,
        grad_w_gate,
        grad_w_up,
        grad_w_down,
        grad_q_gain.reshape(head_cols),
        grad_k_gain.reshape(head_cols),
        grad_attn_gain.reshape(wide),
        grad_ffn_gain.reshape(wide),
    )


def solution(mesh):
    placed = (
        P(("dp", "tensor"), None),
        P("dp", None),
        P(None, "tensor"),
        P(None, "tensor"),
        P(None, "tensor"),
        P("tensor", None),
        P(None, "tensor"),
        P(None, "tensor"),
        P("tensor", None),
        P("tensor"),
        P("tensor"),
        P(),
        P(),
        P(("dp", "tensor"), None),
    )
    return jax.shard_map(
        on_device_fused if dict(mesh.shape) == {"dp": 4, "tensor": 8} else on_device,
        mesh=mesh,
        in_specs=placed,
        out_specs=(
            P(("dp", "tensor"), None),
            P(("dp", "tensor"), None),
            P(None, "tensor"),
            P(None, "tensor"),
            P(None, "tensor"),
            P("tensor", None),
            P(None, "tensor"),
            P(None, "tensor"),
            P("tensor", None),
            P("tensor"),
            P("tensor"),
            P(),
            P(),
        ),
        check_vma=False,
    )
```

```python
import jax
import jax.numpy as jnp
from jax import lax
from jax.experimental import pallas as pl
from jax.experimental.pallas import tpu as pltpu
from jax.sharding import PartitionSpec as P

HD = 128


EPS = 1e-06
THETA = 500000.0


def rounded(value):
    return lax.optimization_barrier(value.astype(jnp.bfloat16)).astype(jnp.float32)


def dot_last(left, right):
    return lax.dot_general(
        left, right, (((1,), (1,)), ((), ())), preferred_element_type=jnp.float32
    )


def dot_first(left, right):
    return lax.dot_general(
        left, right, (((0,), (0,)), ((), ())), preferred_element_type=jnp.float32
    )


def positions_of(segment_ids):
    length = segment_ids.shape[-1]
    places = jnp.arange(length, dtype=jnp.int32)
    below = (segment_ids[:, None, :] < segment_ids[:, :, None]).astype(jnp.int32)
    return places[None, :] - jnp.sum(below, axis=2)


def rotary_tables(positions):
    half = HD // 2
    freq = THETA ** (-(jnp.arange(half, dtype=jnp.float32) * 2.0 / HD))
    angle = positions.astype(jnp.float32)[:, None] * freq[None, :]
    cosine = jnp.concatenate([jnp.cos(angle), jnp.cos(angle)], axis=1)
    sine = jnp.concatenate([jnp.sin(angle), jnp.sin(angle)], axis=1)
    return (cosine, sine)


def rotate(value, cosine, sine):
    half = value.shape[-1] // 2
    turned = jnp.concatenate([-value[..., half:], value[..., :half]], axis=-1)
    return value * cosine[:, None, :] + turned * sine[:, None, :]


def rotate_back(grad, cosine, sine):
    half = grad.shape[-1] // 2
    scaled = grad * sine[:, None, :]
    unturned = jnp.concatenate([scaled[..., half:], -scaled[..., :half]], axis=-1)
    return grad * cosine[:, None, :] + unturned


def norm_back(grad_out, unit, inverse, gain):
    inner = grad_out * gain
    return inverse * (inner - unit * jnp.mean(inner * unit, axis=1, keepdims=True))


def on_device(
    tokens,
    segment_ids,
    w_query,
    w_key,
    w_value,
    w_out,
    w_gate,
    w_up,
    w_down,
    q_gain,
    k_gain,
    attn_gain,
    ffn_gain,
    cotangent,
):
    row_count, full_width = tokens.shape
    head_cols = w_query.shape[1]
    heads_here = head_cols // HD
    ff_cols = w_gate.shape[1]
    seqs_here, seq_len = segment_ids.shape
    token_count = seqs_here * seq_len
    att_scale = HD ** (-0.5)
    whole_x = lax.all_gather(tokens, "tensor", axis=0, tiled=True)
    w_qkv = jnp.concatenate([w_query, w_key, w_value], axis=1)
    projected = jnp.dot(whole_x, w_qkv, preferred_element_type=jnp.float32)
    q_raw = projected[:, :head_cols]
    k_raw = projected[:, head_cols : 2 * head_cols]
    values = projected[:, 2 * head_cols :].astype(jnp.bfloat16)
    q_total, k_total = lax.psum(
        (jnp.sum(q_raw * q_raw, axis=1), jnp.sum(k_raw * k_raw, axis=1)), "tensor"
    )
    q_inverse = lax.rsqrt(q_total / full_width + EPS)[:, None]
    k_inverse = lax.rsqrt(k_total / full_width + EPS)[:, None]
    q_unit = q_raw * q_inverse
    k_unit = k_raw * k_inverse
    cosine, sine = rotary_tables(positions_of(segment_ids).reshape(token_count))
    queries = rotate((q_unit * q_gain).reshape(token_count, heads_here, HD), cosine, sine).astype(
        jnp.bfloat16
    )
    keys = rotate((k_unit * k_gain).reshape(token_count, heads_here, HD), cosine, sine).astype(
        jnp.bfloat16
    )
    shaped = (seqs_here, seq_len, heads_here, HD)
    query_seqs = queries.reshape(shaped)
    key_seqs = keys.reshape(shaped)
    value_seqs = values.reshape(shaped)
    places = jnp.arange(seq_len, dtype=jnp.int32)
    causal = places[:, None] >= places[None, :]

    def scores_of(query_block, key_block, seg_row):
        raw = (
            jnp.einsum("qhd,khd->hqk", query_block, key_block, preferred_element_type=jnp.float32)
            * att_scale
        )
        allowed = causal & (seg_row[:, None] == seg_row[None, :])
        return jnp.where(allowed[None], raw, -1e30)

    def attend(pieces):
        query_block, key_block, value_block, seg_row = pieces
        scores = scores_of(query_block, key_block, seg_row)
        top = jnp.max(scores, axis=-1, keepdims=True)
        expo = jnp.exp(scores - top)
        total = jnp.sum(expo, axis=-1, keepdims=True)
        probs = (expo / total).astype(jnp.bfloat16)
        mixed_block = jnp.einsum(
            "hqk,khd->qhd", probs, value_block, preferred_element_type=jnp.float32
        )
        return (mixed_block.astype(jnp.bfloat16), (top + jnp.log(total))[..., 0])

    mixed, log_total = lax.map(attend, (query_seqs, key_seqs, value_seqs, segment_ids))
    mixed = mixed.reshape(token_count, head_cols)
    x_rows = tokens.astype(jnp.float32)
    branch = lax.psum_scatter(
        jnp.dot(mixed, w_out, preferred_element_type=jnp.float32).astype(jnp.bfloat16),
        "tensor",
        scatter_dimension=0,
        tiled=True,
    ).astype(jnp.float32)
    a_inverse = lax.rsqrt(jnp.mean(branch * branch, axis=1, keepdims=True) + EPS)
    hidden = x_rows + branch * a_inverse * attn_gain
    h_low = lax.all_gather(hidden.astype(jnp.bfloat16), "tensor", axis=0, tiled=True)
    a_unit = branch * a_inverse
    w_gate_up = jnp.concatenate([w_gate, w_up], axis=1)
    gate_up = jnp.dot(h_low, w_gate_up, preferred_element_type=jnp.float32)
    gate = gate_up[:, :ff_cols]
    up = gate_up[:, ff_cols:]
    sigma_gate = jax.nn.sigmoid(gate)
    silu_gate = gate * sigma_gate
    act = (silu_gate * up).astype(jnp.bfloat16)
    down = lax.psum_scatter(
        jnp.dot(act, w_down, preferred_element_type=jnp.float32).astype(jnp.bfloat16),
        "tensor",
        scatter_dimension=0,
        tiled=True,
    ).astype(jnp.float32)
    f_inverse = lax.rsqrt(jnp.mean(down * down, axis=1, keepdims=True) + EPS)
    f_unit = down * f_inverse
    block_out = (hidden + f_unit * ffn_gain).astype(jnp.bfloat16)
    grad_out = cotangent.astype(jnp.float32)
    grad_ffn_part = jnp.sum(grad_out * f_unit, axis=0)
    grad_down = norm_back(grad_out, f_unit, f_inverse, ffn_gain).astype(jnp.bfloat16)
    grad_down_all = lax.all_gather(grad_down, "tensor", axis=0, tiled=True)
    grad_act = dot_last(grad_down_all, w_down)
    grad_w_down = dot_first(act, grad_down_all)
    grad_gate = grad_act * up * sigma_gate * (1.0 + gate * (1.0 - sigma_gate))
    grad_up = grad_act * silu_gate
    grad_gate_up = jnp.concatenate([grad_gate, grad_up], axis=1).astype(jnp.bfloat16)
    grad_w_gate_up = dot_first(h_low, grad_gate_up)
    grad_hidden = grad_out + lax.psum_scatter(
        dot_last(grad_gate_up, w_gate_up).astype(jnp.bfloat16), "tensor", scatter_dimension=0, tiled=True
    ).astype(jnp.float32)
    grad_attn_part = jnp.sum(grad_hidden * a_unit, axis=0)
    grad_branch = norm_back(grad_hidden, a_unit, a_inverse, attn_gain).astype(jnp.bfloat16)
    grad_branch_all = lax.all_gather(grad_branch, "tensor", axis=0, tiled=True)
    grad_w_out = dot_first(mixed, grad_branch_all)
    grad_mixed = dot_last(grad_branch_all, w_out).astype(jnp.bfloat16).reshape(shaped)

    def attend_back(pieces):
        query_block, key_block, value_block, seg_row, log_block, grad_block = pieces
        scores = scores_of(query_block, key_block, seg_row)
        probs = jnp.exp(scores - log_block[..., None])
        grad_probs = jnp.einsum(
            "qhd,khd->hqk", grad_block, value_block, preferred_element_type=jnp.float32
        )
        grad_scores = (
            probs * (grad_probs - jnp.sum(probs * grad_probs, axis=-1, keepdims=True))
        ).astype(jnp.bfloat16)
        grad_query = (
            jnp.einsum("hqk,khd->qhd", grad_scores, key_block, preferred_element_type=jnp.float32)
            * att_scale
        )
        grad_key = (
            jnp.einsum("hqk,qhd->khd", grad_scores, query_block, preferred_element_type=jnp.float32)
            * att_scale
        )
        grad_value = jnp.einsum(
            "hqk,qhd->khd",
            probs.astype(jnp.bfloat16),
            grad_block,
            preferred_element_type=jnp.float32,
        )
        return (grad_query, grad_key, grad_value.astype(jnp.bfloat16))

    grad_query, grad_key, grad_value = lax.map(
        attend_back, (query_seqs, key_seqs, value_seqs, segment_ids, log_total, grad_mixed)
    )
    grad_q_normed = rotate_back(
        rounded(grad_query.reshape(token_count, heads_here, HD)), cosine, sine
    ).reshape(token_count, head_cols)
    grad_k_normed = rotate_back(
        rounded(grad_key.reshape(token_count, heads_here, HD)), cosine, sine
    ).reshape(token_count, head_cols)
    grad_q_gain = jnp.sum(grad_q_normed * q_unit, axis=0)
    grad_k_gain = jnp.sum(grad_k_normed * k_unit, axis=0)
    inner_q = grad_q_normed * q_gain
    inner_k = grad_k_normed * k_gain
    q_inner_sum, k_inner_sum = lax.psum(
        (jnp.sum(inner_q * q_unit, axis=1), jnp.sum(inner_k * k_unit, axis=1)), "tensor"
    )
    grad_q_raw = q_inverse * (inner_q - q_unit * (q_inner_sum / full_width)[:, None])
    grad_k_raw = k_inverse * (inner_k - k_unit * (k_inner_sum / full_width)[:, None])
    grad_qkv = jnp.concatenate(
        [
            grad_q_raw.astype(jnp.bfloat16),
            grad_k_raw.astype(jnp.bfloat16),
            grad_value.reshape(token_count, head_cols),
        ],
        axis=1,
    )
    grad_w_qkv = dot_first(whole_x, grad_qkv)
    grad_tokens = grad_hidden + lax.psum_scatter(
        dot_last(grad_qkv, w_qkv).astype(jnp.bfloat16), "tensor", scatter_dimension=0, tiled=True
    ).astype(jnp.float32)
    grad_w_qkv, grad_w_out, grad_w_gate_up, grad_w_down = [
        lax.psum(part.astype(jnp.bfloat16), "dp").astype(jnp.float32)
        for part in (grad_w_qkv, grad_w_out, grad_w_gate_up, grad_w_down)
    ]
    grad_q_gain, grad_k_gain = lax.psum((grad_q_gain, grad_k_gain), "dp")
    grad_attn_gain, grad_ffn_gain = lax.psum((grad_attn_part, grad_ffn_part), ("dp", "tensor"))
    return (
        block_out,
        grad_tokens,
        grad_w_qkv[:, :head_cols],
        grad_w_qkv[:, head_cols : 2 * head_cols],
        grad_w_qkv[:, 2 * head_cols :],
        grad_w_out,
        grad_w_gate_up[:, :ff_cols],
        grad_w_gate_up[:, ff_cols:],
        grad_w_down,
        grad_q_gain,
        grad_k_gain,
        grad_attn_gain,
        grad_ffn_gain,
    )


MESH = pl.DeviceIdType.MESH
LANES = 2


def places_of():
    d = lax.axis_index("dp")
    t = lax.axis_index("tensor")
    z, c = lax.div(t, 2), lax.rem(t, 2)
    dx = d + 1 - 2 * lax.rem(d, 2)
    dy = lax.rem(d + 2, 4)
    zs = (z, z + 1 - 2 * lax.rem(z, 2), lax.rem(z + 2, 4), 3 - z)
    inner = lax.rem(z + 1, 4) >= 2
    return d, dx, dy, zs, c, inner


def remote(src, dst, send, recv, dp, tensor):
    return pltpu.make_async_remote_copy(
        src_ref=src, dst_ref=dst, send_sem=send, recv_sem=recv, device_id=(dp, tensor), device_id_type=MESH
    )


def enter(d, zs, c, dx=None, dy=None):
    barrier = pltpu.get_barrier_semaphore()
    peers = [(d, 2 * zs[r] + c) for r in (1, 2, 3)] + [(d, 2 * zs[0] + 1 - c)]
    if dx is not None:
        peers += [(dx, 2 * zs[0] + c), (dy, 2 * zs[0] + c)]
    for peer in peers:
        pl.semaphore_signal(barrier, inc=1, device_id=peer, device_id_type=MESH)
    pl.semaphore_wait(barrier, len(peers))


class Gather:
    def __init__(self, full, send, recv, place):
        self.full, self.send, self.recv = full, send, recv
        self.d, _, _, self.zs, self.c, self.inner = place
        self.t = 2 * self.zs[0] + self.c

    def lane(self, r):
        return self.full.at[2 * self.zs[r] + self.c]

    def other(self, r):
        return self.full.at[2 * self.zs[r] + 1 - self.c]

    def to_z(self, r, k, via):
        return remote(self.lane(r), self.lane(r), self.send.at[via if r == 0 else 7], self.recv.at[k], self.d, 2 * self.zs[via] + self.c)

    def to_core(self, r):
        return remote(self.lane(r), self.lane(r), self.send.at[0 if r == 0 else 3 + r], self.recv.at[4 + r], self.d, 2 * self.zs[0] + 1 - self.c)

    def start(self):
        self.to_z(0, 2, 2).start()
        self.to_z(0, 1, 1).start()
        self.to_core(0).start()

    def start_inner(self):
        @pl.when(self.inner)
        def _():
            self.to_z(0, 2, 2).wait_send()
            self.to_z(0, 3, 3).start()

    def arrive(self, r):
        self.to_z(r, r, r).wait_recv()
        if r == 2:
            @pl.when(self.inner)
            def _():
                self.to_z(2, 3, 1).start()
        self.to_core(r).start()

    def ready(self, r):
        remote(self.other(r), self.other(r), self.send.at[0], self.recv.at[4 + r], self.d, self.t).wait_recv()

    def finish(self):
        @pl.when(jnp.logical_not(self.inner))
        def _():
            self.to_z(0, 2, 2).wait_send()

        @pl.when(self.inner)
        def _():
            self.to_z(0, 3, 3).wait_send()
            self.to_z(2, 3, 1).wait_send()

        self.to_z(0, 1, 1).wait_send()
        for r in range(4):
            self.to_core(r).wait_send()


class Scatter:
    def __init__(self, parts, pair, land, send, recv, place):
        self.parts, self.pair, self.land, self.send, self.recv = parts, pair, land, send, recv
        self.d, _, _, self.zs, self.c, self.inner = place
        self.t = 2 * self.zs[0] + self.c
        self.half = parts.shape[2] // 2

    def cut(self, ref, at, r, h):
        if h is None:
            return ref.at[at]
        return ref.at[at, :, pl.ds(h * self.half, self.half)]

    def mine(self, r, h=None):
        return self.cut(self.parts, 2 * self.zs[r] + self.c, r, h)

    def to_core(self, r, h=None):
        src = self.cut(self.parts, 2 * self.zs[r] + 1 - self.c, r, h)
        at = 8 if h == 1 else r
        return remote(src, self.cut(self.pair, r, r, h), self.send.at[at], self.recv.at[at], self.d, 2 * self.zs[0] + 1 - self.c)

    def start_core(self, r):
        for h in (0, 1) if r == 3 else (None,):
            self.to_core(r, h).start()

    def to_z(self, r, k, via, h=None):
        return remote(
            self.mine(r, h), self.cut(self.land, k, r, h), self.send.at[SENT[r, h]], self.recv.at[LANDED[k, h]], self.d,
            2 * self.zs[via] + self.c,
        )

    def add_pair(self, r, h=None):
        halves = (0, 1) if r == 3 and h is None else (h,)
        for h in halves:
            self.to_core(r, h).wait_recv()
            add_into(self.mine(r, h), self.cut(self.pair, r, r, h))

    def pass_on(self, r, h=None):
        if r == 1:
            self.to_z(1, 1, 1).start()
        if r == 2:
            @pl.when(jnp.logical_not(self.inner))
            def _():
                for h in range(2):
                    self.to_z(2, 2, 2, h).start()
        if r == 3:
            halves = (0, 1) if h is None else (h,)

            @pl.when(self.inner)
            def _():
                for h in halves:
                    self.to_z(3, 3, 3, h).start()

            @pl.when(jnp.logical_not(self.inner))
            def _():
                for h in halves:
                    self.to_z(3, 0, 1, h).start()

    def relay(self):
        @pl.when(self.inner)
        def _():
            for h in range(2):
                self.to_z(3, 0, 1, h).wait_recv()
                add_into(self.mine(2, h), self.cut(self.land, 0, 0, h))
                self.to_z(2, 2, 2, h).start()

    def arrived(self):
        self.to_z(1, 1, 1).wait_recv()

        @pl.when(self.inner)
        def _():
            for h in range(2):
                self.to_z(3, 3, 3, h).wait_recv()

        @pl.when(jnp.logical_not(self.inner))
        def _():
            self.land[3] = jnp.zeros(self.land.shape[1:], self.land.dtype)

        for h in range(2):
            self.to_z(2, 2, 2, h).wait_recv()

    def total(self, rows):
        own = self.parts[2 * self.zs[0] + self.c, rows, :].astype(jnp.float32)
        return own + self.land[1, rows, :].astype(jnp.float32) + self.land[2, rows, :].astype(jnp.float32) + self.land[3, rows, :].astype(jnp.float32)

    def finish(self):
        for r in range(3):
            self.to_core(r).wait_send()
        self.to_z(1, 1, 1).wait_send()
        for h in range(2):
            self.to_core(3, h).wait_send()
            self.to_z(2, 2, 2, h).wait_send()
            self.to_z(3, 3, 3, h).wait_send()


SENT = {(1, None): 5, (2, 0): 6, (2, 1): 9, (3, 0): 7, (3, 1): 10}
LANDED = {(1, None): 5, (2, 0): 6, (2, 1): 9, (3, 0): 7, (3, 1): 10, (0, 0): 4, (0, 1): 11}


def add_into(into, other):
    rows = into.shape[0]

    def step(i, carry):
        at = pl.ds(pl.multiple_of(i * 32, 32), 32)
        into[at, :] = (into[at, :].astype(jnp.float32) + other[at, :].astype(jnp.float32)).astype(into.dtype)
        return carry

    lax.fori_loop(0, rows // 32, step, 0)


class Loads:
    def __init__(self, pairs, sem):
        self.copies = [pltpu.make_async_copy(far, near, sem.at[n]) for n, (far, near) in enumerate(pairs)]

    def start(self):
        for copy in self.copies:
            copy.start()

    def wait(self, *which):
        for n in which:
            self.copies[n].wait()


class Spread:
    def __init__(self, full, whole, send, recv, own_sem, place):
        self.full, self.whole, self.send, self.recv, self.own_sem = full, whole, send, recv, own_sem
        self.d, self.dx, self.dy, self.zs, self.c, _ = place
        self.t = 2 * self.zs[0] + self.c
        self.seen = set()

    def ready(self, k, r):
        other = self.whole.at[1 + k, 2 * self.zs[r] + 1 - self.c]
        remote(other, other, self.send.at[0], self.recv.at[12 + k * 4 + r], self.d, self.t).wait_recv()
        self.seen.add((k, r))

    def slot(self, g, r):
        return self.whole.at[g, 2 * self.zs[r] + self.c]

    def own(self, r, k):
        src = self.full.at[2 * self.zs[r] + self.c]
        return remote(src, self.slot(1 + k, r), self.send.at[k * 4 + r], self.recv.at[k * 4 + r], (self.dx, self.dy)[k], self.t)

    def start(self, r):
        self.own(r, 0).start()
        self.own(r, 1).start()

    def hop(self, r):
        group, target = (1, self.dy) if r in (0, 3) else (2, self.dx)
        return remote(self.slot(group, r), self.slot(3, r), self.send.at[8 + r], self.recv.at[8 + r], target, self.t)

    def to_core(self, r, k):
        return remote(self.slot(1 + k, r), self.slot(1 + k, r), self.send.at[12 + k * 4 + r], self.recv.at[12 + k * 4 + r], self.d, 2 * self.zs[0] + 1 - self.c)

    def pass_on(self, r):
        self.own(r, 0).wait_recv()
        self.own(r, 1).wait_recv()
        self.hop(r).start()
        self.to_core(r, 0).start()
        self.to_core(r, 1).start()

    def last(self, r):
        self.hop(r).wait_recv()
        self.to_core(r, 2).start()

    def keep(self):
        return pltpu.make_async_copy(self.full, self.whole.at[0], self.own_sem)

    def finish(self):
        for r in range(4):
            self.own(r, 0).wait_send()
            self.own(r, 1).wait_send()
            self.hop(r).wait_send()
            for k in range(3):
                self.to_core(r, k).wait_send()
                if (k, r) not in self.seen:
                    self.to_core(r, k).wait_recv()
        self.keep().wait()


def dot_tn(left, right):
    return lax.dot_general(left, right, (((0,), (0,)), ((), ())), preferred_element_type=jnp.float32)


def dot_nt(left, right):
    return lax.dot_general(left, right, (((1,), (1,)), ((), ())), preferred_element_type=jnp.float32)


def ffn_kernel(
    x_ref, br_ref, cot_ref, again_ref, gain_ref, wg_hbm, wu_hbm, wd_hbm,
    bo_ref, gh_ref, gb_ref, gains_ref, hall_ref, gdall_ref, og_ref, ou_ref, od_ref, gate_all, up_all,
    hfull, gfull, hid_ref, sums, gate, up, act, gg, gu, parts, pair, land, hbuf, gbuf, ubuf, wg_ref, wu_ref, wd_ref,
    ag_send, ag_recv, rs_send, rs_recv, xy_send, xy_recv, own_sem, load_sem, store_sem, out_sem, weight_sem,
):
    place = places_of()
    d, dx, dy, zs, c, inner = place
    t = 2 * zs[0] + c
    weights = Loads(((wg_hbm, wg_ref), (wu_hbm, wu_ref), (wd_hbm, wd_ref)), weight_sem)
    weights.start()
    width = wg_ref.shape[1]
    rows, wide = x_ref.shape
    ft, dt = 512, 1024
    step_rows = 32
    a_gain, gain = again_ref[...], gain_ref[...]

    def opening(i, carry):
        at = pl.ds(pl.multiple_of(i * step_rows, step_rows), step_rows)
        branch = br_ref[at, :]
        inverse = lax.rsqrt(jnp.mean(branch * branch, axis=1, keepdims=True) + EPS)
        hidden = x_ref[at, :].astype(jnp.float32) + branch * inverse * a_gain
        hid_ref[at, :] = hidden
        hfull[t, at, :] = hidden.astype(jnp.bfloat16)
        return carry

    lax.fori_loop(0, rows // step_rows, opening, 0)
    enter(d, zs, c, dx, dy)

    def unit_forward(zz, after=None):
        both = pl.ds(2 * zz, 2)
        at = pl.ds(pl.multiple_of(zz * 2 * rows, 2 * rows), 2 * rows)

        def mid(j, carry):
            cols = pl.ds(pl.multiple_of(j * ft, ft), ft)
            block = hfull[both].reshape(2 * rows, wide)
            g = jnp.dot(block, wg_ref[:, cols], preferred_element_type=jnp.float32)
            u = jnp.dot(block, wu_ref[:, cols], preferred_element_type=jnp.float32)
            gate[at, cols] = g
            up[at, cols] = u
            act[at, cols] = (g * jax.nn.sigmoid(g) * u).astype(jnp.bfloat16)
            return carry

        lax.fori_loop(0, width // ft, mid, 0)

        def out(j, carry):
            cols = pl.ds(pl.multiple_of(j * dt, dt), dt)
            p = jnp.dot(act[at, :], wd_ref[:, cols], preferred_element_type=jnp.float32)
            parts[both, :, cols] = p.astype(jnp.bfloat16).reshape(2, rows, dt)
            return carry

        if after is None:
            lax.fori_loop(0, wide // dt, out, 0)
        else:
            for j in range(wide // dt):
                out(j, 0)
                after(j)

    def unit_backward(zz, after=None):
        both = pl.ds(2 * zz, 2)
        at = pl.ds(pl.multiple_of(zz * 2 * rows, 2 * rows), 2 * rows)

        def mid(j, carry):
            cols = pl.ds(pl.multiple_of(j * ft, ft), ft)
            block = gfull[both].reshape(2 * rows, wide)
            ga = dot_nt(block, wd_ref[cols, :])
            g, u = gate[at, cols], up[at, cols]
            s = jax.nn.sigmoid(g)
            gg[at, cols] = (ga * u * s * (1.0 + g * (1.0 - s))).astype(jnp.bfloat16)
            gu[at, cols] = (ga * (g * s)).astype(jnp.bfloat16)
            return carry

        lax.fori_loop(0, width // ft, mid, 0)

        def out(j, carry):
            cols = pl.ds(pl.multiple_of(j * dt, dt), dt)
            p = dot_nt(gg[at, :], wg_ref[cols, :]) + dot_nt(gu[at, :], wu_ref[cols, :])
            parts[both, :, cols] = p.astype(jnp.bfloat16).reshape(2, rows, dt)
            return carry

        if after is None:
            lax.fori_loop(0, wide // dt, out, 0)
        else:
            for j in range(wide // dt):
                out(j, 0)
                after(j)

    def own_copies(i, down):
        slot = pl.ds(pl.multiple_of(lax.rem(i, 4) * 256, 256), 256)
        at = pl.ds(pl.multiple_of(i * 256, 256), 256)
        outs = (od_ref.at[at, pl.ds(0, width)], od_ref.at[at, pl.ds(width, width)]) if down else (og_ref.at[at, :], ou_ref.at[at, :])
        return [
            pltpu.make_async_copy(buf.at[slot, :], out, out_sem.at[n, lax.rem(i, 4)])
            for n, (buf, out) in enumerate(zip((gate, up), outs))
        ]

    def own_in(i, carry):
        slot = pl.ds(pl.multiple_of(lax.rem(i, 4) * 256, 256), 256)
        at = pl.ds(pl.multiple_of(i * 256, 256), 256)

        @pl.when(i >= 4)
        def _():
            for copy in own_copies(i - 4, False):
                copy.wait()

        h = hfull[:, :, at].reshape(8 * rows, 256)
        gate[slot, :] = dot_tn(h, gg[...])
        up[slot, :] = dot_tn(h, gu[...])
        for copy in own_copies(i, False):
            copy.start()
        return carry

    def own_down(i, carry):
        at = pl.ds(pl.multiple_of(i * 256, 256), 256)
        for copy in own_copies(i + 4, False):
            copy.wait()
        left = act[:, at]
        for n, buf in enumerate((gate, up)):
            buf[at, :] = dot_tn(left, gfull[:, :, n * width : (n + 1) * width].reshape(8 * rows, width))
        for copy in own_copies(i, True):
            copy.start()
        return carry

    done = []

    def fill(chunks):
        def load(n):
            k, r = chunks[n]
            slot = (base + n) % 2
            return pltpu.make_async_copy(hall_ref.at[1 + k, pl.ds(2 * zs[r], 2)], hbuf.at[slot], load_sem.at[slot])

        base = len(done)
        for n, (k, r) in enumerate(chunks):
            slot = len(done) % 2
            if n == 0:
                xy_h.ready(k, r)
                load(0).start()
            load(n).wait()
            if n + 1 < len(chunks):
                xy_h.ready(*chunks[n + 1])
                load(n + 1).start()
            if len(done) >= 2:
                for copy in stores(len(done) - 2):
                    copy.wait()

            def tile(j, carry):
                cols = pl.ds(pl.multiple_of(j * ft, ft), ft)
                block = hbuf[slot].reshape(2 * rows, wide)
                gbuf[slot, :, cols] = jnp.dot(block, wg_ref[:, cols], preferred_element_type=jnp.float32).astype(jnp.bfloat16)
                ubuf[slot, :, cols] = jnp.dot(block, wu_ref[:, cols], preferred_element_type=jnp.float32).astype(jnp.bfloat16)
                return carry

            lax.fori_loop(0, width // ft, tile, 0)
            done.append((k, r))
            for copy in stores(len(done) - 1):
                copy.start()

    def stores(n):
        k, r = done[n]
        at = pl.ds(pl.multiple_of(zs[r] * 2 * rows, 2 * rows), 2 * rows)
        return [
            pltpu.make_async_copy(buf.at[n % 2], out.at[k, at, :], store_sem.at[m, n % 2])
            for m, (buf, out) in enumerate(((gbuf, gate_all), (ubuf, up_all)))
        ]

    def phase(p, full, whole, unit):
        ag = Gather(full, ag_send.at[p], ag_recv.at[p], place)
        rs = Scatter(parts, pair.at[p], land.at[p], rs_send.at[p], rs_recv.at[p], place)
        xy = xy_h if p == 0 else xy_g
        ag.start()
        xy.start(0)
        ag.ready(0)
        if p == 0:
            weights.wait(0, 1, 2)
        unit(zs[0])
        rs.start_core(0)
        if p == 1:
            fill([(0, 3), (1, 3), (2, 0), (2, 2)])
        xy.pass_on(0)
        ag.start_inner()
        ag.arrive(2)
        xy.start(2)
        ag.arrive(1)
        xy.start(1)
        ag.ready(2)
        unit(zs[2])
        rs.start_core(2)
        ag.ready(1)
        unit(zs[1])
        rs.start_core(1)
        rs.add_pair(2)
        rs.pass_on(2)
        rs.add_pair(1)
        rs.pass_on(1)
        ag.arrive(3)
        xy.start(3)
        ag.ready(3)
        unit(zs[3], lambda j: rs.to_core(3, j).start())
        for h in range(2):
            rs.add_pair(3, h)
            rs.pass_on(3, h)
        xy.keep().start()
        rs.add_pair(0)
        if p == 0:
            fill([(0, 0), (1, 0)])
            xy.pass_on(2)
            xy.pass_on(1)
            fill([(0, 2)])
        else:
            xy.pass_on(2)
            xy.pass_on(1)
            lax.fori_loop(0, 8, own_in, 0)
        rs.relay()
        if p == 0:
            fill([(1, 2), (0, 1), (1, 1)])
        else:
            xy.pass_on(3)
            lax.fori_loop(0, 4, own_down, 0)
            xy.last(0)
            fill([(2, 1), (2, 3)])
            xy.last(2)
            xy.last(1)
        rs.arrived()
        return ag, rs

    xy_h = Spread(hfull, hall_ref, xy_send.at[0], xy_recv.at[0], own_sem.at[0], place)
    xy_g = Spread(gfull, gdall_ref, xy_send.at[1], xy_recv.at[1], own_sem.at[1], place)
    ag, rs = phase(0, hfull, hall_ref, unit_forward)
    sums[...] = jnp.zeros_like(sums)

    def middle(i, carry):
        at = pl.ds(pl.multiple_of(i * step_rows, step_rows), step_rows)
        down = rs.total(at)
        inverse = lax.rsqrt(jnp.mean(down * down, axis=1, keepdims=True) + EPS)
        unit = down * inverse
        bo_ref[at, :] = (hid_ref[at, :] + unit * gain).astype(jnp.bfloat16)
        grad = cot_ref[at, :].astype(jnp.float32)
        sums[0:1, :] += jnp.sum(grad * unit, axis=0, keepdims=True)
        inner_grad = grad * gain
        gfull[t, at, :] = (inverse * (inner_grad - unit * jnp.mean(inner_grad * unit, axis=1, keepdims=True))).astype(jnp.bfloat16)
        return carry

    lax.fori_loop(0, rows // step_rows, middle, 0)
    ag.finish()
    rs.finish()
    xy_h.pass_on(3)
    for r in range(4):
        xy_h.last(r)
    ag, rs = phase(1, gfull, gdall_ref, unit_backward)

    def ending(i, carry):
        at = pl.ds(pl.multiple_of(i * step_rows, step_rows), step_rows)
        grad = cot_ref[at, :].astype(jnp.float32) + rs.total(at)
        gh_ref[at, :] = grad
        branch = br_ref[at, :]
        inverse = lax.rsqrt(jnp.mean(branch * branch, axis=1, keepdims=True) + EPS)
        unit = branch * inverse
        sums[1:2, :] += jnp.sum(grad * unit, axis=0, keepdims=True)
        inner_grad = grad * a_gain
        gb_ref[at, :] = (inverse * (inner_grad - unit * jnp.mean(inner_grad * unit, axis=1, keepdims=True))).astype(jnp.bfloat16)
        return carry

    lax.fori_loop(0, rows // step_rows, ending, 0)
    for i in range(wide // HD):
        gains_ref[i : i + 1, :] = sums[0:1, i * HD : (i + 1) * HD]
        gains_ref[wide // HD + i : wide // HD + i + 1, :] = sums[1:2, i * HD : (i + 1) * HD]
    ag.finish()
    rs.finish()
    xy_g.last(3)
    xy_h.finish()
    for i in range(4):
        for copy in own_copies(i, True):
            copy.wait()
    for n in (len(done) - 2, len(done) - 1):
        for copy in stores(n):
            copy.wait()
    xy_g.finish()


def ffn(x_own, branch, cot, attn_gain, ffn_gain, w_gate, w_up, w_down):
    rows, wide = x_own.shape
    width = w_gate.shape[1]
    groups, world = 4, 8
    vmem = pl.BlockSpec(memory_space=pltpu.VMEM)
    anywhere = pl.BlockSpec(memory_space=pl.ANY)
    bf, f32 = jnp.bfloat16, jnp.float32
    whole = jax.ShapeDtypeStruct((groups, world, rows, wide), bf)
    others = jax.ShapeDtypeStruct((groups - 1, world * rows, width), bf)
    dma = pltpu.SemaphoreType.DMA
    return pl.pallas_call(
        ffn_kernel,
        out_shape=(
            jax.ShapeDtypeStruct((rows, wide), bf),
            jax.ShapeDtypeStruct((rows, wide), f32),
            jax.ShapeDtypeStruct((rows, wide), bf),
            jax.ShapeDtypeStruct((2 * wide // HD, HD), f32),
            whole,
            whole,
            jax.ShapeDtypeStruct((wide, width), f32),
            jax.ShapeDtypeStruct((wide, width), f32),
            jax.ShapeDtypeStruct((width, wide), f32),
            others,
            others,
        ),
        in_specs=[vmem] * 5 + [anywhere] * 3,
        out_specs=(vmem,) * 4 + (anywhere,) * 7,
        scratch_shapes=[
            pltpu.VMEM((world, rows, wide), bf),
            pltpu.VMEM((world, rows, wide), bf),
            pltpu.VMEM((rows, wide), f32),
            pltpu.VMEM((8, wide), f32),
            pltpu.VMEM((world * rows, width), f32),
            pltpu.VMEM((world * rows, width), f32),
            pltpu.VMEM((world * rows, width), bf),
            pltpu.VMEM((world * rows, width), bf),
            pltpu.VMEM((world * rows, width), bf),
            pltpu.VMEM((world, rows, wide), bf),
            pltpu.VMEM((2, 4, rows, wide), bf),
            pltpu.VMEM((2, 4, rows, wide), bf),
            pltpu.VMEM((2, 2, rows, wide), bf),
            pltpu.VMEM((2, 2 * rows, width), bf),
            pltpu.VMEM((2, 2 * rows, width), bf),
            pltpu.VMEM((wide, width), bf),
            pltpu.VMEM((wide, width), bf),
            pltpu.VMEM((width, wide), bf),
            dma((2, 8)),
            dma((2, 8)),
            dma((2, 12)),
            dma((2, 12)),
            dma((2, 24)),
            dma((2, 24)),
            dma((2,)),
            dma((2,)),
            dma((2, 2)),
            dma((2, 4)),
            dma((3,)),
        ],
        compiler_params=pltpu.CompilerParams(
            collective_id=2, has_side_effects=True, vmem_limit_bytes=60 * 2**20
        ),
        name="ffn",
    )(x_own, branch, cot, attn_gain.reshape(1, wide), ffn_gain.reshape(1, wide), w_gate, w_up, w_down)


WINDOW = 3


class Exchange:
    def __init__(self, block, land, send, recv, place):
        self.block, self.land, self.send, self.recv = block, land, send, recv
        self.d, _, _, self.zs, self.c, _ = place
        self.t = 2 * self.zs[0] + self.c

    def copies(self):
        out = []
        for r in range(4):
            for k in range(2):
                if r == 0 and k == 0:
                    continue
                at = 4 * k + r
                core = self.c if k == 0 else 1 - self.c
                out.append((2 * self.zs[r] + core, at))
        return out

    def start(self):
        for peer, at in self.copies():
            remote(self.block, self.land.at[self.t], self.send.at[at], self.recv.at[at], self.d, peer).start()

    def wait(self):
        for peer, at in self.copies():
            remote(self.block, self.land.at[peer], self.send.at[at], self.recv.at[at], self.d, peer).wait()


def enter_all(d, zs, c, dx, dy):
    barrier = pltpu.get_barrier_semaphore()
    peers = [(d, 2 * zs[r] + c) for r in (1, 2, 3)] + [(d, 2 * zs[r] + 1 - c) for r in range(4)]
    peers += [(dx, 2 * zs[0] + c), (dy, 2 * zs[0] + c)]
    for peer in peers:
        pl.semaphore_signal(barrier, inc=1, device_id=peer, device_id_type=MESH)
    pl.semaphore_wait(barrier, len(peers))


def put_column(stat, base, zz, square):
    rows = square.shape[0]
    folded = square[:, :HD]
    for h in range(1, square.shape[1] // HD):
        folded = folded + square[:, h * HD : (h + 1) * HD]
    line = jnp.sum(folded.T, axis=0, keepdims=True)
    for i in range(rows // HD):
        stat[pl.ds(base + 2 * zz + i, 1), :] = line[:, i * HD : (i + 1) * HD]


def get_column(stat_row, count):
    return jnp.broadcast_to(stat_row, (count, HD)).T


def attn_kernel(
    x_ref, wq_hbm, wk_hbm, wv_hbm, wo_hbm, qg_ref, kg_ref, cos_ref, sin_ref, first_ref,
    br_ref, q_out, k_out, v_out, qu_out, ku_out, rq_out, rk_out, mixed_out, xall_ref,
    xfull, parts, pair, land, stat, stats, wq_ref, wk_ref, wv_ref, wo_ref,
    ag_send, ag_recv, rs_send, rs_recv, xy_send, xy_recv, st_send, st_recv, own_sem, weight_sem,
):
    place = places_of()
    d, dx, dy, zs, c, inner = place
    t = 2 * zs[0] + c
    rows, wide = x_ref.shape
    span = 2 * rows
    weights = Loads(((wq_hbm, wq_ref), (wk_hbm, wk_ref), (wv_hbm, wv_ref), (wo_hbm, wo_ref)), weight_sem)
    weights.start()
    heads = wq_ref.shape[1] // HD
    xfull[t] = x_ref[...]
    enter_all(d, zs, c, dx, dy)
    ag = Gather(xfull, ag_send, ag_recv, place)
    rs = Scatter(parts, pair, land, rs_send, rs_recv, place)
    xy = Spread(xfull, xall_ref, xy_send, xy_recv, own_sem, place)
    ex = Exchange(stat, stats, st_send, st_recv, place)

    def at_of(zz):
        return pl.ds(pl.multiple_of(zz * span, span), span)

    def project_qk(zz):
        block = xfull[pl.ds(2 * zz, 2)].reshape(span, wide)
        for w_ref, out, base in ((wq_ref, qu_out, 0), (wk_ref, ku_out, 8)):
            raw = jnp.dot(block, w_ref[...], preferred_element_type=jnp.float32)
            out[at_of(zz), :] = raw
            put_column(stat, base, zz, raw * raw)

    def project_v(zz):
        block = xfull[pl.ds(2 * zz, 2)].reshape(span, wide)
        v_out[at_of(zz), :] = jnp.dot(block, wv_ref[...], preferred_element_type=jnp.float32).astype(jnp.bfloat16)

    ag.start()
    xy.start(0)
    ag.ready(0)
    weights.wait(0, 1, 2, 3)
    project_qk(zs[0])
    project_v(zs[0])
    xy.pass_on(0)
    ag.start_inner()
    ag.arrive(2)
    xy.start(2)
    ag.arrive(1)
    xy.start(1)
    ag.ready(2)
    project_qk(zs[2])
    ag.ready(1)
    project_qk(zs[1])
    project_v(zs[2])
    ag.arrive(3)
    xy.start(3)
    ag.ready(3)
    project_qk(zs[3])
    ex.start()
    project_v(zs[1])
    project_v(zs[3])
    xy.keep().start()
    ex.wait()
    total = stat[...]
    for r in range(4):
        for k in range(2):
            if r or k:
                total = total + stats[2 * zs[r] + (c if k == 0 else 1 - c)]
    inverse = lax.rsqrt(total / (8 * wq_ref.shape[1]) + EPS)
    rq_out[...] = inverse[:8]
    rk_out[...] = inverse[8:]

    def norm_rope(i, carry):
        at = pl.ds(pl.multiple_of(i * HD, HD), HD)
        cosine, sine = cos_ref[at, :], sin_ref[at, :]
        for line, raw, out, gain in ((rq_out, qu_out, q_out, qg_ref), (rk_out, ku_out, k_out, kg_ref)):
            scale = get_column(line[pl.ds(i, 1), :], HD)
            for h in range(heads):
                cols = slice(h * HD, (h + 1) * HD)
                unit = raw[at, cols] * scale
                raw[at, cols] = unit
                normed = unit * gain[:, cols]
                out[at, cols] = (normed * cosine + pltpu.roll(normed, HD // 2, 1) * sine).astype(jnp.bfloat16)
        return carry

    lax.fori_loop(0, 8, norm_rope, 0)

    def attend(zz):
        at = at_of(zz)
        low = jnp.maximum(zz - (WINDOW - 1), 0) * span
        keys_at = pl.ds(pl.multiple_of(low, span), WINDOW * span)
        key_place = low + lax.broadcasted_iota(jnp.int32, (span, WINDOW * span), 1)
        query_place = zz * span + lax.broadcasted_iota(jnp.int32, (span, WINDOW * span), 0)
        allowed = (key_place <= query_place) & (key_place >= first_ref[at, :])
        for h in range(heads):
            cols = slice(h * HD, (h + 1) * HD)
            scores = dot_nt(q_out[at, cols], k_out[keys_at, cols]) * HD**-0.5
            scores = jnp.where(allowed, scores, -1e30)
            top = jnp.max(scores, axis=1, keepdims=True)
            expo = jnp.exp(scores - top)
            probs = expo * (1.0 / jnp.sum(expo, axis=1, keepdims=True))
            mixed_out[at, cols] = jnp.dot(probs.astype(jnp.bfloat16), v_out[keys_at, cols], preferred_element_type=jnp.float32).astype(jnp.bfloat16)
        dt = 1024

        def out(j, carry):
            to = pl.ds(pl.multiple_of(j * dt, dt), dt)
            p = jnp.dot(mixed_out[at, :], wo_ref[:, to], preferred_element_type=jnp.float32)
            parts[pl.ds(2 * zz, 2), :, to] = p.astype(jnp.bfloat16).reshape(2, rows, dt)
            return carry

        lax.fori_loop(0, wide // dt, out, 0)

    attend(zs[3])
    rs.start_core(3)
    attend(zs[2])
    rs.start_core(2)
    rs.add_pair(3)
    rs.pass_on(3)
    attend(zs[1])
    rs.start_core(1)
    rs.add_pair(2)
    rs.pass_on(2)
    rs.add_pair(1)
    rs.pass_on(1)
    attend(zs[0])
    rs.start_core(0)
    rs.add_pair(0)
    xy.pass_on(2)
    xy.pass_on(1)
    rs.relay()
    xy.pass_on(3)
    for r in range(4):
        xy.last(r)
    rs.arrived()

    def ending(i, carry):
        at = pl.ds(pl.multiple_of(i * 32, 32), 32)
        br_ref[at, :] = rs.total(at)
        return carry

    lax.fori_loop(0, rows // 32, ending, 0)
    ag.finish()
    rs.finish()
    xy.finish()


def attention(x_own, w_query, w_key, w_value, w_out, q_gain, k_gain, cosine, sine, first):
    rows, wide = x_own.shape
    head_cols = w_query.shape[1]
    groups, world = 4, 8
    count = world * rows
    vmem = pl.BlockSpec(memory_space=pltpu.VMEM)
    anywhere = pl.BlockSpec(memory_space=pl.ANY)
    bf, f32 = jnp.bfloat16, jnp.float32
    dma = pltpu.SemaphoreType.DMA
    cols = jax.ShapeDtypeStruct((count, head_cols), bf)
    wide_cols = jax.ShapeDtypeStruct((count, head_cols), f32)
    line = jax.ShapeDtypeStruct((8, HD), f32)
    return pl.pallas_call(
        attn_kernel,
        out_shape=(
            jax.ShapeDtypeStruct((rows, wide), f32),
            cols, cols, cols, wide_cols, wide_cols, line, line, cols,
            jax.ShapeDtypeStruct((groups, world, rows, wide), bf),
        ),
        in_specs=[vmem] + [anywhere] * 4 + [vmem] * 5,
        out_specs=(vmem,) * 9 + (pl.BlockSpec(memory_space=pl.ANY),),
        scratch_shapes=[
            pltpu.VMEM((world, rows, wide), bf),
            pltpu.VMEM((world, rows, wide), bf),
            pltpu.VMEM((4, rows, wide), bf),
            pltpu.VMEM((4, rows, wide), bf),
            pltpu.VMEM((16, HD), f32),
            pltpu.VMEM((world, 16, HD), f32),
            pltpu.VMEM((wide, head_cols), bf),
            pltpu.VMEM((wide, head_cols), bf),
            pltpu.VMEM((wide, head_cols), bf),
            pltpu.VMEM((head_cols, wide), bf),
            dma((8,)), dma((8,)), dma((12,)), dma((12,)), dma((24,)), dma((24,)), dma((8,)), dma((8,)),
            pltpu.SemaphoreType.DMA, dma((4,)),
        ],
        compiler_params=pltpu.CompilerParams(
            collective_id=1, has_side_effects=True, vmem_limit_bytes=60 * 2**20
        ),
        name="attn",
    )(x_own, w_query, w_key, w_value, w_out, q_gain.reshape(1, -1), k_gain.reshape(1, -1), cosine, sine, first)


class Background:
    tokens, units = 512, 512

    def __init__(self, hall, gdall, gate_all, up_all, w_down, starts, outs, hbuf, gbuf, gate, up, tile, sums, mids, load_sem, tile_sem, start_sem, out_sem):
        self.hall, self.gdall, self.gate_all, self.up_all, self.w_down, self.starts, self.outs = hall, gdall, gate_all, up_all, w_down, starts, outs
        self.hbuf, self.gbuf, self.gate, self.up, self.tile, self.sums, self.mids = hbuf, gbuf, gate, up, tile, sums, mids
        self.load_sem, self.tile_sem, self.start_sem, self.out_sem = load_sem, tile_sem, start_sem, out_sem
        self.blocks = self.tokens // hall.shape[2]
        self.per_group = hall.shape[1] // self.blocks
        self.per_tile = 3 * self.per_group
        self.tile_count = w_down.shape[0] // self.units
        self.count = self.tile_count * self.per_tile

    def loads(self, n):
        slot, m = n % 2, n % self.per_tile
        group, part = 1 + m // self.per_group, m % self.per_group
        blocks = pl.ds(part * self.blocks, self.blocks)
        rows = pl.ds(part * self.tokens, self.tokens)
        units = pl.ds(n // self.per_tile * self.units, self.units)
        return (
            pltpu.make_async_copy(self.hall.at[group, blocks], self.hbuf.at[slot], self.load_sem.at[0, slot]),
            pltpu.make_async_copy(self.gdall.at[group, blocks], self.gbuf.at[slot], self.load_sem.at[1, slot]),
            pltpu.make_async_copy(self.gate_all.at[group - 1, rows, units], self.gate.at[slot], self.load_sem.at[2, slot]),
            pltpu.make_async_copy(self.up_all.at[group - 1, rows, units], self.up.at[slot], self.load_sem.at[3, slot]),
        )

    def tile_load(self, tile):
        return pltpu.make_async_copy(self.w_down.at[pl.ds(tile * self.units, self.units), :], self.tile, self.tile_sem)

    def moves(self, tile, refs, sem, inward):
        at = pl.ds(tile * self.units, self.units)
        g, u, d = refs
        pairs = zip(self.sums, (g.at[:, at], u.at[:, at], d.at[at, :]))
        return [
            pltpu.make_async_copy(far, near, sem.at[n]) if inward else pltpu.make_async_copy(near, far, sem.at[n])
            for n, (near, far) in enumerate(pairs)
        ]

    def stores(self, tile):
        return self.moves(tile, self.outs, self.out_sem, False)

    def sums_in(self, tile):
        return self.moves(tile, self.starts, self.start_sem, True)

    def begin(self):
        for copy in self.loads(0) + (self.tile_load(0),) + tuple(self.sums_in(0)):
            copy.start()

    def turn(self, tile):
        for copy in self.stores(tile):
            copy.wait()
        for copy in self.sums_in(tile + 1):
            copy.start()

    def step(self, n):
        slot, tile, m = n % 2, n // self.per_tile, n % self.per_tile
        if n + 1 < self.count:
            for copy in self.loads(n + 1):
                copy.start()
        if m == 0:
            self.tile_load(tile).wait()
            for copy in self.sums_in(tile):
                copy.wait()
        for copy in self.loads(n):
            copy.wait()
        hbuf, gbuf, gate, up = self.hbuf.at[slot], self.gbuf.at[slot], self.gate.at[slot], self.up.at[slot]
        wd = self.tile
        act, gg, gu = self.mids
        rows, wide = hbuf.shape[1:]
        g, u = gate[...].astype(jnp.float32), up[...].astype(jnp.float32)
        ga = dot_nt(gbuf[...].reshape(self.tokens, wide), wd[...])
        s = jax.nn.sigmoid(g)
        gs = g * s
        act[...] = (gs * u).astype(jnp.bfloat16)
        gg[...] = (ga * u * s * (1.0 + g * (1.0 - s))).astype(jnp.bfloat16)
        gu[...] = (ga * gs).astype(jnp.bfloat16)
        span = 1024

        def into(i, carry):
            at = pl.ds(pl.multiple_of(i * span, span), span)
            h = hbuf[:, :, at].reshape(self.tokens, span)
            pg = dot_tn(h, gg[...])
            pu = dot_tn(h, gu[...])
            pd = dot_tn(act[...], gbuf[:, :, at].reshape(self.tokens, span))
            self.sums[0][at, :] += pg
            self.sums[1][at, :] += pu
            self.sums[2][:, at] += pd
            return carry

        lax.fori_loop(0, wide // span, into, 0)
        if m == self.per_tile - 1:
            for copy in self.stores(tile):
                copy.start()
            if tile + 1 < self.tile_count:
                self.tile_load(tile + 1).start()

    def finish(self):
        for copy in self.stores(self.tile_count - 1):
            copy.wait()


class SpreadColumns:
    def __init__(self, own, whole, send, recv, own_sem, place):
        self.src, self.whole, self.send, self.recv, self.own_sem = own, whole, send, recv, own_sem
        self.d, self.dx, self.dy, self.zs, self.c, _ = place
        self.t = 2 * self.zs[0] + self.c

    def own(self, p, k):
        return remote(self.src.at[p], self.whole.at[1 + k, p], self.send.at[k * 3 + p], self.recv.at[k * 3 + p], (self.dx, self.dy)[k], self.t)

    def hop(self, p, b):
        half = self.src.shape[1] // 2
        at = pl.ds(b * half, half)
        return remote(self.whole.at[1 + b, p, at], self.whole.at[3, p, at], self.send.at[6 + 2 * p + b], self.recv.at[6 + 2 * p + b], (self.dy, self.dx)[b], self.t)

    def start(self, p):
        self.own(p, 0).start()
        self.own(p, 1).start()

    def pass_on(self, p):
        for b in range(2):
            self.own(p, b).wait_recv()
            self.hop(p, b).start()

    def keep(self):
        return pltpu.make_async_copy(self.src, self.whole.at[0], self.own_sem)

    def finish(self):
        for p in range(3):
            for b in range(2):
                self.own(p, b).wait_send()
                self.hop(p, b).wait()
        self.keep().wait()


class SumHalves:
    def __init__(self, buf, once, twice, send, recv, place):
        self.buf, self.land, self.send, self.recv = buf, (once, twice), send, recv
        self.d, self.dx, self.dy, self.zs, self.c, _ = place
        self.t = 2 * self.zs[0] + self.c

    def move(self, stage, b):
        at = 2 * stage + b
        return remote(self.buf.at[b], self.land[stage].at[b], self.send.at[at], self.recv.at[at], (self.dx, self.dy)[(stage + b) % 2], self.t)

    def start(self, stage):
        for b in range(2):
            self.move(stage, b).start()

    def add(self, stage):
        for b in range(2):
            self.move(stage, b).wait()
            add_into(self.buf.at[b], self.land[stage].at[b])


class ExchangeGroups:
    def __init__(self, block, land, send, recv, place):
        self.block, self.land, self.send, self.recv = block, land, send, recv
        d, dx, dy, zs, c, _ = place
        self.peers, self.t = (dx, dy, 3 - d), 2 * zs[0] + c

    def copies(self):
        return [remote(self.block, self.land.at[k], self.send.at[k], self.recv.at[k], peer, self.t) for k, peer in enumerate(self.peers)]

    def start(self):
        for copy in self.copies():
            copy.start()

    def wait(self):
        for copy in self.copies():
            copy.wait()


def back_kernel(
    gb_ref, gh_ref, q_hbm, k_hbm, v_hbm, mixed_hbm, qu_hbm, ku_hbm, rq_ref, rk_ref, first_ref, cos_ref, sin_ref,
    qg_ref, kg_ref, wq_hbm, wk_hbm, wv_hbm, wo_hbm, gains_ref, hall, gdall, gate_all, up_all, w_down, own_g, own_u, own_d,
    gt_ref, gains_out, dwo_ref, gall_ref, dwg, dwu, dwd,
    full, pair, land, gm, dq, dk, dv, own, wo_once, wo_twice, stat, stats, gland, block, blocks, gacc,
    hbuf, gbuf, gbf, ubf, td, sg, su, sd, act, gg, gu,
    q_ref, k_ref, v_ref, mixed_ref, qu_ref, ku_ref, wq_ref, wk_ref, wv_ref, wo_ref,
    ag_send, ag_recv, rs_send, rs_recv, st_send, st_recv, ga_send, ga_recv, gr_send, gr_recv,
    co_send, co_recv, wo_send, wo_recv, own_sem, load_sem, tile_sem, start_sem, out_sem, input_sem,
):
    place = places_of()
    d, dx, dy, zs, c, inner = place
    t = 2 * zs[0] + c
    rows, wide = gb_ref.shape
    span = 2 * rows
    heads = wq_ref.shape[1] // HD
    count = q_ref.shape[0]
    scale = HD**-0.5
    inputs = Loads(
        (
            (wo_hbm, wo_ref), (mixed_hbm, mixed_ref), (q_hbm, q_ref), (k_hbm, k_ref), (v_hbm, v_ref), (qu_hbm, qu_ref), (ku_hbm, ku_ref),
            (wq_hbm, wq_ref), (wk_hbm, wk_ref), (wv_hbm, wv_ref),
        ),
        input_sem,
    )
    work = Background(
        hall, gdall, gate_all, up_all, w_down, (own_g, own_u, own_d), (dwg, dwu, dwd), hbuf, gbuf, gbf, ubf, td, (sg, su, sd), (act, gg, gu),
        load_sem, tile_sem, start_sem, out_sem,
    )
    work.begin()
    inputs.start()
    full[t] = gb_ref[...]
    barrier = pltpu.get_barrier_semaphore()
    peers = [(d, 2 * zs[r] + c) for r in (1, 2, 3)] + [(d, 2 * zs[r] + 1 - c) for r in range(4)]
    peers += [(dx, t), (dy, t), (3 - d, t)]
    for peer in peers:
        pl.semaphore_signal(barrier, inc=1, device_id=peer, device_id_type=MESH)
    pl.semaphore_wait(barrier, len(peers))
    ag = Gather(full, ag_send, ag_recv, place)
    rs = Scatter(full, pair, land, rs_send, rs_recv, place)
    ex = Exchange(stat, stats, st_send, st_recv, place)
    gains = Exchange(gains_ref, gland, ga_send, ga_recv, place)
    groups = ExchangeGroups(block, blocks, gr_send, gr_recv, place)
    cols_all = SpreadColumns(own, gall_ref, co_send, co_recv, own_sem, place)
    wo_sum = SumHalves(dwo_ref, wo_once, wo_twice, wo_send, wo_recv, place)
    def at_of(zz):
        return pl.ds(pl.multiple_of(zz * span, span), span)

    ag.start()
    gains.start()
    def out_back(j, carry):
        to = pl.ds(pl.multiple_of(j * 512, 512), 512)
        p = dot_tn(mixed_ref[...], full[:, :, to].reshape(count, 512))
        dwo_ref[:, :, to] = p.astype(jnp.bfloat16).reshape(2, p.shape[0] // 2, 512)
        return carry

    def attend_back(zz):
        at = at_of(zz)
        gm[at, :] = dot_nt(full[pl.ds(2 * zz, 2)].reshape(span, wide), wo_ref[...]).astype(jnp.bfloat16)
        low = jnp.maximum(zz - (WINDOW - 1), 0) * span
        keys_at = pl.ds(pl.multiple_of(low, span), WINDOW * span)
        key_place = low + lax.broadcasted_iota(jnp.int32, (span, WINDOW * span), 1)
        query_place = zz * span + lax.broadcasted_iota(jnp.int32, (span, WINDOW * span), 0)
        allowed = (key_place <= query_place) & (key_place >= first_ref[at, :])
        for h in range(heads):
            cols = slice(h * HD, (h + 1) * HD)
            scores = dot_nt(q_ref[at, cols], k_ref[keys_at, cols]) * scale
            scores = jnp.where(allowed, scores, -1e30)
            top = jnp.max(scores, axis=1, keepdims=True)
            expo = jnp.exp(scores - top)
            probs = expo * (1.0 / jnp.sum(expo, axis=1, keepdims=True))
            grad = gm[at, cols]
            gp = dot_nt(grad, v_ref[keys_at, cols])
            gs = (probs * (gp - jnp.sum(probs * gp, axis=1, keepdims=True))).astype(jnp.bfloat16)
            dq[at, cols] = jnp.dot(gs, k_ref[keys_at, cols], preferred_element_type=jnp.float32) * scale
            dk[keys_at, cols] += dot_tn(gs, q_ref[at, cols]) * scale
            dv[keys_at, cols] += dot_tn(probs.astype(jnp.bfloat16), grad)

    dk[...] = jnp.zeros_like(dk)
    dv[...] = jnp.zeros_like(dv)
    work.step(0)
    ag.ready(0)
    inputs.wait(*range(10))
    attend_back(zs[0])
    work.step(1)
    work.step(2)
    ag.start_inner()
    ag.arrive(2)
    ag.arrive(1)
    work.step(3)
    ag.ready(2)
    attend_back(zs[2])
    ag.ready(1)
    attend_back(zs[1])
    ag.arrive(3)
    work.step(4)
    ag.ready(3)
    attend_back(zs[3])
    own[2] = dv[...].astype(jnp.bfloat16)
    cols_all.start(2)
    gacc[...] = jnp.zeros_like(gacc)

    def unrope(i, carry):
        at = pl.ds(pl.multiple_of(i * HD, HD), HD)
        cosine, sine = cos_ref[at, :], sin_ref[at, :]
        for n, (grad, unit_ref, gain) in enumerate(((dq, qu_ref, qg_ref), (dk, ku_ref, kg_ref))):
            total = jnp.zeros((HD, HD), jnp.float32)
            for h in range(heads):
                cols = slice(h * HD, (h + 1) * HD)
                value = grad[at, cols].astype(jnp.bfloat16).astype(jnp.float32)
                value = value * cosine - pltpu.roll(value, HD // 2, 1) * sine
                unit = unit_ref[at, cols]
                row = n * heads + h
                gacc[row : row + 1, :] += jnp.sum(value * unit, axis=0, keepdims=True)
                value = value * gain[:, cols]
                grad[at, cols] = value
                total = total + value * unit
            stat[pl.ds(8 * n + i, 1), :] = jnp.sum(total.T, axis=0, keepdims=True)
        return carry

    lax.fori_loop(0, count // HD, unrope, 0)
    ex.start()
    gains.wait()
    total = gains_ref[...]
    for r in range(4):
        for k in range(2):
            if r or k:
                total = total + gland[2 * zs[r] + (c if k == 0 else 1 - c)]
    lines = gains_ref.shape[0]
    block[:lines, :] = total
    block[lines:, :] = gacc[...]
    groups.start()
    lax.fori_loop(0, wide // 512, out_back, 0)
    wo_sum.start(0)
    ag.finish()
    work.step(5)
    ex.wait()
    total = stat[...]
    for r in range(4):
        for k in range(2):
            if r or k:
                total = total + stats[2 * zs[r] + (c if k == 0 else 1 - c)]
    stat[...] = total * (1.0 / (8 * wq_ref.shape[1]))

    def norm_back_rows(i, carry):
        at = pl.ds(pl.multiple_of(i * HD, HD), HD)
        for n, (grad, unit_ref, inv_ref) in enumerate(((dq, qu_ref, rq_ref), (dk, ku_ref, rk_ref))):
            mean = get_column(stat[pl.ds(8 * n + i, 1), :], HD)
            inverse = get_column(inv_ref[pl.ds(i, 1), :], HD)
            for h in range(heads):
                cols = slice(h * HD, (h + 1) * HD)
                own[n, at, cols] = (inverse * (grad[at, cols] - unit_ref[at, cols] * mean)).astype(jnp.bfloat16)
        return carry

    lax.fori_loop(0, count // HD, norm_back_rows, 0)
    cols_all.start(0)
    cols_all.start(1)
    cols_all.keep().start()

    def tokens_back(zz):
        at = at_of(zz)
        dt = 1024

        def out(j, carry):
            to = pl.ds(pl.multiple_of(j * dt, dt), dt)
            p = dot_nt(own[0, at, :], wq_ref[to, :]) + dot_nt(own[1, at, :], wk_ref[to, :]) + dot_nt(own[2, at, :], wv_ref[to, :])
            full[pl.ds(2 * zz, 2), :, to] = p.astype(jnp.bfloat16).reshape(2, rows, dt)
            return carry

        lax.fori_loop(0, wide // dt, out, 0)

    tokens_back(zs[3])
    rs.start_core(3)
    work.turn(0)
    tokens_back(zs[2])
    rs.start_core(2)
    rs.add_pair(3)
    rs.pass_on(3)
    tokens_back(zs[1])
    rs.start_core(1)
    rs.add_pair(2)
    rs.pass_on(2)
    rs.add_pair(1)
    rs.pass_on(1)
    tokens_back(zs[0])
    rs.start_core(0)
    rs.add_pair(0)
    cols_all.pass_on(2)
    work.step(6)
    rs.relay()
    work.step(7)
    wo_sum.add(0)
    wo_sum.start(1)
    work.step(8)
    work.step(9)
    cols_all.pass_on(0)
    work.step(10)
    cols_all.pass_on(1)
    work.step(11)
    wo_sum.add(1)
    rs.arrived()

    def ending(i, carry):
        at = pl.ds(pl.multiple_of(i * 32, 32), 32)
        gt_ref[at, :] = gh_ref[at, :] + rs.total(at)
        return carry

    lax.fori_loop(0, rows // 32, ending, 0)
    groups.wait()
    gains_out[...] = block[...] + blocks[0] + blocks[1] + blocks[2]
    rs.finish()
    cols_all.finish()
    work.finish()


def backward(grad_branch, grad_hidden, kept, first, cosine, signed, q_gain, k_gain, weights, gains, h_all, gd_all, gate_all, up_all, w_down, own_parts):
    queries, keys, values, mixed, q_unit, k_unit, q_inverse, k_inverse = kept
    rows, wide = grad_branch.shape
    count, head_cols = queries.shape
    heads = head_cols // HD
    world = 8
    width = w_down.shape[0]
    lines = gains.shape[0]
    vmem = pl.BlockSpec(memory_space=pltpu.VMEM)
    anywhere = pl.BlockSpec(memory_space=pl.ANY)
    bf, f32 = jnp.bfloat16, jnp.float32
    dma = pltpu.SemaphoreType.DMA
    tok, unit = Background.tokens, Background.units
    return pl.pallas_call(
        back_kernel,
        out_shape=(
            jax.ShapeDtypeStruct((rows, wide), f32),
            jax.ShapeDtypeStruct((lines + 8, HD), f32),
            jax.ShapeDtypeStruct((2, head_cols // 2, wide), bf),
            jax.ShapeDtypeStruct((4, 3, count, head_cols), bf),
            jax.ShapeDtypeStruct((wide, width), f32),
            jax.ShapeDtypeStruct((wide, width), f32),
            jax.ShapeDtypeStruct((width, wide), f32),
        ),
        in_specs=[vmem] * 2 + [anywhere] * 6 + [vmem] * 7 + [anywhere] * 4 + [vmem] + [anywhere] * 8,
        out_specs=(vmem, vmem, vmem) + (anywhere,) * 4,
        scratch_shapes=[
            pltpu.VMEM((world, rows, wide), bf),
            pltpu.VMEM((4, rows, wide), bf),
            pltpu.VMEM((4, rows, wide), bf),
            pltpu.VMEM((count, head_cols), bf),
            pltpu.VMEM((count, head_cols), f32),
            pltpu.VMEM((count, head_cols), f32),
            pltpu.VMEM((count, head_cols), f32),
            pltpu.VMEM((3, count, head_cols), bf),
            pltpu.VMEM((2, head_cols // 2, wide), bf),
            pltpu.VMEM((2, head_cols // 2, wide), bf),
            pltpu.VMEM((16, HD), f32),
            pltpu.VMEM((world, 16, HD), f32),
            pltpu.VMEM((world, lines, HD), f32),
            pltpu.VMEM((lines + 8, HD), f32),
            pltpu.VMEM((3, lines + 8, HD), f32),
            pltpu.VMEM((8, HD), f32),
            pltpu.VMEM((2, tok // rows, rows, wide), bf),
            pltpu.VMEM((2, tok // rows, rows, wide), bf),
            pltpu.VMEM((2, tok, unit), bf),
            pltpu.VMEM((2, tok, unit), bf),
            pltpu.VMEM((unit, wide), bf),
            pltpu.VMEM((wide, unit), f32),
            pltpu.VMEM((wide, unit), f32),
            pltpu.VMEM((unit, wide), f32),
            pltpu.VMEM((tok, unit), bf),
            pltpu.VMEM((tok, unit), bf),
            pltpu.VMEM((tok, unit), bf),
            pltpu.VMEM((count, head_cols), bf),
            pltpu.VMEM((count, head_cols), bf),
            pltpu.VMEM((count, head_cols), bf),
            pltpu.VMEM((count, head_cols), bf),
            pltpu.VMEM((count, head_cols), f32),
            pltpu.VMEM((count, head_cols), f32),
            pltpu.VMEM((wide, head_cols), bf),
            pltpu.VMEM((wide, head_cols), bf),
            pltpu.VMEM((wide, head_cols), bf),
            pltpu.VMEM((head_cols, wide), bf),
            dma((8,)), dma((8,)), dma((12,)), dma((12,)), dma((8,)), dma((8,)), dma((8,)), dma((8,)), dma((3,)), dma((3,)),
            dma((12,)), dma((12,)), dma((4,)), dma((4,)), pltpu.SemaphoreType.DMA, dma((4, 2)), pltpu.SemaphoreType.DMA, dma((3,)), dma((3,)), dma((10,)),
        ],
        compiler_params=pltpu.CompilerParams(
            collective_id=3, has_side_effects=True, vmem_limit_bytes=62 * 2**20
        ),
        name="back",
    )(
        grad_branch, grad_hidden, queries, keys, values, mixed, q_unit, k_unit, q_inverse, k_inverse, first, cosine, signed,
        q_gain.reshape(1, -1), k_gain.reshape(1, -1), *weights, gains, h_all, gd_all, gate_all, up_all, w_down, *own_parts,
    )


def tail_kernel(
    pg_ref, pu_ref, pd_ref, x_ref, g_ref, wo_ref, gains_ref, og_ref, ou_ref, od_ref, oq_ref, ok_ref, ov_ref, oo_ref, *gain_refs
):
    count, cols = g_ref.shape[2], x_ref.shape[-1]
    og_ref[...] = pg_ref[...]
    ou_ref[...] = pu_ref[...]
    od_ref[...] = pd_ref[...]
    oo_ref[...] = wo_ref[...].reshape(oo_ref.shape).astype(jnp.float32)
    row = 0
    for out in gain_refs:
        out[...] = gains_ref[row : row + out.shape[0], :]
        row += out.shape[0]
    for p, out in enumerate((oq_ref, ok_ref, ov_ref)):
        total = jnp.zeros(out.shape, jnp.float32)
        for g in range(4):
            total = total + dot_tn(x_ref[g].reshape(count, cols), g_ref[g, p])
        out[...] = total


def weight_tail(parts, x_all, grad_qkv, grad_out, gains):
    groups, world, rows, wide = x_all.shape
    count, width = world * rows, parts[0].shape[1]
    head_cols = grad_qkv.shape[-1]
    cols = 512
    f32 = jnp.float32
    down = pl.BlockSpec((cols, width), lambda i: (i, 0))
    across = pl.BlockSpec((width, cols), lambda i: (0, i))
    heads = pl.BlockSpec((cols, head_cols), lambda i: (i, 0))
    lines = [(wide // HD, HD)] * 2 + [(head_cols // HD, HD)] * 2
    return pl.pallas_call(
        tail_kernel,
        grid=(wide // cols,),
        in_specs=[
            down, down, across,
            pl.BlockSpec((groups, world, rows, cols), lambda i: (0, 0, 0, i)),
            pl.BlockSpec(grad_qkv.shape, lambda i: (0, 0, 0, 0)),
            pl.BlockSpec((2, head_cols // 2, cols), lambda i: (0, 0, i)),
            pl.BlockSpec(gains.shape, lambda i: (0, 0)),
        ],
        out_specs=(down, down, across, heads, heads, heads, pl.BlockSpec((head_cols, cols), lambda i: (0, i)))
        + tuple(pl.BlockSpec(shape, lambda i: (0, 0)) for shape in lines),
        out_shape=(
            jax.ShapeDtypeStruct((wide, width), f32),
            jax.ShapeDtypeStruct((wide, width), f32),
            jax.ShapeDtypeStruct((width, wide), f32),
        )
        + (jax.ShapeDtypeStruct((wide, head_cols), f32),) * 3
        + (jax.ShapeDtypeStruct((head_cols, wide), f32),)
        + tuple(jax.ShapeDtypeStruct(shape, f32) for shape in lines),
        compiler_params=pltpu.CompilerParams(vmem_limit_bytes=60 * 2**20),
        cost_estimate=pl.CostEstimate(
            flops=2 * count * wide * 3 * groups * head_cols, bytes_accessed=100 * 2**20, transcendentals=0
        ),
        name="tail",
    )(*parts, x_all, grad_qkv, grad_out, gains)


def on_device_fused(
    tokens,
    segment_ids,
    w_query,
    w_key,
    w_value,
    w_out,
    w_gate,
    w_up,
    w_down,
    q_gain,
    k_gain,
    attn_gain,
    ffn_gain,
    cotangent,
):
    wide = tokens.shape[1]
    token_count = segment_ids.shape[0] * segment_ids.shape[1]
    head_cols = w_query.shape[1]
    first = jnp.sum((segment_ids[:, None, :] < segment_ids[:, :, None]).astype(jnp.int32), axis=2).reshape(token_count, 1)
    half = HD // 2
    freq = THETA ** (-(jnp.arange(half, dtype=jnp.float32) * 2.0 / HD))
    angle = (jnp.arange(token_count, dtype=jnp.int32)[:, None] - first).astype(jnp.float32) * jnp.concatenate([-freq, freq])[None, :]
    cosine, signed = jnp.cos(angle), jnp.sin(angle)
    branch, queries, keys, values, q_unit, k_unit, q_inverse, k_inverse, mixed, x_all = attention(
        tokens, w_query, w_key, w_value, w_out, q_gain, k_gain, cosine, signed, first
    )
    block_out, grad_hidden, grad_branch, gains, h_all, gd_all, own_gate, own_up, own_down, gate_all, up_all = ffn(
        tokens, branch, cotangent, attn_gain, ffn_gain, w_gate, w_up, w_down
    )
    grad_tokens, gains, grad_w_out, grad_qkv, part_gate, part_up, part_down = backward(
        grad_branch, grad_hidden, (queries, keys, values, mixed, q_unit, k_unit, q_inverse, k_inverse),
        first, cosine, signed, q_gain, k_gain, (w_query, w_key, w_value, w_out), gains, h_all, gd_all, gate_all, up_all, w_down,
        (own_gate, own_up, own_down),
    )
    *grad_weights, grad_ffn_gain, grad_attn_gain, grad_q_gain, grad_k_gain = weight_tail(
        (part_gate, part_up, part_down), x_all, grad_qkv, grad_w_out, gains
    )
    grad_w_gate, grad_w_up, grad_w_down, grad_w_query, grad_w_key, grad_w_value, grad_w_out = grad_weights
    return (
        block_out,
        grad_tokens,
        grad_w_query,
        grad_w_key,
        grad_w_value,
        grad_w_out,
        grad_w_gate,
        grad_w_up,
        grad_w_down,
        grad_q_gain.reshape(head_cols),
        grad_k_gain.reshape(head_cols),
        grad_attn_gain.reshape(wide),
        grad_ffn_gain.reshape(wide),
    )


def solution(mesh):
    placed = (
        P(("dp", "tensor"), None),
        P("dp", None),
        P(None, "tensor"),
        P(None, "tensor"),
        P(None, "tensor"),
        P("tensor", None),
        P(None, "tensor"),
        P(None, "tensor"),
        P("tensor", None),
        P("tensor"),
        P("tensor"),
        P(),
        P(),
        P(("dp", "tensor"), None),
    )
    return jax.shard_map(
        on_device_fused if dict(mesh.shape) == {"dp": 4, "tensor": 8} else on_device,
        mesh=mesh,
        in_specs=placed,
        out_specs=(
            P(("dp", "tensor"), None),
            P(("dp", "tensor"), None),
            P(None, "tensor"),
            P(None, "tensor"),
            P(None, "tensor"),
            P("tensor", None),
            P(None, "tensor"),
            P(None, "tensor"),
            P("tensor", None),
            P("tensor"),
            P("tensor"),
            P(),
            P(),
        ),
        check_vma=False,
    )
```
